128 devices in a mesh: ctx: 32 (over z, x, core), exp: 4 (over y).
Axes of the slice: x: 4, y: 4, z: 4, core: 2. Of those that a mesh axis runs over, the one named last changes fastest.
Arguments:
- hidden_in: bfloat16 [16384, 1024], P('ctx'), may hold values from -6 to 6
- teacher: bfloat16 [16384, 1024], P(('ctx', 'exp')), may hold values from -6 to 6
- valid: int32 [16384], replicated, may hold values from 0 to 1, as said below
- block_of: int32 [128], replicated, may hold values from 0 to 127, as said below
- routes: int32 [16384, 8], P(('ctx', 'exp')), may hold values from 0 to 31, all different within a row; in each aligned block of 128 rows (0 to 127, 128 to 255, ...) at most 40 rows name the same one
- gates: float32 [16384, 8], P(('ctx', 'exp')), may hold values from 0.5 to 2
- w_query: bfloat16 [1024, 1024], P('ctx', 'exp'), may hold values from -0.1875 to 0.1875
- w_key: bfloat16 [1024, 512], P('ctx', 'exp'), may hold values from -0.1875 to 0.1875
- w_value: bfloat16 [1024, 512], P('ctx', 'exp'), may hold values from -0.1875 to 0.1875
- w_out: bfloat16 [1024, 1024], P('ctx', 'exp'), may hold values from -4 to 4
- gain_attn: bfloat16 [1024], P('ctx'), may hold values from 0.5 to 1.5
- gain_query: bfloat16 [1024], P('ctx'), may hold values from 0.5 to 1.5
- gain_key: bfloat16 [512], P('ctx'), may hold values from 0.5 to 1.5
- gain_ffn: bfloat16 [1024], P('ctx'), may hold values from 0.5 to 1.5
- w_gate: bfloat16 [32, 1024, 512], P('ctx', None, 'exp'), may hold values from -0.1875 to 0.1875
- w_up: bfloat16 [32, 1024, 512], P('ctx', None, 'exp'), may hold values from -0.1875 to 0.1875
- w_down: bfloat16 [32, 512, 1024], P('ctx', 'exp'), may hold values from -0.25 to 0.25
Outputs:
- block_out: float32 [16384, 1024], P(('ctx', 'exp'))
- loss: float32 [], replicated
- grad_hidden: float32 [16384, 1024], P(('ctx', 'exp'))
- grad_w_query: float32 [1024, 1024], P('ctx', 'exp')
- grad_w_key: float32 [1024, 512], P('ctx', 'exp')
- grad_w_value: float32 [1024, 512], P('ctx', 'exp')
- grad_w_out: float32 [1024, 1024], P('ctx', 'exp')
- grad_gain_attn: float32 [1024], P('ctx')
- grad_gain_query: float32 [1024], P('ctx')
- grad_gain_key: float32 [512], P('ctx')
- grad_gain_ffn: float32 [1024], P('ctx')
- grad_w_gate: float32 [32, 1024, 512], P('ctx', None, 'exp')
- grad_w_up: float32 [32, 1024, 512], P('ctx', None, 'exp')
- grad_w_down: float32 [32, 512, 1024], P('ctx', 'exp')
The draws below stay inside these ranges and needn't reach their ends.
Inputs may be any that keep to these rules, and one draw needn't show every extreme that they name: `valid`: the first of every 128 stored rows is 1. `block_of`: A permutation of the 128 logical blocks. Logical blocks below 64 hold the prompt in order; the others hold whole continuations of 1024 tokens in order. Each run of 4 stored blocks (one index of ctx) holds 2 prompt blocks followed by 2 continuation blocks. `routes`: each row names 8 different experts. In each aligned block of 128 rows (the rows of one device) no expert is named by more than 40 rows, and in some block an expert is named by exactly 40 rows.
All inputs are finite; a program needn't handle non-finite values.
Results may differ from the reference program's by a relative error of at most 0.014.
Values may be sent and summed in bfloat16 or wider, within the bound.
No kernel may reach another device: no remote copies, remote signals or barrier semaphores. Data moves between devices by JAX's collectives and lax.ppermute only.
A program may use at most 384 MiB of HBM per device.

```python
import math
import jax
import jax.numpy as jnp
import numpy as np
from jax import lax

D = 1024
HEADS = 16
KV_HEADS = 8
HD = 64
FF = 512
EXPERTS = 32
TOP = 8
BLK = 128
CONT_LEN = 1024
SEQ_BLK = 2
TOKENS = 16384
NBLK = 128
TOK_DEV = 128
MOST = 40
N_CTX = 32
N_EXP = 4


def draw_valid(key, part):
    key = jax.random.fold_in(key, 11)
    draws = jax.random.randint(key, (TOKENS,), 0, 1000)
    row_ids = jnp.arange(TOKENS, dtype=jnp.int32)
    limit = 250 + 500 * row_ids // TOKENS
    first_row = row_ids % BLK == 0
    return jnp.where((draws < limit) | first_row, 1, 0).astype(jnp.int32)


def draw_block_of(key, part):
    key = jax.random.fold_in(key, 23)
    key_one, key_two = jax.random.split(key)
    half_count = NBLK // 2
    prompt_blocks = jax.random.permutation(key_one, half_count).reshape(-1, SEQ_BLK)
    cont_blocks = (jax.random.permutation(key_two, half_count) + half_count).reshape(-1, SEQ_BLK)
    return jnp.concatenate([prompt_blocks, cont_blocks], axis=1).reshape(NBLK).astype(jnp.int32)


def shard_levels(own_key, shape, shards, low, high):
    level = 1.0
    for dim, blocks in shards:
        steps = jax.random.uniform(jax.random.fold_in(jax.random.fold_in(own_key, 6), dim), (blocks,), jnp.float32, low / len(shards), high / len(shards))
        level = level * jnp.repeat(jnp.exp(steps), shape[dim] // blocks).reshape((-1,) + (1,) * (len(shape) - 1 - dim))
    return level


def assign_block(own_key, own, number, rows, amount, top, most, slope):
    sequence = jax.random.permutation(own_key, amount)
    packed, common = portions_of(amount, rows * top, most, slope, True), portions_of(amount, rows * top, most, slope, False)
    places = jnp.arange(amount)

    def named(lengths, turn):
        used = int((lengths > 0).sum())
        fixed = max(1, used // 4)
        passed = fixed + (places - fixed + turn * (used - fixed)) % max(1, amount - fixed)
        return jnp.zeros((amount,), jnp.int32).at[sequence[jnp.where(places < fixed, places, passed)]].set(jnp.asarray(lengths, jnp.int32))

    lengths = jnp.where(number % 4 == 0, named(packed, number // 4), named(common, number - number // 4 - 1))
    mixed = jax.random.permutation(jax.random.fold_in(own, 3), amount)
    source_of, sink = mixed[0:amount // 2 * 2:2], mixed[1:amount // 2 * 2:2]
    room = jnp.minimum(lengths[source_of] - 1, most - lengths[sink]) // 2
    room = jnp.where((source_of == sequence[0]) | (sink == sequence[0]) | (lengths[sink] == 0), 0, jnp.maximum(room, 0))
    passed = jax.random.randint(jax.random.fold_in(own, 4), (amount // 2,), 0, 1 << 20) % (room + 1)
    lengths = lengths.at[source_of].add(-passed).at[sink].add(passed)
    labels = jnp.searchsorted(jnp.cumsum(lengths), jnp.arange(rows * top), side="right").astype(jnp.int32)
    table = labels.reshape(top, rows).T
    table = table[jax.random.permutation(jax.random.fold_in(own, 1), rows)]
    turn = jax.random.randint(jax.random.fold_in(own, 2), (rows, 1), 0, top)
    return jnp.take_along_axis(table, (jnp.arange(top)[None, :] + turn) % top, axis=1)


def portions_of(count, total, bound, lean, full):
    portions = [(1 << 20) // math.isqrt(rank ** lean) + 1 for rank in range(1, count + 1)]
    largest = bound if full else min(bound, max(-(-total // count), total * portions[0] // sum(portions)))
    least = 1 if total - largest >= count - 1 else 0
    counts, spare = [largest] + [least] * (count - 1), total - largest - least * (count - 1)
    while spare > 0:
        movable = [i for i in range(1, count) if counts[i] < largest] or [i for i in range(1, count) if counts[i] < bound]
        mass, left = sum([portions[i] for i in movable]), spare
        for i in movable:
            extra = min(bound - counts[i], max(1, left * portions[i] // mass), spare)
            counts[i] = counts[i] + extra
            spare = spare - extra
    return np.array(counts)


def normal_values(own_key, extent, spread, most, shards=(), kind=jnp.bfloat16):
    drawn = jax.random.normal(own_key, extent, jnp.float32) * spread
    if len(shards) > 0:
        drawn = shard_levels(own_key, extent, shards, -0.22, 0.18) * drawn
    return jnp.clip(drawn, min=-most, max=most).astype(kind)


def setup_inputs(seed: int = 0) -> dict:
    arg_keys = jax.random.split(jax.random.key(seed), 18)
    hidden_in = normal_values(arg_keys[0], (TOKENS, D), 1.0, 6.0, ((0, 32),))
    teacher = normal_values(arg_keys[1], (TOKENS, D), 1.0, 6.0, ((0, 128),))
    valid = draw_valid(jax.random.fold_in(arg_keys[17], 71), 0)
    block_of = draw_block_of(jax.random.fold_in(arg_keys[17], 71), 0)
    routes_keys = jax.random.split(jax.random.fold_in(arg_keys[4], 1), TOKENS // TOK_DEV)
    routes_turns = jax.random.permutation(jax.random.fold_in(arg_keys[4], 3), TOKENS // TOK_DEV)
    routes = jax.vmap(lambda own, number: assign_block(jax.random.fold_in(arg_keys[4], 2), own, number, TOK_DEV, EXPERTS, TOP, MOST, 1))(routes_keys, routes_turns).reshape((TOKENS, TOP))
    gates = jnp.clip(jnp.exp(math.log(2.0) - 1.3862944 * jax.random.uniform(arg_keys[5], (TOKENS, TOP), jnp.float32) ** shard_levels(arg_keys[5], (TOKENS, TOP), ((0, 128),), -0.2, 0.2)), 0.5, 2.0)
    w_query = normal_values(arg_keys[6], (D, HEADS * HD), D ** -0.5, 0.1875, ((0, 32), (1, 4)))
    w_key = normal_values(arg_keys[7], (D, KV_HEADS * HD), D ** -0.5, 0.1875, ((0, 32), (1, 4)))
    w_value = normal_values(arg_keys[8], (D, KV_HEADS * HD), D ** -0.5, 0.1875, ((0, 32), (1, 4)))
    w_out = normal_values(arg_keys[9], (D, HEADS * HD), (max(1, D // 512)) ** -0.5, 4.0, ((0, 32), (1, 4)))
    gain_attn = jnp.clip(1.0 + 0.1 * jax.random.normal(arg_keys[10], (D,), jnp.float32), 0.5, 1.5).astype(jnp.bfloat16)
    gain_query = jnp.clip(1.0 + 0.1 * jax.random.normal(arg_keys[11], (HEADS * HD,), jnp.float32), 0.5, 1.5).astype(jnp.bfloat16)
    gain_key = jnp.clip(1.0 + 0.1 * jax.random.normal(arg_keys[12], (KV_HEADS * HD,), jnp.float32), 0.5, 1.5).astype(jnp.bfloat16)
    gain_ffn = jnp.clip(1.0 + 0.1 * jax.random.normal(arg_keys[13], (D,), jnp.float32), 0.5, 1.5).astype(jnp.bfloat16)
    w_gate = normal_values(arg_keys[14], (EXPERTS, D, FF), D ** -0.5, 0.1875, ((0, 32), (2, 4)))
    w_up = normal_values(arg_keys[15], (EXPERTS, D, FF), D ** -0.5, 0.1875, ((0, 32), (2, 4)))
    w_down = normal_values(arg_keys[16], (EXPERTS, FF, D), FF ** -0.5, 0.25, ((0, 32), (1, 4)))
    return {"hidden_in": hidden_in, "teacher": teacher, "valid": valid, "block_of": block_of, "routes": routes, "gates": gates, "w_query": w_query, "w_key": w_key, "w_value": w_value, "w_out": w_out, "gain_attn": gain_attn, "gain_query": gain_query, "gain_key": gain_key, "gain_ffn": gain_ffn, "w_gate": w_gate, "w_up": w_up, "w_down": w_down}


NORM_EPSILON = 1e-05
ROPE_BASE = 10000.0
MASK_FLOOR = -1e+30
HIGHEST = lax.Precision.HIGHEST

@jax.custom_vjp
def low(v):
    return lax.optimization_barrier(v.astype(jnp.bfloat16)).astype(jnp.float32)

@jax.custom_vjp
def low_back(v):
    return v

def low_keep(v):
    return (low(v), None)

def low_pass(kept, grad):
    return (grad,)

def back_keep(v):
    return (v, None)

def back_low(kept, grad):
    return (low(grad),)
low.defvjp(low_keep, low_pass)
low_back.defvjp(back_keep, back_low)

def inverse_rms(values):
    return lax.rsqrt(lax.optimization_barrier(jnp.mean(values * values, axis=-1, keepdims=True)) + NORM_EPSILON)

def matmul(left, right):
    return jnp.dot(left, right, precision=HIGHEST, preferred_element_type=jnp.float32)

def token_places(block_table):
    prompt_len = TOKENS // 2
    row_ids = jnp.arange(TOKENS, dtype=jnp.int32)
    logical = block_table.astype(jnp.int32)[row_ids // BLK]
    token_ids = logical * BLK + row_ids % BLK
    in_cont = token_ids >= prompt_len
    seq_ids = jnp.where(in_cont, 1 + (token_ids - prompt_len) // CONT_LEN, 0)
    position = jnp.where(in_cont, prompt_len + (token_ids - prompt_len) % CONT_LEN, token_ids)
    return (seq_ids.astype(jnp.int32), position.astype(jnp.float32))

def rope_tables(position):
    half_dim = HD // 2
    frequency = ROPE_BASE ** (-(jnp.arange(half_dim, dtype=jnp.float32) * 2.0 / HD))
    angles = position[:, None] * frequency[None, :]
    return (jnp.cos(angles)[:, None, :], jnp.sin(angles)[:, None, :])

def rotate(values, cosine, sine):
    shaped = values.reshape(values.shape[0], -1, HD)
    first_half = shaped[..., :HD // 2]
    second_half = shaped[..., HD // 2:]
    turned = jnp.concatenate([first_half * cosine - second_half * sine, second_half * cosine + first_half * sine], axis=-1)
    return turned.reshape(values.shape)

def attend(queries_rot, keys_rot, values_low, seq_ids, position):
    block_rows = 512 if TOKENS % 512 == 0 else TOKENS
    block_count = TOKENS // block_rows
    group = HEADS // KV_HEADS
    keys_heads = jnp.repeat(keys_rot.reshape(TOKENS, KV_HEADS, HD), group, axis=1)
    values_heads = jnp.repeat(values_low.reshape(TOKENS, KV_HEADS, HD), group, axis=1)

    def one_block(pieces):
        query_block, seq_block, pos_block = pieces
        raw_scores = jnp.einsum('qhd,khd->hqk', query_block, keys_heads, precision=HIGHEST) * HD ** (-0.5)
        scores = low_back(raw_scores)
        visible = (seq_ids[None, :] == seq_block[:, None]) & (position[None, :] <= pos_block[:, None]) | (seq_block[:, None] > 0) & (seq_ids[None, :] == 0)
        scores = jnp.where(visible[None], scores, MASK_FLOOR)
        probs = low(jax.nn.softmax(scores, axis=-1))
        return jnp.einsum('hqk,khd->qhd', probs, values_heads, precision=HIGHEST)
    outputs = lax.map(jax.checkpoint(one_block), (queries_rot.reshape(block_count, block_rows, HEADS, HD), seq_ids.reshape(block_count, block_rows), position.reshape(block_count, block_rows)))
    return outputs.reshape(TOKENS, HEADS * HD)

def experts(normed_ffn, routes, gates, gate_weights, up_weights, down_weights):
    capacity = MOST * N_CTX * N_EXP
    quarter = FF // N_EXP
    route_flat = routes.reshape(-1).astype(jnp.int32)
    one_hot = (route_flat[:, None] == jnp.arange(EXPERTS, dtype=jnp.int32)[None, :]).astype(jnp.int32)
    slot_rank = lax.optimization_barrier(jnp.sum(jnp.cumsum(one_hot, axis=0) * one_hot, axis=1)) - 1
    slot_ids = route_flat * capacity + slot_rank
    copy_token = jnp.arange(TOKENS * TOP, dtype=jnp.int32) // TOP
    owner = jnp.zeros((EXPERTS * capacity,), jnp.int32).at[slot_ids].set(copy_token)
    used = jnp.zeros((EXPERTS * capacity,), jnp.float32).at[slot_ids].set(1.0)
    weight = jnp.zeros((EXPERTS * capacity,), jnp.float32).at[slot_ids].set(gates.reshape(-1))
    normed_low = low(normed_ffn)
    rows_in = normed_low[owner] * used[:, None]

    def one_expert(pieces):
        expert_in, gate_w, up_w, down_w = pieces
        quarters = low_back(jnp.broadcast_to(expert_in[None], (N_EXP, capacity, D)))
        gate_pre = low_back(jnp.einsum('qcd,dqf->qcf', quarters, gate_w.reshape(D, N_EXP, quarter), precision=HIGHEST))
        up_pre = low_back(jnp.einsum('qcd,dqf->qcf', quarters, up_w.reshape(D, N_EXP, quarter), precision=HIGHEST))
        hidden_act = low(jax.nn.silu(gate_pre) * up_pre)
        parts = low(jnp.einsum('qcf,qfd->qcd', hidden_act, down_w.reshape(N_EXP, quarter, D), precision=HIGHEST))
        return low_back(lax.optimization_barrier(jnp.sum(parts, axis=0)))
    outputs = lax.map(jax.checkpoint(one_expert), (rows_in.reshape(EXPERTS, capacity, D), gate_weights, up_weights, down_weights))
    return jnp.zeros((TOKENS, D), jnp.float32).at[owner].add(weight[:, None] * outputs.reshape(EXPERTS * capacity, D))

def layer(hidden_f, gain_attn, w_query, w_key, w_value, w_out, gain_query, gain_key, gain_ffn, w_gate, w_up, w_down, routes, gates, seq_ids, position):
    normed = low(hidden_f * inverse_rms(hidden_f) * gain_attn)
    queries = low_back(matmul(normed, w_query))
    keys_pre = low_back(matmul(normed, w_key))
    values_low = low_back(low(matmul(normed, w_value)))
    cosine, sine = rope_tables(position)
    queries_rot = low(rotate(queries * inverse_rms(queries) * gain_query, cosine, sine))
    keys_rot = low(rotate(keys_pre * inverse_rms(keys_pre) * gain_key, cosine, sine))
    heads_out = low_back(low(attend(queries_rot, keys_rot, values_low, seq_ids, position)))
    branch = low_back(jnp.dot(heads_out, w_out.T, precision=HIGHEST, preferred_element_type=jnp.float32))
    resid = hidden_f + branch
    normed_ffn = resid * inverse_rms(resid) * gain_ffn
    return resid + experts(normed_ffn, routes, gates, w_gate, w_up, w_down)

def reference(hidden_in, teacher, valid, block_of, routes, gates, w_query, w_key, w_value, w_out, gain_attn, gain_query, gain_key, gain_ffn, w_gate, w_up, w_down):
    seq_ids, position = token_places(block_of)
    row_mask = valid.astype(jnp.float32)
    valid_count = jnp.sum(row_mask)
    target = teacher.astype(jnp.float32)

    def scaled(hidden_f, g_attn, wq_f, wk_f, wv_f, wo_f, g_query, g_key, g_ffn, wg_f, wu_f, wd_f):
        block_out = layer(hidden_f, g_attn, wq_f, wk_f, wv_f, wo_f, g_query, g_key, g_ffn, wg_f, wu_f, wd_f, routes, gates, seq_ids, position)
        misfit = block_out - target
        loss = jnp.sum(row_mask[:, None] * misfit * misfit) / (valid_count * D)
        return (loss * (TOKENS * D / 2.0), (block_out, loss))
    primals = tuple((item.astype(jnp.float32) for item in (hidden_in, gain_attn, w_query, w_key, w_value, w_out, gain_query, gain_key, gain_ffn, w_gate, w_up, w_down)))
    value, pullback, aux = jax.vjp(scaled, *primals, has_aux=True)
    grads = pullback(jnp.ones_like(value))
    block_out, loss = aux
    return (block_out, loss, grads[0], grads[2], grads[3], grads[4], grads[5], grads[1], grads[6], grads[7], grads[8], grads[9], grads[10], grads[11])
```

```python
import functools

import jax
import jax.numpy as jnp
from jax import lax
from jax.experimental import pallas as pl
from jax.experimental.pallas import tpu as pltpu
from jax.sharding import PartitionSpec as P

HD = 64
BLK = 128
CONT_LEN = 1024
CONT_BLKS = CONT_LEN // BLK
LANES = 128

NORM_EPSILON = 1e-05
ROPE_BASE = 10000.0
MASK_FLOOR = -1e30
F32 = jnp.float32
BF16 = jnp.bfloat16
NT = (((1,), (1,)), ((), ()))
NN = (((1,), (0,)), ((), ()))
TN = (((0,), (0,)), ((), ()))


def dot(left, right, dims):
    return lax.dot_general(left, right, dims, preferred_element_type=F32)


def key_ranges(block, half, tile_blocks):
    cont = block >= half
    inner = jnp.where(cont, (block - half) % CONT_BLKS, 0)
    n_a = jnp.where(cont, half // tile_blocks, block // tile_blocks)
    cont_base = half + (block - half) // CONT_BLKS * CONT_BLKS
    base = jnp.where(cont, cont_base, block // tile_blocks * tile_blocks) * BLK
    return n_a, base, inner // tile_blocks


def gather_blocks(table, total, moves):
    def start(i, carry):
        to = pl.multiple_of(table[i] * BLK, BLK)
        for source, target, sem in moves:
            pltpu.make_async_copy(source(i), target(to), sem).start()
        return carry

    lax.fori_loop(0, total, start, 0)


def wait_all(ref, sem):
    pltpu.make_async_copy(ref, ref, sem).wait()


def rows_of(ref, per_ctx):
    def place(i):
        first = i // 4 * per_ctx + i % 4 * BLK
        return ref.at[pl.ds(pl.multiple_of(first, 16), BLK)]

    return place


def causal(shape, key_first, query_first, rows_are_queries):
    row = lax.broadcasted_iota(jnp.int32, shape, 0) % BLK
    col = lax.broadcasted_iota(jnp.int32, shape, 1)
    if rows_are_queries:
        return key_first + col <= query_first + row
    return key_first + row <= query_first + col


def to_half(tile, source, target):
    values = tile.astype(F32)
    if source != target:
        values = pltpu.roll(values, HD, 1)
    lane = lax.broadcasted_iota(jnp.int32, values.shape, 1)
    return jnp.where(lane // HD == target, values, 0.0)


def turn(tile, cosine, sine):
    lane = lax.broadcasted_iota(jnp.int32, tile.shape, 1)
    ahead = pltpu.roll(tile, LANES - HD // 2, 1)
    behind = pltpu.roll(tile, HD // 2, 1)
    return tile * cosine + jnp.where(lane % HD < HD // 2, ahead, behind) * sine


def rows_by_head(source_ref, block_rows, target_ref):
    for h in range(4):
        m, g = h // 2, h % 2
        tile = source_ref[block_rows, m * LANES : (m + 1) * LANES]
        target_ref[h * BLK : (h + 1) * BLK, :] = to_half(tile, g, m).astype(BF16)


def rows_by_token(values):
    tiles = []
    for m in range(2):
        first = values[2 * m * BLK : (2 * m + 1) * BLK]
        second = values[(2 * m + 1) * BLK : (2 * m + 2) * BLK]
        tiles.append(to_half(first, m, 0) + to_half(second, m, 1))
    return tiles


def turn_kernel(pre_ref, scale_ref, gain_ref, cos_ref, sin_ref, q_ref, kv_ref):
    for col in range(3):
        lanes = slice(col * LANES, (col + 1) * LANES)
        which = 0 if col < 2 else 1
        hat = pre_ref[:, lanes] * scale_ref[:, which : which + 1]
        turned = turn(hat * gain_ref[:, lanes], cos_ref[...], sin_ref[...]).astype(BF16)
        if which == 0:
            q_ref[:, lanes] = (turned.astype(F32) * HD**-0.5).astype(BF16)
        else:
            kv_ref[:, :LANES] = turned
    kv_ref[:, LANES:] = pre_ref[:, 3 * LANES :].astype(BF16)


def attend_kernel(
    total, half, tile_blocks, table, own, q_in, kv, o_ref, lse_ref, kv_s, q_ref, acc, peak, sem
):
    gather_blocks(
        table,
        total,
        [
            (
                rows_of(kv, 4 * BLK),
                lambda to: kv_s.at[pl.ds(to, BLK), pl.ds(0, 2 * LANES)],
                sem.at[0],
            )
        ],
    )
    kv_s[:, 2 * LANES :] = jnp.ones((total * BLK, LANES), BF16)
    wait_all(kv_s.at[:, pl.ds(0, 2 * LANES)], sem.at[0])
    width = tile_blocks * BLK

    def query_block(i, carry):
        block = own[i]
        n_a, base, n_b = key_ranges(block, half, tile_blocks)
        rows = pl.ds(pl.multiple_of(i * BLK, BLK), BLK)
        lanes = pl.ds(pl.multiple_of(i % 2 * BLK, BLK), BLK)
        rows_by_head(q_in, rows, q_ref)

        def first_key(j):
            return pl.multiple_of(jnp.where(j < n_a, j * width, base + (j - n_a) * width), BLK)

        def tile(start, masked):
            scores = dot(q_ref[...], kv_s[pl.ds(start, width), :LANES], NT)
            probs = jnp.exp(scores)
            if masked:
                probs = jnp.where(causal(probs.shape, start, block * BLK, True), probs, 0.0)
            acc[...] += dot(probs.astype(BF16), kv_s[pl.ds(start, width), LANES:], NN)

        def clear_tile(j, carry):
            tile(first_key(j), False)
            return carry

        def store(out, log_sum):
            first, second = rows_by_token(out)
            o_ref[rows, :LANES] = first
            o_ref[rows, LANES:] = second
            for h in range(4):
                lse_ref[i // 2, h : h + 1, lanes] = log_sum[h * BLK : (h + 1) * BLK].T[:1]

        acc[...] = jnp.zeros_like(acc)
        lax.fori_loop(0, n_a + n_b, clear_tile, 0)
        tile(first_key(n_a + n_b), True)
        sums = acc[:, LANES:]
        in_range = (jnp.max(sums) < 2.0**100) & (jnp.min(sums) > 2.0**-40)

        @pl.when(in_range)
        def _():
            store(acc[:, :LANES] / sums, jnp.log(sums))

        @pl.when(jnp.logical_not(in_range))
        def _():
            acc[...] = jnp.zeros_like(acc)
            peak[...] = jnp.full_like(peak, MASK_FLOOR)

            def safe_tile(j, carry):
                start = first_key(j)
                scores = dot(q_ref[...], kv_s[pl.ds(start, width), :LANES], NT)
                seen = causal(scores.shape, start, block * BLK, True)
                scores = jnp.where(seen, scores, MASK_FLOOR)
                old = peak[...]
                new = jnp.maximum(old, jnp.max(scores, axis=1, keepdims=True))
                probs = jnp.where(seen, jnp.exp(scores - new[:, :1]), 0.0)
                keep = jnp.exp(old - new)
                acc[...] = acc[...] * keep[:, :1] + dot(
                    probs.astype(BF16), kv_s[pl.ds(start, width), LANES:], NN
                )
                peak[...] = new
                return carry

            lax.fori_loop(0, n_a + n_b + 1, safe_tile, 0)
            safe_sums = acc[:, LANES:]
            store(acc[:, :LANES] / safe_sums, peak[...] + jnp.log(safe_sums))

        return carry

    lax.fori_loop(0, 4, query_block, 0)


def query_grad_kernel(
    total,
    half,
    tile_blocks,
    table,
    own,
    q_in,
    do_in,
    o_in,
    lse_in,
    cos_ref,
    sin_ref,
    kv,
    dq_ref,
    kv_s,
    q_ref,
    do_ref,
    lse_ref,
    delta_ref,
    acc,
    sem,
):
    gather_blocks(
        table, total, [(rows_of(kv, 4 * BLK), lambda to: kv_s.at[pl.ds(to, BLK)], sem.at[0])]
    )
    wait_all(kv_s, sem.at[0])
    width = tile_blocks * BLK

    def query_block(i, carry):
        block = own[i]
        n_a, base, n_b = key_ranges(block, half, tile_blocks)
        rows = pl.ds(pl.multiple_of(i * BLK, BLK), BLK)
        lanes = pl.ds(pl.multiple_of(i % 2 * BLK, BLK), BLK)
        rows_by_head(q_in, rows, q_ref)
        rows_by_head(do_in, rows, do_ref)
        for h in range(4):
            part = slice(h * BLK, (h + 1) * BLK)
            pair = slice(h // 2 * LANES, (h // 2 + 1) * LANES)
            product = do_in[rows, pair].astype(F32) * o_in[rows, pair]
            own_half = to_half(product, h % 2, h % 2)
            delta = jnp.sum(own_half, axis=1, keepdims=True)
            delta_ref[part, :] = jnp.broadcast_to(delta, (BLK, LANES))
            row = lse_in[i // 2, h : h + 1, lanes]
            lse_ref[part, :] = jnp.broadcast_to(row, (LANES, BLK)).T

        def first_key(j):
            return pl.multiple_of(jnp.where(j < n_a, j * width, base + (j - n_a) * width), BLK)

        def tile(start, masked):
            keys = kv_s[pl.ds(start, width), :LANES]
            scores = dot(q_ref[...], keys, NT)
            prob_grad = dot(do_ref[...], kv_s[pl.ds(start, width), LANES:], NT)
            probs = jnp.exp(scores - lse_ref[:, :1])
            score_grad = probs * (prob_grad - delta_ref[:, :1])
            if masked:
                seen = causal(probs.shape, start, block * BLK, True)
                score_grad = jnp.where(seen, score_grad, 0.0)
            acc[...] += dot(score_grad.astype(BF16), keys, NN)

        def clear_tile(j, carry):
            tile(first_key(j), False)
            return carry

        acc[...] = jnp.zeros_like(acc)
        lax.fori_loop(0, n_a + n_b, clear_tile, 0)
        tile(first_key(n_a + n_b), True)
        for m, gradient in enumerate(rows_by_token(acc[...])):
            back = turn(gradient * HD**-0.5, cos_ref[rows, :], -sin_ref[rows, :])
            dq_ref[rows, m * LANES : (m + 1) * LANES] = back
        return carry

    lax.fori_loop(0, 4, query_block, 0)


def pair_grad_kernel(
    total,
    half,
    tile_blocks,
    do_rows,
    table,
    own,
    kv_in,
    cos_ref,
    sin_ref,
    q_all,
    do_all,
    aux,
    out_ref,
    q_s,
    do_s,
    aux_s,
    k_ref,
    v_ref,
    dk_ref,
    dv_ref,
    sem,
):
    gather_blocks(
        table,
        total,
        [
            (rows_of(q_all, 4 * BLK), lambda to: q_s.at[pl.ds(to, BLK)], sem.at[0]),
            (rows_of(do_all, do_rows), lambda to: do_s.at[pl.ds(to, BLK)], sem.at[1]),
            (
                lambda i: aux.at[i // 4, i // 2 % 2, :, pl.ds(pl.multiple_of(i % 2 * BLK, BLK), BLK)],
                lambda to: aux_s.at[:, pl.ds(to, BLK)],
                sem.at[2],
            ),
        ],
    )

    def place(blk, h):
        return (h * 2 + blk) * BLK if blk < 2 else ((blk * 4) + h) * BLK

    k_ref[...] = jnp.zeros_like(k_ref)
    v_ref[...] = jnp.zeros_like(v_ref)
    dk_ref[...] = jnp.zeros_like(dk_ref)
    dv_ref[...] = jnp.zeros_like(dv_ref)
    for blk in range(4):
        source = slice(blk * BLK, (blk + 1) * BLK)
        for h in range(4):
            m, g = h // 2, h % 2
            target = slice(place(blk, h), place(blk, h) + BLK)
            pair = slice(m * LANES, (m + 1) * LANES)
            k_ref[target, pair] = to_half(kv_in[source, :LANES], m, g).astype(BF16)
            v_ref[target, pair] = to_half(kv_in[source, LANES:], m, g).astype(BF16)
    wait_all(q_s, sem.at[0])
    wait_all(do_s, sem.at[1])
    wait_all(aux_s, sem.at[2])
    width = tile_blocks * BLK

    def tile(first_row, per_head, start, keys_first, masked):
        rows = pl.ds(first_row, 4 * per_head)
        queries = q_s[pl.ds(start, width), :]
        grads = do_s[pl.ds(start, width), :]
        scores = dot(k_ref[rows, :], queries, NT)
        prob_grad = dot(v_ref[rows, :], grads, NT)
        probs_low = []
        score_low = []
        for h in range(4):
            part = slice(h * per_head, (h + 1) * per_head)
            probs = jnp.exp(scores[part] - aux_s[h : h + 1, pl.ds(start, width)])
            if masked:
                seen = [causal((BLK, width), first, start, False) for first in keys_first]
                probs = jnp.where(jnp.concatenate(seen, axis=0), probs, 0.0)
            probs_low.append(probs.astype(BF16))
            shifted = prob_grad[part] - aux_s[4 + h : 5 + h, pl.ds(start, width)]
            score_low.append((probs * shifted).astype(BF16))
        dv_ref[rows, :] += dot(jnp.concatenate(probs_low, axis=0), grads, NN)
        dk_ref[rows, :] += dot(jnp.concatenate(score_low, axis=0), queries, NN)

    low = jnp.minimum(own[0], own[1])
    high = jnp.maximum(own[0], own[1])

    def edge_tile(j, carry):
        firsts = [own[0] * BLK, own[1] * BLK]
        tile(0, 2 * BLK, pl.multiple_of(j * width, width), firsts, True)
        return carry

    def clear_tile(j, carry):
        tile(0, 2 * BLK, pl.multiple_of(j * width, width), None, False)
        return carry

    lax.fori_loop(low // tile_blocks, high // tile_blocks + 1, edge_tile, 0)
    lax.fori_loop(high // tile_blocks + 1, total // tile_blocks, clear_tile, 0)
    for which in range(2):
        block = own[2 + which]
        stop = half + ((block - half) // CONT_BLKS + 1) * CONT_BLKS

        def cont_tile(j, carry, which=which, block=block):
            first_row = (8 + 4 * which) * BLK
            tile(first_row, BLK, pl.multiple_of(j * width, width), [block * BLK], True)
            return carry

        lax.fori_loop(block // tile_blocks, stop // tile_blocks, cont_tile, 0)

    def collect(ref, blk):
        tile_sum = None
        for h in range(4):
            m, g = h // 2, h % 2
            part = ref[place(blk, h) : place(blk, h) + BLK, m * LANES : (m + 1) * LANES]
            moved = to_half(part, g, m)
            tile_sum = moved if tile_sum is None else tile_sum + moved
        return tile_sum

    for blk in range(4):
        rows = slice(blk * BLK, (blk + 1) * BLK)
        out_ref[rows, :LANES] = turn(collect(dk_ref, blk), cos_ref[rows, :], -sin_ref[rows, :])
        out_ref[rows, LANES:] = collect(dv_ref, blk)


def block_of_whole(shape):
    return pl.BlockSpec(shape, lambda i, *_: (0,) * len(shape))


def kernel_call(kernel, name, prefetch, ins, outs, scratch, flops):
    hbm = pl.BlockSpec(memory_space=pl.ANY)
    moved = sum(x.size * x.dtype.itemsize for x, _ in ins)
    return pl.pallas_call(
        kernel,
        out_shape=tuple(outs),
        grid_spec=pltpu.PrefetchScalarGridSpec(
            num_scalar_prefetch=len(prefetch),
            grid=(1,),
            in_specs=[hbm if far else block_of_whole(x.shape) for x, far in ins],
            out_specs=tuple(block_of_whole(out.shape) for out in outs),
            scratch_shapes=scratch,
        ),
        compiler_params=pltpu.CompilerParams(vmem_limit_bytes=48 << 20),
        cost_estimate=pl.CostEstimate(flops=flops, bytes_accessed=moved, transcendentals=0),
        name=name,
    )(*prefetch, *(x for x, _ in ins))


def turn_heads(projected, scales, gain, cosine, sine):
    rows = projected.shape[0]
    out = jax.ShapeDtypeStruct((rows, 2 * LANES), BF16)
    ins = [(x, False) for x in (projected, scales, gain, cosine, sine)]
    return kernel_call(turn_kernel, "turn_heads", (), ins, [out, out], [], 10**6)


def attend(table, own, q, kv_all):
    total = table.shape[0]
    return kernel_call(
        functools.partial(attend_kernel, total, total // 2, 8),
        "attend",
        (table, own),
        [(q, False), (kv_all, True)],
        [
            jax.ShapeDtypeStruct((4 * BLK, 2 * LANES), F32),
            jax.ShapeDtypeStruct((2, 4, 2 * BLK), F32),
        ],
        [
            pltpu.VMEM((total * BLK, 3 * LANES), BF16),
            pltpu.VMEM((4 * BLK, LANES), BF16),
            pltpu.VMEM((4 * BLK, 2 * LANES), F32),
            pltpu.VMEM((4 * BLK, LANES), F32),
            pltpu.SemaphoreType.DMA((1,)),
        ],
        20 * 10**9,
    )


def query_grad(table, own, q, out_grad, heads, lse, cosine, sine, kv_all):
    total = table.shape[0]
    ins = [(x, False) for x in (q, out_grad, heads, lse, cosine, sine)]
    return kernel_call(
        functools.partial(query_grad_kernel, total, total // 2, 4),
        "query_grad",
        (table, own),
        ins + [(kv_all, True)],
        [jax.ShapeDtypeStruct((4 * BLK, 2 * LANES), F32)],
        [
            pltpu.VMEM((total * BLK, 2 * LANES), BF16),
            pltpu.VMEM((4 * BLK, LANES), BF16),
            pltpu.VMEM((4 * BLK, LANES), BF16),
            pltpu.VMEM((4 * BLK, LANES), F32),
            pltpu.VMEM((4 * BLK, LANES), F32),
            pltpu.VMEM((4 * BLK, LANES), F32),
            pltpu.SemaphoreType.DMA((1,)),
        ],
        30 * 10**9,
    )[0]


def pair_grad(table, own, kv, cosine, sine, q_all, do_all, do_rows, aux):
    total = table.shape[0]
    ins = [(x, False) for x in (kv, cosine, sine)] + [(x, True) for x in (q_all, do_all, aux)]
    return kernel_call(
        functools.partial(pair_grad_kernel, total, total // 2, 2, do_rows),
        "pair_grad",
        (table, own),
        ins,
        [jax.ShapeDtypeStruct((4 * BLK, 2 * LANES), F32)],
        [
            pltpu.VMEM((total * BLK, 2 * LANES), BF16),
            pltpu.VMEM((total * BLK, 2 * LANES), BF16),
            pltpu.VMEM((8, total * BLK), F32),
            pltpu.VMEM((16 * BLK, 2 * LANES), BF16),
            pltpu.VMEM((16 * BLK, 2 * LANES), BF16),
            pltpu.VMEM((16 * BLK, 2 * LANES), F32),
            pltpu.VMEM((16 * BLK, 2 * LANES), F32),
            pltpu.SemaphoreType.DMA((3,)),
        ],
        40 * 10**9,
    )[0]


def turn_tables(position):
    half_dim = HD // 2
    frequency = ROPE_BASE ** (-(jnp.arange(half_dim, dtype=F32) * 2.0 / HD))
    angles = position[:, None] * frequency[None, :]
    cosine, sine = jnp.cos(angles), jnp.sin(angles)
    return jnp.concatenate([cosine] * 4, axis=1), jnp.concatenate([-sine, sine] * 2, axis=1)


def norm_back(grad_normed, hat_values, scale_values, gain_values):
    grad_hat = grad_normed * gain_values
    return scale_values * (
        grad_hat - hat_values * jnp.mean(grad_hat * hat_values, axis=-1, keepdims=True)
    )


def pieces(values, count):
    parts = []
    for _ in range(count):
        part = lax.reduce_precision(values, 8, 7)
        parts.append(part.astype(BF16))
        values = values - part
    return parts


def exchange(values, axis):
    return lax.all_to_all(values, axis, split_axis=0, concat_axis=0, tiled=True)


def spread(values, axis, count):
    return exchange(jnp.broadcast_to(values[None], (count,) + values.shape), axis)


def gather_small(values, axis, index, count):
    come = [values]
    for step in range(1, count):
        come.append(lax.ppermute(values, axis, [(i, (i + step) % count) for i in range(count)]))
    twice = jnp.stack(come[::-1] + come[:0:-1], axis=0)
    return lax.dynamic_slice_in_dim(twice, count - 1 - index, count, 0)


def on_device(
    hidden_in,
    teacher,
    valid,
    block_of,
    routes,
    gates,
    w_query,
    w_key,
    w_value,
    w_out,
    gain_attn,
    gain_query,
    gain_key,
    gain_ffn,
    w_gate,
    w_up,
    w_down,
):
    ctx_count = lax.axis_size("ctx")
    exp_count = lax.axis_size("exp")
    ctx_index = lax.axis_index("ctx")
    exp_index = lax.axis_index("exp")
    ctx_rows, model_width = hidden_in.shape
    own_rows = ctx_rows // exp_count
    token_total = block_of.shape[0] * BLK
    head_cols = w_query.shape[1]
    kv_cols = w_key.shape[1]
    kv_total = kv_cols * exp_count
    qkv_cols = head_cols + 2 * kv_cols
    shard_rows = w_query.shape[0]

    own_qkv = jnp.concatenate([w_query, w_key, w_value], axis=1)
    gain_row = jnp.concatenate([gain_attn, gain_query, gain_ffn, gain_key])
    gain_rows = jnp.pad(gain_row, (0, 16 * qkv_cols - gain_row.shape[0])).reshape(16, qkv_cols)
    first_parts = spread(jnp.concatenate([own_qkv, gain_rows], axis=0), "ctx", ctx_count)
    full_qkv = first_parts[:, :shard_rows].reshape(model_width, qkv_cols)
    gains = first_parts[:, shard_rows:].reshape(ctx_count, -1).astype(F32)
    attn_gain = gains[:, :shard_rows].reshape(model_width)
    query_gain_all = gains[:, shard_rows : 2 * shard_rows].reshape(model_width)
    ffn_gain = gains[:, 2 * shard_rows : 3 * shard_rows].reshape(model_width)
    key_gain_all = gains[:, 3 * shard_rows : 3 * shard_rows + gain_key.shape[0]].reshape(kv_total)
    query_gain = lax.dynamic_slice_in_dim(query_gain_all, exp_index * head_cols, head_cols)
    key_gain = lax.dynamic_slice_in_dim(key_gain_all, exp_index * kv_cols, kv_cols)

    out_strip = gather_small(w_out, "exp", exp_index, exp_count)
    width = w_gate.shape[2]
    own_expert = jnp.concatenate([w_gate[0], w_up[0], w_down[0].T], axis=1)
    expert = lax.all_gather(own_expert, "exp", axis=0, tiled=False)

    hidden_f = hidden_in.astype(F32)
    attn_scale = lax.rsqrt(jnp.mean(hidden_f * hidden_f, axis=-1, keepdims=True) + NORM_EPSILON)
    attn_hat = hidden_f * attn_scale
    normed = (attn_hat * attn_gain).astype(BF16)
    projected = dot(normed, full_qkv, NN)
    query_pre = projected[:, :head_cols]
    key_pre = projected[:, head_cols : head_cols + kv_cols]
    query_square, key_square = lax.psum(
        jnp.stack([jnp.sum(query_pre * query_pre, axis=1), jnp.sum(key_pre * key_pre, axis=1)]),
        "exp",
    )
    query_scale = lax.rsqrt(query_square / model_width + NORM_EPSILON)[:, None]
    key_scale = lax.rsqrt(key_square / kv_total + NORM_EPSILON)[:, None]
    query_hat = query_pre * query_scale
    key_hat = key_pre * key_scale
    own_blocks = lax.dynamic_slice_in_dim(block_of, ctx_index * 4, 4)
    token_ids = (own_blocks[:, None] * BLK + jnp.arange(BLK, dtype=jnp.int32)[None]).reshape(-1)
    prompt_len = token_total // 2
    position = jnp.where(
        token_ids >= prompt_len, prompt_len + (token_ids - prompt_len) % CONT_LEN, token_ids
    ).astype(F32)
    cosine, sine = turn_tables(position)
    queries_rot, own_kv = turn_heads(
        projected,
        jnp.concatenate([query_scale, key_scale], axis=1),
        jnp.concatenate([query_gain, key_gain])[None],
        cosine,
        sine,
    )
    own_kv, expert = lax.optimization_barrier((own_kv, expert))
    gate_strips = [expert[u, :, :width] for u in range(exp_count)]
    up_strips = [expert[u, :, width : 2 * width] for u in range(exp_count)]
    wide_gate_up = jnp.concatenate(gate_strips + up_strips, axis=1)
    wide_down = jnp.concatenate([expert[u, :, 2 * width :] for u in range(exp_count)], axis=1)
    kv_all = lax.all_gather(own_kv, "ctx", axis=0, tiled=True)
    kv_all, out_strip = lax.optimization_barrier((kv_all, out_strip))
    full_out = lax.all_gather(out_strip, "ctx", axis=1, tiled=True)
    heads_f, lse = attend(block_of, own_blocks, queries_rot, kv_all)
    heads_low = heads_f.astype(BF16)

    own_heads = exchange(heads_low.reshape(exp_count, own_rows, head_cols), "exp")
    own_heads, full_out, later_q = lax.optimization_barrier((own_heads, full_out, queries_rot))
    q_all = lax.all_gather(later_q, "ctx", axis=0, tiled=True)
    attn_rows = jnp.einsum("erk,eok->ro", own_heads, full_out, preferred_element_type=F32)
    hidden_rows = lax.dynamic_slice_in_dim(hidden_f, exp_index * own_rows, own_rows, 0)
    resid = hidden_rows + attn_rows
    ffn_scale = lax.rsqrt(jnp.mean(resid * resid, axis=-1, keepdims=True) + NORM_EPSILON)
    ffn_hat = resid * ffn_scale
    normed_ffn = (ffn_hat * ffn_gain).astype(BF16)

    expert_total = ctx_count
    capacity = max(2, own_rows * routes.shape[1] * 5 // (expert_total * 4))
    slots = expert_total * capacity
    names = routes[:, :, None] == jnp.arange(expert_total, dtype=jnp.int32)[None, None, :]
    named = jnp.any(names, axis=1)
    gate_of = jnp.sum(jnp.where(names, gates[:, :, None], 0.0), axis=1)
    before = jnp.tril(jnp.ones((own_rows, own_rows), BF16), -1)
    rank = dot(before, named.astype(BF16), NN).astype(jnp.int32)
    slot_rank = jnp.where(named, rank, -1).T[:, None, :]
    holds = slot_rank == jnp.arange(capacity, dtype=jnp.int32)[None, :, None]
    pick = holds.astype(BF16).reshape(slots, own_rows)
    weigh = jnp.where(holds, gate_of.T[:, None, :], 0.0).reshape(slots, own_rows)
    slot_gate = jnp.sum(weigh, axis=1, keepdims=True)

    def send(rows):
        return exchange(rows.reshape(ctx_count, capacity, model_width), "ctx").reshape(
            slots, model_width
        )

    expert_in = send(dot(pick, normed_ffn, NN).astype(BF16))
    pre = dot(expert_in, wide_gate_up, NN)
    gate_pre = pre[:, : exp_count * width]
    up_pre = pre[:, exp_count * width :]
    gate_sig = jax.nn.sigmoid(gate_pre)
    gate_act = gate_pre * gate_sig
    hidden_act = (gate_act * up_pre).astype(BF16)
    returned = send(dot(hidden_act, wide_down, NT).astype(BF16))
    returned, q_all, later_qkv = lax.optimization_barrier((returned, q_all, full_qkv))
    all_qkv = lax.all_gather(later_qkv, "exp", axis=0, tiled=False)
    moe_rows = sum(dot(part, returned, TN) for part in pieces(weigh, 2))
    block_out = resid + moe_rows

    row_start = (ctx_index * exp_count + exp_index) * own_rows
    row_valid = lax.dynamic_slice_in_dim(valid, row_start, own_rows, 0).astype(F32)
    valid_count = jnp.sum(valid.astype(F32))
    misfit = block_out - teacher.astype(F32)
    local_loss = jnp.sum(row_valid[:, None] * misfit * misfit)
    out_grad_rows = misfit * row_valid[:, None] * (token_total / valid_count)
    copy_grad = sum(dot(pick, part, NN) for part in pieces(out_grad_rows, 2))
    grad_copies = send((slot_gate * copy_grad).astype(BF16))
    act_grad = dot(grad_copies, wide_down, NN)
    gate_grad = (act_grad * up_pre * gate_sig * (1.0 + gate_pre * (1.0 - gate_sig))).astype(BF16)
    up_grad = (act_grad * gate_act).astype(BF16)
    both_grad = jnp.concatenate([gate_grad, up_grad], axis=1)
    arrived_grad = send(dot(both_grad, wide_gate_up, NT).astype(BF16))
    arrived_grad, all_qkv = lax.optimization_barrier((arrived_grad, all_qkv))
    ffn_normed_grad = dot(pick, arrived_grad, TN)

    ffn_gain_part = jnp.sum(ffn_normed_grad * ffn_hat, axis=0)
    resid_grad = out_grad_rows + norm_back(ffn_normed_grad, ffn_hat, ffn_scale, ffn_gain)
    branch_rows = resid_grad.astype(BF16)

    do_rows = jnp.einsum("ro,eok->erk", branch_rows, full_out, preferred_element_type=F32)
    out_grad = exchange(do_rows.astype(BF16), "exp").reshape(ctx_rows, head_cols)
    branch_grad = gather_small(branch_rows, "exp", exp_index, exp_count).reshape(
        ctx_rows, model_width
    )
    grad_out = dot(branch_grad, heads_low, TN)
    head_of = jnp.arange(head_cols, dtype=jnp.int32)[None] // HD
    head_ones = (head_of == jnp.arange(4, dtype=jnp.int32)[:, None]).astype(F32)
    delta = lax.dot_general(
        head_ones,
        out_grad.astype(F32) * heads_f,
        NT,
        precision=lax.Precision.HIGHEST,
        preferred_element_type=F32,
    )
    delta = delta.reshape(4, 2, 2 * BLK).transpose(1, 0, 2)
    row_stats = jnp.concatenate([lse, delta], axis=1)
    stat_parts = jnp.stack(pieces(row_stats, 3), axis=0).reshape(-1, 2 * BLK)
    stat_rows = stat_parts.shape[0]
    do_all = lax.all_gather(
        jnp.concatenate([out_grad, stat_parts], axis=0), "ctx", axis=0, tiled=False
    )
    query_n_grad = query_grad(
        block_of, own_blocks, queries_rot, out_grad, heads_f, lse, cosine, sine, kv_all
    )

    do_all, expert_in, both_grad, hidden_act, grad_copies = lax.optimization_barrier(
        (do_all, expert_in, both_grad, hidden_act, grad_copies)
    )
    gate_up_part = dot(expert_in, both_grad, TN)
    down_part = dot(grad_copies, hidden_act, TN)
    strips = []
    for u in range(exp_count):
        own = slice(u * width, (u + 1) * width)
        of_up = slice((exp_count + u) * width, (exp_count + u + 1) * width)
        strips.append(
            jnp.concatenate(
                [gate_up_part[:, own], gate_up_part[:, of_up], down_part[:, own]], axis=1
            )
        )
    grad_expert = lax.psum_scatter(
        jnp.concatenate(strips, axis=0), "exp", scatter_dimension=0, tiled=True
    )
    grad_w_gate = grad_expert[None, :, :width]
    grad_w_up = grad_expert[None, :, width : 2 * width]
    grad_w_down = grad_expert[:, 2 * width :].T[None]

    aux = jnp.sum(
        do_all[:, ctx_rows:].reshape(ctx_count, 3, 2, 8, 2 * BLK).astype(F32), axis=1
    )
    pair_grads = pair_grad(
        block_of,
        own_blocks,
        own_kv,
        cosine,
        sine,
        q_all,
        do_all.reshape(-1, head_cols),
        ctx_rows + stat_rows,
        aux,
    )
    key_n_grad = pair_grads[:, :kv_cols]
    value_grad = pair_grads[:, kv_cols:].astype(BF16)
    query_gain_part = jnp.sum(query_n_grad * query_hat, axis=0)
    key_gain_part = jnp.sum(key_n_grad * key_hat, axis=0)
    query_hat_grad = query_n_grad * query_gain
    key_hat_grad = key_n_grad * key_gain

    stats = jnp.concatenate(
        [
            jnp.sum(query_hat_grad * query_hat, axis=1),
            jnp.sum(key_hat_grad * key_hat, axis=1),
            lax.dynamic_update_slice_in_dim(
                jnp.zeros((model_width,), F32), query_gain_part, exp_index * head_cols, 0
            ),
            ffn_gain_part,
            lax.dynamic_update_slice_in_dim(
                jnp.zeros((kv_total,), F32), key_gain_part, exp_index * kv_cols, 0
            ),
            jnp.full((kv_total,), local_loss),
        ]
    )
    stats = lax.psum(stats.reshape(-1, LANES), "exp").reshape(-1)
    query_stat = stats[:ctx_rows, None] / model_width
    key_stat = stats[ctx_rows : 2 * ctx_rows, None] / kv_total
    sums = stats[2 * ctx_rows :]
    query_low = (query_scale * (query_hat_grad - query_hat * query_stat)).astype(BF16)
    key_low = (key_scale * (key_hat_grad - key_hat * key_stat)).astype(BF16)
    grad_low = jnp.concatenate([query_low, key_low, value_grad], axis=1)

    grad_qkv = dot(normed, grad_low, TN)
    wide_sums = jnp.stack(
        [
            sums[:model_width].reshape(ctx_count, shard_rows),
            sums[model_width : 2 * model_width].reshape(ctx_count, shard_rows),
            jnp.repeat(
                sums[2 * model_width : 2 * model_width + kv_total].reshape(ctx_count, -1), 2, axis=1
            ),
            jnp.broadcast_to(sums[-1], (ctx_count, shard_rows)),
        ],
        axis=-1,
    )
    sum_parts = jnp.concatenate(pieces(wide_sums, 3), axis=-1)
    sum_parts = jnp.pad(sum_parts, ((0, 0), (0, 0), (0, LANES - sum_parts.shape[-1])))
    shards = exchange(
        jnp.concatenate(
            [
                grad_qkv.astype(BF16).reshape(ctx_count, shard_rows, qkv_cols),
                grad_out.astype(BF16).reshape(ctx_count, shard_rows, head_cols),
                sum_parts,
            ],
            axis=2,
        ),
        "ctx",
    )
    shards = jnp.sum(shards.astype(F32), axis=0)
    own_grad_qkv = shards[:, :qkv_cols]
    own_grad_out = shards[:, qkv_cols : qkv_cols + head_cols]
    tail = shards[:, qkv_cols + head_cols :]
    tail = tail[:, 0:4] + tail[:, 4:8] + tail[:, 8:12]
    loss = tail[0, 3] / (valid_count * model_width)

    gain_part = jnp.sum(own_grad_qkv * own_qkv.astype(F32), axis=1)
    gain_parts = jnp.stack(pieces(gain_part, 3), axis=0)
    gain_parts = jnp.pad(gain_parts, ((0, 13), (0, qkv_cols - shard_rows)))
    carried = jnp.broadcast_to(gain_parts[None], (exp_count, 16, qkv_cols))
    back = exchange(
        jnp.concatenate([grad_low.reshape(exp_count, own_rows, qkv_cols), carried], axis=1), "exp"
    )
    gain_sum = jnp.sum(back[:, own_rows : own_rows + 3, :shard_rows].astype(F32), axis=(0, 1))
    grad_gain_attn = gain_sum / gain_attn.astype(F32)
    normed_rows = jnp.einsum(
        "erk,edk->rd", back[:, :own_rows], all_qkv, preferred_element_type=F32
    )
    own_hat = lax.dynamic_slice_in_dim(attn_hat, exp_index * own_rows, own_rows, 0)
    own_scale = lax.dynamic_slice_in_dim(attn_scale, exp_index * own_rows, own_rows, 0)
    grad_hidden = resid_grad + norm_back(normed_rows, own_hat, own_scale, attn_gain)
    return (
        block_out,
        loss,
        grad_hidden,
        own_grad_qkv[:, :head_cols],
        own_grad_qkv[:, head_cols : head_cols + kv_cols],
        own_grad_qkv[:, head_cols + kv_cols :],
        own_grad_out,
        grad_gain_attn,
        tail[:, 0],
        tail[::2, 2],
        tail[:, 1],
        grad_w_gate,
        grad_w_up,
        grad_w_down,
    )


def solution(mesh):
    return jax.shard_map(
        on_device,
        mesh=mesh,
        in_specs=(
            P("ctx", None),
            P(("ctx", "exp"), None),
            P(),
            P(),
            P(("ctx", "exp"), None),
            P(("ctx", "exp"), None),
            P("ctx", "exp"),
            P("ctx", "exp"),
            P("ctx", "exp"),
            P("ctx", "exp"),
            P("ctx"),
            P("ctx"),
            P("ctx"),
            P("ctx"),
            P("ctx", None, "exp"),
            P("ctx", None, "exp"),
            P("ctx", "exp", None),
        ),
        out_specs=(
            P(("ctx", "exp"), None),
            P(),
            P(("ctx", "exp"), None),
            P("ctx", "exp"),
            P("ctx", "exp"),
            P("ctx", "exp"),
            P("ctx", "exp"),
            P("ctx"),
            P("ctx"),
            P("ctx"),
            P("ctx"),
            P("ctx", None, "exp"),
            P("ctx", None, "exp"),
            P("ctx", "exp", None),
        ),
        check_vma=False,
    )
```

```python
import functools

import jax
import jax.numpy as jnp
from jax import lax
from jax.experimental import pallas as pl
from jax.experimental.pallas import tpu as pltpu
from jax.sharding import PartitionSpec as P

HD = 64
BLK = 128
CONT_LEN = 1024
CONT_BLKS = CONT_LEN // BLK
LANES = 128

NORM_EPSILON = 1e-05
ROPE_BASE = 10000.0
MASK_FLOOR = -1e30
F32 = jnp.float32
BF16 = jnp.bfloat16
NT = (((1,), (1,)), ((), ()))
NN = (((1,), (0,)), ((), ()))
TN = (((0,), (0,)), ((), ()))


def dot(left, right, dims):
    return lax.dot_general(left, right, dims, preferred_element_type=F32)


def key_ranges(block, half, tile_blocks):
    cont = block >= half
    inner = jnp.where(cont, (block - half) % CONT_BLKS, 0)
    n_a = jnp.where(cont, half // tile_blocks, block // tile_blocks)
    cont_base = half + (block - half) // CONT_BLKS * CONT_BLKS
    base = jnp.where(cont, cont_base, block // tile_blocks * tile_blocks) * BLK
    return n_a, base, inner // tile_blocks


def gather_blocks(table, total, moves):
    def start(i, carry):
        to = pl.multiple_of(table[i] * BLK, BLK)
        for source, target, sem in moves:
            pltpu.make_async_copy(source(i), target(to), sem).start()
        return carry

    lax.fori_loop(0, total, start, 0)


def wait_all(ref, sem):
    pltpu.make_async_copy(ref, ref, sem).wait()


def rows_of(ref, per_ctx):
    def place(i):
        first = i // 4 * per_ctx + i % 4 * BLK
        return ref.at[pl.ds(pl.multiple_of(first, 16), BLK)]

    return place


def causal(shape, key_first, query_first, rows_are_queries):
    row = lax.broadcasted_iota(jnp.int32, shape, 0) % BLK
    col = lax.broadcasted_iota(jnp.int32, shape, 1)
    if rows_are_queries:
        return key_first + col <= query_first + row
    return key_first + row <= query_first + col


def to_half(tile, source, target):
    values = tile.astype(F32)
    if source != target:
        values = pltpu.roll(values, HD, 1)
    lane = lax.broadcasted_iota(jnp.int32, values.shape, 1)
    return jnp.where(lane // HD == target, values, 0.0)


def turn(tile, cosine, sine):
    lane = lax.broadcasted_iota(jnp.int32, tile.shape, 1)
    ahead = pltpu.roll(tile, LANES - HD // 2, 1)
    behind = pltpu.roll(tile, HD // 2, 1)
    return tile * cosine + jnp.where(lane % HD < HD // 2, ahead, behind) * sine


def rows_by_head(source_ref, block_rows, target_ref):
    for h in range(4):
        m, g = h // 2, h % 2
        tile = source_ref[block_rows, m * LANES : (m + 1) * LANES]
        target_ref[h * BLK : (h + 1) * BLK, :] = to_half(tile, g, m).astype(BF16)


def rows_by_token(values):
    tiles = []
    for m in range(2):
        first = values[2 * m * BLK : (2 * m + 1) * BLK]
        second = values[(2 * m + 1) * BLK : (2 * m + 2) * BLK]
        tiles.append(to_half(first, m, 0) + to_half(second, m, 1))
    return tiles


def turn_kernel(pre_ref, scale_ref, gain_ref, cos_ref, sin_ref, q_ref, kv_ref):
    for col in range(3):
        lanes = slice(col * LANES, (col + 1) * LANES)
        which = 0 if col < 2 else 1
        hat = pre_ref[:, lanes] * scale_ref[:, which : which + 1]
        turned = turn(hat * gain_ref[:, lanes], cos_ref[...], sin_ref[...]).astype(BF16)
        if which == 0:
            q_ref[:, lanes] = (turned.astype(F32) * HD**-0.5).astype(BF16)
        else:
            kv_ref[:, :LANES] = turned
    kv_ref[:, LANES:] = pre_ref[:, 3 * LANES :].astype(BF16)


def attend_kernel(
    total, half, tile_blocks, table, own, q_in, kv, o_ref, lse_ref, kv_s, q_ref, acc, peak, sem
):
    gather_blocks(
        table,
        total,
        [
            (
                rows_of(kv, 4 * BLK),
                lambda to: kv_s.at[pl.ds(to, BLK), pl.ds(0, 2 * LANES)],
                sem.at[0],
            )
        ],
    )
    kv_s[:, 2 * LANES :] = jnp.ones((total * BLK, LANES), BF16)
    wait_all(kv_s.at[:, pl.ds(0, 2 * LANES)], sem.at[0])
    width = tile_blocks * BLK

    def query_block(i, carry):
        block = own[i]
        n_a, base, n_b = key_ranges(block, half, tile_blocks)
        rows = pl.ds(pl.multiple_of(i * BLK, BLK), BLK)
        lanes = pl.ds(pl.multiple_of(i % 2 * BLK, BLK), BLK)
        rows_by_head(q_in, rows, q_ref)

        def first_key(j):
            return pl.multiple_of(jnp.where(j < n_a, j * width, base + (j - n_a) * width), BLK)

        def tile(start, masked):
            scores = dot(q_ref[...], kv_s[pl.ds(start, width), :LANES], NT)
            probs = jnp.exp(scores)
            if masked:
                probs = jnp.where(causal(probs.shape, start, block * BLK, True), probs, 0.0)
            acc[...] += dot(probs.astype(BF16), kv_s[pl.ds(start, width), LANES:], NN)

        def clear_tile(j, carry):
            tile(first_key(j), False)
            return carry

        def store(out, log_sum):
            first, second = rows_by_token(out)
            o_ref[rows, :LANES] = first
            o_ref[rows, LANES:] = second
            for h in range(4):
                lse_ref[i // 2, h : h + 1, lanes] = log_sum[h * BLK : (h + 1) * BLK].T[:1]

        acc[...] = jnp.zeros_like(acc)
        lax.fori_loop(0, n_a + n_b, clear_tile, 0)
        tile(first_key(n_a + n_b), True)
        sums = acc[:, LANES:]
        in_range = (jnp.max(sums) < 2.0**100) & (jnp.min(sums) > 2.0**-40)

        @pl.when(in_range)
        def _():
            store(acc[:, :LANES] / sums, jnp.log(sums))

        @pl.when(jnp.logical_not(in_range))
        def _():
            acc[...] = jnp.zeros_like(acc)
            peak[...] = jnp.full_like(peak, MASK_FLOOR)

            def safe_tile(j, carry):
                start = first_key(j)
                scores = dot(q_ref[...], kv_s[pl.ds(start, width), :LANES], NT)
                seen = causal(scores.shape, start, block * BLK, True)
                scores = jnp.where(seen, scores, MASK_FLOOR)
                old = peak[...]
                new = jnp.maximum(old, jnp.max(scores, axis=1, keepdims=True))
                probs = jnp.where(seen, jnp.exp(scores - new[:, :1]), 0.0)
                keep = jnp.exp(old - new)
                acc[...] = acc[...] * keep[:, :1] + dot(
                    probs.astype(BF16), kv_s[pl.ds(start, width), LANES:], NN
                )
                peak[...] = new
                return carry

            lax.fori_loop(0, n_a + n_b + 1, safe_tile, 0)
            safe_sums = acc[:, LANES:]
            store(acc[:, :LANES] / safe_sums, peak[...] + jnp.log(safe_sums))

        return carry

    lax.fori_loop(0, 4, query_block, 0)


def query_grad_kernel(
    total,
    half,
    tile_blocks,
    table,
    own,
    q_in,
    do_in,
    o_in,
    lse_in,
    cos_ref,
    sin_ref,
    kv,
    dq_ref,
    kv_s,
    q_ref,
    do_ref,
    lse_ref,
    delta_ref,
    acc,
    sem,
):
    gather_blocks(
        table, total, [(rows_of(kv, 4 * BLK), lambda to: kv_s.at[pl.ds(to, BLK)], sem.at[0])]
    )
    wait_all(kv_s, sem.at[0])
    width = tile_blocks * BLK

    def query_block(i, carry):
        block = own[i]
        n_a, base, n_b = key_ranges(block, half, tile_blocks)
        rows = pl.ds(pl.multiple_of(i * BLK, BLK), BLK)
        lanes = pl.ds(pl.multiple_of(i % 2 * BLK, BLK), BLK)
        rows_by_head(q_in, rows, q_ref)
        rows_by_head(do_in, rows, do_ref)
        for h in range(4):
            part = slice(h * BLK, (h + 1) * BLK)
            pair = slice(h // 2 * LANES, (h // 2 + 1) * LANES)
            product = do_in[rows, pair].astype(F32) * o_in[rows, pair]
            own_half = to_half(product, h % 2, h % 2)
            delta = jnp.sum(own_half, axis=1, keepdims=True)
            delta_ref[part, :] = jnp.broadcast_to(delta, (BLK, LANES))
            row = lse_in[i // 2, h : h + 1, lanes]
            lse_ref[part, :] = jnp.broadcast_to(row, (LANES, BLK)).T

        def first_key(j):
            return pl.multiple_of(jnp.where(j < n_a, j * width, base + (j - n_a) * width), BLK)

        def tile(start, masked):
            keys = kv_s[pl.ds(start, width), :LANES]
            scores = dot(q_ref[...], keys, NT)
            prob_grad = dot(do_ref[...], kv_s[pl.ds(start, width), LANES:], NT)
            probs = jnp.exp(scores - lse_ref[:, :1])
            score_grad = probs * (prob_grad - delta_ref[:, :1])
            if masked:
                seen = causal(probs.shape, start, block * BLK, True)
                score_grad = jnp.where(seen, score_grad, 0.0)
            acc[...] += dot(score_grad.astype(BF16), keys, NN)

        def clear_tile(j, carry):
            tile(first_key(j), False)
            return carry

        acc[...] = jnp.zeros_like(acc)
        lax.fori_loop(0, n_a + n_b, clear_tile, 0)
        tile(first_key(n_a + n_b), True)
        for m, gradient in enumerate(rows_by_token(acc[...])):
            back = turn(gradient * HD**-0.5, cos_ref[rows, :], -sin_ref[rows, :])
            dq_ref[rows, m * LANES : (m + 1) * LANES] = back
        return carry

    lax.fori_loop(0, 4, query_block, 0)


def pair_grad_kernel(
    total,
    half,
    tile_blocks,
    do_rows,
    table,
    own,
    kv_in,
    cos_ref,
    sin_ref,
    q_all,
    do_all,
    aux,
    out_ref,
    q_s,
    do_s,
    aux_s,
    k_ref,
    v_ref,
    dk_ref,
    dv_ref,
    sem,
):
    gather_blocks(
        table,
        total,
        [
            (rows_of(q_all, 4 * BLK), lambda to: q_s.at[pl.ds(to, BLK)], sem.at[0]),
            (rows_of(do_all, do_rows), lambda to: do_s.at[pl.ds(to, BLK)], sem.at[1]),
            (
                lambda i: aux.at[i // 4, i // 2 % 2, :, pl.ds(pl.multiple_of(i % 2 * BLK, BLK), BLK)],
                lambda to: aux_s.at[:, pl.ds(to, BLK)],
                sem.at[2],
            ),
        ],
    )

    def place(blk, h):
        return (h * 2 + blk) * BLK if blk < 2 else ((blk * 4) + h) * BLK

    k_ref[...] = jnp.zeros_like(k_ref)
    v_ref[...] = jnp.zeros_like(v_ref)
    dk_ref[...] = jnp.zeros_like(dk_ref)
    dv_ref[...] = jnp.zeros_like(dv_ref)
    for blk in range(4):
        source = slice(blk * BLK, (blk + 1) * BLK)
        for h in range(4):
            m, g = h // 2, h % 2
            target = slice(place(blk, h), place(blk, h) + BLK)
            pair = slice(m * LANES, (m + 1) * LANES)
            k_ref[target, pair] = to_half(kv_in[source, :LANES], m, g).astype(BF16)
            v_ref[target, pair] = to_half(kv_in[source, LANES:], m, g).astype(BF16)
    wait_all(q_s, sem.at[0])
    wait_all(do_s, sem.at[1])
    wait_all(aux_s, sem.at[2])
    width = tile_blocks * BLK

    def tile(first_row, per_head, start, keys_first, masked):
        rows = pl.ds(first_row, 4 * per_head)
        queries = q_s[pl.ds(start, width), :]
        grads = do_s[pl.ds(start, width), :]
        scores = dot(k_ref[rows, :], queries, NT)
        prob_grad = dot(v_ref[rows, :], grads, NT)
        probs_low = []
        score_low = []
        for h in range(4):
            part = slice(h * per_head, (h + 1) * per_head)
            probs = jnp.exp(scores[part] - aux_s[h : h + 1, pl.ds(start, width)])
            if masked:
                seen = [causal((BLK, width), first, start, False) for first in keys_first]
                probs = jnp.where(jnp.concatenate(seen, axis=0), probs, 0.0)
            probs_low.append(probs.astype(BF16))
            shifted = prob_grad[part] - aux_s[4 + h : 5 + h, pl.ds(start, width)]
            score_low.append((probs * shifted).astype(BF16))
        dv_ref[rows, :] += dot(jnp.concatenate(probs_low, axis=0), grads, NN)
        dk_ref[rows, :] += dot(jnp.concatenate(score_low, axis=0), queries, NN)

    low = jnp.minimum(own[0], own[1])
    high = jnp.maximum(own[0], own[1])

    def edge_tile(j, carry):
        firsts = [own[0] * BLK, own[1] * BLK]
        tile(0, 2 * BLK, pl.multiple_of(j * width, width), firsts, True)
        return carry

    def clear_tile(j, carry):
        tile(0, 2 * BLK, pl.multiple_of(j * width, width), None, False)
        return carry

    lax.fori_loop(low // tile_blocks, high // tile_blocks + 1, edge_tile, 0)
    lax.fori_loop(high // tile_blocks + 1, total // tile_blocks, clear_tile, 0)
    for which in range(2):
        block = own[2 + which]
        stop = half + ((block - half) // CONT_BLKS + 1) * CONT_BLKS

        def cont_tile(j, carry, which=which, block=block):
            first_row = (8 + 4 * which) * BLK
            tile(first_row, BLK, pl.multiple_of(j * width, width), [block * BLK], True)
            return carry

        lax.fori_loop(block // tile_blocks, stop // tile_blocks, cont_tile, 0)

    def collect(ref, blk):
        tile_sum = None
        for h in range(4):
            m, g = h // 2, h % 2
            part = ref[place(blk, h) : place(blk, h) + BLK, m * LANES : (m + 1) * LANES]
            moved = to_half(part, g, m)
            tile_sum = moved if tile_sum is None else tile_sum + moved
        return tile_sum

    for blk in range(4):
        rows = slice(blk * BLK, (blk + 1) * BLK)
        out_ref[rows, :LANES] = turn(collect(dk_ref, blk), cos_ref[rows, :], -sin_ref[rows, :])
        out_ref[rows, LANES:] = collect(dv_ref, blk)


def down_strips(w_ref, pair, width):
    strips = [w_ref[u, :, 2 * width : 3 * width] for u in (2 * pair, 2 * pair + 1)]
    return jnp.concatenate(strips, axis=1)


def expert_kernel(quarters, width, x_ref, w_ref, out_ref, gate_ref, up_ref):
    acts = []
    for u in range(quarters):
        cols = slice(u * width, (u + 1) * width)
        pre = dot(x_ref[...], w_ref[u, :, : 2 * width], NN)
        gate, up = pre[:, :width], pre[:, width:]
        gate_ref[:, cols] = gate
        up_ref[:, cols] = up
        acts.append((gate * jax.nn.sigmoid(gate) * up).astype(BF16))
    out = None
    for pair in range(quarters // 2):
        act = jnp.concatenate(acts[2 * pair : 2 * pair + 2], axis=1)
        part = dot(act, down_strips(w_ref, pair, width), NT)
        out = part if out is None else out + part
    out_ref[...] = out.astype(BF16)


def expert_grad_kernel(
    quarters, width, dy_ref, gate_ref, up_ref, w_ref, dx_ref, dgate_ref, dup_ref, act_ref
):
    total = None
    for pair in range(quarters // 2):
        both = dot(dy_ref[...], down_strips(w_ref, pair, width), NN)
        for side in range(2):
            u = 2 * pair + side
            cols = slice(u * width, (u + 1) * width)
            act_grad = both[:, side * width : (side + 1) * width]
            gate, up = gate_ref[:, cols], up_ref[:, cols]
            sig = jax.nn.sigmoid(gate)
            gate_act = gate * sig
            act_ref[:, cols] = (gate_act * up).astype(BF16)
            gate_grad = (act_grad * up * sig * (1.0 + gate * (1.0 - sig))).astype(BF16)
            up_grad = (act_grad * gate_act).astype(BF16)
            dgate_ref[:, cols] = gate_grad
            dup_ref[:, cols] = up_grad
            grads = jnp.concatenate([gate_grad, up_grad], axis=1)
            part = dot(grads, w_ref[u, :, : 2 * width], NT)
            total = part if total is None else total + part
    dx_ref[...] = total.astype(BF16)


def block_of_whole(shape):
    return pl.BlockSpec(shape, lambda i, *_: (0,) * len(shape))


def kernel_call(kernel, name, prefetch, ins, outs, scratch, flops):
    hbm = pl.BlockSpec(memory_space=pl.ANY)
    moved = sum(x.size * x.dtype.itemsize for x, _ in ins)
    return pl.pallas_call(
        kernel,
        out_shape=tuple(outs),
        grid_spec=pltpu.PrefetchScalarGridSpec(
            num_scalar_prefetch=len(prefetch),
            grid=(1,),
            in_specs=[hbm if far else block_of_whole(x.shape) for x, far in ins],
            out_specs=tuple(block_of_whole(out.shape) for out in outs),
            scratch_shapes=scratch,
        ),
        compiler_params=pltpu.CompilerParams(vmem_limit_bytes=48 << 20),
        cost_estimate=pl.CostEstimate(flops=flops, bytes_accessed=moved, transcendentals=0),
        name=name,
    )(*prefetch, *(x for x, _ in ins))


def by_rows(kernel, name, rows, ins, outs, flops):
    def spec(shape):
        if len(shape) == 3:
            return pl.BlockSpec(shape, lambda i: (0, 0, 0))
        return pl.BlockSpec((rows, shape[1]), lambda i: (i, 0))

    return pl.pallas_call(
        kernel,
        out_shape=tuple(outs),
        grid=(outs[0].shape[0] // rows,),
        in_specs=[spec(x.shape) for x in ins],
        out_specs=tuple(spec(out.shape) for out in outs),
        compiler_params=pltpu.CompilerParams(vmem_limit_bytes=40 << 20),
        cost_estimate=pl.CostEstimate(flops=flops, bytes_accessed=10**7, transcendentals=0),
        name=name,
    )(*ins)


def expert_forward(rows_in, weights):
    slots, model_width = rows_in.shape
    quarters, _, cols = weights.shape
    width = cols // 3
    hidden = jax.ShapeDtypeStruct((slots, quarters * width), F32)
    return by_rows(
        functools.partial(expert_kernel, quarters, width),
        "expert",
        slots // 5,
        [rows_in, weights],
        [jax.ShapeDtypeStruct((slots, model_width), BF16), hidden, hidden],
        6 * slots * model_width * quarters * width,
    )


def expert_backward(rows_grad, gate_pre, up_pre, weights):
    slots, model_width = rows_grad.shape
    quarters, _, cols = weights.shape
    width = cols // 3
    hidden = jax.ShapeDtypeStruct((slots, quarters * width), BF16)
    return by_rows(
        functools.partial(expert_grad_kernel, quarters, width),
        "expert_grad",
        slots // 5,
        [rows_grad, gate_pre, up_pre, weights],
        [jax.ShapeDtypeStruct((slots, model_width), BF16), hidden, hidden, hidden],
        6 * slots * model_width * quarters * width,
    )


def turn_heads(projected, scales, gain, cosine, sine):
    rows = projected.shape[0]
    out = jax.ShapeDtypeStruct((rows, 2 * LANES), BF16)
    ins = [(x, False) for x in (projected, scales, gain, cosine, sine)]
    return kernel_call(turn_kernel, "turn_heads", (), ins, [out, out], [], 10**6)


def attend(table, own, q, kv_all):
    total = table.shape[0]
    return kernel_call(
        functools.partial(attend_kernel, total, total // 2, 8),
        "attend",
        (table, own),
        [(q, False), (kv_all, True)],
        [
            jax.ShapeDtypeStruct((4 * BLK, 2 * LANES), F32),
            jax.ShapeDtypeStruct((2, 4, 2 * BLK), F32),
        ],
        [
            pltpu.VMEM((total * BLK, 3 * LANES), BF16),
            pltpu.VMEM((4 * BLK, LANES), BF16),
            pltpu.VMEM((4 * BLK, 2 * LANES), F32),
            pltpu.VMEM((4 * BLK, LANES), F32),
            pltpu.SemaphoreType.DMA((1,)),
        ],
        20 * 10**9,
    )


def query_grad(table, own, q, out_grad, heads, lse, cosine, sine, kv_all):
    total = table.shape[0]
    ins = [(x, False) for x in (q, out_grad, heads, lse, cosine, sine)]
    return kernel_call(
        functools.partial(query_grad_kernel, total, total // 2, 4),
        "query_grad",
        (table, own),
        ins + [(kv_all, True)],
        [jax.ShapeDtypeStruct((4 * BLK, 2 * LANES), F32)],
        [
            pltpu.VMEM((total * BLK, 2 * LANES), BF16),
            pltpu.VMEM((4 * BLK, LANES), BF16),
            pltpu.VMEM((4 * BLK, LANES), BF16),
            pltpu.VMEM((4 * BLK, LANES), F32),
            pltpu.VMEM((4 * BLK, LANES), F32),
            pltpu.VMEM((4 * BLK, LANES), F32),
            pltpu.SemaphoreType.DMA((1,)),
        ],
        30 * 10**9,
    )[0]


def pair_grad(table, own, kv, cosine, sine, q_all, do_all, do_rows, aux):
    total = table.shape[0]
    ins = [(x, False) for x in (kv, cosine, sine)] + [(x, True) for x in (q_all, do_all, aux)]
    return kernel_call(
        functools.partial(pair_grad_kernel, total, total // 2, 2, do_rows),
        "pair_grad",
        (table, own),
        ins,
        [jax.ShapeDtypeStruct((4 * BLK, 2 * LANES), F32)],
        [
            pltpu.VMEM((total * BLK, 2 * LANES), BF16),
            pltpu.VMEM((total * BLK, 2 * LANES), BF16),
            pltpu.VMEM((8, total * BLK), F32),
            pltpu.VMEM((16 * BLK, 2 * LANES), BF16),
            pltpu.VMEM((16 * BLK, 2 * LANES), BF16),
            pltpu.VMEM((16 * BLK, 2 * LANES), F32),
            pltpu.VMEM((16 * BLK, 2 * LANES), F32),
            pltpu.SemaphoreType.DMA((3,)),
        ],
        40 * 10**9,
    )[0]


def turn_tables(position):
    half_dim = HD // 2
    frequency = ROPE_BASE ** (-(jnp.arange(half_dim, dtype=F32) * 2.0 / HD))
    angles = position[:, None] * frequency[None, :]
    cosine, sine = jnp.cos(angles), jnp.sin(angles)
    return jnp.concatenate([cosine] * 4, axis=1), jnp.concatenate([-sine, sine] * 2, axis=1)


def norm_back(grad_normed, hat_values, scale_values, gain_values):
    grad_hat = grad_normed * gain_values
    return scale_values * (
        grad_hat - hat_values * jnp.mean(grad_hat * hat_values, axis=-1, keepdims=True)
    )


def pieces(values, count):
    parts = []
    for _ in range(count):
        part = lax.reduce_precision(values, 8, 7)
        parts.append(part.astype(BF16))
        values = values - part
    return parts


def exchange(values, axis):
    return lax.all_to_all(values, axis, split_axis=0, concat_axis=0, tiled=True)


def spread(values, axis, count):
    return exchange(jnp.broadcast_to(values[None], (count,) + values.shape), axis)


def shifted(values, axis, count):
    parts = [values]
    for step in range(1, count):
        parts.append(lax.ppermute(values, axis, [(i, (i + step) % count) for i in range(count)]))
    return parts


def gather_short(values, axis, index, count):
    parts = shifted(values, axis, count)
    ordered = []
    for place in range(count):
        back = (index - place) % count
        part = parts[0]
        for step in range(1, count):
            part = jnp.where(back == step, parts[step], part)
        ordered.append(part)
    return jnp.stack(ordered, axis=0)


def ride_along(values):
    parts = jnp.concatenate(pieces(values, 3), axis=-1)
    return jnp.pad(parts, ((0, 0), (0, 0), (0, LANES - parts.shape[-1])))


def parted(sums, count):
    return sum(sums[:, i * count : (i + 1) * count] for i in range(3))


def on_device(
    hidden_in,
    teacher,
    valid,
    block_of,
    routes,
    gates,
    w_query,
    w_key,
    w_value,
    w_out,
    gain_attn,
    gain_query,
    gain_key,
    gain_ffn,
    w_gate,
    w_up,
    w_down,
):
    ctx_count = lax.axis_size("ctx")
    exp_count = lax.axis_size("exp")
    ctx_index = lax.axis_index("ctx")
    exp_index = lax.axis_index("exp")
    ctx_rows, model_width = hidden_in.shape
    own_rows = ctx_rows // exp_count
    token_total = block_of.shape[0] * BLK
    head_cols = w_query.shape[1]
    kv_cols = w_key.shape[1]
    kv_total = kv_cols * exp_count
    qkv_cols = head_cols + 2 * kv_cols
    shard_rows = w_query.shape[0]

    own_qkv = jnp.concatenate([w_query, w_key, w_value], axis=1)
    full_qkv = spread(own_qkv, "ctx", ctx_count).reshape(model_width, qkv_cols)
    gain_row = jnp.concatenate([gain_attn, gain_query, gain_ffn, gain_key])
    gain_row = jnp.pad(gain_row, (0, -gain_row.shape[0] % LANES)).reshape(-1, LANES)
    gains = spread(gain_row, "ctx", ctx_count).reshape(ctx_count, -1).astype(F32)
    attn_gain = gains[:, :shard_rows].reshape(model_width)
    query_gain_all = gains[:, shard_rows : 2 * shard_rows].reshape(model_width)
    ffn_gain = gains[:, 2 * shard_rows : 3 * shard_rows].reshape(model_width)
    key_gain_all = gains[:, 3 * shard_rows : 3 * shard_rows + gain_key.shape[0]].reshape(kv_total)
    query_gain = lax.dynamic_slice_in_dim(query_gain_all, exp_index * head_cols, head_cols)
    key_gain = lax.dynamic_slice_in_dim(key_gain_all, exp_index * kv_cols, kv_cols)

    width = w_gate.shape[2]
    own_expert = jnp.concatenate([w_gate[0], w_up[0], w_down[0].T], axis=1)
    expert = lax.all_gather(own_expert, "exp", axis=0, tiled=False)

    hidden_f = hidden_in.astype(F32)
    attn_scale = lax.rsqrt(jnp.mean(hidden_f * hidden_f, axis=-1, keepdims=True) + NORM_EPSILON)
    attn_hat = hidden_f * attn_scale
    normed = (attn_hat * attn_gain).astype(BF16)
    projected = dot(normed, full_qkv, NN)
    query_pre = projected[:, :head_cols]
    key_pre = projected[:, head_cols : head_cols + kv_cols]
    query_square, key_square = lax.psum(
        jnp.stack([jnp.sum(query_pre * query_pre, axis=1), jnp.sum(key_pre * key_pre, axis=1)]),
        "exp",
    )
    query_scale = lax.rsqrt(query_square / model_width + NORM_EPSILON)[:, None]
    key_scale = lax.rsqrt(key_square / kv_total + NORM_EPSILON)[:, None]
    query_hat = query_pre * query_scale
    key_hat = key_pre * key_scale
    own_blocks = lax.dynamic_slice_in_dim(block_of, ctx_index * 4, 4)
    token_ids = (own_blocks[:, None] * BLK + jnp.arange(BLK, dtype=jnp.int32)[None]).reshape(-1)
    prompt_len = token_total // 2
    position = jnp.where(
        token_ids >= prompt_len, prompt_len + (token_ids - prompt_len) % CONT_LEN, token_ids
    ).astype(F32)
    cosine, sine = turn_tables(position)
    queries_rot, own_kv = turn_heads(
        projected,
        jnp.concatenate([query_scale, key_scale], axis=1),
        jnp.concatenate([query_gain, key_gain])[None],
        cosine,
        sine,
    )
    own_kv, expert = lax.optimization_barrier((own_kv, expert))
    kv_all = lax.all_gather(own_kv, "ctx", axis=0, tiled=True)
    own_out, _ = lax.optimization_barrier((w_out, own_kv))
    full_out = gather_short(
        spread(own_out, "ctx", ctx_count).reshape(model_width, head_cols),
        "exp",
        exp_index,
        exp_count,
    )
    heads_f, lse = attend(block_of, own_blocks, queries_rot, kv_all)
    heads_low = heads_f.astype(BF16)

    own_heads = exchange(heads_low.reshape(exp_count, own_rows, head_cols), "exp")
    own_heads, later_q = lax.optimization_barrier((own_heads, queries_rot))
    q_all = lax.all_gather(later_q, "ctx", axis=0, tiled=True)
    attn_rows = jnp.einsum("erk,eok->ro", own_heads, full_out, preferred_element_type=F32)
    hidden_rows = lax.dynamic_slice_in_dim(hidden_f, exp_index * own_rows, own_rows, 0)
    resid = hidden_rows + attn_rows
    ffn_scale = lax.rsqrt(jnp.mean(resid * resid, axis=-1, keepdims=True) + NORM_EPSILON)
    ffn_hat = resid * ffn_scale
    normed_ffn = (ffn_hat * ffn_gain).astype(BF16)

    expert_total = ctx_count
    capacity = max(2, own_rows * routes.shape[1] * 5 // (expert_total * 4))
    slots = expert_total * capacity
    names = routes[:, :, None] == jnp.arange(expert_total, dtype=jnp.int32)[None, None, :]
    named = jnp.any(names, axis=1)
    gate_of = jnp.sum(jnp.where(names, gates[:, :, None], 0.0), axis=1)
    before = jnp.tril(jnp.ones((own_rows, own_rows), BF16), -1)
    rank = dot(before, named.astype(BF16), NN).astype(jnp.int32)
    slot_rank = jnp.where(named, rank, -1).T[:, None, :]
    holds = slot_rank == jnp.arange(capacity, dtype=jnp.int32)[None, :, None]
    pick = holds.astype(BF16).reshape(slots, own_rows)
    weigh = jnp.where(holds, gate_of.T[:, None, :], 0.0).reshape(slots, own_rows)
    slot_gate = jnp.sum(weigh, axis=1, keepdims=True)

    def send(rows):
        return exchange(rows.reshape(ctx_count, capacity, model_width), "ctx").reshape(
            slots, model_width
        )

    expert_in = send(dot(pick, normed_ffn, NN).astype(BF16))
    expert_out, gate_pre, up_pre = expert_forward(expert_in, expert)
    returned = send(expert_out)
    returned, q_all, later_qkv = lax.optimization_barrier((returned, q_all, full_qkv))
    all_qkv = lax.all_gather(later_qkv, "exp", axis=0, tiled=False)
    moe_parts = dot(jnp.concatenate(pieces(weigh, 2), axis=1), returned, TN)
    moe_rows = moe_parts[:own_rows] + moe_parts[own_rows:]
    block_out = resid + moe_rows

    row_start = (ctx_index * exp_count + exp_index) * own_rows
    row_valid = lax.dynamic_slice_in_dim(valid, row_start, own_rows, 0).astype(F32)
    valid_count = jnp.sum(valid.astype(F32))
    misfit = block_out - teacher.astype(F32)
    local_loss = jnp.sum(row_valid[:, None] * misfit * misfit)
    out_grad_rows = misfit * row_valid[:, None] * (token_total / valid_count)
    copy_grad = dot(
        jnp.concatenate([pick, pick], axis=1),
        jnp.concatenate(pieces(out_grad_rows, 2), axis=0),
        NN,
    )
    grad_copies = send((slot_gate * copy_grad).astype(BF16))
    input_grad, gate_grad, up_grad, hidden_act = expert_backward(
        grad_copies, gate_pre, up_pre, expert
    )
    arrived_grad = send(input_grad)
    arrived_grad, all_qkv = lax.optimization_barrier((arrived_grad, all_qkv))
    ffn_normed_grad = dot(pick, arrived_grad, TN)

    ffn_gain_part = jnp.sum(ffn_normed_grad * ffn_hat, axis=0)
    resid_grad = out_grad_rows + norm_back(ffn_normed_grad, ffn_hat, ffn_scale, ffn_gain)
    branch_rows = resid_grad.astype(BF16)

    do_rows = jnp.einsum("ro,eok->erk", branch_rows, full_out, preferred_element_type=F32)
    out_grad = exchange(do_rows.astype(BF16), "exp").reshape(ctx_rows, head_cols)
    branch_parts = shifted(branch_rows, "exp", exp_count)
    head_of = jnp.arange(head_cols, dtype=jnp.int32)[None] // HD
    head_ones = (head_of == jnp.arange(4, dtype=jnp.int32)[:, None]).astype(F32)
    delta = lax.dot_general(
        head_ones,
        out_grad.astype(F32) * heads_f,
        NT,
        precision=lax.Precision.HIGHEST,
        preferred_element_type=F32,
    )
    delta = delta.reshape(4, 2, 2 * BLK).transpose(1, 0, 2)
    row_stats = jnp.concatenate([lse, delta], axis=1)
    stat_parts = jnp.stack(pieces(row_stats, 3), axis=0).reshape(-1, 2 * BLK)
    stat_rows = stat_parts.shape[0]
    do_all = lax.all_gather(
        jnp.concatenate([out_grad, stat_parts], axis=0), "ctx", axis=0, tiled=False
    )
    query_n_grad = query_grad(
        block_of, own_blocks, queries_rot, out_grad, heads_f, lse, cosine, sine, kv_all
    )

    grad_out = None
    for step, part in enumerate(branch_parts):
        first = (exp_index - step) % exp_count * own_rows
        term = dot(part, lax.dynamic_slice_in_dim(heads_low, first, own_rows, 0), TN)
        grad_out = term if grad_out is None else grad_out + term

    gate_part = dot(expert_in, gate_grad, TN)
    up_part = dot(expert_in, up_grad, TN)
    down_part = dot(hidden_act, grad_copies, TN)
    gate_part = gate_part.reshape(model_width, exp_count, width).transpose(1, 0, 2)
    up_part = up_part.reshape(model_width, exp_count, width).transpose(1, 0, 2)
    do_all, gate_part, up_part, down_part = lax.optimization_barrier(
        (do_all, gate_part, up_part, down_part)
    )
    grad_w_gate = lax.psum_scatter(gate_part, "exp", scatter_dimension=0, tiled=True)
    grad_w_up = lax.psum_scatter(up_part, "exp", scatter_dimension=0, tiled=True)
    grad_w_down = lax.psum_scatter(down_part, "exp", scatter_dimension=0, tiled=True)[None]

    query_gain_part = jnp.sum(query_n_grad * query_hat, axis=0)
    query_hat_grad = query_n_grad * query_gain
    early = jnp.concatenate(
        [
            jnp.sum(query_hat_grad * query_hat, axis=1),
            lax.dynamic_update_slice_in_dim(
                jnp.zeros((model_width,), F32), query_gain_part, exp_index * head_cols, 0
            ),
            ffn_gain_part,
            jnp.full((4 * LANES,), local_loss),
        ]
    )
    early = lax.psum(early.reshape(-1, LANES), "exp").reshape(-1)
    do_all, early = lax.optimization_barrier((do_all, early))
    query_stat = early[:ctx_rows, None] / model_width
    query_low = (query_scale * (query_hat_grad - query_hat * query_stat)).astype(BF16)
    early_sums = jnp.stack(
        [
            early[ctx_rows : ctx_rows + model_width].reshape(ctx_count, shard_rows),
            early[ctx_rows + model_width : ctx_rows + 2 * model_width].reshape(
                ctx_count, shard_rows
            ),
            jnp.broadcast_to(early[-1], (ctx_count, shard_rows)),
        ],
        axis=-1,
    )
    early_shards = exchange(
        jnp.concatenate(
            [
                dot(normed, query_low, TN).astype(BF16).reshape(ctx_count, shard_rows, head_cols),
                grad_out.astype(BF16).reshape(ctx_count, shard_rows, head_cols),
                ride_along(early_sums),
            ],
            axis=2,
        ),
        "ctx",
    )
    early_back = exchange(query_low.reshape(exp_count, own_rows, head_cols), "exp")

    aux = jnp.sum(
        do_all[:, ctx_rows:].reshape(ctx_count, 3, 2, 8, 2 * BLK).astype(F32), axis=1
    )
    pair_grads = pair_grad(
        block_of,
        own_blocks,
        own_kv,
        cosine,
        sine,
        q_all,
        do_all.reshape(-1, head_cols),
        ctx_rows + stat_rows,
        aux,
    )
    key_n_grad = pair_grads[:, :kv_cols]
    value_grad = pair_grads[:, kv_cols:].astype(BF16)
    key_gain_part = jnp.sum(key_n_grad * key_hat, axis=0)
    key_hat_grad = key_n_grad * key_gain
    late = jnp.concatenate(
        [
            jnp.sum(key_hat_grad * key_hat, axis=1),
            lax.dynamic_update_slice_in_dim(
                jnp.zeros((kv_total,), F32), key_gain_part, exp_index * kv_cols, 0
            ),
        ]
    )
    late = lax.psum(late.reshape(-1, LANES), "exp").reshape(-1)
    key_stat = late[:ctx_rows, None] / kv_total
    key_low = (key_scale * (key_hat_grad - key_hat * key_stat)).astype(BF16)
    pair_low = jnp.concatenate([key_low, value_grad], axis=1)
    key_sums = jnp.repeat(late[ctx_rows:].reshape(ctx_count, -1), 2, axis=1)[:, :, None]
    late_shards = exchange(
        jnp.concatenate(
            [
                dot(normed, pair_low, TN).astype(BF16).reshape(ctx_count, shard_rows, 2 * kv_cols),
                ride_along(key_sums),
            ],
            axis=2,
        ),
        "ctx",
    )
    late_back = exchange(pair_low.reshape(exp_count, own_rows, 2 * kv_cols), "exp")
    early_shards = jnp.sum(early_shards.astype(F32), axis=0)
    late_shards = jnp.sum(late_shards.astype(F32), axis=0)
    grad_w_query = early_shards[:, :head_cols]
    grad_w_out = early_shards[:, head_cols : 2 * head_cols]
    early_tail = parted(early_shards[:, 2 * head_cols :], 3)
    loss = early_tail[0, 2] / (valid_count * model_width)
    grad_w_key = late_shards[:, :kv_cols]
    grad_w_value = late_shards[:, kv_cols : 2 * kv_cols]
    key_tail = parted(late_shards[:, 2 * kv_cols :], 1)

    gain_part = jnp.sum(grad_w_query * w_query.astype(F32), axis=1)
    gain_part += jnp.sum(grad_w_key * w_key.astype(F32), axis=1)
    gain_part += jnp.sum(grad_w_value * w_value.astype(F32), axis=1)
    grad_gain_attn = lax.psum(gain_part, "exp") / gain_attn.astype(F32)
    normed_rows = jnp.einsum(
        "erk,edk->rd",
        jnp.concatenate([early_back, late_back], axis=2),
        all_qkv,
        preferred_element_type=F32,
    )
    own_hat = lax.dynamic_slice_in_dim(attn_hat, exp_index * own_rows, own_rows, 0)
    own_scale = lax.dynamic_slice_in_dim(attn_scale, exp_index * own_rows, own_rows, 0)
    grad_hidden = resid_grad + norm_back(normed_rows, own_hat, own_scale, attn_gain)
    return (
        block_out,
        loss,
        grad_hidden,
        grad_w_query,
        grad_w_key,
        grad_w_value,
        grad_w_out,
        grad_gain_attn,
        early_tail[:, 0],
        key_tail[::2, 0],
        early_tail[:, 1],
        grad_w_gate,
        grad_w_up,
        grad_w_down,
    )


def solution(mesh):
    return jax.shard_map(
        on_device,
        mesh=mesh,
        in_specs=(
            P("ctx", None),
            P(("ctx", "exp"), None),
            P(),
            P(),
            P(("ctx", "exp"), None),
            P(("ctx", "exp"), None),
            P("ctx", "exp"),
            P("ctx", "exp"),
            P("ctx", "exp"),
            P("ctx", "exp"),
            P("ctx"),
            P("ctx"),
            P("ctx"),
            P("ctx"),
            P("ctx", None, "exp"),
            P("ctx", None, "exp"),
            P("ctx", "exp", None),
        ),
        out_specs=(
            P(("ctx", "exp"), None),
            P(),
            P(("ctx", "exp"), None),
            P("ctx", "exp"),
            P("ctx", "exp"),
            P("ctx", "exp"),
            P("ctx", "exp"),
            P("ctx"),
            P("ctx"),
            P("ctx"),
            P("ctx"),
            P("ctx", None, "exp"),
            P("ctx", None, "exp"),
            P("ctx", "exp", None),
        ),
        check_vma=False,
    )
```

```python
import functools

import jax
import jax.numpy as jnp
from jax import lax
from jax.experimental import pallas as pl
from jax.experimental.pallas import tpu as pltpu
from jax.sharding import PartitionSpec as P

HD = 64
BLK = 128
CONT_LEN = 1024
CONT_BLKS = CONT_LEN // BLK
LANES = 128

NORM_EPSILON = 1e-05
ROPE_BASE = 10000.0
MASK_FLOOR = -1e30
F32 = jnp.float32
BF16 = jnp.bfloat16
NT = (((1,), (1,)), ((), ()))
NN = (((1,), (0,)), ((), ()))
TN = (((0,), (0,)), ((), ()))


def dot(left, right, dims):
    return lax.dot_general(left, right, dims, preferred_element_type=F32)


def key_ranges(block, half, tile_blocks):
    cont = block >= half
    inner = jnp.where(cont, (block - half) % CONT_BLKS, 0)
    n_a = jnp.where(cont, half // tile_blocks, block // tile_blocks)
    cont_base = half + (block - half) // CONT_BLKS * CONT_BLKS
    base = jnp.where(cont, cont_base, block // tile_blocks * tile_blocks) * BLK
    return n_a, base, inner // tile_blocks


def gather_blocks(table, total, moves):
    def start(i, carry):
        to = pl.multiple_of(table[i] * BLK, BLK)
        for source, target, sem in moves:
            pltpu.make_async_copy(source(i), target(to), sem).start()
        return carry

    lax.fori_loop(0, total, start, 0)


def wait_all(ref, sem):
    pltpu.make_async_copy(ref, ref, sem).wait()


def rows_of(ref, per_ctx):
    def place(i):
        first = i // 4 * per_ctx + i % 4 * BLK
        return ref.at[pl.ds(pl.multiple_of(first, 16), BLK)]

    return place


def causal(shape, key_first, query_first, rows_are_queries):
    row = lax.broadcasted_iota(jnp.int32, shape, 0) % BLK
    col = lax.broadcasted_iota(jnp.int32, shape, 1)
    if rows_are_queries:
        return key_first + col <= query_first + row
    return key_first + row <= query_first + col


def to_half(tile, source, target):
    values = tile.astype(F32)
    if source != target:
        values = pltpu.roll(values, HD, 1)
    lane = lax.broadcasted_iota(jnp.int32, values.shape, 1)
    return jnp.where(lane // HD == target, values, 0.0)


def turn(tile, cosine, sine):
    lane = lax.broadcasted_iota(jnp.int32, tile.shape, 1)
    ahead = pltpu.roll(tile, LANES - HD // 2, 1)
    behind = pltpu.roll(tile, HD // 2, 1)
    return tile * cosine + jnp.where(lane % HD < HD // 2, ahead, behind) * sine


def rows_by_head(source_ref, block_rows, target_ref):
    for h in range(4):
        m, g = h // 2, h % 2
        tile = source_ref[block_rows, m * LANES : (m + 1) * LANES]
        target_ref[h * BLK : (h + 1) * BLK, :] = to_half(tile, g, m).astype(BF16)


def rows_by_token(values):
    tiles = []
    for m in range(2):
        first = values[2 * m * BLK : (2 * m + 1) * BLK]
        second = values[(2 * m + 1) * BLK : (2 * m + 2) * BLK]
        tiles.append(to_half(first, m, 0) + to_half(second, m, 1))
    return tiles


def turn_kernel(pre_ref, scale_ref, gain_ref, cos_ref, sin_ref, q_ref, kv_ref):
    for col in range(3):
        lanes = slice(col * LANES, (col + 1) * LANES)
        which = 0 if col < 2 else 1
        hat = pre_ref[:, lanes] * scale_ref[:, which : which + 1]
        turned = turn(hat * gain_ref[:, lanes], cos_ref[...], sin_ref[...]).astype(BF16)
        if which == 0:
            q_ref[:, lanes] = (turned.astype(F32) * HD**-0.5).astype(BF16)
        else:
            kv_ref[:, :LANES] = turned
    kv_ref[:, LANES:] = pre_ref[:, 3 * LANES :].astype(BF16)


def attend_kernel(
    total, half, tile_blocks, table, own, q_in, kv, o_ref, lse_ref, kv_s, q_ref, acc, peak, sem
):
    gather_blocks(
        table,
        total,
        [
            (
                rows_of(kv, 4 * BLK),
                lambda to: kv_s.at[pl.ds(to, BLK), pl.ds(0, 2 * LANES)],
                sem.at[0],
            )
        ],
    )
    kv_s[:, 2 * LANES :] = jnp.ones((total * BLK, LANES), BF16)
    wait_all(kv_s.at[:, pl.ds(0, 2 * LANES)], sem.at[0])
    width = tile_blocks * BLK

    def query_block(i, carry):
        block = own[i]
        n_a, base, n_b = key_ranges(block, half, tile_blocks)
        rows = pl.ds(pl.multiple_of(i * BLK, BLK), BLK)
        lanes = pl.ds(pl.multiple_of(i % 2 * BLK, BLK), BLK)
        rows_by_head(q_in, rows, q_ref)

        def first_key(j):
            return pl.multiple_of(jnp.where(j < n_a, j * width, base + (j - n_a) * width), BLK)

        def tile(start, masked):
            scores = dot(q_ref[...], kv_s[pl.ds(start, width), :LANES], NT)
            probs = jnp.exp(scores)
            if masked:
                probs = jnp.where(causal(probs.shape, start, block * BLK, True), probs, 0.0)
            acc[...] += dot(probs.astype(BF16), kv_s[pl.ds(start, width), LANES:], NN)

        def clear_tile(j, carry):
            tile(first_key(j), False)
            return carry

        def store(out, log_sum):
            first, second = rows_by_token(out)
            o_ref[rows, :LANES] = first
            o_ref[rows, LANES:] = second
            for h in range(4):
                lse_ref[i // 2, h : h + 1, lanes] = log_sum[h * BLK : (h + 1) * BLK].T[:1]

        acc[...] = jnp.zeros_like(acc)
        lax.fori_loop(0, n_a + n_b, clear_tile, 0)
        tile(first_key(n_a + n_b), True)
        sums = acc[:, LANES:]
        in_range = (jnp.max(sums) < 2.0**100) & (jnp.min(sums) > 2.0**-40)

        @pl.when(in_range)
        def _():
            store(acc[:, :LANES] / sums, jnp.log(sums))

        @pl.when(jnp.logical_not(in_range))
        def _():
            acc[...] = jnp.zeros_like(acc)
            peak[...] = jnp.full_like(peak, MASK_FLOOR)

            def safe_tile(j, carry):
                start = first_key(j)
                scores = dot(q_ref[...], kv_s[pl.ds(start, width), :LANES], NT)
                seen = causal(scores.shape, start, block * BLK, True)
                scores = jnp.where(seen, scores, MASK_FLOOR)
                old = peak[...]
                new = jnp.maximum(old, jnp.max(scores, axis=1, keepdims=True))
                probs = jnp.where(seen, jnp.exp(scores - new[:, :1]), 0.0)
                keep = jnp.exp(old - new)
                acc[...] = acc[...] * keep[:, :1] + dot(
                    probs.astype(BF16), kv_s[pl.ds(start, width), LANES:], NN
                )
                peak[...] = new
                return carry

            lax.fori_loop(0, n_a + n_b + 1, safe_tile, 0)
            safe_sums = acc[:, LANES:]
            store(acc[:, :LANES] / safe_sums, peak[...] + jnp.log(safe_sums))

        return carry

    lax.fori_loop(0, 4, query_block, 0)


def query_grad_kernel(
    total,
    half,
    tile_blocks,
    table,
    own,
    q_in,
    do_in,
    o_in,
    lse_in,
    cos_ref,
    sin_ref,
    kv,
    dq_ref,
    kv_s,
    q_ref,
    do_ref,
    lse_ref,
    delta_ref,
    acc,
    sem,
):
    gather_blocks(
        table, total, [(rows_of(kv, 4 * BLK), lambda to: kv_s.at[pl.ds(to, BLK)], sem.at[0])]
    )
    wait_all(kv_s, sem.at[0])
    width = tile_blocks * BLK

    def query_block(i, carry):
        block = own[i]
        n_a, base, n_b = key_ranges(block, half, tile_blocks)
        rows = pl.ds(pl.multiple_of(i * BLK, BLK), BLK)
        lanes = pl.ds(pl.multiple_of(i % 2 * BLK, BLK), BLK)
        rows_by_head(q_in, rows, q_ref)
        rows_by_head(do_in, rows, do_ref)
        for h in range(4):
            part = slice(h * BLK, (h + 1) * BLK)
            pair = slice(h // 2 * LANES, (h // 2 + 1) * LANES)
            product = do_in[rows, pair].astype(F32) * o_in[rows, pair]
            own_half = to_half(product, h % 2, h % 2)
            delta = jnp.sum(own_half, axis=1, keepdims=True)
            delta_ref[part, :] = jnp.broadcast_to(delta, (BLK, LANES))
            row = lse_in[i // 2, h : h + 1, lanes]
            lse_ref[part, :] = jnp.broadcast_to(row, (LANES, BLK)).T

        def first_key(j):
            return pl.multiple_of(jnp.where(j < n_a, j * width, base + (j - n_a) * width), BLK)

        def tile(start, masked):
            keys = kv_s[pl.ds(start, width), :LANES]
            scores = dot(q_ref[...], keys, NT)
            prob_grad = dot(do_ref[...], kv_s[pl.ds(start, width), LANES:], NT)
            probs = jnp.exp(scores - lse_ref[:, :1])
            score_grad = probs * (prob_grad - delta_ref[:, :1])
            if masked:
                seen = causal(probs.shape, start, block * BLK, True)
                score_grad = jnp.where(seen, score_grad, 0.0)
            acc[...] += dot(score_grad.astype(BF16), keys, NN)

        def clear_tile(j, carry):
            tile(first_key(j), False)
            return carry

        acc[...] = jnp.zeros_like(acc)
        lax.fori_loop(0, n_a + n_b, clear_tile, 0)
        tile(first_key(n_a + n_b), True)
        for m, gradient in enumerate(rows_by_token(acc[...])):
            back = turn(gradient * HD**-0.5, cos_ref[rows, :], -sin_ref[rows, :])
            dq_ref[rows, m * LANES : (m + 1) * LANES] = back
        return carry

    lax.fori_loop(0, 4, query_block, 0)


def pair_grad_kernel(
    total,
    half,
    tile_blocks,
    do_rows,
    table,
    own,
    kv_in,
    cos_ref,
    sin_ref,
    q_all,
    do_all,
    aux,
    out_ref,
    q_s,
    do_s,
    aux_s,
    k_ref,
    v_ref,
    dk_ref,
    dv_ref,
    sem,
):
    gather_blocks(
        table,
        total,
        [
            (rows_of(q_all, 4 * BLK), lambda to: q_s.at[pl.ds(to, BLK)], sem.at[0]),
            (rows_of(do_all, do_rows), lambda to: do_s.at[pl.ds(to, BLK)], sem.at[1]),
            (
                lambda i: aux.at[i // 4, i // 2 % 2, :, pl.ds(pl.multiple_of(i % 2 * BLK, BLK), BLK)],
                lambda to: aux_s.at[:, pl.ds(to, BLK)],
                sem.at[2],
            ),
        ],
    )

    def place(blk, h):
        return (h * 2 + blk) * BLK if blk < 2 else ((blk * 4) + h) * BLK

    k_ref[...] = jnp.zeros_like(k_ref)
    v_ref[...] = jnp.zeros_like(v_ref)
    dk_ref[...] = jnp.zeros_like(dk_ref)
    dv_ref[...] = jnp.zeros_like(dv_ref)
    for blk in range(4):
        source = slice(blk * BLK, (blk + 1) * BLK)
        for h in range(4):
            m, g = h // 2, h % 2
            target = slice(place(blk, h), place(blk, h) + BLK)
            pair = slice(m * LANES, (m + 1) * LANES)
            k_ref[target, pair] = to_half(kv_in[source, :LANES], m, g).astype(BF16)
            v_ref[target, pair] = to_half(kv_in[source, LANES:], m, g).astype(BF16)
    wait_all(q_s, sem.at[0])
    wait_all(do_s, sem.at[1])
    wait_all(aux_s, sem.at[2])
    width = tile_blocks * BLK

    def tile(first_row, per_head, start, keys_first, masked):
        rows = pl.ds(first_row, 4 * per_head)
        queries = q_s[pl.ds(start, width), :]
        grads = do_s[pl.ds(start, width), :]
        scores = dot(k_ref[rows, :], queries, NT)
        prob_grad = dot(v_ref[rows, :], grads, NT)
        probs_low = []
        score_low = []
        for h in range(4):
            part = slice(h * per_head, (h + 1) * per_head)
            probs = jnp.exp(scores[part] - aux_s[h : h + 1, pl.ds(start, width)])
            if masked:
                seen = [causal((BLK, width), first, start, False) for first in keys_first]
                probs = jnp.where(jnp.concatenate(seen, axis=0), probs, 0.0)
            probs_low.append(probs.astype(BF16))
            shifted = prob_grad[part] - aux_s[4 + h : 5 + h, pl.ds(start, width)]
            score_low.append((probs * shifted).astype(BF16))
        dv_ref[rows, :] += dot(jnp.concatenate(probs_low, axis=0), grads, NN)
        dk_ref[rows, :] += dot(jnp.concatenate(score_low, axis=0), queries, NN)

    low = jnp.minimum(own[0], own[1])
    high = jnp.maximum(own[0], own[1])

    def edge_tile(j, carry):
        firsts = [own[0] * BLK, own[1] * BLK]
        tile(0, 2 * BLK, pl.multiple_of(j * width, width), firsts, True)
        return carry

    def clear_tile(j, carry):
        tile(0, 2 * BLK, pl.multiple_of(j * width, width), None, False)
        return carry

    lax.fori_loop(low // tile_blocks, high // tile_blocks + 1, edge_tile, 0)
    lax.fori_loop(high // tile_blocks + 1, total // tile_blocks, clear_tile, 0)
    for which in range(2):
        block = own[2 + which]
        stop = half + ((block - half) // CONT_BLKS + 1) * CONT_BLKS

        def cont_tile(j, carry, which=which, block=block):
            first_row = (8 + 4 * which) * BLK
            tile(first_row, BLK, pl.multiple_of(j * width, width), [block * BLK], True)
            return carry

        lax.fori_loop(block // tile_blocks, stop // tile_blocks, cont_tile, 0)

    def collect(ref, blk):
        tile_sum = None
        for h in range(4):
            m, g = h // 2, h % 2
            part = ref[place(blk, h) : place(blk, h) + BLK, m * LANES : (m + 1) * LANES]
            moved = to_half(part, g, m)
            tile_sum = moved if tile_sum is None else tile_sum + moved
        return tile_sum

    for blk in range(4):
        rows = slice(blk * BLK, (blk + 1) * BLK)
        out_ref[rows, :LANES] = turn(collect(dk_ref, blk), cos_ref[rows, :], -sin_ref[rows, :])
        out_ref[rows, LANES:] = collect(dv_ref, blk)


def down_strips(w_ref, pair, width):
    strips = [w_ref[u, :, 2 * width : 3 * width] for u in (2 * pair, 2 * pair + 1)]
    return jnp.concatenate(strips, axis=1)


def expert_kernel(quarters, width, x_ref, w_ref, out_ref, gate_ref, up_ref):
    acts = []
    for u in range(quarters):
        cols = slice(u * width, (u + 1) * width)
        pre = dot(x_ref[...], w_ref[u, :, : 2 * width], NN)
        gate, up = pre[:, :width], pre[:, width:]
        gate_ref[:, cols] = gate
        up_ref[:, cols] = up
        acts.append((gate * jax.nn.sigmoid(gate) * up).astype(BF16))
    out = None
    for pair in range(quarters // 2):
        act = jnp.concatenate(acts[2 * pair : 2 * pair + 2], axis=1)
        part = dot(act, down_strips(w_ref, pair, width), NT)
        out = part if out is None else out + part
    out_ref[...] = out.astype(BF16)


def expert_grad_kernel(
    quarters, width, dy_ref, gate_ref, up_ref, w_ref, dx_ref, dgate_ref, dup_ref, act_ref
):
    total = None
    for pair in range(quarters // 2):
        both = dot(dy_ref[...], down_strips(w_ref, pair, width), NN)
        for side in range(2):
            u = 2 * pair + side
            cols = slice(u * width, (u + 1) * width)
            act_grad = both[:, side * width : (side + 1) * width]
            gate, up = gate_ref[:, cols], up_ref[:, cols]
            sig = jax.nn.sigmoid(gate)
            gate_act = gate * sig
            act_ref[:, cols] = (gate_act * up).astype(BF16)
            gate_grad = (act_grad * up * sig * (1.0 + gate * (1.0 - sig))).astype(BF16)
            up_grad = (act_grad * gate_act).astype(BF16)
            dgate_ref[:, cols] = gate_grad
            dup_ref[:, cols] = up_grad
            grads = jnp.concatenate([gate_grad, up_grad], axis=1)
            part = dot(grads, w_ref[u, :, : 2 * width], NT)
            total = part if total is None else total + part
    dx_ref[...] = total.astype(BF16)


def block_of_whole(shape):
    return pl.BlockSpec(shape, lambda i, *_: (0,) * len(shape))


def kernel_call(kernel, name, prefetch, ins, outs, scratch, flops):
    hbm = pl.BlockSpec(memory_space=pl.ANY)
    moved = sum(x.size * x.dtype.itemsize for x, _ in ins)
    return pl.pallas_call(
        kernel,
        out_shape=tuple(outs),
        grid_spec=pltpu.PrefetchScalarGridSpec(
            num_scalar_prefetch=len(prefetch),
            grid=(1,),
            in_specs=[hbm if far else block_of_whole(x.shape) for x, far in ins],
            out_specs=tuple(block_of_whole(out.shape) for out in outs),
            scratch_shapes=scratch,
        ),
        compiler_params=pltpu.CompilerParams(vmem_limit_bytes=48 << 20),
        cost_estimate=pl.CostEstimate(flops=flops, bytes_accessed=moved, transcendentals=0),
        name=name,
    )(*prefetch, *(x for x, _ in ins))


def by_rows(kernel, name, rows, ins, outs, flops):
    def spec(shape):
        if len(shape) == 3:
            return pl.BlockSpec(shape, lambda i: (0, 0, 0))
        return pl.BlockSpec((rows, shape[1]), lambda i: (i, 0))

    return pl.pallas_call(
        kernel,
        out_shape=tuple(outs),
        grid=(outs[0].shape[0] // rows,),
        in_specs=[spec(x.shape) for x in ins],
        out_specs=tuple(spec(out.shape) for out in outs),
        compiler_params=pltpu.CompilerParams(vmem_limit_bytes=40 << 20),
        cost_estimate=pl.CostEstimate(flops=flops, bytes_accessed=10**7, transcendentals=0),
        name=name,
    )(*ins)


def expert_forward(rows_in, weights):
    slots, model_width = rows_in.shape
    quarters, _, cols = weights.shape
    width = cols // 3
    hidden = jax.ShapeDtypeStruct((slots, quarters * width), F32)
    return by_rows(
        functools.partial(expert_kernel, quarters, width),
        "expert",
        slots // 5,
        [rows_in, weights],
        [jax.ShapeDtypeStruct((slots, model_width), BF16), hidden, hidden],
        6 * slots * model_width * quarters * width,
    )


def expert_backward(rows_grad, gate_pre, up_pre, weights):
    slots, model_width = rows_grad.shape
    quarters, _, cols = weights.shape
    width = cols // 3
    hidden = jax.ShapeDtypeStruct((slots, quarters * width), BF16)
    return by_rows(
        functools.partial(expert_grad_kernel, quarters, width),
        "expert_grad",
        slots // 2,
        [rows_grad, gate_pre, up_pre, weights],
        [jax.ShapeDtypeStruct((slots, model_width), BF16), hidden, hidden, hidden],
        6 * slots * model_width * quarters * width,
    )


def turn_heads(projected, scales, gain, cosine, sine):
    rows = projected.shape[0]
    out = jax.ShapeDtypeStruct((rows, 2 * LANES), BF16)
    ins = [(x, False) for x in (projected, scales, gain, cosine, sine)]
    return kernel_call(turn_kernel, "turn_heads", (), ins, [out, out], [], 10**6)


def attend(table, own, q, kv_all):
    total = table.shape[0]
    return kernel_call(
        functools.partial(attend_kernel, total, total // 2, 8),
        "attend",
        (table, own),
        [(q, False), (kv_all, True)],
        [
            jax.ShapeDtypeStruct((4 * BLK, 2 * LANES), F32),
            jax.ShapeDtypeStruct((2, 4, 2 * BLK), F32),
        ],
        [
            pltpu.VMEM((total * BLK, 3 * LANES), BF16),
            pltpu.VMEM((4 * BLK, LANES), BF16),
            pltpu.VMEM((4 * BLK, 2 * LANES), F32),
            pltpu.VMEM((4 * BLK, LANES), F32),
            pltpu.SemaphoreType.DMA((1,)),
        ],
        20 * 10**9,
    )


def query_grad(table, own, q, out_grad, heads, lse, cosine, sine, kv_all):
    total = table.shape[0]
    ins = [(x, False) for x in (q, out_grad, heads, lse, cosine, sine)]
    return kernel_call(
        functools.partial(query_grad_kernel, total, total // 2, 4),
        "query_grad",
        (table, own),
        ins + [(kv_all, True)],
        [jax.ShapeDtypeStruct((4 * BLK, 2 * LANES), F32)],
        [
            pltpu.VMEM((total * BLK, 2 * LANES), BF16),
            pltpu.VMEM((4 * BLK, LANES), BF16),
            pltpu.VMEM((4 * BLK, LANES), BF16),
            pltpu.VMEM((4 * BLK, LANES), F32),
            pltpu.VMEM((4 * BLK, LANES), F32),
            pltpu.VMEM((4 * BLK, LANES), F32),
            pltpu.SemaphoreType.DMA((1,)),
        ],
        30 * 10**9,
    )[0]


def pair_grad(table, own, kv, cosine, sine, q_all, do_all, do_rows, aux):
    total = table.shape[0]
    ins = [(x, False) for x in (kv, cosine, sine)] + [(x, True) for x in (q_all, do_all, aux)]
    return kernel_call(
        functools.partial(pair_grad_kernel, total, total // 2, 2, do_rows),
        "pair_grad",
        (table, own),
        ins,
        [jax.ShapeDtypeStruct((4 * BLK, 2 * LANES), F32)],
        [
            pltpu.VMEM((total * BLK, 2 * LANES), BF16),
            pltpu.VMEM((total * BLK, 2 * LANES), BF16),
            pltpu.VMEM((8, total * BLK), F32),
            pltpu.VMEM((16 * BLK, 2 * LANES), BF16),
            pltpu.VMEM((16 * BLK, 2 * LANES), BF16),
            pltpu.VMEM((16 * BLK, 2 * LANES), F32),
            pltpu.VMEM((16 * BLK, 2 * LANES), F32),
            pltpu.SemaphoreType.DMA((3,)),
        ],
        40 * 10**9,
    )[0]


def turn_tables(position):
    half_dim = HD // 2
    frequency = ROPE_BASE ** (-(jnp.arange(half_dim, dtype=F32) * 2.0 / HD))
    angles = position[:, None] * frequency[None, :]
    cosine, sine = jnp.cos(angles), jnp.sin(angles)
    return jnp.concatenate([cosine] * 4, axis=1), jnp.concatenate([-sine, sine] * 2, axis=1)


def norm_back(grad_normed, hat_values, scale_values, gain_values):
    grad_hat = grad_normed * gain_values
    return scale_values * (
        grad_hat - hat_values * jnp.mean(grad_hat * hat_values, axis=-1, keepdims=True)
    )


def pieces(values, count):
    parts = []
    for _ in range(count):
        part = lax.reduce_precision(values, 8, 7)
        parts.append(part.astype(BF16))
        values = values - part
    return parts


def exchange(values, axis):
    return lax.all_to_all(values, axis, split_axis=0, concat_axis=0, tiled=True)


def spread(values, axis, count):
    return exchange(jnp.broadcast_to(values[None], (count,) + values.shape), axis)


def shifted(values, axis, count):
    parts = [values]
    for step in range(1, count):
        parts.append(lax.ppermute(values, axis, [(i, (i + step) % count) for i in range(count)]))
    return parts


def gather_short(values, axis, index, count):
    parts = shifted(values, axis, count)
    ordered = []
    for place in range(count):
        back = (index - place) % count
        part = parts[0]
        for step in range(1, count):
            part = jnp.where(back == step, parts[step], part)
        ordered.append(part)
    return jnp.stack(ordered, axis=0)


def ride_along(values):
    parts = jnp.concatenate(pieces(values, 3), axis=-1)
    return jnp.pad(parts, ((0, 0), (0, 0), (0, LANES - parts.shape[-1])))


def parted(sums, count):
    return sum(sums[:, i * count : (i + 1) * count] for i in range(3))


def on_device(
    hidden_in,
    teacher,
    valid,
    block_of,
    routes,
    gates,
    w_query,
    w_key,
    w_value,
    w_out,
    gain_attn,
    gain_query,
    gain_key,
    gain_ffn,
    w_gate,
    w_up,
    w_down,
):
    ctx_count = lax.axis_size("ctx")
    exp_count = lax.axis_size("exp")
    ctx_index = lax.axis_index("ctx")
    exp_index = lax.axis_index("exp")
    ctx_rows, model_width = hidden_in.shape
    own_rows = ctx_rows // exp_count
    token_total = block_of.shape[0] * BLK
    head_cols = w_query.shape[1]
    kv_cols = w_key.shape[1]
    kv_total = kv_cols * exp_count
    qkv_cols = head_cols + 2 * kv_cols
    shard_rows = w_query.shape[0]

    own_qkv = jnp.concatenate([w_query, w_key, w_value], axis=1)
    mine = jnp.arange(model_width, dtype=jnp.int32) // shard_rows == ctx_index
    places = [
        jnp.where(mine, jnp.tile(gain, ctx_count), 0).astype(BF16)
        for gain in (gain_attn, gain_query, gain_ffn)
    ]
    mine_key = jnp.arange(kv_total, dtype=jnp.int32) // gain_key.shape[0] == ctx_index
    places.append(jnp.where(mine_key, jnp.tile(gain_key, ctx_count), 0).astype(BF16))
    gain_rows = jnp.concatenate(places)
    gain_rows = jnp.pad(gain_rows, (0, 8 * qkv_cols - gain_rows.shape[0])).reshape(8, qkv_cols)
    first_parts = spread(jnp.concatenate([own_qkv, gain_rows], axis=0), "ctx", ctx_count)
    full_qkv = first_parts[:, :shard_rows].reshape(model_width, qkv_cols)
    gains = jnp.sum(first_parts[:, shard_rows:].astype(F32), axis=0).reshape(-1)
    attn_gain = gains[:model_width]
    query_gain_all = gains[model_width : 2 * model_width]
    ffn_gain = gains[2 * model_width : 3 * model_width]
    key_gain_all = gains[3 * model_width : 3 * model_width + kv_total]
    query_gain = lax.dynamic_slice_in_dim(query_gain_all, exp_index * head_cols, head_cols)
    key_gain = lax.dynamic_slice_in_dim(key_gain_all, exp_index * kv_cols, kv_cols)

    hidden_f = hidden_in.astype(F32)
    attn_scale = lax.rsqrt(jnp.mean(hidden_f * hidden_f, axis=-1, keepdims=True) + NORM_EPSILON)
    attn_hat = hidden_f * attn_scale
    normed = (attn_hat * attn_gain).astype(BF16)
    projected = dot(normed, full_qkv, NN)
    query_pre = projected[:, :head_cols]
    key_pre = projected[:, head_cols : head_cols + kv_cols]
    query_square, key_square = lax.psum(
        jnp.stack([jnp.sum(query_pre * query_pre, axis=1), jnp.sum(key_pre * key_pre, axis=1)]),
        "exp",
    )
    query_scale = lax.rsqrt(query_square / model_width + NORM_EPSILON)[:, None]
    key_scale = lax.rsqrt(key_square / kv_total + NORM_EPSILON)[:, None]
    query_hat = query_pre * query_scale
    key_hat = key_pre * key_scale
    own_blocks = lax.dynamic_slice_in_dim(block_of, ctx_index * 4, 4)
    token_ids = (own_blocks[:, None] * BLK + jnp.arange(BLK, dtype=jnp.int32)[None]).reshape(-1)
    prompt_len = token_total // 2
    position = jnp.where(
        token_ids >= prompt_len, prompt_len + (token_ids - prompt_len) % CONT_LEN, token_ids
    ).astype(F32)
    cosine, sine = turn_tables(position)
    queries_rot, own_kv = turn_heads(
        projected,
        jnp.concatenate([query_scale, key_scale], axis=1),
        jnp.concatenate([query_gain, key_gain])[None],
        cosine,
        sine,
    )
    kv_all = lax.all_gather(own_kv, "ctx", axis=0, tiled=True)
    own_out, own_gate, own_up, own_down, _ = lax.optimization_barrier(
        (w_out, w_gate[0], w_up[0], w_down[0], own_kv)
    )
    width = w_gate.shape[2]
    own_expert = jnp.concatenate([own_gate, own_up, own_down.T], axis=1)
    expert = lax.all_gather(own_expert, "exp", axis=0, tiled=False)
    full_out = gather_short(
        spread(own_out, "ctx", ctx_count).reshape(model_width, head_cols),
        "exp",
        exp_index,
        exp_count,
    )
    expert_total = ctx_count
    capacity = max(2, own_rows * routes.shape[1] * 5 // (expert_total * 4))
    slots = expert_total * capacity
    names = routes[:, :, None] == jnp.arange(expert_total, dtype=jnp.int32)[None, None, :]
    named = jnp.any(names, axis=1)
    gate_of = jnp.sum(jnp.where(names, gates[:, :, None], 0.0), axis=1)
    before = jnp.tril(jnp.ones((own_rows, own_rows), BF16), -1)
    rank = dot(before, named.astype(BF16), NN).astype(jnp.int32)
    slot_rank = jnp.where(named, rank, -1).T[:, None, :]
    holds = slot_rank == jnp.arange(capacity, dtype=jnp.int32)[None, :, None]
    pick = holds.astype(BF16).reshape(slots, own_rows)
    weigh = jnp.where(holds, gate_of.T[:, None, :], 0.0).reshape(slots, own_rows)
    slot_gate = jnp.sum(weigh, axis=1, keepdims=True)

    kv_all, full_out, pick, weigh, slot_gate = lax.optimization_barrier(
        (kv_all, full_out, pick, weigh, slot_gate)
    )
    heads_f, lse = attend(block_of, own_blocks, queries_rot, kv_all)
    heads_low = heads_f.astype(BF16)

    own_heads = exchange(heads_low.reshape(exp_count, own_rows, head_cols), "exp")
    own_heads, later_q = lax.optimization_barrier((own_heads, queries_rot))
    q_all = lax.all_gather(later_q, "ctx", axis=0, tiled=True)
    attn_rows = jnp.einsum("erk,eok->ro", own_heads, full_out, preferred_element_type=F32)
    hidden_rows = lax.dynamic_slice_in_dim(hidden_in, exp_index * own_rows, own_rows, 0)
    hidden_rows = hidden_rows.astype(F32)
    resid = hidden_rows + attn_rows
    ffn_scale = lax.rsqrt(jnp.mean(resid * resid, axis=-1, keepdims=True) + NORM_EPSILON)
    ffn_hat = resid * ffn_scale
    normed_ffn = (ffn_hat * ffn_gain).astype(BF16)

    def send(rows):
        return exchange(rows.reshape(ctx_count, capacity, model_width), "ctx").reshape(
            slots, model_width
        )

    expert_in = send(dot(pick, normed_ffn, NN).astype(BF16))
    expert_out, gate_pre, up_pre = expert_forward(expert_in, expert)
    returned = send(expert_out)
    returned, q_all, later_qkv = lax.optimization_barrier((returned, q_all, full_qkv))
    all_qkv = lax.all_gather(later_qkv, "exp", axis=0, tiled=False)
    moe_parts = dot(jnp.concatenate(pieces(weigh, 2), axis=1), returned, TN)
    moe_rows = moe_parts[:own_rows] + moe_parts[own_rows:]
    block_out = resid + moe_rows

    row_start = (ctx_index * exp_count + exp_index) * own_rows
    row_valid = lax.dynamic_slice_in_dim(valid, row_start, own_rows, 0).astype(F32)
    valid_count = jnp.sum(valid.astype(F32))
    misfit = block_out - teacher.astype(F32)
    local_loss = jnp.sum(row_valid[:, None] * misfit * misfit)
    out_grad_rows = misfit * row_valid[:, None] * (token_total / valid_count)
    copy_grad = dot(
        jnp.concatenate([pick, pick], axis=1),
        jnp.concatenate(pieces(out_grad_rows, 2), axis=0),
        NN,
    )
    grad_copies = send((slot_gate * copy_grad).astype(BF16))
    input_grad, gate_grad, up_grad, hidden_act = expert_backward(
        grad_copies, gate_pre, up_pre, expert
    )
    arrived_grad = send(input_grad)
    arrived_grad, all_qkv = lax.optimization_barrier((arrived_grad, all_qkv))
    ffn_normed_grad = dot(pick, arrived_grad, TN)

    ffn_gain_part = jnp.sum(ffn_normed_grad * ffn_hat, axis=0)
    resid_grad = out_grad_rows + norm_back(ffn_normed_grad, ffn_hat, ffn_scale, ffn_gain)
    branch_rows = resid_grad.astype(BF16)

    do_rows = jnp.einsum("ro,eok->erk", branch_rows, full_out, preferred_element_type=F32)
    out_grad = exchange(do_rows.astype(BF16), "exp").reshape(ctx_rows, head_cols)
    branch_parts = shifted(branch_rows, "exp", exp_count)
    head_of = jnp.arange(head_cols, dtype=jnp.int32)[None] // HD
    head_ones = (head_of == jnp.arange(4, dtype=jnp.int32)[:, None]).astype(F32)
    delta = lax.dot_general(
        head_ones,
        out_grad.astype(F32) * heads_f,
        NT,
        precision=lax.Precision.HIGHEST,
        preferred_element_type=F32,
    )
    delta = delta.reshape(4, 2, 2 * BLK).transpose(1, 0, 2)
    row_stats = jnp.concatenate([lse, delta], axis=1)
    stat_parts = jnp.stack(pieces(row_stats, 3), axis=0).reshape(-1, 2 * BLK)
    stat_rows = stat_parts.shape[0]
    do_all = lax.all_gather(
        jnp.concatenate([out_grad, stat_parts], axis=0), "ctx", axis=0, tiled=False
    )
    query_n_grad = query_grad(
        block_of, own_blocks, queries_rot, out_grad, heads_f, lse, cosine, sine, kv_all
    )

    grad_out = None
    for step, part in enumerate(branch_parts):
        first = (exp_index - step) % exp_count * own_rows
        term = dot(part, lax.dynamic_slice_in_dim(heads_low, first, own_rows, 0), TN)
        grad_out = term if grad_out is None else grad_out + term

    gate_part = dot(expert_in, gate_grad, TN)
    up_part = dot(expert_in, up_grad, TN)
    down_part = dot(hidden_act, grad_copies, TN)
    gate_part = gate_part.reshape(model_width, exp_count, width).transpose(1, 0, 2)
    up_part = up_part.reshape(model_width, exp_count, width).transpose(1, 0, 2)
    do_all, query_n_grad, grad_out, gate_part, up_part, down_part = lax.optimization_barrier(
        (do_all, query_n_grad, grad_out, gate_part, up_part, down_part)
    )
    grad_w_gate = lax.psum_scatter(gate_part, "exp", scatter_dimension=0, tiled=True)
    grad_w_up = lax.psum_scatter(up_part, "exp", scatter_dimension=0, tiled=True)
    grad_w_down = lax.psum_scatter(down_part, "exp", scatter_dimension=0, tiled=True)[None]

    query_gain_part = jnp.sum(query_n_grad * query_hat, axis=0)
    query_hat_grad = query_n_grad * query_gain
    early = jnp.concatenate(
        [
            jnp.sum(query_hat_grad * query_hat, axis=1),
            lax.dynamic_update_slice_in_dim(
                jnp.zeros((model_width,), F32), query_gain_part, exp_index * head_cols, 0
            ),
            ffn_gain_part,
            jnp.full((4 * LANES,), local_loss),
        ]
    )
    early = lax.psum(early.reshape(-1, LANES), "exp").reshape(-1)
    do_all, early = lax.optimization_barrier((do_all, early))
    query_stat = early[:ctx_rows, None] / model_width
    query_low = (query_scale * (query_hat_grad - query_hat * query_stat)).astype(BF16)
    early_sums = jnp.stack(
        [
            early[ctx_rows : ctx_rows + model_width].reshape(ctx_count, shard_rows),
            early[ctx_rows + model_width : ctx_rows + 2 * model_width].reshape(
                ctx_count, shard_rows
            ),
            jnp.broadcast_to(early[-1], (ctx_count, shard_rows)),
        ],
        axis=-1,
    )
    early_shards = exchange(
        jnp.concatenate(
            [
                dot(normed, query_low, TN).astype(BF16).reshape(ctx_count, shard_rows, head_cols),
                grad_out.astype(BF16).reshape(ctx_count, shard_rows, head_cols),
                ride_along(early_sums),
            ],
            axis=2,
        ),
        "ctx",
    )
    early_back = exchange(query_low.reshape(exp_count, own_rows, head_cols), "exp")

    aux = jnp.sum(
        do_all[:, ctx_rows:].reshape(ctx_count, 3, 2, 8, 2 * BLK).astype(F32), axis=1
    )
    pair_grads = pair_grad(
        block_of,
        own_blocks,
        own_kv,
        cosine,
        sine,
        q_all,
        do_all.reshape(-1, head_cols),
        ctx_rows + stat_rows,
        aux,
    )
    pair_grads, early_shards, early_back = lax.optimization_barrier(
        (pair_grads, early_shards, early_back)
    )
    key_n_grad = pair_grads[:, :kv_cols]
    value_grad = pair_grads[:, kv_cols:].astype(BF16)
    key_gain_part = jnp.sum(key_n_grad * key_hat, axis=0)
    key_hat_grad = key_n_grad * key_gain
    late = jnp.concatenate(
        [
            jnp.sum(key_hat_grad * key_hat, axis=1),
            lax.dynamic_update_slice_in_dim(
                jnp.zeros((kv_total,), F32), key_gain_part, exp_index * kv_cols, 0
            ),
        ]
    )
    late = lax.psum(late.reshape(-1, LANES), "exp").reshape(-1)
    key_stat = late[:ctx_rows, None] / kv_total
    key_low = (key_scale * (key_hat_grad - key_hat * key_stat)).astype(BF16)
    pair_low = jnp.concatenate([key_low, value_grad], axis=1)
    key_sums = jnp.repeat(late[ctx_rows:].reshape(ctx_count, -1), 2, axis=1)[:, :, None]
    late_shards = exchange(
        jnp.concatenate(
            [
                dot(normed, pair_low, TN).astype(BF16).reshape(ctx_count, shard_rows, 2 * kv_cols),
                ride_along(key_sums),
            ],
            axis=2,
        ),
        "ctx",
    )
    late_back = exchange(pair_low.reshape(exp_count, own_rows, 2 * kv_cols), "exp")
    early_shards = jnp.sum(early_shards.astype(F32), axis=0)
    late_shards = jnp.sum(late_shards.astype(F32), axis=0)
    grad_w_query = early_shards[:, :head_cols]
    grad_w_out = early_shards[:, head_cols : 2 * head_cols]
    early_tail = parted(early_shards[:, 2 * head_cols :], 3)
    loss = early_tail[0, 2] / (valid_count * model_width)
    grad_w_key = late_shards[:, :kv_cols]
    grad_w_value = late_shards[:, kv_cols : 2 * kv_cols]
    key_tail = parted(late_shards[:, 2 * kv_cols :], 1)

    gain_part = jnp.sum(grad_w_query * w_query.astype(F32), axis=1)
    gain_part += jnp.sum(grad_w_key * w_key.astype(F32), axis=1)
    gain_part += jnp.sum(grad_w_value * w_value.astype(F32), axis=1)
    grad_gain_attn = lax.psum(gain_part, "exp") / gain_attn.astype(F32)
    normed_rows = jnp.einsum(
        "erk,edk->rd",
        jnp.concatenate([early_back, late_back], axis=2),
        all_qkv,
        preferred_element_type=F32,
    )
    own_scale = lax.dynamic_slice_in_dim(attn_scale, exp_index * own_rows, own_rows, 0)
    own_hat = hidden_rows * own_scale
    grad_hidden = resid_grad + norm_back(normed_rows, own_hat, own_scale, attn_gain)
    return (
        block_out,
        loss,
        grad_hidden,
        grad_w_query,
        grad_w_key,
        grad_w_value,
        grad_w_out,
        grad_gain_attn,
        early_tail[:, 0],
        key_tail[::2, 0],
        early_tail[:, 1],
        grad_w_gate,
        grad_w_up,
        grad_w_down,
    )


def solution(mesh):
    return jax.shard_map(
        on_device,
        mesh=mesh,
        in_specs=(
            P("ctx", None),
            P(("ctx", "exp"), None),
            P(),
            P(),
            P(("ctx", "exp"), None),
            P(("ctx", "exp"), None),
            P("ctx", "exp"),
            P("ctx", "exp"),
            P("ctx", "exp"),
            P("ctx", "exp"),
            P("ctx"),
            P("ctx"),
            P("ctx"),
            P("ctx"),
            P("ctx", None, "exp"),
            P("ctx", None, "exp"),
            P("ctx", "exp", None),
        ),
        out_specs=(
            P(("ctx", "exp"), None),
            P(),
            P(("ctx", "exp"), None),
            P("ctx", "exp"),
            P("ctx", "exp"),
            P("ctx", "exp"),
            P("ctx", "exp"),
            P("ctx"),
            P("ctx"),
            P("ctx"),
            P("ctx"),
            P("ctx", None, "exp"),
            P("ctx", None, "exp"),
            P("ctx", "exp", None),
        ),
        check_vma=False,
    )
```

```python
import functools

import jax
import jax.numpy as jnp
from jax import lax
from jax.experimental import pallas as pl
from jax.experimental.pallas import tpu as pltpu
from jax.sharding import PartitionSpec as P

HD = 64
BLK = 128
CONT_LEN = 1024
CONT_BLKS = CONT_LEN // BLK
LANES = 128

NORM_EPSILON = 1e-05
ROPE_BASE = 10000.0
MASK_FLOOR = -1e30
F32 = jnp.float32
BF16 = jnp.bfloat16
NT = (((1,), (1,)), ((), ()))
NN = (((1,), (0,)), ((), ()))
TN = (((0,), (0,)), ((), ()))


def dot(left, right, dims):
    return lax.dot_general(left, right, dims, preferred_element_type=F32)


def key_ranges(block, half, tile_blocks):
    cont = block >= half
    inner = jnp.where(cont, (block - half) % CONT_BLKS, 0)
    n_a = jnp.where(cont, half // tile_blocks, block // tile_blocks)
    cont_base = half + (block - half) // CONT_BLKS * CONT_BLKS
    base = jnp.where(cont, cont_base, block // tile_blocks * tile_blocks) * BLK
    return n_a, base, inner // tile_blocks


def gather_blocks(table, total, moves):
    def start(i, carry):
        to = pl.multiple_of(table[i] * BLK, BLK)
        for source, target, sem in moves:
            pltpu.make_async_copy(source(i), target(to), sem).start()
        return carry

    lax.fori_loop(0, total, start, 0)


def wait_all(ref, sem):
    pltpu.make_async_copy(ref, ref, sem).wait()


def rows_of(ref, per_ctx):
    def place(i):
        first = i // 4 * per_ctx + i % 4 * BLK
        return ref.at[pl.ds(pl.multiple_of(first, 16), BLK)]

    return place


def causal(shape, key_first, query_first, rows_are_queries):
    row = lax.broadcasted_iota(jnp.int32, shape, 0) % BLK
    col = lax.broadcasted_iota(jnp.int32, shape, 1)
    if rows_are_queries:
        return key_first + col <= query_first + row
    return key_first + row <= query_first + col


def to_half(tile, source, target):
    values = tile.astype(F32)
    if source != target:
        values = pltpu.roll(values, HD, 1)
    lane = lax.broadcasted_iota(jnp.int32, values.shape, 1)
    return jnp.where(lane // HD == target, values, 0.0)


def turn(tile, cosine, sine):
    lane = lax.broadcasted_iota(jnp.int32, tile.shape, 1)
    ahead = pltpu.roll(tile, LANES - HD // 2, 1)
    behind = pltpu.roll(tile, HD // 2, 1)
    return tile * cosine + jnp.where(lane % HD < HD // 2, ahead, behind) * sine


def rows_by_head(source_ref, block_rows, target_ref):
    for h in range(4):
        m, g = h // 2, h % 2
        tile = source_ref[block_rows, m * LANES : (m + 1) * LANES]
        target_ref[h * BLK : (h + 1) * BLK, :] = to_half(tile, g, m).astype(BF16)


def rows_by_token(values):
    tiles = []
    for m in range(2):
        first = values[2 * m * BLK : (2 * m + 1) * BLK]
        second = values[(2 * m + 1) * BLK : (2 * m + 2) * BLK]
        tiles.append(to_half(first, m, 0) + to_half(second, m, 1))
    return tiles


def turn_kernel(pre_ref, scale_ref, gain_ref, cos_ref, sin_ref, q_ref, kv_ref):
    for col in range(3):
        lanes = slice(col * LANES, (col + 1) * LANES)
        which = 0 if col < 2 else 1
        hat = pre_ref[:, lanes] * scale_ref[:, which : which + 1]
        turned = turn(hat * gain_ref[:, lanes], cos_ref[...], sin_ref[...]).astype(BF16)
        if which == 0:
            q_ref[:, lanes] = (turned.astype(F32) * HD**-0.5).astype(BF16)
        else:
            kv_ref[:, :LANES] = turned
    kv_ref[:, LANES:] = pre_ref[:, 3 * LANES :].astype(BF16)


def attend_kernel(
    total, half, tile_blocks, table, own, q_in, kv, o_ref, lse_ref, kv_s, q_ref, acc, peak, s_buf, sem
):
    gather_blocks(
        table,
        total,
        [
            (
                rows_of(kv, 4 * BLK),
                lambda to: kv_s.at[pl.ds(to, BLK), pl.ds(0, 2 * LANES)],
                sem.at[0],
            )
        ],
    )
    kv_s[:, 2 * LANES :] = jnp.ones((total * BLK, LANES), BF16)
    wait_all(kv_s.at[:, pl.ds(0, 2 * LANES)], sem.at[0])
    width = tile_blocks * BLK

    def query_block(i, carry):
        block = own[i]
        n_a, base, n_b = key_ranges(block, half, tile_blocks)
        rows = pl.ds(pl.multiple_of(i * BLK, BLK), BLK)
        lanes = pl.ds(pl.multiple_of(i % 2 * BLK, BLK), BLK)
        rows_by_head(q_in, rows, q_ref)

        def first_key(j):
            return pl.multiple_of(jnp.where(j < n_a, j * width, base + (j - n_a) * width), BLK)

        def tile(start, masked):
            scores = dot(q_ref[...], kv_s[pl.ds(start, width), :LANES], NT)
            probs = jnp.exp(scores)
            if masked:
                probs = jnp.where(causal(probs.shape, start, block * BLK, True), probs, 0.0)
            acc[...] += dot(probs.astype(BF16), kv_s[pl.ds(start, width), LANES:], NN)

        def clear_tile(j, carry):
            tile(first_key(j), False)
            return carry

        def store(out, log_sum):
            first, second = rows_by_token(out)
            o_ref[rows, :LANES] = first
            o_ref[rows, LANES:] = second
            for h in range(4):
                lse_ref[i // 2, h : h + 1, lanes] = log_sum[h * BLK : (h + 1) * BLK].T[:1]

        def score(j):
            return dot(q_ref[...], kv_s[pl.ds(first_key(j), width), :LANES], NT)

        def weigh(scores, j, masked):
            start = first_key(j)
            probs = jnp.exp(scores)
            if masked:
                probs = jnp.where(causal(probs.shape, start, block * BLK, True), probs, 0.0)
            acc[...] += dot(probs.astype(BF16), kv_s[pl.ds(start, width), LANES:], NN)

        acc[...] = jnp.zeros_like(acc)
        count = n_a + n_b
        s_buf[0] = score(0)

        def two_tiles(i2, carry):
            j = 2 * i2
            s_buf[1] = score(j + 1)
            weigh(s_buf[0], j, False)
            s_buf[0] = score(j + 2)
            weigh(s_buf[1], j + 1, False)
            return carry

        lax.fori_loop(0, count // 2, two_tiles, 0)

        @pl.when(count % 2 == 1)
        def _():
            s_buf[1] = score(count)
            weigh(s_buf[0], count - 1, False)
            weigh(s_buf[1], count, True)

        @pl.when(count % 2 == 0)
        def _():
            weigh(s_buf[0], count, True)

        sums = acc[:, LANES:]
        in_range = (jnp.max(sums) < 2.0**100) & (jnp.min(sums) > 2.0**-40)

        @pl.when(in_range)
        def _():
            store(acc[:, :LANES] / sums, jnp.log(sums))

        @pl.when(jnp.logical_not(in_range))
        def _():
            acc[...] = jnp.zeros_like(acc)
            peak[...] = jnp.full_like(peak, MASK_FLOOR)

            def safe_tile(j, carry):
                start = first_key(j)
                scores = dot(q_ref[...], kv_s[pl.ds(start, width), :LANES], NT)
                seen = causal(scores.shape, start, block * BLK, True)
                scores = jnp.where(seen, scores, MASK_FLOOR)
                old = peak[...]
                new = jnp.maximum(old, jnp.max(scores, axis=1, keepdims=True))
                probs = jnp.where(seen, jnp.exp(scores - new[:, :1]), 0.0)
                keep = jnp.exp(old - new)
                acc[...] = acc[...] * keep[:, :1] + dot(
                    probs.astype(BF16), kv_s[pl.ds(start, width), LANES:], NN
                )
                peak[...] = new
                return carry

            lax.fori_loop(0, n_a + n_b + 1, safe_tile, 0)
            safe_sums = acc[:, LANES:]
            store(acc[:, :LANES] / safe_sums, peak[...] + jnp.log(safe_sums))

        return carry

    lax.fori_loop(0, 4, query_block, 0)


def query_grad_kernel(
    total,
    half,
    tile_blocks,
    table,
    own,
    q_in,
    do_in,
    o_in,
    lse_in,
    cos_ref,
    sin_ref,
    kv,
    dq_ref,
    kv_s,
    q_ref,
    do_ref,
    lse_ref,
    delta_ref,
    acc,
    sem,
):
    gather_blocks(
        table, total, [(rows_of(kv, 4 * BLK), lambda to: kv_s.at[pl.ds(to, BLK)], sem.at[0])]
    )
    wait_all(kv_s, sem.at[0])
    width = tile_blocks * BLK

    def query_block(i, carry):
        block = own[i]
        n_a, base, n_b = key_ranges(block, half, tile_blocks)
        rows = pl.ds(pl.multiple_of(i * BLK, BLK), BLK)
        lanes = pl.ds(pl.multiple_of(i % 2 * BLK, BLK), BLK)
        rows_by_head(q_in, rows, q_ref)
        rows_by_head(do_in, rows, do_ref)
        for h in range(4):
            part = slice(h * BLK, (h + 1) * BLK)
            pair = slice(h // 2 * LANES, (h // 2 + 1) * LANES)
            product = do_in[rows, pair].astype(F32) * o_in[rows, pair]
            own_half = to_half(product, h % 2, h % 2)
            delta = jnp.sum(own_half, axis=1, keepdims=True)
            delta_ref[part, :] = jnp.broadcast_to(delta, (BLK, LANES))
            row = lse_in[i // 2, h : h + 1, lanes]
            lse_ref[part, :] = jnp.broadcast_to(row, (LANES, BLK)).T

        def first_key(j):
            return pl.multiple_of(jnp.where(j < n_a, j * width, base + (j - n_a) * width), BLK)

        def tile(start, masked):
            keys = kv_s[pl.ds(start, width), :LANES]
            scores = dot(q_ref[...], keys, NT)
            prob_grad = dot(do_ref[...], kv_s[pl.ds(start, width), LANES:], NT)
            probs = jnp.exp(scores - lse_ref[:, :1])
            score_grad = probs * (prob_grad - delta_ref[:, :1])
            if masked:
                seen = causal(probs.shape, start, block * BLK, True)
                score_grad = jnp.where(seen, score_grad, 0.0)
            acc[...] += dot(score_grad.astype(BF16), keys, NN)

        def clear_tile(j, carry):
            tile(first_key(j), False)
            return carry

        acc[...] = jnp.zeros_like(acc)
        lax.fori_loop(0, n_a + n_b, clear_tile, 0)
        tile(first_key(n_a + n_b), True)
        for m, gradient in enumerate(rows_by_token(acc[...])):
            back = turn(gradient * HD**-0.5, cos_ref[rows, :], -sin_ref[rows, :])
            dq_ref[rows, m * LANES : (m + 1) * LANES] = back
        return carry

    lax.fori_loop(0, 4, query_block, 0)


def pair_grad_kernel(
    total,
    half,
    tile_blocks,
    do_rows,
    table,
    own,
    kv_in,
    cos_ref,
    sin_ref,
    q_all,
    do_all,
    aux,
    out_ref,
    q_s,
    do_s,
    aux_s,
    k_ref,
    v_ref,
    dk_ref,
    dv_ref,
    s_buf,
    p_buf,
    sem,
):
    gather_blocks(
        table,
        total,
        [
            (rows_of(q_all, 4 * BLK), lambda to: q_s.at[pl.ds(to, BLK)], sem.at[0]),
            (rows_of(do_all, do_rows), lambda to: do_s.at[pl.ds(to, BLK)], sem.at[1]),
            (
                lambda i: aux.at[i // 4, i // 2 % 2, :, pl.ds(pl.multiple_of(i % 2 * BLK, BLK), BLK)],
                lambda to: aux_s.at[:, pl.ds(to, BLK)],
                sem.at[2],
            ),
        ],
    )

    def place(blk, h):
        return (h * 2 + blk) * BLK if blk < 2 else ((blk * 4) + h) * BLK

    k_ref[...] = jnp.zeros_like(k_ref)
    v_ref[...] = jnp.zeros_like(v_ref)
    dk_ref[...] = jnp.zeros_like(dk_ref)
    dv_ref[...] = jnp.zeros_like(dv_ref)
    for blk in range(4):
        source = slice(blk * BLK, (blk + 1) * BLK)
        for h in range(4):
            m, g = h // 2, h % 2
            target = slice(place(blk, h), place(blk, h) + BLK)
            pair = slice(m * LANES, (m + 1) * LANES)
            k_ref[target, pair] = to_half(kv_in[source, :LANES], m, g).astype(BF16)
            v_ref[target, pair] = to_half(kv_in[source, LANES:], m, g).astype(BF16)
    wait_all(q_s, sem.at[0])
    wait_all(do_s, sem.at[1])
    wait_all(aux_s, sem.at[2])
    width = tile_blocks * BLK

    def score(first_row, per_head, j):
        rows = pl.ds(first_row, 4 * per_head)
        start = pl.multiple_of(j * width, width)
        scores = dot(k_ref[rows, :], q_s[pl.ds(start, width), :], NT)
        return scores, dot(v_ref[rows, :], do_s[pl.ds(start, width), :], NT)

    def add(first_row, per_head, j, scores, prob_grad, keys_first):
        rows = pl.ds(first_row, 4 * per_head)
        start = pl.multiple_of(j * width, width)
        probs_low = []
        score_low = []
        for h in range(4):
            part = slice(h * per_head, (h + 1) * per_head)
            probs = jnp.exp(scores[part] - aux_s[h : h + 1, pl.ds(start, width)])
            if keys_first is not None:
                seen = [causal((BLK, width), first, start, False) for first in keys_first]
                probs = jnp.where(jnp.concatenate(seen, axis=0), probs, 0.0)
            probs_low.append(probs.astype(BF16))
            shifted = prob_grad[part] - aux_s[4 + h : 5 + h, pl.ds(start, width)]
            score_low.append((probs * shifted).astype(BF16))
        grads = do_s[pl.ds(start, width), :]
        dv_ref[rows, :] += dot(jnp.concatenate(probs_low, axis=0), grads, NN)
        queries = q_s[pl.ds(start, width), :]
        dk_ref[rows, :] += dot(jnp.concatenate(score_low, axis=0), queries, NN)

    low = jnp.minimum(own[0], own[1])
    high = jnp.maximum(own[0], own[1])
    last = total // tile_blocks - 1

    def fill(side, j):
        s_buf[side], p_buf[side] = score(0, 2 * BLK, jnp.minimum(j, last))

    def two_tiles(keys_first):
        def step(i, carry):
            fill(1, 2 * i + 1)
            add(0, 2 * BLK, 2 * i, s_buf[0], p_buf[0], keys_first)
            fill(0, 2 * i + 2)
            add(0, 2 * BLK, 2 * i + 1, s_buf[1], p_buf[1], keys_first)
            return carry

        return step

    pair = 2 * tile_blocks
    fill(0, low // pair * 2)
    edge = [own[0] * BLK, own[1] * BLK]
    lax.fori_loop(low // pair, high // pair + 1, two_tiles(edge), 0)
    lax.fori_loop(high // pair + 1, total // pair, two_tiles(None), 0)
    for which in range(2):
        block = own[2 + which]
        stop = half + ((block - half) // CONT_BLKS + 1) * CONT_BLKS

        def cont_tile(j, carry, which=which, block=block):
            first_row = (8 + 4 * which) * BLK
            add(first_row, BLK, j, *score(first_row, BLK, j), [block * BLK])
            return carry

        lax.fori_loop(block // tile_blocks, stop // tile_blocks, cont_tile, 0)

    def collect(ref, blk):
        tile_sum = None
        for h in range(4):
            m, g = h // 2, h % 2
            part = ref[place(blk, h) : place(blk, h) + BLK, m * LANES : (m + 1) * LANES]
            moved = to_half(part, g, m)
            tile_sum = moved if tile_sum is None else tile_sum + moved
        return tile_sum

    for blk in range(4):
        rows = slice(blk * BLK, (blk + 1) * BLK)
        out_ref[rows, :LANES] = turn(collect(dk_ref, blk), cos_ref[rows, :], -sin_ref[rows, :])
        out_ref[rows, LANES:] = collect(dv_ref, blk)


def down_strips(w_ref, pair, width):
    strips = [w_ref[u, :, 2 * width : 3 * width] for u in (2 * pair, 2 * pair + 1)]
    return jnp.concatenate(strips, axis=1)


def expert_kernel(quarters, width, x_ref, w_ref, out_ref, gate_ref, up_ref):
    acts = []
    for u in range(quarters):
        cols = slice(u * width, (u + 1) * width)
        pre = dot(x_ref[...], w_ref[u, :, : 2 * width], NN)
        gate, up = pre[:, :width], pre[:, width:]
        gate_ref[:, cols] = gate
        up_ref[:, cols] = up
        acts.append((gate * jax.nn.sigmoid(gate) * up).astype(BF16))
    out = None
    for pair in range(quarters // 2):
        act = jnp.concatenate(acts[2 * pair : 2 * pair + 2], axis=1)
        part = dot(act, down_strips(w_ref, pair, width), NT)
        out = part if out is None else out + part
    out_ref[...] = out.astype(BF16)


def expert_grad_kernel(
    quarters, width, dy_ref, gate_ref, up_ref, w_ref, dx_ref, dgate_ref, dup_ref, act_ref
):
    total = None
    for pair in range(quarters // 2):
        both = dot(dy_ref[...], down_strips(w_ref, pair, width), NN)
        for side in range(2):
            u = 2 * pair + side
            cols = slice(u * width, (u + 1) * width)
            act_grad = both[:, side * width : (side + 1) * width]
            gate, up = gate_ref[:, cols], up_ref[:, cols]
            sig = jax.nn.sigmoid(gate)
            gate_act = gate * sig
            act_ref[:, cols] = (gate_act * up).astype(BF16)
            gate_grad = (act_grad * up * sig * (1.0 + gate * (1.0 - sig))).astype(BF16)
            up_grad = (act_grad * gate_act).astype(BF16)
            dgate_ref[:, cols] = gate_grad
            dup_ref[:, cols] = up_grad
            grads = jnp.concatenate([gate_grad, up_grad], axis=1)
            part = dot(grads, w_ref[u, :, : 2 * width], NT)
            total = part if total is None else total + part
    dx_ref[...] = total.astype(BF16)


def block_of_whole(shape):
    return pl.BlockSpec(shape, lambda i, *_: (0,) * len(shape))


def kernel_call(kernel, name, prefetch, ins, outs, scratch, flops):
    hbm = pl.BlockSpec(memory_space=pl.ANY)
    moved = sum(x.size * x.dtype.itemsize for x, _ in ins)
    return pl.pallas_call(
        kernel,
        out_shape=tuple(outs),
        grid_spec=pltpu.PrefetchScalarGridSpec(
            num_scalar_prefetch=len(prefetch),
            grid=(1,),
            in_specs=[hbm if far else block_of_whole(x.shape) for x, far in ins],
            out_specs=tuple(block_of_whole(out.shape) for out in outs),
            scratch_shapes=scratch,
        ),
        compiler_params=pltpu.CompilerParams(vmem_limit_bytes=48 << 20),
        cost_estimate=pl.CostEstimate(flops=flops, bytes_accessed=moved, transcendentals=0),
        name=name,
    )(*prefetch, *(x for x, _ in ins))


def by_rows(kernel, name, rows, ins, outs, flops):
    def spec(shape):
        if len(shape) == 3:
            return pl.BlockSpec(shape, lambda i: (0, 0, 0))
        return pl.BlockSpec((rows, shape[1]), lambda i: (i, 0))

    return pl.pallas_call(
        kernel,
        out_shape=tuple(outs),
        grid=(outs[0].shape[0] // rows,),
        in_specs=[spec(x.shape) for x in ins],
        out_specs=tuple(spec(out.shape) for out in outs),
        compiler_params=pltpu.CompilerParams(vmem_limit_bytes=40 << 20),
        cost_estimate=pl.CostEstimate(flops=flops, bytes_accessed=10**7, transcendentals=0),
        name=name,
    )(*ins)


def expert_forward(rows_in, weights):
    slots, model_width = rows_in.shape
    quarters, _, cols = weights.shape
    width = cols // 3
    hidden = jax.ShapeDtypeStruct((slots, quarters * width), F32)
    return by_rows(
        functools.partial(expert_kernel, quarters, width),
        "expert",
        slots // 5,
        [rows_in, weights],
        [jax.ShapeDtypeStruct((slots, model_width), BF16), hidden, hidden],
        6 * slots * model_width * quarters * width,
    )


def expert_backward(rows_grad, gate_pre, up_pre, weights):
    slots, model_width = rows_grad.shape
    quarters, _, cols = weights.shape
    width = cols // 3
    hidden = jax.ShapeDtypeStruct((slots, quarters * width), BF16)
    return by_rows(
        functools.partial(expert_grad_kernel, quarters, width),
        "expert_grad",
        slots // 2,
        [rows_grad, gate_pre, up_pre, weights],
        [jax.ShapeDtypeStruct((slots, model_width), BF16), hidden, hidden, hidden],
        6 * slots * model_width * quarters * width,
    )


def turn_heads(projected, scales, gain, cosine, sine):
    rows = projected.shape[0]
    out = jax.ShapeDtypeStruct((rows, 2 * LANES), BF16)
    ins = [(x, False) for x in (projected, scales, gain, cosine, sine)]
    return kernel_call(turn_kernel, "turn_heads", (), ins, [out, out], [], 10**6)


def attend(table, own, q, kv_all):
    total = table.shape[0]
    return kernel_call(
        functools.partial(attend_kernel, total, total // 2, 8),
        "attend",
        (table, own),
        [(q, False), (kv_all, True)],
        [
            jax.ShapeDtypeStruct((4 * BLK, 2 * LANES), F32),
            jax.ShapeDtypeStruct((2, 4, 2 * BLK), F32),
        ],
        [
            pltpu.VMEM((total * BLK, 3 * LANES), BF16),
            pltpu.VMEM((4 * BLK, LANES), BF16),
            pltpu.VMEM((4 * BLK, 2 * LANES), F32),
            pltpu.VMEM((4 * BLK, LANES), F32),
            pltpu.VMEM((2, 4 * BLK, 8 * BLK), F32),
            pltpu.SemaphoreType.DMA((1,)),
        ],
        20 * 10**9,
    )


def query_grad(table, own, q, out_grad, heads, lse, cosine, sine, kv_all):
    total = table.shape[0]
    ins = [(x, False) for x in (q, out_grad, heads, lse, cosine, sine)]
    return kernel_call(
        functools.partial(query_grad_kernel, total, total // 2, 4),
        "query_grad",
        (table, own),
        ins + [(kv_all, True)],
        [jax.ShapeDtypeStruct((4 * BLK, 2 * LANES), F32)],
        [
            pltpu.VMEM((total * BLK, 2 * LANES), BF16),
            pltpu.VMEM((4 * BLK, LANES), BF16),
            pltpu.VMEM((4 * BLK, LANES), BF16),
            pltpu.VMEM((4 * BLK, LANES), F32),
            pltpu.VMEM((4 * BLK, LANES), F32),
            pltpu.VMEM((4 * BLK, LANES), F32),
            pltpu.SemaphoreType.DMA((1,)),
        ],
        30 * 10**9,
    )[0]


def pair_grad(table, own, kv, cosine, sine, q_all, do_all, do_rows, aux):
    total = table.shape[0]
    ins = [(x, False) for x in (kv, cosine, sine)] + [(x, True) for x in (q_all, do_all, aux)]
    return kernel_call(
        functools.partial(pair_grad_kernel, total, total // 2, 4, do_rows),
        "pair_grad",
        (table, own),
        ins,
        [jax.ShapeDtypeStruct((4 * BLK, 2 * LANES), F32)],
        [
            pltpu.VMEM((total * BLK, 2 * LANES), BF16),
            pltpu.VMEM((total * BLK, 2 * LANES), BF16),
            pltpu.VMEM((8, total * BLK), F32),
            pltpu.VMEM((16 * BLK, 2 * LANES), BF16),
            pltpu.VMEM((16 * BLK, 2 * LANES), BF16),
            pltpu.VMEM((16 * BLK, 2 * LANES), F32),
            pltpu.VMEM((16 * BLK, 2 * LANES), F32),
            pltpu.VMEM((2, 8 * BLK, 4 * BLK), F32),
            pltpu.VMEM((2, 8 * BLK, 4 * BLK), F32),
            pltpu.SemaphoreType.DMA((3,)),
        ],
        40 * 10**9,
    )[0]


def turn_tables(position):
    half_dim = HD // 2
    frequency = ROPE_BASE ** (-(jnp.arange(half_dim, dtype=F32) * 2.0 / HD))
    angles = position[:, None] * frequency[None, :]
    cosine, sine = jnp.cos(angles), jnp.sin(angles)
    return jnp.concatenate([cosine] * 4, axis=1), jnp.concatenate([-sine, sine] * 2, axis=1)


def norm_back(grad_normed, hat_values, scale_values, gain_values):
    grad_hat = grad_normed * gain_values
    return scale_values * (
        grad_hat - hat_values * jnp.mean(grad_hat * hat_values, axis=-1, keepdims=True)
    )


def pieces(values, count):
    parts = []
    for _ in range(count):
        part = lax.reduce_precision(values, 8, 7)
        parts.append(part.astype(BF16))
        values = values - part
    return parts


def exchange(values, axis):
    return lax.all_to_all(values, axis, split_axis=0, concat_axis=0, tiled=True)


def spread(values, axis, count):
    return exchange(jnp.broadcast_to(values[None], (count,) + values.shape), axis)


def shifted(values, axis, count):
    parts = [values]
    for step in range(1, count):
        parts.append(lax.ppermute(values, axis, [(i, (i + step) % count) for i in range(count)]))
    return parts


def gather_short(values, axis, index, count):
    parts = shifted(values, axis, count)
    ordered = []
    for place in range(count):
        back = (index - place) % count
        part = parts[0]
        for step in range(1, count):
            part = jnp.where(back == step, parts[step], part)
        ordered.append(part)
    return jnp.stack(ordered, axis=0)


def ride_along(values):
    parts = jnp.concatenate(pieces(values, 3), axis=-1)
    return jnp.pad(parts, ((0, 0), (0, 0), (0, LANES - parts.shape[-1])))


def parted(sums, count):
    return sum(sums[:, i * count : (i + 1) * count] for i in range(3))


def on_device(
    hidden_in,
    teacher,
    valid,
    block_of,
    routes,
    gates,
    w_query,
    w_key,
    w_value,
    w_out,
    gain_attn,
    gain_query,
    gain_key,
    gain_ffn,
    w_gate,
    w_up,
    w_down,
):
    ctx_count = lax.axis_size("ctx")
    exp_count = lax.axis_size("exp")
    ctx_index = lax.axis_index("ctx")
    exp_index = lax.axis_index("exp")
    ctx_rows, model_width = hidden_in.shape
    own_rows = ctx_rows // exp_count
    token_total = block_of.shape[0] * BLK
    head_cols = w_query.shape[1]
    kv_cols = w_key.shape[1]
    kv_total = kv_cols * exp_count
    qkv_cols = head_cols + 2 * kv_cols
    shard_rows = w_query.shape[0]

    own_qkv = jnp.concatenate([w_query, w_key, w_value], axis=1)
    mine = jnp.arange(model_width, dtype=jnp.int32) // shard_rows == ctx_index
    places = [
        jnp.where(mine, jnp.tile(gain, ctx_count), 0).astype(BF16)
        for gain in (gain_attn, gain_query, gain_ffn)
    ]
    mine_key = jnp.arange(kv_total, dtype=jnp.int32) // gain_key.shape[0] == ctx_index
    places.append(jnp.where(mine_key, jnp.tile(gain_key, ctx_count), 0).astype(BF16))
    gain_rows = jnp.concatenate(places)
    gain_rows = jnp.pad(gain_rows, (0, 8 * qkv_cols - gain_rows.shape[0])).reshape(8, qkv_cols)
    first_parts = spread(jnp.concatenate([own_qkv, gain_rows], axis=0), "ctx", ctx_count)
    full_qkv = first_parts[:, :shard_rows].reshape(model_width, qkv_cols)
    gains = jnp.sum(first_parts[:, shard_rows:].astype(F32), axis=0).reshape(-1)
    attn_gain = gains[:model_width]
    query_gain_all = gains[model_width : 2 * model_width]
    ffn_gain = gains[2 * model_width : 3 * model_width]
    key_gain_all = gains[3 * model_width : 3 * model_width + kv_total]
    query_gain = lax.dynamic_slice_in_dim(query_gain_all, exp_index * head_cols, head_cols)
    key_gain = lax.dynamic_slice_in_dim(key_gain_all, exp_index * kv_cols, kv_cols)

    hidden_f = hidden_in.astype(F32)
    attn_scale = lax.rsqrt(jnp.mean(hidden_f * hidden_f, axis=-1, keepdims=True) + NORM_EPSILON)
    attn_hat = hidden_f * attn_scale
    normed = (attn_hat * attn_gain).astype(BF16)
    projected = dot(normed, full_qkv, NN)
    query_pre = projected[:, :head_cols]
    key_pre = projected[:, head_cols : head_cols + kv_cols]
    query_square, key_square = lax.psum(
        jnp.stack([jnp.sum(query_pre * query_pre, axis=1), jnp.sum(key_pre * key_pre, axis=1)]),
        "exp",
    )
    query_scale = lax.rsqrt(query_square / model_width + NORM_EPSILON)[:, None]
    key_scale = lax.rsqrt(key_square / kv_total + NORM_EPSILON)[:, None]
    query_hat = query_pre * query_scale
    key_hat = key_pre * key_scale
    own_blocks = lax.dynamic_slice_in_dim(block_of, ctx_index * 4, 4)
    token_ids = (own_blocks[:, None] * BLK + jnp.arange(BLK, dtype=jnp.int32)[None]).reshape(-1)
    prompt_len = token_total // 2
    position = jnp.where(
        token_ids >= prompt_len, prompt_len + (token_ids - prompt_len) % CONT_LEN, token_ids
    ).astype(F32)
    cosine, sine = turn_tables(position)
    queries_rot, own_kv = turn_heads(
        projected,
        jnp.concatenate([query_scale, key_scale], axis=1),
        jnp.concatenate([query_gain, key_gain])[None],
        cosine,
        sine,
    )
    kv_all = lax.all_gather(own_kv, "ctx", axis=0, tiled=True)
    own_out, own_gate, own_up, own_down, _ = lax.optimization_barrier(
        (w_out, w_gate[0], w_up[0], w_down[0], own_kv)
    )
    width = w_gate.shape[2]
    own_expert = jnp.concatenate([own_gate, own_up, own_down.T], axis=1)
    expert = lax.all_gather(own_expert, "exp", axis=0, tiled=False)
    full_out = gather_short(
        spread(own_out, "ctx", ctx_count).reshape(model_width, head_cols),
        "exp",
        exp_index,
        exp_count,
    )
    expert_total = ctx_count
    capacity = max(2, own_rows * routes.shape[1] * 5 // (expert_total * 4))
    slots = expert_total * capacity
    names = routes[:, :, None] == jnp.arange(expert_total, dtype=jnp.int32)[None, None, :]
    named = jnp.any(names, axis=1)
    gate_of = jnp.sum(jnp.where(names, gates[:, :, None], 0.0), axis=1)
    before = jnp.tril(jnp.ones((own_rows, own_rows), BF16), -1)
    rank = dot(before, named.astype(BF16), NN).astype(jnp.int32)
    slot_rank = jnp.where(named, rank, -1).T[:, None, :]
    holds = slot_rank == jnp.arange(capacity, dtype=jnp.int32)[None, :, None]
    pick = holds.astype(BF16).reshape(slots, own_rows)
    weigh = jnp.where(holds, gate_of.T[:, None, :], 0.0).reshape(slots, own_rows)
    slot_gate = jnp.sum(weigh, axis=1, keepdims=True)

    kv_all, full_out, pick, weigh, slot_gate = lax.optimization_barrier(
        (kv_all, full_out, pick, weigh, slot_gate)
    )
    heads_f, lse = attend(block_of, own_blocks, queries_rot, kv_all)
    heads_low = heads_f.astype(BF16)

    own_heads = exchange(heads_low.reshape(exp_count, own_rows, head_cols), "exp")
    own_heads, later_q = lax.optimization_barrier((own_heads, queries_rot))
    q_all = lax.all_gather(later_q, "ctx", axis=0, tiled=True)
    attn_rows = jnp.einsum("erk,eok->ro", own_heads, full_out, preferred_element_type=F32)
    hidden_rows = lax.dynamic_slice_in_dim(hidden_in, exp_index * own_rows, own_rows, 0)
    hidden_rows = hidden_rows.astype(F32)
    resid = hidden_rows + attn_rows
    ffn_scale = lax.rsqrt(jnp.mean(resid * resid, axis=-1, keepdims=True) + NORM_EPSILON)
    ffn_hat = resid * ffn_scale
    normed_ffn = (ffn_hat * ffn_gain).astype(BF16)

    def send(rows):
        return exchange(rows.reshape(ctx_count, capacity, model_width), "ctx").reshape(
            slots, model_width
        )

    expert_in = send(dot(pick, normed_ffn, NN).astype(BF16))
    expert_out, gate_pre, up_pre = expert_forward(expert_in, expert)
    returned = send(expert_out)
    returned, q_all, later_qkv = lax.optimization_barrier((returned, q_all, full_qkv))
    all_qkv = lax.all_gather(later_qkv, "exp", axis=0, tiled=False)
    moe_parts = dot(jnp.concatenate(pieces(weigh, 2), axis=1), returned, TN)
    moe_rows = moe_parts[:own_rows] + moe_parts[own_rows:]
    block_out = resid + moe_rows

    row_start = (ctx_index * exp_count + exp_index) * own_rows
    row_valid = lax.dynamic_slice_in_dim(valid, row_start, own_rows, 0).astype(F32)
    valid_count = jnp.sum(valid.astype(F32))
    misfit = block_out - teacher.astype(F32)
    local_loss = jnp.sum(row_valid[:, None] * misfit * misfit)
    out_grad_rows = misfit * row_valid[:, None] * (token_total / valid_count)
    copy_grad = dot(
        jnp.concatenate([pick, pick], axis=1),
        jnp.concatenate(pieces(out_grad_rows, 2), axis=0),
        NN,
    )
    grad_copies = send((slot_gate * copy_grad).astype(BF16))
    input_grad, gate_grad, up_grad, hidden_act = expert_backward(
        grad_copies, gate_pre, up_pre, expert
    )
    arrived_grad = send(input_grad)

    gate_part = dot(expert_in, gate_grad, TN)
    up_part = dot(expert_in, up_grad, TN)
    down_part = dot(hidden_act, grad_copies, TN)
    gate_part = gate_part.reshape(model_width, exp_count, width).transpose(1, 0, 2)
    up_part = up_part.reshape(model_width, exp_count, width).transpose(1, 0, 2)
    arrived_grad, all_qkv, gate_part, up_part, down_part = lax.optimization_barrier(
        (arrived_grad, all_qkv, gate_part, up_part, down_part)
    )
    ffn_normed_grad = dot(pick, arrived_grad, TN)

    ffn_gain_part = jnp.sum(ffn_normed_grad * ffn_hat, axis=0)
    resid_grad = out_grad_rows + norm_back(ffn_normed_grad, ffn_hat, ffn_scale, ffn_gain)
    branch_rows = resid_grad.astype(BF16)

    do_rows = jnp.einsum("ro,eok->erk", branch_rows, full_out, preferred_element_type=F32)
    out_grad = exchange(do_rows.astype(BF16), "exp").reshape(ctx_rows, head_cols)
    branch_parts = shifted(branch_rows, "exp", exp_count)
    head_of = jnp.arange(head_cols, dtype=jnp.int32)[None] // HD
    head_ones = (head_of == jnp.arange(4, dtype=jnp.int32)[:, None]).astype(F32)
    delta = lax.dot_general(
        head_ones,
        out_grad.astype(F32) * heads_f,
        NT,
        precision=lax.Precision.HIGHEST,
        preferred_element_type=F32,
    )
    delta = delta.reshape(4, 2, 2 * BLK).transpose(1, 0, 2)
    row_stats = jnp.concatenate([lse, delta], axis=1)
    stat_parts = jnp.stack(pieces(row_stats, 3), axis=0).reshape(-1, 2 * BLK)
    stat_rows = stat_parts.shape[0]
    do_all = lax.all_gather(
        jnp.concatenate([out_grad, stat_parts], axis=0), "ctx", axis=0, tiled=False
    )
    query_n_grad = query_grad(
        block_of, own_blocks, queries_rot, out_grad, heads_f, lse, cosine, sine, kv_all
    )

    grad_out = None
    for step, part in enumerate(branch_parts):
        first = (exp_index - step) % exp_count * own_rows
        term = dot(part, lax.dynamic_slice_in_dim(heads_low, first, own_rows, 0), TN)
        grad_out = term if grad_out is None else grad_out + term

    do_all, query_n_grad, grad_out, gate_part, up_part, down_part = lax.optimization_barrier(
        (do_all, query_n_grad, grad_out, gate_part, up_part, down_part)
    )
    grad_w_gate = lax.psum_scatter(gate_part, "exp", scatter_dimension=0, tiled=True)
    grad_w_up = lax.psum_scatter(up_part, "exp", scatter_dimension=0, tiled=True)
    grad_w_down = lax.psum_scatter(down_part, "exp", scatter_dimension=0, tiled=True)[None]

    aux = jnp.sum(
        do_all[:, ctx_rows:].reshape(ctx_count, 3, 2, 8, 2 * BLK).astype(F32), axis=1
    )
    pair_grads = pair_grad(
        block_of,
        own_blocks,
        own_kv,
        cosine,
        sine,
        q_all,
        do_all.reshape(-1, head_cols),
        ctx_rows + stat_rows,
        aux,
    )
    key_n_grad = pair_grads[:, :kv_cols]
    value_grad = pair_grads[:, kv_cols:].astype(BF16)
    query_gain_part = jnp.sum(query_n_grad * query_hat, axis=0)
    key_gain_part = jnp.sum(key_n_grad * key_hat, axis=0)
    query_hat_grad = query_n_grad * query_gain
    key_hat_grad = key_n_grad * key_gain
    stats = jnp.concatenate(
        [
            jnp.sum(query_hat_grad * query_hat, axis=1),
            jnp.sum(key_hat_grad * key_hat, axis=1),
            lax.dynamic_update_slice_in_dim(
                jnp.zeros((model_width,), F32), query_gain_part, exp_index * head_cols, 0
            ),
            ffn_gain_part,
            lax.dynamic_update_slice_in_dim(
                jnp.zeros((kv_total,), F32), key_gain_part, exp_index * kv_cols, 0
            ),
            jnp.full((kv_total,), local_loss),
        ]
    )
    stats = lax.psum(stats.reshape(-1, LANES), "exp").reshape(-1)
    query_stat = stats[:ctx_rows, None] / model_width
    key_stat = stats[ctx_rows : 2 * ctx_rows, None] / kv_total
    sums = stats[2 * ctx_rows :]
    query_low = (query_scale * (query_hat_grad - query_hat * query_stat)).astype(BF16)
    key_low = (key_scale * (key_hat_grad - key_hat * key_stat)).astype(BF16)
    grad_low = jnp.concatenate([query_low, key_low, value_grad], axis=1)

    wide_sums = jnp.stack(
        [
            sums[:model_width].reshape(ctx_count, shard_rows),
            sums[model_width : 2 * model_width].reshape(ctx_count, shard_rows),
            jnp.repeat(
                sums[2 * model_width : 2 * model_width + kv_total].reshape(ctx_count, -1), 2, axis=1
            ),
            jnp.broadcast_to(sums[-1], (ctx_count, shard_rows)),
        ],
        axis=-1,
    )
    grad_qkv = dot(normed, grad_low, TN)
    shards = exchange(
        jnp.concatenate(
            [
                grad_qkv.astype(BF16).reshape(ctx_count, shard_rows, qkv_cols),
                grad_out.astype(BF16).reshape(ctx_count, shard_rows, head_cols),
                ride_along(wide_sums),
            ],
            axis=2,
        ),
        "ctx",
    )
    back = exchange(grad_low.reshape(exp_count, own_rows, qkv_cols), "exp")
    shards = jnp.sum(shards.astype(F32), axis=0)
    grad_w_query = shards[:, :head_cols]
    grad_w_key = shards[:, head_cols : head_cols + kv_cols]
    grad_w_value = shards[:, head_cols + kv_cols : qkv_cols]
    grad_w_out = shards[:, qkv_cols : qkv_cols + head_cols]
    tail = parted(shards[:, qkv_cols + head_cols :], 4)
    loss = tail[0, 3] / (valid_count * model_width)

    gain_part = jnp.sum(grad_w_query * w_query.astype(F32), axis=1)
    gain_part += jnp.sum(grad_w_key * w_key.astype(F32), axis=1)
    gain_part += jnp.sum(grad_w_value * w_value.astype(F32), axis=1)
    grad_gain_attn = lax.psum(gain_part, "exp") / gain_attn.astype(F32)
    normed_rows = jnp.einsum("erk,edk->rd", back, all_qkv, preferred_element_type=F32)
    own_scale = lax.dynamic_slice_in_dim(attn_scale, exp_index * own_rows, own_rows, 0)
    own_hat = hidden_rows * own_scale
    grad_hidden = resid_grad + norm_back(normed_rows, own_hat, own_scale, attn_gain)
    return (
        block_out,
        loss,
        grad_hidden,
        grad_w_query,
        grad_w_key,
        grad_w_value,
        grad_w_out,
        grad_gain_attn,
        tail[:, 0],
        tail[::2, 2],
        tail[:, 1],
        grad_w_gate,
        grad_w_up,
        grad_w_down,
    )


def solution(mesh):
    return jax.shard_map(
        on_device,
        mesh=mesh,
        in_specs=(
            P("ctx", None),
            P(("ctx", "exp"), None),
            P(),
            P(),
            P(("ctx", "exp"), None),
            P(("ctx", "exp"), None),
            P("ctx", "exp"),
            P("ctx", "exp"),
            P("ctx", "exp"),
            P("ctx", "exp"),
            P("ctx"),
            P("ctx"),
            P("ctx"),
            P("ctx"),
            P("ctx", None, "exp"),
            P("ctx", None, "exp"),
            P("ctx", "exp", None),
        ),
        out_specs=(
            P(("ctx", "exp"), None),
            P(),
            P(("ctx", "exp"), None),
            P("ctx", "exp"),
            P("ctx", "exp"),
            P("ctx", "exp"),
            P("ctx", "exp"),
            P("ctx"),
            P("ctx"),
            P("ctx"),
            P("ctx"),
            P("ctx", None, "exp"),
            P("ctx", None, "exp"),
            P("ctx", "exp", None),
        ),
        check_vma=False,
    )
```

```python
import functools

import jax
import jax.numpy as jnp
from jax import lax
from jax.experimental import pallas as pl
from jax.experimental.pallas import tpu as pltpu
from jax.sharding import PartitionSpec as P

HD = 64
BLK = 128
CONT_LEN = 1024
CONT_BLKS = CONT_LEN // BLK
LANES = 128

NORM_EPSILON = 1e-05
ROPE_BASE = 10000.0
MASK_FLOOR = -1e30
F32 = jnp.float32
BF16 = jnp.bfloat16
NT = (((1,), (1,)), ((), ()))
NN = (((1,), (0,)), ((), ()))
TN = (((0,), (0,)), ((), ()))


def dot(left, right, dims):
    return lax.dot_general(left, right, dims, preferred_element_type=F32)


def key_ranges(block, half, tile_blocks):
    cont = block >= half
    inner = jnp.where(cont, (block - half) % CONT_BLKS, 0)
    n_a = jnp.where(cont, half // tile_blocks, block // tile_blocks)
    cont_base = half + (block - half) // CONT_BLKS * CONT_BLKS
    base = jnp.where(cont, cont_base, block // tile_blocks * tile_blocks) * BLK
    return n_a, base, inner // tile_blocks


def gather_blocks(table, total, moves):
    def start(i, carry):
        to = pl.multiple_of(table[i] * BLK, BLK)
        for source, target, sem in moves:
            pltpu.make_async_copy(source(i), target(to), sem).start()
        return carry

    lax.fori_loop(0, total, start, 0)


def wait_all(ref, sem):
    pltpu.make_async_copy(ref, ref, sem).wait()


def rows_of(ref, per_ctx):
    def place(i):
        first = i // 4 * per_ctx + i % 4 * BLK
        return ref.at[pl.ds(pl.multiple_of(first, 16), BLK)]

    return place


def causal(shape, key_first, query_first, rows_are_queries):
    row = lax.broadcasted_iota(jnp.int32, shape, 0) % BLK
    col = lax.broadcasted_iota(jnp.int32, shape, 1)
    if rows_are_queries:
        return key_first + col <= query_first + row
    return key_first + row <= query_first + col


def to_half(tile, source, target):
    values = tile.astype(F32)
    if source != target:
        values = pltpu.roll(values, HD, 1)
    lane = lax.broadcasted_iota(jnp.int32, values.shape, 1)
    return jnp.where(lane // HD == target, values, 0.0)


def turn(tile, cosine, sine):
    lane = lax.broadcasted_iota(jnp.int32, tile.shape, 1)
    ahead = pltpu.roll(tile, LANES - HD // 2, 1)
    behind = pltpu.roll(tile, HD // 2, 1)
    return tile * cosine + jnp.where(lane % HD < HD // 2, ahead, behind) * sine


def rows_by_head(source_ref, block_rows, target_ref):
    for h in range(4):
        m, g = h // 2, h % 2
        tile = source_ref[block_rows, m * LANES : (m + 1) * LANES]
        target_ref[h * BLK : (h + 1) * BLK, :] = to_half(tile, g, m).astype(BF16)


def rows_by_token(values):
    tiles = []
    for m in range(2):
        first = values[2 * m * BLK : (2 * m + 1) * BLK]
        second = values[(2 * m + 1) * BLK : (2 * m + 2) * BLK]
        tiles.append(to_half(first, m, 0) + to_half(second, m, 1))
    return tiles


def turn_kernel(pre_ref, scale_ref, gain_ref, cos_ref, sin_ref, q_ref, kv_ref):
    for col in range(3):
        lanes = slice(col * LANES, (col + 1) * LANES)
        which = 0 if col < 2 else 1
        hat = pre_ref[:, lanes] * scale_ref[:, which : which + 1]
        turned = turn(hat * gain_ref[:, lanes], cos_ref[...], sin_ref[...]).astype(BF16)
        if which == 0:
            q_ref[:, lanes] = (turned.astype(F32) * HD**-0.5).astype(BF16)
        else:
            kv_ref[:, :LANES] = turned
    kv_ref[:, LANES:] = pre_ref[:, 3 * LANES :].astype(BF16)


def attend_kernel(
    total, half, tile_blocks, table, own, q_in, kv, o_ref, lse_ref, kv_s, q_ref, acc, peak, s_buf, sem
):
    gather_blocks(
        table,
        total,
        [
            (
                rows_of(kv, 4 * BLK),
                lambda to: kv_s.at[pl.ds(to, BLK), pl.ds(0, 2 * LANES)],
                sem.at[0],
            )
        ],
    )
    kv_s[:, 2 * LANES :] = jnp.ones((total * BLK, LANES), BF16)
    wait_all(kv_s.at[:, pl.ds(0, 2 * LANES)], sem.at[0])
    width = tile_blocks * BLK

    def query_block(i, carry):
        block = own[i]
        n_a, base, n_b = key_ranges(block, half, tile_blocks)
        rows = pl.ds(pl.multiple_of(i * BLK, BLK), BLK)
        lanes = pl.ds(pl.multiple_of(i % 2 * BLK, BLK), BLK)
        rows_by_head(q_in, rows, q_ref)

        def first_key(j):
            return pl.multiple_of(jnp.where(j < n_a, j * width, base + (j - n_a) * width), BLK)

        def tile(start, masked):
            scores = dot(q_ref[...], kv_s[pl.ds(start, width), :LANES], NT)
            probs = jnp.exp(scores)
            if masked:
                probs = jnp.where(causal(probs.shape, start, block * BLK, True), probs, 0.0)
            acc[...] += dot(probs.astype(BF16), kv_s[pl.ds(start, width), LANES:], NN)

        def clear_tile(j, carry):
            tile(first_key(j), False)
            return carry

        def store(out, log_sum):
            first, second = rows_by_token(out)
            o_ref[rows, :LANES] = first
            o_ref[rows, LANES:] = second
            for h in range(4):
                lse_ref[i // 2, h : h + 1, lanes] = log_sum[h * BLK : (h + 1) * BLK].T[:1]

        def score(j):
            return dot(q_ref[...], kv_s[pl.ds(first_key(j), width), :LANES], NT)

        def weigh(scores, j, masked):
            start = first_key(j)
            probs = jnp.exp(scores)
            if masked:
                probs = jnp.where(causal(probs.shape, start, block * BLK, True), probs, 0.0)
            acc[...] += dot(probs.astype(BF16), kv_s[pl.ds(start, width), LANES:], NN)

        acc[...] = jnp.zeros_like(acc)
        count = n_a + n_b
        s_buf[0] = score(0)

        def two_tiles(i2, carry):
            j = 2 * i2
            s_buf[1] = score(j + 1)
            weigh(s_buf[0], j, False)
            s_buf[0] = score(j + 2)
            weigh(s_buf[1], j + 1, False)
            return carry

        lax.fori_loop(0, count // 2, two_tiles, 0)

        @pl.when(count % 2 == 1)
        def _():
            s_buf[1] = score(count)
            weigh(s_buf[0], count - 1, False)
            weigh(s_buf[1], count, True)

        @pl.when(count % 2 == 0)
        def _():
            weigh(s_buf[0], count, True)

        sums = acc[:, LANES:]
        in_range = (jnp.max(sums) < 2.0**100) & (jnp.min(sums) > 2.0**-40)

        @pl.when(in_range)
        def _():
            store(acc[:, :LANES] / sums, jnp.log(sums))

        @pl.when(jnp.logical_not(in_range))
        def _():
            acc[...] = jnp.zeros_like(acc)
            peak[...] = jnp.full_like(peak, MASK_FLOOR)

            def safe_tile(j, carry):
                start = first_key(j)
                scores = dot(q_ref[...], kv_s[pl.ds(start, width), :LANES], NT)
                seen = causal(scores.shape, start, block * BLK, True)
                scores = jnp.where(seen, scores, MASK_FLOOR)
                old = peak[...]
                new = jnp.maximum(old, jnp.max(scores, axis=1, keepdims=True))
                probs = jnp.where(seen, jnp.exp(scores - new[:, :1]), 0.0)
                keep = jnp.exp(old - new)
                acc[...] = acc[...] * keep[:, :1] + dot(
                    probs.astype(BF16), kv_s[pl.ds(start, width), LANES:], NN
                )
                peak[...] = new
                return carry

            lax.fori_loop(0, n_a + n_b + 1, safe_tile, 0)
            safe_sums = acc[:, LANES:]
            store(acc[:, :LANES] / safe_sums, peak[...] + jnp.log(safe_sums))

        return carry

    lax.fori_loop(0, 4, query_block, 0)


def query_grad_kernel(
    total,
    half,
    tile_blocks,
    table,
    own,
    q_in,
    do_in,
    o_in,
    lse_in,
    cos_ref,
    sin_ref,
    kv,
    dq_ref,
    kv_s,
    q_ref,
    do_ref,
    lse_ref,
    delta_ref,
    acc,
    sem,
):
    gather_blocks(
        table, total, [(rows_of(kv, 4 * BLK), lambda to: kv_s.at[pl.ds(to, BLK)], sem.at[0])]
    )
    wait_all(kv_s, sem.at[0])
    width = tile_blocks * BLK

    def query_block(i, carry):
        block = own[i]
        n_a, base, n_b = key_ranges(block, half, tile_blocks)
        rows = pl.ds(pl.multiple_of(i * BLK, BLK), BLK)
        lanes = pl.ds(pl.multiple_of(i % 2 * BLK, BLK), BLK)
        rows_by_head(q_in, rows, q_ref)
        rows_by_head(do_in, rows, do_ref)
        for h in range(4):
            part = slice(h * BLK, (h + 1) * BLK)
            pair = slice(h // 2 * LANES, (h // 2 + 1) * LANES)
            product = do_in[rows, pair].astype(F32) * o_in[rows, pair]
            own_half = to_half(product, h % 2, h % 2)
            delta = jnp.sum(own_half, axis=1, keepdims=True)
            delta_ref[part, :] = jnp.broadcast_to(delta, (BLK, LANES))
            row = lse_in[i // 2, h : h + 1, lanes]
            lse_ref[part, :] = jnp.broadcast_to(row, (LANES, BLK)).T

        def first_key(j):
            return pl.multiple_of(jnp.where(j < n_a, j * width, base + (j - n_a) * width), BLK)

        def tile(start, masked):
            keys = kv_s[pl.ds(start, width), :LANES]
            scores = dot(q_ref[...], keys, NT)
            prob_grad = dot(do_ref[...], kv_s[pl.ds(start, width), LANES:], NT)
            probs = jnp.exp(scores - lse_ref[:, :1])
            score_grad = probs * (prob_grad - delta_ref[:, :1])
            if masked:
                seen = causal(probs.shape, start, block * BLK, True)
                score_grad = jnp.where(seen, score_grad, 0.0)
            acc[...] += dot(score_grad.astype(BF16), keys, NN)

        def clear_tile(j, carry):
            tile(first_key(j), False)
            return carry

        acc[...] = jnp.zeros_like(acc)
        lax.fori_loop(0, n_a + n_b, clear_tile, 0)
        tile(first_key(n_a + n_b), True)
        for m, gradient in enumerate(rows_by_token(acc[...])):
            back = turn(gradient * HD**-0.5, cos_ref[rows, :], -sin_ref[rows, :])
            dq_ref[rows, m * LANES : (m + 1) * LANES] = back
        return carry

    lax.fori_loop(0, 4, query_block, 0)


def pair_grad_kernel(
    total,
    half,
    tile_blocks,
    do_rows,
    table,
    own,
    kv_in,
    cos_ref,
    sin_ref,
    q_all,
    do_all,
    aux,
    out_ref,
    q_s,
    do_s,
    aux_s,
    k_ref,
    v_ref,
    dk_ref,
    dv_ref,
    s_buf,
    p_buf,
    sem,
):
    gather_blocks(
        table,
        total,
        [
            (rows_of(q_all, 4 * BLK), lambda to: q_s.at[pl.ds(to, BLK)], sem.at[0]),
            (rows_of(do_all, do_rows), lambda to: do_s.at[pl.ds(to, BLK)], sem.at[1]),
            (
                lambda i: aux.at[i // 4, i // 2 % 2, :, pl.ds(pl.multiple_of(i % 2 * BLK, BLK), BLK)],
                lambda to: aux_s.at[:, pl.ds(to, BLK)],
                sem.at[2],
            ),
        ],
    )

    def place(blk, h):
        return (h * 2 + blk) * BLK if blk < 2 else ((blk * 4) + h) * BLK

    k_ref[...] = jnp.zeros_like(k_ref)
    v_ref[...] = jnp.zeros_like(v_ref)
    dk_ref[...] = jnp.zeros_like(dk_ref)
    dv_ref[...] = jnp.zeros_like(dv_ref)
    for blk in range(4):
        source = slice(blk * BLK, (blk + 1) * BLK)
        for h in range(4):
            m, g = h // 2, h % 2
            target = slice(place(blk, h), place(blk, h) + BLK)
            pair = slice(m * LANES, (m + 1) * LANES)
            k_ref[target, pair] = to_half(kv_in[source, :LANES], m, g).astype(BF16)
            v_ref[target, pair] = to_half(kv_in[source, LANES:], m, g).astype(BF16)
    wait_all(q_s, sem.at[0])
    wait_all(do_s, sem.at[1])
    wait_all(aux_s, sem.at[2])
    width = tile_blocks * BLK

    def score(first_row, per_head, j):
        rows = pl.ds(first_row, 4 * per_head)
        start = pl.multiple_of(j * width, width)
        scores = dot(k_ref[rows, :], q_s[pl.ds(start, width), :], NT)
        return scores, dot(v_ref[rows, :], do_s[pl.ds(start, width), :], NT)

    def add(first_row, per_head, j, scores, prob_grad, keys_first):
        rows = pl.ds(first_row, 4 * per_head)
        start = pl.multiple_of(j * width, width)
        probs_low = []
        score_low = []
        for h in range(4):
            part = slice(h * per_head, (h + 1) * per_head)
            probs = jnp.exp(scores[part] - aux_s[h : h + 1, pl.ds(start, width)])
            if keys_first is not None:
                seen = [causal((BLK, width), first, start, False) for first in keys_first]
                probs = jnp.where(jnp.concatenate(seen, axis=0), probs, 0.0)
            probs_low.append(probs.astype(BF16))
            shifted = prob_grad[part] - aux_s[4 + h : 5 + h, pl.ds(start, width)]
            score_low.append((probs * shifted).astype(BF16))
        grads = do_s[pl.ds(start, width), :]
        dv_ref[rows, :] += dot(jnp.concatenate(probs_low, axis=0), grads, NN)
        queries = q_s[pl.ds(start, width), :]
        dk_ref[rows, :] += dot(jnp.concatenate(score_low, axis=0), queries, NN)

    low = jnp.minimum(own[0], own[1])
    high = jnp.maximum(own[0], own[1])
    last = total // tile_blocks - 1

    def fill(side, j):
        s_buf[side], p_buf[side] = score(0, 2 * BLK, jnp.minimum(j, last))

    def two_tiles(keys_first):
        def step(i, carry):
            fill(1, 2 * i + 1)
            add(0, 2 * BLK, 2 * i, s_buf[0], p_buf[0], keys_first)
            fill(0, 2 * i + 2)
            add(0, 2 * BLK, 2 * i + 1, s_buf[1], p_buf[1], keys_first)
            return carry

        return step

    pair = 2 * tile_blocks
    fill(0, low // pair * 2)
    edge = [own[0] * BLK, own[1] * BLK]
    lax.fori_loop(low // pair, high // pair + 1, two_tiles(edge), 0)
    lax.fori_loop(high // pair + 1, total // pair, two_tiles(None), 0)
    for which in range(2):
        block = own[2 + which]
        stop = half + ((block - half) // CONT_BLKS + 1) * CONT_BLKS

        def cont_tile(j, carry, which=which, block=block):
            first_row = (8 + 4 * which) * BLK
            add(first_row, BLK, j, *score(first_row, BLK, j), [block * BLK])
            return carry

        lax.fori_loop(block // tile_blocks, stop // tile_blocks, cont_tile, 0)

    def collect(ref, blk):
        tile_sum = None
        for h in range(4):
            m, g = h // 2, h % 2
            part = ref[place(blk, h) : place(blk, h) + BLK, m * LANES : (m + 1) * LANES]
            moved = to_half(part, g, m)
            tile_sum = moved if tile_sum is None else tile_sum + moved
        return tile_sum

    for blk in range(4):
        rows = slice(blk * BLK, (blk + 1) * BLK)
        out_ref[rows, :LANES] = turn(collect(dk_ref, blk), cos_ref[rows, :], -sin_ref[rows, :])
        out_ref[rows, LANES:] = collect(dv_ref, blk)


def down_strips(w_ref, pair, width):
    strips = [w_ref[u, :, 2 * width : 3 * width] for u in (2 * pair, 2 * pair + 1)]
    return jnp.concatenate(strips, axis=1)


def expert_kernel(quarters, width, x_ref, w_ref, out_ref, gate_ref, up_ref):
    acts = []
    for u in range(quarters):
        cols = slice(u * width, (u + 1) * width)
        pre = dot(x_ref[...], w_ref[u, :, : 2 * width], NN)
        gate, up = pre[:, :width], pre[:, width:]
        gate_ref[:, cols] = gate
        up_ref[:, cols] = up
        acts.append((gate * jax.nn.sigmoid(gate) * up).astype(BF16))
    out = None
    for pair in range(quarters // 2):
        act = jnp.concatenate(acts[2 * pair : 2 * pair + 2], axis=1)
        part = dot(act, down_strips(w_ref, pair, width), NT)
        out = part if out is None else out + part
    out_ref[...] = out.astype(BF16)


def expert_grad_kernel(
    quarters, width, dy_ref, gate_ref, up_ref, w_ref, wt_ref, dx_ref, dgate_ref, dup_ref, act_ref
):
    total = None
    for pair in range(quarters // 2):
        both = dot(dy_ref[...], down_strips(w_ref, pair, width), NN)
        for side in range(2):
            u = 2 * pair + side
            cols = slice(u * width, (u + 1) * width)
            act_grad = both[:, side * width : (side + 1) * width]
            gate, up = gate_ref[:, cols], up_ref[:, cols]
            sig = jax.nn.sigmoid(gate)
            gate_act = gate * sig
            act_ref[:, cols] = (gate_act * up).astype(BF16)
            gate_grad = (act_grad * up * sig * (1.0 + gate * (1.0 - sig))).astype(BF16)
            up_grad = (act_grad * gate_act).astype(BF16)
            dgate_ref[:, cols] = gate_grad
            dup_ref[:, cols] = up_grad
            grads = jnp.concatenate([gate_grad, up_grad], axis=1)
            part = dot(grads, wt_ref[u], NN)
            total = part if total is None else total + part
    dx_ref[...] = total.astype(BF16)


def block_of_whole(shape):
    return pl.BlockSpec(shape, lambda i, *_: (0,) * len(shape))


def kernel_call(kernel, name, prefetch, ins, outs, scratch, flops):
    hbm = pl.BlockSpec(memory_space=pl.ANY)
    moved = sum(x.size * x.dtype.itemsize for x, _ in ins)
    return pl.pallas_call(
        kernel,
        out_shape=tuple(outs),
        grid_spec=pltpu.PrefetchScalarGridSpec(
            num_scalar_prefetch=len(prefetch),
            grid=(1,),
            in_specs=[hbm if far else block_of_whole(x.shape) for x, far in ins],
            out_specs=tuple(block_of_whole(out.shape) for out in outs),
            scratch_shapes=scratch,
        ),
        compiler_params=pltpu.CompilerParams(vmem_limit_bytes=48 << 20),
        cost_estimate=pl.CostEstimate(flops=flops, bytes_accessed=moved, transcendentals=0),
        name=name,
    )(*prefetch, *(x for x, _ in ins))


def by_rows(kernel, name, rows, ins, outs, flops):
    def spec(shape):
        if len(shape) == 3:
            return pl.BlockSpec(shape, lambda i: (0, 0, 0))
        return pl.BlockSpec((rows, shape[1]), lambda i: (i, 0))

    return pl.pallas_call(
        kernel,
        out_shape=tuple(pltpu.HBM(out.shape, out.dtype) for out in outs),
        grid=(outs[0].shape[0] // rows,),
        in_specs=[spec(x.shape) for x in ins],
        out_specs=tuple(spec(out.shape) for out in outs),
        compiler_params=pltpu.CompilerParams(vmem_limit_bytes=40 << 20),
        cost_estimate=pl.CostEstimate(flops=flops, bytes_accessed=10**7, transcendentals=0),
        name=name,
    )(*ins)


def expert_forward(rows_in, weights):
    slots, model_width = rows_in.shape
    quarters, _, cols = weights.shape
    width = cols // 3
    hidden = jax.ShapeDtypeStruct((slots, quarters * width), F32)
    return by_rows(
        functools.partial(expert_kernel, quarters, width),
        "expert",
        slots // 5,
        [rows_in, weights],
        [jax.ShapeDtypeStruct((slots, model_width), BF16), hidden, hidden],
        6 * slots * model_width * quarters * width,
    )


def expert_backward(rows_grad, gate_pre, up_pre, weights, turned):
    slots, model_width = rows_grad.shape
    quarters, _, cols = weights.shape
    width = cols // 3
    hidden = jax.ShapeDtypeStruct((slots, quarters * width), BF16)
    return by_rows(
        functools.partial(expert_grad_kernel, quarters, width),
        "expert_grad",
        slots // 2,
        [rows_grad, gate_pre, up_pre, weights, turned],
        [jax.ShapeDtypeStruct((slots, model_width), BF16), hidden, hidden, hidden],
        6 * slots * model_width * quarters * width,
    )


def turn_heads(projected, scales, gain, cosine, sine):
    rows = projected.shape[0]
    out = jax.ShapeDtypeStruct((rows, 2 * LANES), BF16)
    ins = [(x, False) for x in (projected, scales, gain, cosine, sine)]
    return kernel_call(turn_kernel, "turn_heads", (), ins, [out, out], [], 10**6)


def attend(table, own, q, kv_all):
    total = table.shape[0]
    return kernel_call(
        functools.partial(attend_kernel, total, total // 2, 8),
        "attend",
        (table, own),
        [(q, False), (kv_all, True)],
        [
            jax.ShapeDtypeStruct((4 * BLK, 2 * LANES), F32),
            jax.ShapeDtypeStruct((2, 4, 2 * BLK), F32),
        ],
        [
            pltpu.VMEM((total * BLK, 3 * LANES), BF16),
            pltpu.VMEM((4 * BLK, LANES), BF16),
            pltpu.VMEM((4 * BLK, 2 * LANES), F32),
            pltpu.VMEM((4 * BLK, LANES), F32),
            pltpu.VMEM((2, 4 * BLK, 8 * BLK), F32),
            pltpu.SemaphoreType.DMA((1,)),
        ],
        20 * 10**9,
    )


def query_grad(table, own, q, out_grad, heads, lse, cosine, sine, kv_all):
    total = table.shape[0]
    ins = [(x, False) for x in (q, out_grad, heads, lse, cosine, sine)]
    return kernel_call(
        functools.partial(query_grad_kernel, total, total // 2, 4),
        "query_grad",
        (table, own),
        ins + [(kv_all, True)],
        [jax.ShapeDtypeStruct((4 * BLK, 2 * LANES), F32)],
        [
            pltpu.VMEM((total * BLK, 2 * LANES), BF16),
            pltpu.VMEM((4 * BLK, LANES), BF16),
            pltpu.VMEM((4 * BLK, LANES), BF16),
            pltpu.VMEM((4 * BLK, LANES), F32),
            pltpu.VMEM((4 * BLK, LANES), F32),
            pltpu.VMEM((4 * BLK, LANES), F32),
            pltpu.SemaphoreType.DMA((1,)),
        ],
        30 * 10**9,
    )[0]


def pair_grad(table, own, kv, cosine, sine, q_all, do_all, do_rows, aux):
    total = table.shape[0]
    ins = [(x, False) for x in (kv, cosine, sine)] + [(x, True) for x in (q_all, do_all, aux)]
    return kernel_call(
        functools.partial(pair_grad_kernel, total, total // 2, 4, do_rows),
        "pair_grad",
        (table, own),
        ins,
        [jax.ShapeDtypeStruct((4 * BLK, 2 * LANES), F32)],
        [
            pltpu.VMEM((total * BLK, 2 * LANES), BF16),
            pltpu.VMEM((total * BLK, 2 * LANES), BF16),
            pltpu.VMEM((8, total * BLK), F32),
            pltpu.VMEM((16 * BLK, 2 * LANES), BF16),
            pltpu.VMEM((16 * BLK, 2 * LANES), BF16),
            pltpu.VMEM((16 * BLK, 2 * LANES), F32),
            pltpu.VMEM((16 * BLK, 2 * LANES), F32),
            pltpu.VMEM((2, 8 * BLK, 4 * BLK), F32),
            pltpu.VMEM((2, 8 * BLK, 4 * BLK), F32),
            pltpu.SemaphoreType.DMA((3,)),
        ],
        40 * 10**9,
    )[0]


def turn_tables(position):
    half_dim = HD // 2
    frequency = ROPE_BASE ** (-(jnp.arange(half_dim, dtype=F32) * 2.0 / HD))
    angles = position[:, None] * frequency[None, :]
    cosine, sine = jnp.cos(angles), jnp.sin(angles)
    return jnp.concatenate([cosine] * 4, axis=1), jnp.concatenate([-sine, sine] * 2, axis=1)


def norm_back(grad_normed, hat_values, scale_values, gain_values):
    grad_hat = grad_normed * gain_values
    return scale_values * (
        grad_hat - hat_values * jnp.mean(grad_hat * hat_values, axis=-1, keepdims=True)
    )


def pieces(values, count):
    parts = []
    for _ in range(count):
        part = lax.reduce_precision(values, 8, 7)
        parts.append(part.astype(BF16))
        values = values - part
    return parts


def exchange(values, axis):
    return lax.all_to_all(values, axis, split_axis=0, concat_axis=0, tiled=True)


def spread(values, axis, count):
    return exchange(jnp.broadcast_to(values[None], (count,) + values.shape), axis)


def shifted(values, axis, count):
    parts = [values]
    for step in range(1, count):
        parts.append(lax.ppermute(values, axis, [(i, (i + step) % count) for i in range(count)]))
    return parts


def exchange_short(values, axis, index, count):
    rows = values.shape[0] // count
    come = []
    for step in range(count):
        to = (index + step) % count
        part = lax.dynamic_slice_in_dim(values, to * rows, rows, 0)
        if step > 0:
            part = lax.ppermute(part, axis, [(i, (i + step) % count) for i in range(count)])
        come.append(part)
    return jnp.concatenate(come, axis=1)


def in_order(parts, index, count):
    ordered = []
    for place in range(count):
        back = (index - place) % count
        part = parts[0]
        for step in range(1, count):
            part = jnp.where(back == step, parts[step], part)
        ordered.append(part)
    return jnp.stack(ordered, axis=0)


def ride_along(values):
    parts = jnp.concatenate(pieces(values, 3), axis=-1)
    return jnp.pad(parts, ((0, 0), (0, 0), (0, LANES - parts.shape[-1])))


def parted(sums, count):
    return sum(sums[:, i * count : (i + 1) * count] for i in range(3))


def on_device(
    hidden_in,
    teacher,
    valid,
    block_of,
    routes,
    gates,
    w_query,
    w_key,
    w_value,
    w_out,
    gain_attn,
    gain_query,
    gain_key,
    gain_ffn,
    w_gate,
    w_up,
    w_down,
):
    ctx_count = lax.axis_size("ctx")
    exp_count = lax.axis_size("exp")
    ctx_index = lax.axis_index("ctx")
    exp_index = lax.axis_index("exp")
    ctx_rows, model_width = hidden_in.shape
    own_rows = ctx_rows // exp_count
    token_total = block_of.shape[0] * BLK
    head_cols = w_query.shape[1]
    kv_cols = w_key.shape[1]
    kv_total = kv_cols * exp_count
    qkv_cols = head_cols + 2 * kv_cols
    shard_rows = w_query.shape[0]

    own_qkv = jnp.concatenate([w_query, w_key, w_value], axis=1)
    mine = jnp.arange(model_width, dtype=jnp.int32) // shard_rows == ctx_index
    places = [
        jnp.where(mine, jnp.tile(gain, ctx_count), 0).astype(BF16)
        for gain in (gain_attn, gain_query, gain_ffn)
    ]
    mine_key = jnp.arange(kv_total, dtype=jnp.int32) // gain_key.shape[0] == ctx_index
    places.append(jnp.where(mine_key, jnp.tile(gain_key, ctx_count), 0).astype(BF16))
    gain_rows = jnp.concatenate(places)
    gain_rows = jnp.pad(gain_rows, (0, 8 * qkv_cols - gain_rows.shape[0])).reshape(8, qkv_cols)
    first_parts = spread(jnp.concatenate([own_qkv, gain_rows], axis=0), "ctx", ctx_count)
    full_qkv = first_parts[:, :shard_rows].reshape(model_width, qkv_cols)
    gains = jnp.sum(first_parts[:, shard_rows:].astype(F32), axis=0).reshape(-1)
    attn_gain = gains[:model_width]
    query_gain_all = gains[model_width : 2 * model_width]
    ffn_gain = gains[2 * model_width : 3 * model_width]
    key_gain_all = gains[3 * model_width : 3 * model_width + kv_total]
    query_gain = lax.dynamic_slice_in_dim(query_gain_all, exp_index * head_cols, head_cols)
    key_gain = lax.dynamic_slice_in_dim(key_gain_all, exp_index * kv_cols, kv_cols)

    hidden_f = hidden_in.astype(F32)
    attn_scale = lax.rsqrt(jnp.mean(hidden_f * hidden_f, axis=-1, keepdims=True) + NORM_EPSILON)
    attn_hat = hidden_f * attn_scale
    normed = (attn_hat * attn_gain).astype(BF16)
    projected = dot(normed, full_qkv, NN)
    query_pre = projected[:, :head_cols]
    key_pre = projected[:, head_cols : head_cols + kv_cols]
    query_square, key_square = lax.psum(
        jnp.stack([jnp.sum(query_pre * query_pre, axis=1), jnp.sum(key_pre * key_pre, axis=1)]),
        "exp",
    )
    query_scale = lax.rsqrt(query_square / model_width + NORM_EPSILON)[:, None]
    key_scale = lax.rsqrt(key_square / kv_total + NORM_EPSILON)[:, None]
    query_hat = query_pre * query_scale
    key_hat = key_pre * key_scale
    own_blocks = lax.dynamic_slice_in_dim(block_of, ctx_index * 4, 4)
    token_ids = (own_blocks[:, None] * BLK + jnp.arange(BLK, dtype=jnp.int32)[None]).reshape(-1)
    prompt_len = token_total // 2
    position = jnp.where(
        token_ids >= prompt_len, prompt_len + (token_ids - prompt_len) % CONT_LEN, token_ids
    ).astype(F32)
    cosine, sine = turn_tables(position)
    queries_rot, own_kv = turn_heads(
        projected,
        jnp.concatenate([query_scale, key_scale], axis=1),
        jnp.concatenate([query_gain, key_gain])[None],
        cosine,
        sine,
    )
    kv_all = lax.all_gather(own_kv, "ctx", axis=0, tiled=True)
    own_out, own_gate, own_up, own_down, _ = lax.optimization_barrier(
        (w_out, w_gate[0], w_up[0], w_down[0], own_kv)
    )
    width = w_gate.shape[2]
    own_expert = jnp.concatenate([own_gate, own_up, own_down.T], axis=1)
    expert = lax.all_gather(own_expert, "exp", axis=0, tiled=False)
    out_parts = shifted(
        spread(own_out, "ctx", ctx_count).reshape(model_width, head_cols), "exp", exp_count
    )
    wide_out = jnp.concatenate(out_parts, axis=1)
    full_out = in_order(out_parts, exp_index, exp_count)
    expert_total = ctx_count
    capacity = max(2, own_rows * routes.shape[1] * 5 // (expert_total * 4))
    slots = expert_total * capacity
    names = routes[:, :, None] == jnp.arange(expert_total, dtype=jnp.int32)[None, None, :]
    named = jnp.any(names, axis=1)
    gate_of = jnp.sum(jnp.where(names, gates[:, :, None], 0.0), axis=1)
    before = jnp.tril(jnp.ones((own_rows, own_rows), BF16), -1)
    rank = dot(before, named.astype(BF16), NN).astype(jnp.int32)
    slot_rank = jnp.where(named, rank, -1).T[:, None, :]
    holds = slot_rank == jnp.arange(capacity, dtype=jnp.int32)[None, :, None]
    pick = holds.astype(BF16).reshape(slots, own_rows)
    weigh = jnp.where(holds, gate_of.T[:, None, :], 0.0).reshape(slots, own_rows)
    slot_gate = jnp.sum(weigh, axis=1, keepdims=True)

    kv_all, wide_out, full_out, pick, weigh, slot_gate = lax.optimization_barrier(
        (kv_all, wide_out, full_out, pick, weigh, slot_gate)
    )
    heads_f, lse = attend(block_of, own_blocks, queries_rot, kv_all)
    heads_low = heads_f.astype(BF16)

    own_heads = exchange_short(heads_low, "exp", exp_index, exp_count)
    own_heads, later_q = lax.optimization_barrier((own_heads, queries_rot))
    q_all = lax.all_gather(later_q, "ctx", axis=0, tiled=True)
    attn_rows = dot(own_heads, wide_out, NT)
    hidden_rows = lax.dynamic_slice_in_dim(hidden_in, exp_index * own_rows, own_rows, 0)
    hidden_rows = hidden_rows.astype(F32)
    resid = hidden_rows + attn_rows
    ffn_scale = lax.rsqrt(jnp.mean(resid * resid, axis=-1, keepdims=True) + NORM_EPSILON)
    ffn_hat = resid * ffn_scale
    normed_ffn = (ffn_hat * ffn_gain).astype(BF16)

    def send(rows):
        return exchange(rows.reshape(ctx_count, capacity, model_width), "ctx").reshape(
            slots, model_width
        )

    expert_in = send(dot(pick, normed_ffn, NN).astype(BF16))
    expert_out, gate_pre, up_pre = expert_forward(expert_in, expert)
    returned = send(expert_out)
    turned = expert[:, :, : 2 * width].transpose(0, 2, 1)
    returned, q_all, later_qkv, turned = lax.optimization_barrier(
        (returned, q_all, full_qkv, turned)
    )
    wide_qkv = jnp.concatenate(shifted(later_qkv, "exp", exp_count), axis=1)
    moe_parts = dot(jnp.concatenate(pieces(weigh, 2), axis=1), returned, TN)
    moe_rows = moe_parts[:own_rows] + moe_parts[own_rows:]
    block_out = resid + moe_rows

    row_start = (ctx_index * exp_count + exp_index) * own_rows
    row_valid = lax.dynamic_slice_in_dim(valid, row_start, own_rows, 0).astype(F32)
    valid_count = jnp.sum(valid.astype(F32))
    misfit = block_out - teacher.astype(F32)
    local_loss = jnp.sum(row_valid[:, None] * misfit * misfit)
    out_grad_rows = misfit * row_valid[:, None] * (token_total / valid_count)
    copy_grad = dot(
        jnp.concatenate([pick, pick], axis=1),
        jnp.concatenate(pieces(out_grad_rows, 2), axis=0),
        NN,
    )
    grad_copies = send((slot_gate * copy_grad).astype(BF16))
    input_grad, gate_grad, up_grad, hidden_act = expert_backward(
        grad_copies, gate_pre, up_pre, expert, turned
    )
    arrived_grad = send(input_grad)

    gate_part = dot(expert_in, gate_grad, TN)
    up_part = dot(expert_in, up_grad, TN)
    down_part = dot(hidden_act, grad_copies, TN)
    gate_part = gate_part.reshape(model_width, exp_count, width).transpose(1, 0, 2)
    up_part = up_part.reshape(model_width, exp_count, width).transpose(1, 0, 2)
    arrived_grad, wide_qkv, gate_part, up_part, down_part = lax.optimization_barrier(
        (arrived_grad, wide_qkv, gate_part, up_part, down_part)
    )
    ffn_normed_grad = dot(pick, arrived_grad, TN)

    ffn_gain_part = jnp.sum(ffn_normed_grad * ffn_hat, axis=0)
    resid_grad = out_grad_rows + norm_back(ffn_normed_grad, ffn_hat, ffn_scale, ffn_gain)
    branch_rows = resid_grad.astype(BF16)

    do_rows = jnp.einsum("ro,eok->erk", branch_rows, full_out, preferred_element_type=F32)
    out_grad = exchange(do_rows.astype(BF16), "exp").reshape(ctx_rows, head_cols)
    branch_parts = shifted(branch_rows, "exp", exp_count)
    head_of = jnp.arange(head_cols, dtype=jnp.int32)[None] // HD
    head_ones = (head_of == jnp.arange(4, dtype=jnp.int32)[:, None]).astype(F32)
    delta = lax.dot_general(
        head_ones,
        out_grad.astype(F32) * heads_f,
        NT,
        precision=lax.Precision.HIGHEST,
        preferred_element_type=F32,
    )
    delta = delta.reshape(4, 2, 2 * BLK).transpose(1, 0, 2)
    row_stats = jnp.concatenate([lse, delta], axis=1)
    stat_parts = jnp.stack(pieces(row_stats, 3), axis=0).reshape(-1, 2 * BLK)
    stat_rows = stat_parts.shape[0]
    do_all = lax.all_gather(
        jnp.concatenate([out_grad, stat_parts], axis=0), "ctx", axis=0, tiled=False
    )
    query_n_grad = query_grad(
        block_of, own_blocks, queries_rot, out_grad, heads_f, lse, cosine, sine, kv_all
    )

    grad_out = None
    for step, part in enumerate(branch_parts):
        first = (exp_index - step) % exp_count * own_rows
        term = dot(part, lax.dynamic_slice_in_dim(heads_low, first, own_rows, 0), TN)
        grad_out = term if grad_out is None else grad_out + term

    do_all, query_n_grad, grad_out, gate_part, up_part, down_part = lax.optimization_barrier(
        (do_all, query_n_grad, grad_out, gate_part, up_part, down_part)
    )
    grad_w_gate = lax.psum_scatter(gate_part, "exp", scatter_dimension=0, tiled=True)
    grad_w_up = lax.psum_scatter(up_part, "exp", scatter_dimension=0, tiled=True)
    grad_w_down = lax.psum_scatter(down_part, "exp", scatter_dimension=0, tiled=True)[None]

    aux = jnp.sum(
        do_all[:, ctx_rows:].reshape(ctx_count, 3, 2, 8, 2 * BLK).astype(F32), axis=1
    )
    pair_grads = pair_grad(
        block_of,
        own_blocks,
        own_kv,
        cosine,
        sine,
        q_all,
        do_all.reshape(-1, head_cols),
        ctx_rows + stat_rows,
        aux,
    )
    key_n_grad = pair_grads[:, :kv_cols]
    value_grad = pair_grads[:, kv_cols:].astype(BF16)
    query_gain_part = jnp.sum(query_n_grad * query_hat, axis=0)
    key_gain_part = jnp.sum(key_n_grad * key_hat, axis=0)
    query_hat_grad = query_n_grad * query_gain
    key_hat_grad = key_n_grad * key_gain
    stats = jnp.concatenate(
        [
            jnp.sum(query_hat_grad * query_hat, axis=1),
            jnp.sum(key_hat_grad * key_hat, axis=1),
            lax.dynamic_update_slice_in_dim(
                jnp.zeros((model_width,), F32), query_gain_part, exp_index * head_cols, 0
            ),
            ffn_gain_part,
            lax.dynamic_update_slice_in_dim(
                jnp.zeros((kv_total,), F32), key_gain_part, exp_index * kv_cols, 0
            ),
            jnp.full((kv_total,), local_loss),
        ]
    )
    stats = lax.psum(stats.reshape(-1, LANES), "exp").reshape(-1)
    query_stat = stats[:ctx_rows, None] / model_width
    key_stat = stats[ctx_rows : 2 * ctx_rows, None] / kv_total
    sums = stats[2 * ctx_rows :]
    query_low = (query_scale * (query_hat_grad - query_hat * query_stat)).astype(BF16)
    key_low = (key_scale * (key_hat_grad - key_hat * key_stat)).astype(BF16)
    grad_low = jnp.concatenate([query_low, key_low, value_grad], axis=1)

    wide_sums = jnp.stack(
        [
            sums[:model_width].reshape(ctx_count, shard_rows),
            sums[model_width : 2 * model_width].reshape(ctx_count, shard_rows),
            jnp.repeat(
                sums[2 * model_width : 2 * model_width + kv_total].reshape(ctx_count, -1), 2, axis=1
            ),
            jnp.broadcast_to(sums[-1], (ctx_count, shard_rows)),
        ],
        axis=-1,
    )
    grad_qkv = dot(normed, grad_low, TN)
    shards = exchange(
        jnp.concatenate(
            [
                grad_qkv.astype(BF16).reshape(ctx_count, shard_rows, qkv_cols),
                grad_out.astype(BF16).reshape(ctx_count, shard_rows, head_cols),
                ride_along(wide_sums),
            ],
            axis=2,
        ),
        "ctx",
    )
    back = exchange_short(grad_low, "exp", exp_index, exp_count)
    shards = jnp.sum(shards.astype(F32), axis=0)
    grad_w_query = shards[:, :head_cols]
    grad_w_key = shards[:, head_cols : head_cols + kv_cols]
    grad_w_value = shards[:, head_cols + kv_cols : qkv_cols]
    grad_w_out = shards[:, qkv_cols : qkv_cols + head_cols]
    tail = parted(shards[:, qkv_cols + head_cols :], 4)
    loss = tail[0, 3] / (valid_count * model_width)

    gain_part = jnp.sum(grad_w_query * w_query.astype(F32), axis=1)
    gain_part += jnp.sum(grad_w_key * w_key.astype(F32), axis=1)
    gain_part += jnp.sum(grad_w_value * w_value.astype(F32), axis=1)
    grad_gain_attn = lax.psum(gain_part, "exp") / gain_attn.astype(F32)
    normed_rows = dot(back, wide_qkv, NT)
    own_scale = lax.dynamic_slice_in_dim(attn_scale, exp_index * own_rows, own_rows, 0)
    own_hat = hidden_rows * own_scale
    grad_hidden = resid_grad + norm_back(normed_rows, own_hat, own_scale, attn_gain)
    return (
        block_out,
        loss,
        grad_hidden,
        grad_w_query,
        grad_w_key,
        grad_w_value,
        grad_w_out,
        grad_gain_attn,
        tail[:, 0],
        tail[::2, 2],
        tail[:, 1],
        grad_w_gate,
        grad_w_up,
        grad_w_down,
    )


def solution(mesh):
    return jax.shard_map(
        on_device,
        mesh=mesh,
        in_specs=(
            P("ctx", None),
            P(("ctx", "exp"), None),
            P(),
            P(),
            P(("ctx", "exp"), None),
            P(("ctx", "exp"), None),
            P("ctx", "exp"),
            P("ctx", "exp"),
            P("ctx", "exp"),
            P("ctx", "exp"),
            P("ctx"),
            P("ctx"),
            P("ctx"),
            P("ctx"),
            P("ctx", None, "exp"),
            P("ctx", None, "exp"),
            P("ctx", "exp", None),
        ),
        out_specs=(
            P(("ctx", "exp"), None),
            P(),
            P(("ctx", "exp"), None),
            P("ctx", "exp"),
            P("ctx", "exp"),
            P("ctx", "exp"),
            P("ctx", "exp"),
            P("ctx"),
            P("ctx"),
            P("ctx"),
            P("ctx"),
            P("ctx", None, "exp"),
            P("ctx", None, "exp"),
            P("ctx", "exp", None),
        ),
        check_vma=False,
    )
```

```python
import functools

import jax
import jax.numpy as jnp
from jax import lax
from jax.experimental import pallas as pl
from jax.experimental.pallas import tpu as pltpu
from jax.sharding import PartitionSpec as P

HD = 64
BLK = 128
CONT_LEN = 1024
CONT_BLKS = CONT_LEN // BLK
LANES = 128

NORM_EPSILON = 1e-05
ROPE_BASE = 10000.0
MASK_FLOOR = -1e30
F32 = jnp.float32
BF16 = jnp.bfloat16
NT = (((1,), (1,)), ((), ()))
NN = (((1,), (0,)), ((), ()))
TN = (((0,), (0,)), ((), ()))


def dot(left, right, dims):
    return lax.dot_general(left, right, dims, preferred_element_type=F32)


def key_ranges(block, half, tile_blocks):
    cont = block >= half
    inner = jnp.where(cont, (block - half) % CONT_BLKS, 0)
    n_a = jnp.where(cont, half // tile_blocks, block // tile_blocks)
    cont_base = half + (block - half) // CONT_BLKS * CONT_BLKS
    base = jnp.where(cont, cont_base, block // tile_blocks * tile_blocks) * BLK
    return n_a, base, inner // tile_blocks


def gather_blocks(table, total, moves):
    def start(i, carry):
        to = pl.multiple_of(table[i] * BLK, BLK)
        for source, target, sem in moves:
            pltpu.make_async_copy(source(i), target(to), sem).start()
        return carry

    lax.fori_loop(0, total, start, 0)


def wait_all(ref, sem):
    pltpu.make_async_copy(ref, ref, sem).wait()


def rows_of(ref, per_ctx):
    def place(i):
        first = i // 4 * per_ctx + i % 4 * BLK
        return ref.at[pl.ds(pl.multiple_of(first, 16), BLK)]

    return place


def stats_of(ref):
    return lambda i: ref.at[i // 4, i // 2 % 2, :, pl.ds(pl.multiple_of(i % 2 * BLK, BLK), BLK)]


def causal(shape, key_first, query_first, rows_are_queries):
    row = lax.broadcasted_iota(jnp.int32, shape, 0) % BLK
    col = lax.broadcasted_iota(jnp.int32, shape, 1)
    if rows_are_queries:
        return key_first + col <= query_first + row
    return key_first + row <= query_first + col


def to_half(tile, source, target):
    values = tile.astype(F32)
    if source != target:
        values = pltpu.roll(values, HD, 1)
    lane = lax.broadcasted_iota(jnp.int32, values.shape, 1)
    return jnp.where(lane // HD == target, values, 0.0)


def turn(tile, cosine, sine):
    lane = lax.broadcasted_iota(jnp.int32, tile.shape, 1)
    ahead = pltpu.roll(tile, LANES - HD // 2, 1)
    behind = pltpu.roll(tile, HD // 2, 1)
    return tile * cosine + jnp.where(lane % HD < HD // 2, ahead, behind) * sine


def rows_by_head(source_ref, block_rows, target_ref):
    for h in range(4):
        m, g = h // 2, h % 2
        tile = source_ref[block_rows, m * LANES : (m + 1) * LANES]
        target_ref[h * BLK : (h + 1) * BLK, :] = to_half(tile, g, m).astype(BF16)


def rows_by_token(values):
    tiles = []
    for m in range(2):
        first = values[2 * m * BLK : (2 * m + 1) * BLK]
        second = values[(2 * m + 1) * BLK : (2 * m + 2) * BLK]
        tiles.append(to_half(first, m, 0) + to_half(second, m, 1))
    return tiles


def turn_kernel(pre_ref, scale_ref, gain_ref, cos_ref, sin_ref, q_ref, kv_ref):
    for col in range(3):
        lanes = slice(col * LANES, (col + 1) * LANES)
        which = 0 if col < 2 else 1
        hat = pre_ref[:, lanes] * scale_ref[:, which : which + 1]
        turned = turn(hat * gain_ref[:, lanes], cos_ref[...], sin_ref[...]).astype(BF16)
        if which == 0:
            q_ref[:, lanes] = (turned.astype(F32) * HD**-0.5).astype(BF16)
        else:
            kv_ref[:, :LANES] = turned
    kv_ref[:, LANES:] = pre_ref[:, 3 * LANES :].astype(BF16)


def attend_kernel(
    total, half, tile_blocks, table, own, q_in, kv, o_ref, lse_ref, kv_s, q_ref, acc, peak, s_buf, sem
):
    gather_blocks(
        table,
        total,
        [
            (
                rows_of(kv, 4 * BLK),
                lambda to: kv_s.at[pl.ds(to, BLK), pl.ds(0, 2 * LANES)],
                sem.at[0],
            )
        ],
    )
    kv_s[:, 2 * LANES :] = jnp.ones((total * BLK, LANES), BF16)
    wait_all(kv_s.at[:, pl.ds(0, 2 * LANES)], sem.at[0])
    width = tile_blocks * BLK

    def query_block(i, carry):
        block = own[i]
        n_a, base, n_b = key_ranges(block, half, tile_blocks)
        rows = pl.ds(pl.multiple_of(i * BLK, BLK), BLK)
        lanes = pl.ds(pl.multiple_of(i % 2 * BLK, BLK), BLK)
        rows_by_head(q_in, rows, q_ref)

        def first_key(j):
            return pl.multiple_of(jnp.where(j < n_a, j * width, base + (j - n_a) * width), BLK)

        def tile(start, masked):
            scores = dot(q_ref[...], kv_s[pl.ds(start, width), :LANES], NT)
            probs = jnp.exp(scores)
            if masked:
                probs = jnp.where(causal(probs.shape, start, block * BLK, True), probs, 0.0)
            acc[...] += dot(probs.astype(BF16), kv_s[pl.ds(start, width), LANES:], NN)

        def clear_tile(j, carry):
            tile(first_key(j), False)
            return carry

        def store(out, log_sum):
            first, second = rows_by_token(out)
            o_ref[rows, :LANES] = first
            o_ref[rows, LANES:] = second
            for h in range(4):
                lse_ref[i // 2, h : h + 1, lanes] = log_sum[h * BLK : (h + 1) * BLK].T[:1]

        def score(j):
            return dot(q_ref[...], kv_s[pl.ds(first_key(j), width), :LANES], NT)

        def weigh(scores, j, masked):
            start = first_key(j)
            probs = jnp.exp(scores)
            if masked:
                probs = jnp.where(causal(probs.shape, start, block * BLK, True), probs, 0.0)
            acc[...] += dot(probs.astype(BF16), kv_s[pl.ds(start, width), LANES:], NN)

        acc[...] = jnp.zeros_like(acc)
        count = n_a + n_b
        s_buf[0] = score(0)

        def two_tiles(i2, carry):
            j = 2 * i2
            s_buf[1] = score(j + 1)
            weigh(s_buf[0], j, False)
            s_buf[0] = score(j + 2)
            weigh(s_buf[1], j + 1, False)
            return carry

        lax.fori_loop(0, count // 2, two_tiles, 0)

        @pl.when(count % 2 == 1)
        def _():
            s_buf[1] = score(count)
            weigh(s_buf[0], count - 1, False)
            weigh(s_buf[1], count, True)

        @pl.when(count % 2 == 0)
        def _():
            weigh(s_buf[0], count, True)

        sums = acc[:, LANES:]
        in_range = (jnp.max(sums) < 2.0**100) & (jnp.min(sums) > 2.0**-40)

        @pl.when(in_range)
        def _():
            store(acc[:, :LANES] / sums, jnp.log(sums))

        @pl.when(jnp.logical_not(in_range))
        def _():
            acc[...] = jnp.zeros_like(acc)
            peak[...] = jnp.full_like(peak, MASK_FLOOR)

            def safe_tile(j, carry):
                start = first_key(j)
                scores = dot(q_ref[...], kv_s[pl.ds(start, width), :LANES], NT)
                seen = causal(scores.shape, start, block * BLK, True)
                scores = jnp.where(seen, scores, MASK_FLOOR)
                old = peak[...]
                new = jnp.maximum(old, jnp.max(scores, axis=1, keepdims=True))
                probs = jnp.where(seen, jnp.exp(scores - new[:, :1]), 0.0)
                keep = jnp.exp(old - new)
                acc[...] = acc[...] * keep[:, :1] + dot(
                    probs.astype(BF16), kv_s[pl.ds(start, width), LANES:], NN
                )
                peak[...] = new
                return carry

            lax.fori_loop(0, n_a + n_b + 1, safe_tile, 0)
            safe_sums = acc[:, LANES:]
            store(acc[:, :LANES] / safe_sums, peak[...] + jnp.log(safe_sums))

        return carry

    lax.fori_loop(0, 4, query_block, 0)


def query_grad_kernel(
    total,
    half,
    tile_blocks,
    table,
    own,
    q_in,
    do_in,
    o_in,
    lse_in,
    cos_ref,
    sin_ref,
    kv,
    dq_ref,
    kv_s,
    q_ref,
    do_ref,
    lse_ref,
    delta_ref,
    acc,
    sem,
):
    gather_blocks(
        table, total, [(rows_of(kv, 4 * BLK), lambda to: kv_s.at[pl.ds(to, BLK)], sem.at[0])]
    )
    wait_all(kv_s, sem.at[0])
    width = tile_blocks * BLK

    def query_block(i, carry):
        block = own[i]
        n_a, base, n_b = key_ranges(block, half, tile_blocks)
        rows = pl.ds(pl.multiple_of(i * BLK, BLK), BLK)
        lanes = pl.ds(pl.multiple_of(i % 2 * BLK, BLK), BLK)
        rows_by_head(q_in, rows, q_ref)
        rows_by_head(do_in, rows, do_ref)
        for h in range(4):
            part = slice(h * BLK, (h + 1) * BLK)
            pair = slice(h // 2 * LANES, (h // 2 + 1) * LANES)
            product = do_in[rows, pair].astype(F32) * o_in[rows, pair]
            own_half = to_half(product, h % 2, h % 2)
            delta = jnp.sum(own_half, axis=1, keepdims=True)
            delta_ref[part, :] = jnp.broadcast_to(delta, (BLK, LANES))
            row = lse_in[i // 2, h : h + 1, lanes]
            lse_ref[part, :] = jnp.broadcast_to(row, (LANES, BLK)).T

        def first_key(j):
            return pl.multiple_of(jnp.where(j < n_a, j * width, base + (j - n_a) * width), BLK)

        def tile(start, masked):
            keys = kv_s[pl.ds(start, width), :LANES]
            scores = dot(q_ref[...], keys, NT)
            prob_grad = dot(do_ref[...], kv_s[pl.ds(start, width), LANES:], NT)
            probs = jnp.exp(scores - lse_ref[:, :1])
            score_grad = probs * (prob_grad - delta_ref[:, :1])
            if masked:
                seen = causal(probs.shape, start, block * BLK, True)
                score_grad = jnp.where(seen, score_grad, 0.0)
            acc[...] += dot(score_grad.astype(BF16), keys, NN)

        def clear_tile(j, carry):
            tile(first_key(j), False)
            return carry

        acc[...] = jnp.zeros_like(acc)
        lax.fori_loop(0, n_a + n_b, clear_tile, 0)
        tile(first_key(n_a + n_b), True)
        for m, gradient in enumerate(rows_by_token(acc[...])):
            back = turn(gradient * HD**-0.5, cos_ref[rows, :], -sin_ref[rows, :])
            dq_ref[rows, m * LANES : (m + 1) * LANES] = back
        return carry

    lax.fori_loop(0, 4, query_block, 0)


def place(blk, h):
    return (h * 2 + blk) * BLK if blk < 2 else ((blk * 4) + h) * BLK


def spread_heads(source_ref, lanes, target_ref):
    target_ref[...] = jnp.zeros_like(target_ref)
    for blk in range(4):
        for h in range(4):
            m, g = h // 2, h % 2
            rows = slice(place(blk, h), place(blk, h) + BLK)
            tile = source_ref[blk * BLK : (blk + 1) * BLK, lanes]
            target_ref[rows, m * LANES : (m + 1) * LANES] = to_half(tile, m, g).astype(BF16)


def cont_tiles(own, which, half, tile_blocks):
    block = own[2 + which]
    base = half + (block - half) // CONT_BLKS * CONT_BLKS
    return block, block // tile_blocks, (base + CONT_BLKS) // tile_blocks, base // tile_blocks


def pair_probs_kernel(
    total, half, tile_blocks, q_rows, table, own, kv_in, q_all, lse_all, p_ref, pc_ref, q_s, lse_s, k_ref, sem
):
    step = pl.program_id(0)
    width = tile_blocks * BLK
    pair = 2 * tile_blocks

    @pl.when(step == 0)
    def _():
        gather_blocks(
            table,
            total,
            [
                (rows_of(q_all, q_rows), lambda to: q_s.at[pl.ds(to, BLK)], sem.at[0]),
                (stats_of(lse_all), lambda to: lse_s.at[:, pl.ds(to, BLK)], sem.at[1]),
            ],
        )
        spread_heads(kv_in, slice(0, LANES), k_ref)
        wait_all(q_s, sem.at[0])
        wait_all(lse_s, sem.at[1])

    def probs_of(first_row, per_head, j, keys_first, store):
        start = pl.multiple_of(j * width, width)
        keys = k_ref[first_row : first_row + 4 * per_head, :]
        scores = dot(keys, q_s[pl.ds(start, width), :], NT)
        for h in range(4):
            part = slice(h * per_head, (h + 1) * per_head)
            probs = jnp.exp(scores[part] - lse_s[h : h + 1, pl.ds(start, width)])
            if keys_first is not None:
                seen = [causal((BLK, width), first, start, False) for first in keys_first]
                probs = jnp.where(jnp.concatenate(seen, axis=0), probs, 0.0)
            store(part, probs.astype(BF16))

    low = jnp.minimum(own[0], own[1])
    high = jnp.maximum(own[0], own[1])

    def prompt(keys_first):
        for side in range(2):

            def store(part, probs, side=side):
                p_ref[0, part, side * width : (side + 1) * width] = probs

            probs_of(0, 2 * BLK, 2 * step + side, keys_first, store)

    @pl.when((step >= low // pair) & (step <= high // pair))
    def _():
        prompt([own[0] * BLK, own[1] * BLK])

    @pl.when(step > high // pair)
    def _():
        prompt(None)

    @pl.when(step == pl.num_programs(0) - 1)
    def _():
        for which in range(2):
            block, first, stop, base = cont_tiles(own, which, half, tile_blocks)

            def cont_tile(j, carry, which=which, block=block, base=base):
                def store(part, probs):
                    pc_ref[which, j - base, part, :] = probs

                probs_of((8 + 4 * which) * BLK, BLK, j, [block * BLK], store)
                return carry

            lax.fori_loop(first, stop, cont_tile, 0)


def pair_grad_kernel(
    total,
    half,
    tile_blocks,
    q_rows,
    do_rows,
    table,
    own,
    kv_in,
    cos_ref,
    sin_ref,
    q_all,
    do_all,
    delta_all,
    p_ref,
    pc_ref,
    out_ref,
    q_s,
    do_s,
    delta_s,
    v_ref,
    dk_ref,
    dv_ref,
    d_buf,
    sem,
):
    step = pl.program_id(0)
    width = tile_blocks * BLK
    pair = 2 * tile_blocks

    @pl.when(step == 0)
    def _():
        gather_blocks(
            table,
            total,
            [
                (rows_of(q_all, q_rows), lambda to: q_s.at[pl.ds(to, BLK)], sem.at[0]),
                (rows_of(do_all, do_rows), lambda to: do_s.at[pl.ds(to, BLK)], sem.at[1]),
                (stats_of(delta_all), lambda to: delta_s.at[:, pl.ds(to, BLK)], sem.at[2]),
            ],
        )
        dk_ref[...] = jnp.zeros_like(dk_ref)
        dv_ref[...] = jnp.zeros_like(dv_ref)
        spread_heads(kv_in, slice(LANES, 2 * LANES), v_ref)
        wait_all(q_s, sem.at[0])
        wait_all(do_s, sem.at[1])
        wait_all(delta_s, sem.at[2])

    def prob_grad(first_row, per_head, j):
        start = pl.multiple_of(j * width, width)
        values = v_ref[first_row : first_row + 4 * per_head, :]
        return dot(values, do_s[pl.ds(start, width), :], NT)

    def add(first_row, per_head, j, probs, grads_in):
        rows = pl.ds(first_row, 4 * per_head)
        start = pl.multiple_of(j * width, width)
        score_low = []
        for h in range(4):
            part = slice(h * per_head, (h + 1) * per_head)
            shifted_grad = grads_in[part] - delta_s[h : h + 1, pl.ds(start, width)]
            score_low.append((probs[part].astype(F32) * shifted_grad).astype(BF16))
        dv_ref[rows, :] += dot(probs, do_s[pl.ds(start, width), :], NN)
        queries = q_s[pl.ds(start, width), :]
        dk_ref[rows, :] += dot(jnp.concatenate(score_low, axis=0), queries, NN)

    low = jnp.minimum(own[0], own[1])
    last = total // tile_blocks - 1

    @pl.when(step == low // pair)
    def _():
        d_buf[0] = prob_grad(0, 2 * BLK, 2 * step)

    @pl.when(step >= low // pair)
    def _():
        d_buf[1] = prob_grad(0, 2 * BLK, 2 * step + 1)
        add(0, 2 * BLK, 2 * step, p_ref[0, :, :width], d_buf[0])
        d_buf[0] = prob_grad(0, 2 * BLK, jnp.minimum(2 * step + 2, last))
        add(0, 2 * BLK, 2 * step + 1, p_ref[0, :, width:], d_buf[1])

    def collect(ref, blk):
        tile_sum = None
        for h in range(4):
            m, g = h // 2, h % 2
            part = ref[place(blk, h) : place(blk, h) + BLK, m * LANES : (m + 1) * LANES]
            moved = to_half(part, g, m)
            tile_sum = moved if tile_sum is None else tile_sum + moved
        return tile_sum

    @pl.when(step == pl.num_programs(0) - 1)
    def _():
        for which in range(2):
            _, first, stop, base = cont_tiles(own, which, half, tile_blocks)

            def cont_tile(j, carry, which=which, base=base):
                first_row = (8 + 4 * which) * BLK
                grads_in = prob_grad(first_row, BLK, j)
                add(first_row, BLK, j, pc_ref[which, j - base], grads_in)
                return carry

            lax.fori_loop(first, stop, cont_tile, 0)
        for blk in range(4):
            rows = slice(blk * BLK, (blk + 1) * BLK)
            out_ref[rows, :LANES] = turn(collect(dk_ref, blk), cos_ref[rows, :], -sin_ref[rows, :])
            out_ref[rows, LANES:] = collect(dv_ref, blk)


def down_strips(w_ref, pair, width):
    strips = [w_ref[u, :, 2 * width : 3 * width] for u in (2 * pair, 2 * pair + 1)]
    return jnp.concatenate(strips, axis=1)


def expert_kernel(quarters, width, x_ref, w_ref, out_ref, gate_ref, up_ref):
    acts = []
    for u in range(quarters):
        cols = slice(u * width, (u + 1) * width)
        pre = dot(x_ref[...], w_ref[u, :, : 2 * width], NN)
        gate, up = pre[:, :width], pre[:, width:]
        gate_ref[:, cols] = gate
        up_ref[:, cols] = up
        acts.append((gate * jax.nn.sigmoid(gate) * up).astype(BF16))
    out = None
    for pair in range(quarters // 2):
        act = jnp.concatenate(acts[2 * pair : 2 * pair + 2], axis=1)
        part = dot(act, down_strips(w_ref, pair, width), NT)
        out = part if out is None else out + part
    out_ref[...] = out.astype(BF16)


def expert_grad_kernel(
    quarters, width, dy_ref, gate_ref, up_ref, w_ref, wt_ref, dx_ref, dgate_ref, dup_ref, act_ref
):
    total = None
    for pair in range(quarters // 2):
        both = dot(dy_ref[...], down_strips(w_ref, pair, width), NN)
        for side in range(2):
            u = 2 * pair + side
            cols = slice(u * width, (u + 1) * width)
            act_grad = both[:, side * width : (side + 1) * width]
            gate, up = gate_ref[:, cols], up_ref[:, cols]
            sig = jax.nn.sigmoid(gate)
            gate_act = gate * sig
            act_ref[:, cols] = (gate_act * up).astype(BF16)
            gate_grad = (act_grad * up * sig * (1.0 + gate * (1.0 - sig))).astype(BF16)
            up_grad = (act_grad * gate_act).astype(BF16)
            dgate_ref[:, cols] = gate_grad
            dup_ref[:, cols] = up_grad
            grads = jnp.concatenate([gate_grad, up_grad], axis=1)
            part = dot(grads, wt_ref[u], NN)
            total = part if total is None else total + part
    dx_ref[...] = total.astype(BF16)


def block_of_whole(shape):
    return pl.BlockSpec(shape, lambda i, *_: (0,) * len(shape))


def kernel_call(kernel, name, prefetch, ins, outs, scratch, flops):
    hbm = pl.BlockSpec(memory_space=pl.ANY)
    moved = sum(x.size * x.dtype.itemsize for x, _ in ins)
    return pl.pallas_call(
        kernel,
        out_shape=tuple(outs),
        grid_spec=pltpu.PrefetchScalarGridSpec(
            num_scalar_prefetch=len(prefetch),
            grid=(1,),
            in_specs=[hbm if far else block_of_whole(x.shape) for x, far in ins],
            out_specs=tuple(block_of_whole(out.shape) for out in outs),
            scratch_shapes=scratch,
        ),
        compiler_params=pltpu.CompilerParams(vmem_limit_bytes=48 << 20),
        cost_estimate=pl.CostEstimate(flops=flops, bytes_accessed=moved, transcendentals=0),
        name=name,
    )(*prefetch, *(x for x, _ in ins))


def by_rows(kernel, name, rows, ins, outs, flops):
    def spec(shape):
        if len(shape) == 3:
            return pl.BlockSpec(shape, lambda i: (0, 0, 0))
        return pl.BlockSpec((rows, shape[1]), lambda i: (i, 0))

    return pl.pallas_call(
        kernel,
        out_shape=tuple(pltpu.HBM(out.shape, out.dtype) for out in outs),
        grid=(outs[0].shape[0] // rows,),
        in_specs=[spec(x.shape) for x in ins],
        out_specs=tuple(spec(out.shape) for out in outs),
        compiler_params=pltpu.CompilerParams(vmem_limit_bytes=40 << 20),
        cost_estimate=pl.CostEstimate(flops=flops, bytes_accessed=10**7, transcendentals=0),
        name=name,
    )(*(pltpu.with_memory_space_constraint(x, pltpu.HBM) for x in ins))


def expert_forward(rows_in, weights):
    slots, model_width = rows_in.shape
    quarters, _, cols = weights.shape
    width = cols // 3
    hidden = jax.ShapeDtypeStruct((slots, quarters * width), F32)
    return by_rows(
        functools.partial(expert_kernel, quarters, width),
        "expert",
        slots // 5,
        [rows_in, weights],
        [jax.ShapeDtypeStruct((slots, model_width), BF16), hidden, hidden],
        6 * slots * model_width * quarters * width,
    )


def expert_backward(rows_grad, gate_pre, up_pre, weights, turned):
    slots, model_width = rows_grad.shape
    quarters, _, cols = weights.shape
    width = cols // 3
    hidden = jax.ShapeDtypeStruct((slots, quarters * width), BF16)
    return by_rows(
        functools.partial(expert_grad_kernel, quarters, width),
        "expert_grad",
        slots // 2,
        [rows_grad, gate_pre, up_pre, weights, turned],
        [jax.ShapeDtypeStruct((slots, model_width), BF16), hidden, hidden, hidden],
        6 * slots * model_width * quarters * width,
    )


def turn_heads(projected, scales, gain, cosine, sine):
    rows = projected.shape[0]
    out = jax.ShapeDtypeStruct((rows, 2 * LANES), BF16)
    ins = [(x, False) for x in (projected, scales, gain, cosine, sine)]
    return kernel_call(turn_kernel, "turn_heads", (), ins, [out, out], [], 10**6)


def attend(table, own, q, kv_all):
    total = table.shape[0]
    return kernel_call(
        functools.partial(attend_kernel, total, total // 2, 8),
        "attend",
        (table, own),
        [(q, False), (kv_all, True)],
        [
            jax.ShapeDtypeStruct((4 * BLK, 2 * LANES), F32),
            jax.ShapeDtypeStruct((2, 4, 2 * BLK), F32),
        ],
        [
            pltpu.VMEM((total * BLK, 3 * LANES), BF16),
            pltpu.VMEM((4 * BLK, LANES), BF16),
            pltpu.VMEM((4 * BLK, 2 * LANES), F32),
            pltpu.VMEM((4 * BLK, LANES), F32),
            pltpu.VMEM((2, 4 * BLK, 8 * BLK), F32),
            pltpu.SemaphoreType.DMA((1,)),
        ],
        20 * 10**9,
    )


def query_grad(table, own, q, out_grad, heads, lse, cosine, sine, kv_all):
    total = table.shape[0]
    ins = [(x, False) for x in (q, out_grad, heads, lse, cosine, sine)]
    return kernel_call(
        functools.partial(query_grad_kernel, total, total // 2, 4),
        "query_grad",
        (table, own),
        ins + [(kv_all, True)],
        [jax.ShapeDtypeStruct((4 * BLK, 2 * LANES), F32)],
        [
            pltpu.VMEM((total * BLK, 2 * LANES), BF16),
            pltpu.VMEM((4 * BLK, LANES), BF16),
            pltpu.VMEM((4 * BLK, LANES), BF16),
            pltpu.VMEM((4 * BLK, LANES), F32),
            pltpu.VMEM((4 * BLK, LANES), F32),
            pltpu.VMEM((4 * BLK, LANES), F32),
            pltpu.SemaphoreType.DMA((1,)),
        ],
        30 * 10**9,
    )[0]


def pair_call(kernel, name, table, own, ins, blocks, outs, out_blocks, scratch, flops):
    steps = table.shape[0] // 8

    def tile_place(step, table_ref, own_ref):
        return (jnp.maximum(step, jnp.minimum(own_ref[0], own_ref[1]) // 8), 0, 0)

    def spec(shape, block):
        if block is None:
            return pl.BlockSpec(memory_space=pl.ANY)
        if block == shape:
            return pl.BlockSpec(shape, lambda *_: (0,) * len(shape))
        return pl.BlockSpec(block, tile_place)

    return pl.pallas_call(
        kernel,
        out_shape=tuple(outs),
        grid_spec=pltpu.PrefetchScalarGridSpec(
            num_scalar_prefetch=2,
            grid=(steps,),
            in_specs=[spec(x.shape, block) for x, block in zip(ins, blocks)],
            out_specs=tuple(spec(x.shape, block) for x, block in zip(outs, out_blocks)),
            scratch_shapes=scratch,
        ),
        compiler_params=pltpu.CompilerParams(vmem_limit_bytes=48 << 20),
        cost_estimate=pl.CostEstimate(flops=flops, bytes_accessed=4 * 10**7, transcendentals=0),
        name=name,
    )(table, own, *ins)


PROB_BLOCK = (1, 8 * BLK, 8 * BLK)
CONT_SHAPE = (2, CONT_BLKS // 4, 4 * BLK, 4 * BLK)


def pair_probs(table, own, kv, q_all, q_rows, lse_all):
    total = table.shape[0]
    return pair_call(
        functools.partial(pair_probs_kernel, total, total // 2, 4, q_rows),
        "pair_probs",
        table,
        own,
        [kv, q_all, lse_all],
        [kv.shape, None, None],
        [
            jax.ShapeDtypeStruct((total // 8,) + PROB_BLOCK[1:], BF16),
            jax.ShapeDtypeStruct(CONT_SHAPE, BF16),
        ],
        [PROB_BLOCK, CONT_SHAPE],
        [
            pltpu.VMEM((total * BLK, 2 * LANES), BF16),
            pltpu.VMEM((4, total * BLK), F32),
            pltpu.VMEM((16 * BLK, 2 * LANES), BF16),
            pltpu.SemaphoreType.DMA((2,)),
        ],
        20 * 10**9,
    )


def pair_grad(table, own, kv, cosine, sine, q_all, q_rows, do_all, do_rows, delta_all, probs):
    total = table.shape[0]
    return pair_call(
        functools.partial(pair_grad_kernel, total, total // 2, 4, q_rows, do_rows),
        "pair_grad",
        table,
        own,
        [kv, cosine, sine, q_all, do_all, delta_all, *probs],
        [kv.shape, cosine.shape, sine.shape, None, None, None, PROB_BLOCK, CONT_SHAPE],
        [jax.ShapeDtypeStruct((4 * BLK, 2 * LANES), F32)],
        [(4 * BLK, 2 * LANES)],
        [
            pltpu.VMEM((total * BLK, 2 * LANES), BF16),
            pltpu.VMEM((total * BLK, 2 * LANES), BF16),
            pltpu.VMEM((4, total * BLK), F32),
            pltpu.VMEM((16 * BLK, 2 * LANES), BF16),
            pltpu.VMEM((16 * BLK, 2 * LANES), F32),
            pltpu.VMEM((16 * BLK, 2 * LANES), F32),
            pltpu.VMEM((2, 8 * BLK, 4 * BLK), F32),
            pltpu.SemaphoreType.DMA((3,)),
        ],
        30 * 10**9,
    )[0]


def turn_tables(position):
    half_dim = HD // 2
    frequency = ROPE_BASE ** (-(jnp.arange(half_dim, dtype=F32) * 2.0 / HD))
    angles = position[:, None] * frequency[None, :]
    cosine, sine = jnp.cos(angles), jnp.sin(angles)
    return jnp.concatenate([cosine] * 4, axis=1), jnp.concatenate([-sine, sine] * 2, axis=1)


def norm_back(grad_normed, hat_values, scale_values, gain_values):
    grad_hat = grad_normed * gain_values
    return scale_values * (
        grad_hat - hat_values * jnp.mean(grad_hat * hat_values, axis=-1, keepdims=True)
    )


def pieces(values, count):
    parts = []
    for _ in range(count):
        part = lax.reduce_precision(values, 8, 7)
        parts.append(part.astype(BF16))
        values = values - part
    return parts


def exchange(values, axis):
    return lax.all_to_all(values, axis, split_axis=0, concat_axis=0, tiled=True)


def spread(values, axis, count):
    return exchange(jnp.broadcast_to(values[None], (count,) + values.shape), axis)


def shifted(values, axis, count):
    parts = [values]
    for step in range(1, count):
        parts.append(lax.ppermute(values, axis, [(i, (i + step) % count) for i in range(count)]))
    return parts


def exchange_short(values, axis, index, count):
    rows = values.shape[0] // count
    come = []
    for step in range(count):
        to = (index + step) % count
        part = lax.dynamic_slice_in_dim(values, to * rows, rows, 0)
        if step > 0:
            part = lax.ppermute(part, axis, [(i, (i + step) % count) for i in range(count)])
        come.append(part)
    return jnp.concatenate(come, axis=1)


def in_order(parts, index, count):
    ordered = []
    for place in range(count):
        back = (index - place) % count
        part = parts[0]
        for step in range(1, count):
            part = jnp.where(back == step, parts[step], part)
        ordered.append(part)
    return jnp.stack(ordered, axis=0)


def with_stats(rows, stats):
    parts = jnp.stack(pieces(stats, 3), axis=0).reshape(-1, rows.shape[1])
    return jnp.concatenate([rows, jnp.pad(parts, ((0, -parts.shape[0] % 16), (0, 0)))], axis=0)


def stats_in(gathered, first):
    parts = gathered[:, first : first + 24].reshape(-1, 3, 2, 4, gathered.shape[2])
    return jnp.sum(parts.astype(F32), axis=1)


def ride_along(values):
    parts = jnp.concatenate(pieces(values, 3), axis=-1)
    return jnp.pad(parts, ((0, 0), (0, 0), (0, LANES - parts.shape[-1])))


def parted(sums, count):
    return sum(sums[:, i * count : (i + 1) * count] for i in range(3))


def on_device(
    hidden_in,
    teacher,
    valid,
    block_of,
    routes,
    gates,
    w_query,
    w_key,
    w_value,
    w_out,
    gain_attn,
    gain_query,
    gain_key,
    gain_ffn,
    w_gate,
    w_up,
    w_down,
):
    ctx_count = lax.axis_size("ctx")
    exp_count = lax.axis_size("exp")
    ctx_index = lax.axis_index("ctx")
    exp_index = lax.axis_index("exp")
    ctx_rows, model_width = hidden_in.shape
    own_rows = ctx_rows // exp_count
    token_total = block_of.shape[0] * BLK
    head_cols = w_query.shape[1]
    kv_cols = w_key.shape[1]
    kv_total = kv_cols * exp_count
    qkv_cols = head_cols + 2 * kv_cols
    shard_rows = w_query.shape[0]

    own_weights = jnp.concatenate([w_query, w_key, w_value, w_out], axis=1)
    gain_row = jnp.concatenate([gain_attn, gain_query, gain_ffn, gain_key])
    gain_rows = jnp.pad(
        gain_row, (0, 8 * own_weights.shape[1] - gain_row.shape[0])
    ).reshape(8, -1)
    first_parts = spread(jnp.concatenate([own_weights, gain_rows], axis=0), "ctx", ctx_count)
    full_weights = first_parts[:, :shard_rows].reshape(model_width, -1)
    full_qkv = full_weights[:, :qkv_cols]
    gains = first_parts[:, shard_rows:].reshape(ctx_count, -1)[:, : gain_row.shape[0]].astype(F32)
    attn_gain = gains[:, :shard_rows].reshape(model_width)
    query_gain_all = gains[:, shard_rows : 2 * shard_rows].reshape(model_width)
    ffn_gain = gains[:, 2 * shard_rows : 3 * shard_rows].reshape(model_width)
    key_gain_all = gains[:, 3 * shard_rows :].reshape(kv_total)
    query_gain = lax.dynamic_slice_in_dim(query_gain_all, exp_index * head_cols, head_cols)
    key_gain = lax.dynamic_slice_in_dim(key_gain_all, exp_index * kv_cols, kv_cols)

    hidden_f = hidden_in.astype(F32)
    attn_scale = lax.rsqrt(jnp.mean(hidden_f * hidden_f, axis=-1, keepdims=True) + NORM_EPSILON)
    attn_hat = hidden_f * attn_scale
    normed = (attn_hat * attn_gain).astype(BF16)
    projected = dot(normed, full_qkv, NN)
    query_pre = projected[:, :head_cols]
    key_pre = projected[:, head_cols : head_cols + kv_cols]
    query_square, key_square = lax.psum(
        jnp.stack([jnp.sum(query_pre * query_pre, axis=1), jnp.sum(key_pre * key_pre, axis=1)]),
        "exp",
    )
    query_scale = lax.rsqrt(query_square / model_width + NORM_EPSILON)[:, None]
    key_scale = lax.rsqrt(key_square / kv_total + NORM_EPSILON)[:, None]
    query_hat = query_pre * query_scale
    key_hat = key_pre * key_scale
    own_blocks = lax.dynamic_slice_in_dim(block_of, ctx_index * 4, 4)
    token_ids = (own_blocks[:, None] * BLK + jnp.arange(BLK, dtype=jnp.int32)[None]).reshape(-1)
    prompt_len = token_total // 2
    position = jnp.where(
        token_ids >= prompt_len, prompt_len + (token_ids - prompt_len) % CONT_LEN, token_ids
    ).astype(F32)
    cosine, sine = turn_tables(position)
    queries_rot, own_kv = turn_heads(
        projected,
        jnp.concatenate([query_scale, key_scale], axis=1),
        jnp.concatenate([query_gain, key_gain])[None],
        cosine,
        sine,
    )
    kv_all = lax.all_gather(own_kv, "ctx", axis=0, tiled=True)
    own_out, own_gate, own_up, own_down, _ = lax.optimization_barrier(
        (full_weights[:, qkv_cols:], w_gate[0], w_up[0], w_down[0], own_kv)
    )
    width = w_gate.shape[2]
    own_expert = jnp.concatenate([own_gate, own_up, own_down.T], axis=1)
    expert = lax.all_gather(own_expert, "exp", axis=0, tiled=False)
    out_parts = shifted(own_out, "exp", exp_count)
    wide_out = jnp.concatenate(out_parts, axis=1)
    full_out = in_order(out_parts, exp_index, exp_count)
    expert_total = ctx_count
    capacity = max(2, own_rows * routes.shape[1] * 5 // (expert_total * 4))
    slots = expert_total * capacity
    names = routes[:, :, None] == jnp.arange(expert_total, dtype=jnp.int32)[None, None, :]
    named = jnp.any(names, axis=1)
    gate_of = jnp.sum(jnp.where(names, gates[:, :, None], 0.0), axis=1)
    before = jnp.tril(jnp.ones((own_rows, own_rows), BF16), -1)
    rank = dot(before, named.astype(BF16), NN).astype(jnp.int32)
    slot_rank = jnp.where(named, rank, -1).T[:, None, :]
    holds = slot_rank == jnp.arange(capacity, dtype=jnp.int32)[None, :, None]
    pick = holds.astype(BF16).reshape(slots, own_rows)
    weigh = jnp.where(holds, gate_of.T[:, None, :], 0.0).reshape(slots, own_rows)
    slot_gate = jnp.sum(weigh, axis=1, keepdims=True)

    kv_all, wide_out, full_out, pick, weigh, slot_gate = lax.optimization_barrier(
        (kv_all, wide_out, full_out, pick, weigh, slot_gate)
    )
    heads_f, lse = attend(block_of, own_blocks, queries_rot, kv_all)
    heads_low = heads_f.astype(BF16)

    own_heads = exchange_short(heads_low, "exp", exp_index, exp_count)
    own_heads, later_q, lse = lax.optimization_barrier((own_heads, queries_rot, lse))
    q_all = lax.all_gather(with_stats(later_q, lse), "ctx", axis=0, tiled=False)
    attn_rows = dot(own_heads, wide_out, NT)
    hidden_rows = lax.dynamic_slice_in_dim(hidden_in, exp_index * own_rows, own_rows, 0)
    hidden_rows = hidden_rows.astype(F32)
    resid = hidden_rows + attn_rows
    ffn_scale = lax.rsqrt(jnp.mean(resid * resid, axis=-1, keepdims=True) + NORM_EPSILON)
    ffn_hat = resid * ffn_scale
    normed_ffn = (ffn_hat * ffn_gain).astype(BF16)

    def send(rows):
        return exchange(rows.reshape(ctx_count, capacity, model_width), "ctx").reshape(
            slots, model_width
        )

    expert_in = send(dot(pick, normed_ffn, NN).astype(BF16))
    expert_out, gate_pre, up_pre = expert_forward(expert_in, expert)
    returned = send(expert_out)
    turned = expert[:, :, : 2 * width].transpose(0, 2, 1)
    returned, q_all, later_qkv, turned = lax.optimization_barrier(
        (returned, q_all, full_qkv, turned)
    )
    probs = pair_probs(
        block_of,
        own_blocks,
        own_kv,
        q_all.reshape(-1, head_cols),
        q_all.shape[1],
        stats_in(q_all, ctx_rows),
    )
    wide_qkv = jnp.concatenate(shifted(later_qkv, "exp", exp_count), axis=1)
    moe_parts = dot(jnp.concatenate(pieces(weigh, 2), axis=1), returned, TN)
    moe_rows = moe_parts[:own_rows] + moe_parts[own_rows:]
    block_out = resid + moe_rows

    row_start = (ctx_index * exp_count + exp_index) * own_rows
    row_valid = lax.dynamic_slice_in_dim(valid, row_start, own_rows, 0).astype(F32)
    valid_count = jnp.sum(valid.astype(F32))
    misfit = block_out - teacher.astype(F32)
    local_loss = jnp.sum(row_valid[:, None] * misfit * misfit)
    out_grad_rows = misfit * row_valid[:, None] * (token_total / valid_count)
    copy_grad = dot(
        jnp.concatenate([pick, pick], axis=1),
        jnp.concatenate(pieces(out_grad_rows, 2), axis=0),
        NN,
    )
    grad_copies = send((slot_gate * copy_grad).astype(BF16))
    grad_copies, probs = lax.optimization_barrier((grad_copies, probs))
    input_grad, gate_grad, up_grad, hidden_act = expert_backward(
        grad_copies, gate_pre, up_pre, expert, turned
    )
    arrived_grad = send(input_grad)

    gate_part = dot(expert_in, gate_grad, TN)
    up_part = dot(expert_in, up_grad, TN)
    down_part = dot(hidden_act, grad_copies, TN)
    gate_part = gate_part.reshape(model_width, exp_count, width).transpose(1, 0, 2)
    up_part = up_part.reshape(model_width, exp_count, width).transpose(1, 0, 2)
    arrived_grad, wide_qkv, gate_part, up_part, down_part = lax.optimization_barrier(
        (arrived_grad, wide_qkv, gate_part, up_part, down_part)
    )
    ffn_normed_grad = dot(pick, arrived_grad, TN)

    ffn_gain_part = jnp.sum(ffn_normed_grad * ffn_hat, axis=0)
    resid_grad = out_grad_rows + norm_back(ffn_normed_grad, ffn_hat, ffn_scale, ffn_gain)
    branch_rows = resid_grad.astype(BF16)

    do_rows = jnp.einsum("ro,eok->erk", branch_rows, full_out, preferred_element_type=F32)
    out_grad = exchange(do_rows.astype(BF16), "exp").reshape(ctx_rows, head_cols)
    branch_parts = shifted(branch_rows, "exp", exp_count)
    head_of = jnp.arange(head_cols, dtype=jnp.int32)[None] // HD
    head_ones = (head_of == jnp.arange(4, dtype=jnp.int32)[:, None]).astype(F32)
    delta = lax.dot_general(
        head_ones,
        out_grad.astype(F32) * heads_f,
        NT,
        precision=lax.Precision.HIGHEST,
        preferred_element_type=F32,
    )
    delta = delta.reshape(4, 2, 2 * BLK).transpose(1, 0, 2)
    do_all = lax.all_gather(with_stats(out_grad, delta), "ctx", axis=0, tiled=False)
    query_n_grad = query_grad(
        block_of, own_blocks, queries_rot, out_grad, heads_f, lse, cosine, sine, kv_all
    )

    grad_out = None
    for step, part in enumerate(branch_parts):
        first = (exp_index - step) % exp_count * own_rows
        term = dot(part, lax.dynamic_slice_in_dim(heads_low, first, own_rows, 0), TN)
        grad_out = term if grad_out is None else grad_out + term

    do_all, query_n_grad, grad_out, gate_part, up_part, down_part = lax.optimization_barrier(
        (do_all, query_n_grad, grad_out, gate_part, up_part, down_part)
    )
    grad_w_gate = lax.psum_scatter(gate_part, "exp", scatter_dimension=0, tiled=True)
    grad_w_up = lax.psum_scatter(up_part, "exp", scatter_dimension=0, tiled=True)
    grad_w_down = lax.psum_scatter(down_part, "exp", scatter_dimension=0, tiled=True)[None]

    pair_grads = pair_grad(
        block_of,
        own_blocks,
        own_kv,
        cosine,
        sine,
        q_all.reshape(-1, head_cols),
        q_all.shape[1],
        do_all.reshape(-1, head_cols),
        do_all.shape[1],
        stats_in(do_all, ctx_rows),
        probs,
    )
    key_n_grad = pair_grads[:, :kv_cols]
    value_grad = pair_grads[:, kv_cols:].astype(BF16)
    query_gain_part = jnp.sum(query_n_grad * query_hat, axis=0)
    key_gain_part = jnp.sum(key_n_grad * key_hat, axis=0)
    query_hat_grad = query_n_grad * query_gain
    key_hat_grad = key_n_grad * key_gain
    stats = jnp.concatenate(
        [
            jnp.sum(query_hat_grad * query_hat, axis=1),
            jnp.sum(key_hat_grad * key_hat, axis=1),
            lax.dynamic_update_slice_in_dim(
                jnp.zeros((model_width,), F32), query_gain_part, exp_index * head_cols, 0
            ),
            ffn_gain_part,
            lax.dynamic_update_slice_in_dim(
                jnp.zeros((kv_total,), F32), key_gain_part, exp_index * kv_cols, 0
            ),
            jnp.full((kv_total,), local_loss),
        ]
    )
    stats = lax.psum(stats.reshape(-1, LANES), "exp").reshape(-1)
    query_stat = stats[:ctx_rows, None] / model_width
    key_stat = stats[ctx_rows : 2 * ctx_rows, None] / kv_total
    sums = stats[2 * ctx_rows :]
    query_low = (query_scale * (query_hat_grad - query_hat * query_stat)).astype(BF16)
    key_low = (key_scale * (key_hat_grad - key_hat * key_stat)).astype(BF16)
    grad_low = jnp.concatenate([query_low, key_low, value_grad], axis=1)

    wide_sums = jnp.stack(
        [
            sums[:model_width].reshape(ctx_count, shard_rows),
            sums[model_width : 2 * model_width].reshape(ctx_count, shard_rows),
            jnp.repeat(
                sums[2 * model_width : 2 * model_width + kv_total].reshape(ctx_count, -1), 2, axis=1
            ),
            jnp.broadcast_to(sums[-1], (ctx_count, shard_rows)),
        ],
        axis=-1,
    )
    grad_qkv = dot(normed, grad_low, TN)
    shards = exchange(
        jnp.concatenate(
            [
                grad_qkv.astype(BF16).reshape(ctx_count, shard_rows, qkv_cols),
                grad_out.astype(BF16).reshape(ctx_count, shard_rows, head_cols),
                ride_along(wide_sums),
            ],
            axis=2,
        ),
        "ctx",
    )
    back = exchange_short(grad_low, "exp", exp_index, exp_count)
    shards = jnp.sum(shards.astype(F32), axis=0)
    grad_w_query = shards[:, :head_cols]
    grad_w_key = shards[:, head_cols : head_cols + kv_cols]
    grad_w_value = shards[:, head_cols + kv_cols : qkv_cols]
    grad_w_out = shards[:, qkv_cols : qkv_cols + head_cols]
    tail = parted(shards[:, qkv_cols + head_cols :], 4)
    loss = tail[0, 3] / (valid_count * model_width)

    gain_part = jnp.sum(grad_w_query * w_query.astype(F32), axis=1)
    gain_part += jnp.sum(grad_w_key * w_key.astype(F32), axis=1)
    gain_part += jnp.sum(grad_w_value * w_value.astype(F32), axis=1)
    grad_gain_attn = lax.psum(gain_part, "exp") / gain_attn.astype(F32)
    normed_rows = dot(back, wide_qkv, NT)
    own_scale = lax.dynamic_slice_in_dim(attn_scale, exp_index * own_rows, own_rows, 0)
    own_hat = hidden_rows * own_scale
    grad_hidden = resid_grad + norm_back(normed_rows, own_hat, own_scale, attn_gain)
    return (
        block_out,
        loss,
        grad_hidden,
        grad_w_query,
        grad_w_key,
        grad_w_value,
        grad_w_out,
        grad_gain_attn,
        tail[:, 0],
        tail[::2, 2],
        tail[:, 1],
        grad_w_gate,
        grad_w_up,
        grad_w_down,
    )


def solution(mesh):
    return jax.shard_map(
        on_device,
        mesh=mesh,
        in_specs=(
            P("ctx", None),
            P(("ctx", "exp"), None),
            P(),
            P(),
            P(("ctx", "exp"), None),
            P(("ctx", "exp"), None),
            P("ctx", "exp"),
            P("ctx", "exp"),
            P("ctx", "exp"),
            P("ctx", "exp"),
            P("ctx"),
            P("ctx"),
            P("ctx"),
            P("ctx"),
            P("ctx", None, "exp"),
            P("ctx", None, "exp"),
            P("ctx", "exp", None),
        ),
        out_specs=(
            P(("ctx", "exp"), None),
            P(),
            P(("ctx", "exp"), None),
            P("ctx", "exp"),
            P("ctx", "exp"),
            P("ctx", "exp"),
            P("ctx", "exp"),
            P("ctx"),
            P("ctx"),
            P("ctx"),
            P("ctx"),
            P("ctx", None, "exp"),
            P("ctx", None, "exp"),
            P("ctx", "exp", None),
        ),
        check_vma=False,
    )
```

```python
import functools

import jax
import jax.numpy as jnp
from jax import lax
from jax.experimental import pallas as pl
from jax.experimental.pallas import tpu as pltpu
from jax.sharding import PartitionSpec as P

HD = 64
BLK = 128
CONT_LEN = 1024
CONT_BLKS = CONT_LEN // BLK
LANES = 128

NORM_EPSILON = 1e-05
ROPE_BASE = 10000.0
MASK_FLOOR = -1e30
F32 = jnp.float32
BF16 = jnp.bfloat16
NT = (((1,), (1,)), ((), ()))
NN = (((1,), (0,)), ((), ()))
TN = (((0,), (0,)), ((), ()))


def dot(left, right, dims):
    return lax.dot_general(left, right, dims, preferred_element_type=F32)


def key_ranges(block, half, tile_blocks):
    cont = block >= half
    inner = jnp.where(cont, (block - half) % CONT_BLKS, 0)
    n_a = jnp.where(cont, half // tile_blocks, block // tile_blocks)
    cont_base = half + (block - half) // CONT_BLKS * CONT_BLKS
    base = jnp.where(cont, cont_base, block // tile_blocks * tile_blocks) * BLK
    return n_a, base, inner // tile_blocks


def gather_blocks(table, total, moves):
    def start(i, carry):
        to = pl.multiple_of(table[i] * BLK, BLK)
        for source, target, sem in moves:
            pltpu.make_async_copy(source(i), target(to), sem).start()
        return carry

    lax.fori_loop(0, total, start, 0)


def wait_all(ref, sem):
    pltpu.make_async_copy(ref, ref, sem).wait()


def rows_of(ref, per_ctx):
    def place(i):
        first = i // 4 * per_ctx + i % 4 * BLK
        return ref.at[pl.ds(pl.multiple_of(first, 16), BLK)]

    return place


def stats_of(ref):
    return lambda i: ref.at[i // 4, i // 2 % 2, :, pl.ds(pl.multiple_of(i % 2 * BLK, BLK), BLK)]


def causal(shape, key_first, query_first, rows_are_queries):
    row = lax.broadcasted_iota(jnp.int32, shape, 0) % BLK
    col = lax.broadcasted_iota(jnp.int32, shape, 1)
    if rows_are_queries:
        return key_first + col <= query_first + row
    return key_first + row <= query_first + col


def to_half(tile, source, target):
    values = tile.astype(F32)
    if source != target:
        values = pltpu.roll(values, HD, 1)
    lane = lax.broadcasted_iota(jnp.int32, values.shape, 1)
    return jnp.where(lane // HD == target, values, 0.0)


def turn(tile, cosine, sine):
    lane = lax.broadcasted_iota(jnp.int32, tile.shape, 1)
    ahead = pltpu.roll(tile, LANES - HD // 2, 1)
    behind = pltpu.roll(tile, HD // 2, 1)
    return tile * cosine + jnp.where(lane % HD < HD // 2, ahead, behind) * sine


def rows_by_head(source_ref, block_rows, target_ref):
    for h in range(4):
        m, g = h // 2, h % 2
        tile = source_ref[block_rows, m * LANES : (m + 1) * LANES]
        target_ref[h * BLK : (h + 1) * BLK, :] = to_half(tile, g, m).astype(BF16)


def rows_by_token(values):
    tiles = []
    for m in range(2):
        first = values[2 * m * BLK : (2 * m + 1) * BLK]
        second = values[(2 * m + 1) * BLK : (2 * m + 2) * BLK]
        tiles.append(to_half(first, m, 0) + to_half(second, m, 1))
    return tiles


def turn_kernel(pre_ref, scale_ref, gain_ref, cos_ref, sin_ref, q_ref, kv_ref):
    for col in range(3):
        lanes = slice(col * LANES, (col + 1) * LANES)
        which = 0 if col < 2 else 1
        hat = pre_ref[:, lanes] * scale_ref[:, which : which + 1]
        turned = turn(hat * gain_ref[:, lanes], cos_ref[...], sin_ref[...]).astype(BF16)
        if which == 0:
            q_ref[:, lanes] = (turned.astype(F32) * HD**-0.5).astype(BF16)
        else:
            kv_ref[:, :LANES] = turned
    kv_ref[:, LANES:] = pre_ref[:, 3 * LANES :].astype(BF16)


def attend_kernel(
    total, half, tile_blocks, table, own, q_in, kv, o_ref, lse_ref, kv_s, q_ref, acc, peak, s_buf, sem
):
    gather_blocks(
        table,
        total,
        [
            (
                rows_of(kv, 4 * BLK),
                lambda to: kv_s.at[pl.ds(to, BLK), pl.ds(0, 2 * LANES)],
                sem.at[0],
            )
        ],
    )
    kv_s[:, 2 * LANES :] = jnp.ones((total * BLK, LANES), BF16)
    wait_all(kv_s.at[:, pl.ds(0, 2 * LANES)], sem.at[0])
    width = tile_blocks * BLK

    def query_block(i, carry):
        block = own[i]
        n_a, base, n_b = key_ranges(block, half, tile_blocks)
        rows = pl.ds(pl.multiple_of(i * BLK, BLK), BLK)
        lanes = pl.ds(pl.multiple_of(i % 2 * BLK, BLK), BLK)
        rows_by_head(q_in, rows, q_ref)

        def first_key(j):
            return pl.multiple_of(jnp.where(j < n_a, j * width, base + (j - n_a) * width), BLK)

        def tile(start, masked):
            scores = dot(q_ref[...], kv_s[pl.ds(start, width), :LANES], NT)
            probs = jnp.exp(scores)
            if masked:
                probs = jnp.where(causal(probs.shape, start, block * BLK, True), probs, 0.0)
            acc[...] += dot(probs.astype(BF16), kv_s[pl.ds(start, width), LANES:], NN)

        def clear_tile(j, carry):
            tile(first_key(j), False)
            return carry

        def store(out, log_sum):
            first, second = rows_by_token(out)
            o_ref[rows, :LANES] = first
            o_ref[rows, LANES:] = second
            for h in range(4):
                lse_ref[i // 2, h : h + 1, lanes] = log_sum[h * BLK : (h + 1) * BLK].T[:1]

        def score(j):
            return dot(q_ref[...], kv_s[pl.ds(first_key(j), width), :LANES], NT)

        def weigh(scores, j, masked):
            start = first_key(j)
            probs = jnp.exp(scores)
            if masked:
                probs = jnp.where(causal(probs.shape, start, block * BLK, True), probs, 0.0)
            acc[...] += dot(probs.astype(BF16), kv_s[pl.ds(start, width), LANES:], NN)

        acc[...] = jnp.zeros_like(acc)
        count = n_a + n_b
        s_buf[0] = score(0)

        def two_tiles(i2, carry):
            j = 2 * i2
            s_buf[1] = score(j + 1)
            weigh(s_buf[0], j, False)
            s_buf[0] = score(j + 2)
            weigh(s_buf[1], j + 1, False)
            return carry

        lax.fori_loop(0, count // 2, two_tiles, 0)

        @pl.when(count % 2 == 1)
        def _():
            s_buf[1] = score(count)
            weigh(s_buf[0], count - 1, False)
            weigh(s_buf[1], count, True)

        @pl.when(count % 2 == 0)
        def _():
            weigh(s_buf[0], count, True)

        sums = acc[:, LANES:]
        in_range = (jnp.max(sums) < 2.0**100) & (jnp.min(sums) > 2.0**-40)

        @pl.when(in_range)
        def _():
            store(acc[:, :LANES] / sums, jnp.log(sums))

        @pl.when(jnp.logical_not(in_range))
        def _():
            acc[...] = jnp.zeros_like(acc)
            peak[...] = jnp.full_like(peak, MASK_FLOOR)

            def safe_tile(j, carry):
                start = first_key(j)
                scores = dot(q_ref[...], kv_s[pl.ds(start, width), :LANES], NT)
                seen = causal(scores.shape, start, block * BLK, True)
                scores = jnp.where(seen, scores, MASK_FLOOR)
                old = peak[...]
                new = jnp.maximum(old, jnp.max(scores, axis=1, keepdims=True))
                probs = jnp.where(seen, jnp.exp(scores - new[:, :1]), 0.0)
                keep = jnp.exp(old - new)
                acc[...] = acc[...] * keep[:, :1] + dot(
                    probs.astype(BF16), kv_s[pl.ds(start, width), LANES:], NN
                )
                peak[...] = new
                return carry

            lax.fori_loop(0, n_a + n_b + 1, safe_tile, 0)
            safe_sums = acc[:, LANES:]
            store(acc[:, :LANES] / safe_sums, peak[...] + jnp.log(safe_sums))

        return carry

    lax.fori_loop(0, 4, query_block, 0)


def query_grad_kernel(
    total,
    half,
    tile_blocks,
    table,
    own,
    q_in,
    do_in,
    o_in,
    lse_in,
    cos_ref,
    sin_ref,
    kv,
    dq_ref,
    kv_s,
    q_ref,
    do_ref,
    lse_ref,
    delta_ref,
    acc,
    sem,
):
    gather_blocks(
        table, total, [(rows_of(kv, 4 * BLK), lambda to: kv_s.at[pl.ds(to, BLK)], sem.at[0])]
    )
    wait_all(kv_s, sem.at[0])
    width = tile_blocks * BLK

    def query_block(i, carry):
        block = own[i]
        n_a, base, n_b = key_ranges(block, half, tile_blocks)
        rows = pl.ds(pl.multiple_of(i * BLK, BLK), BLK)
        lanes = pl.ds(pl.multiple_of(i % 2 * BLK, BLK), BLK)
        rows_by_head(q_in, rows, q_ref)
        rows_by_head(do_in, rows, do_ref)
        for h in range(4):
            part = slice(h * BLK, (h + 1) * BLK)
            pair = slice(h // 2 * LANES, (h // 2 + 1) * LANES)
            product = do_in[rows, pair].astype(F32) * o_in[rows, pair]
            own_half = to_half(product, h % 2, h % 2)
            delta = jnp.sum(own_half, axis=1, keepdims=True)
            delta_ref[part, :] = jnp.broadcast_to(delta, (BLK, LANES))
            row = lse_in[i // 2, h : h + 1, lanes]
            lse_ref[part, :] = jnp.broadcast_to(row, (LANES, BLK)).T

        def first_key(j):
            return pl.multiple_of(jnp.where(j < n_a, j * width, base + (j - n_a) * width), BLK)

        def tile(start, masked):
            keys = kv_s[pl.ds(start, width), :LANES]
            scores = dot(q_ref[...], keys, NT)
            prob_grad = dot(do_ref[...], kv_s[pl.ds(start, width), LANES:], NT)
            probs = jnp.exp(scores - lse_ref[:, :1])
            score_grad = probs * (prob_grad - delta_ref[:, :1])
            if masked:
                seen = causal(probs.shape, start, block * BLK, True)
                score_grad = jnp.where(seen, score_grad, 0.0)
            acc[...] += dot(score_grad.astype(BF16), keys, NN)

        def clear_tile(j, carry):
            tile(first_key(j), False)
            return carry

        acc[...] = jnp.zeros_like(acc)
        lax.fori_loop(0, n_a + n_b, clear_tile, 0)
        tile(first_key(n_a + n_b), True)
        for m, gradient in enumerate(rows_by_token(acc[...])):
            back = turn(gradient * HD**-0.5, cos_ref[rows, :], -sin_ref[rows, :])
            dq_ref[rows, m * LANES : (m + 1) * LANES] = back
        return carry

    lax.fori_loop(0, 4, query_block, 0)


def place(blk, h):
    return (h * 2 + blk) * BLK if blk < 2 else ((blk * 4) + h) * BLK


def spread_heads(source_ref, lanes, target_ref):
    target_ref[...] = jnp.zeros_like(target_ref)
    for blk in range(4):
        for h in range(4):
            m, g = h // 2, h % 2
            rows = slice(place(blk, h), place(blk, h) + BLK)
            tile = source_ref[blk * BLK : (blk + 1) * BLK, lanes]
            target_ref[rows, m * LANES : (m + 1) * LANES] = to_half(tile, m, g).astype(BF16)


def cont_tiles(own, which, half, tile_blocks):
    block = own[2 + which]
    base = half + (block - half) // CONT_BLKS * CONT_BLKS
    return block, block // tile_blocks, (base + CONT_BLKS) // tile_blocks, base // tile_blocks


def pair_probs_kernel(
    total, half, tile_blocks, q_rows, table, own, kv_in, q_all, lse_all, p_ref, pc_ref, q_s, lse_s, k_ref, sem
):
    step = pl.program_id(0)
    width = tile_blocks * BLK
    pair = 2 * tile_blocks

    @pl.when(step == 0)
    def _():
        gather_blocks(
            table,
            total,
            [
                (rows_of(q_all, q_rows), lambda to: q_s.at[pl.ds(to, BLK)], sem.at[0]),
                (stats_of(lse_all), lambda to: lse_s.at[:, pl.ds(to, BLK)], sem.at[1]),
            ],
        )
        spread_heads(kv_in, slice(0, LANES), k_ref)
        wait_all(q_s, sem.at[0])
        wait_all(lse_s, sem.at[1])

    def probs_of(first_row, per_head, j, keys_first, store):
        start = pl.multiple_of(j * width, width)
        keys = k_ref[first_row : first_row + 4 * per_head, :]
        scores = dot(keys, q_s[pl.ds(start, width), :], NT)
        for h in range(4):
            part = slice(h * per_head, (h + 1) * per_head)
            probs = jnp.exp(scores[part] - lse_s[h : h + 1, pl.ds(start, width)])
            if keys_first is not None:
                seen = [causal((BLK, width), first, start, False) for first in keys_first]
                probs = jnp.where(jnp.concatenate(seen, axis=0), probs, 0.0)
            store(part, probs.astype(BF16))

    low = jnp.minimum(own[0], own[1])
    high = jnp.maximum(own[0], own[1])

    def prompt(keys_first):
        for side in range(2):

            def store(part, probs, side=side):
                p_ref[0, part, side * width : (side + 1) * width] = probs

            probs_of(0, 2 * BLK, 2 * step + side, keys_first, store)

    @pl.when((step >= low // pair) & (step <= high // pair))
    def _():
        prompt([own[0] * BLK, own[1] * BLK])

    @pl.when(step > high // pair)
    def _():
        prompt(None)

    @pl.when(step == pl.num_programs(0) - 1)
    def _():
        for which in range(2):
            block, first, stop, base = cont_tiles(own, which, half, tile_blocks)

            def cont_tile(j, carry, which=which, block=block, base=base):
                def store(part, probs):
                    pc_ref[which, j - base, part, :] = probs

                probs_of((8 + 4 * which) * BLK, BLK, j, [block * BLK], store)
                return carry

            lax.fori_loop(first, stop, cont_tile, 0)


def pair_grad_kernel(
    total,
    half,
    tile_blocks,
    q_rows,
    do_rows,
    table,
    own,
    kv_in,
    cos_ref,
    sin_ref,
    q_all,
    do_all,
    delta_all,
    p_ref,
    pc_ref,
    out_ref,
    q_s,
    do_s,
    delta_s,
    v_ref,
    dk_ref,
    dv_ref,
    d_buf,
    sem,
):
    step = pl.program_id(0)
    width = tile_blocks * BLK
    pair = 2 * tile_blocks

    @pl.when(step == 0)
    def _():
        gather_blocks(
            table,
            total,
            [
                (rows_of(q_all, q_rows), lambda to: q_s.at[pl.ds(to, BLK)], sem.at[0]),
                (rows_of(do_all, do_rows), lambda to: do_s.at[pl.ds(to, BLK)], sem.at[1]),
                (stats_of(delta_all), lambda to: delta_s.at[:, pl.ds(to, BLK)], sem.at[2]),
            ],
        )
        dk_ref[...] = jnp.zeros_like(dk_ref)
        dv_ref[...] = jnp.zeros_like(dv_ref)
        spread_heads(kv_in, slice(LANES, 2 * LANES), v_ref)
        wait_all(q_s, sem.at[0])
        wait_all(do_s, sem.at[1])
        wait_all(delta_s, sem.at[2])

    def prob_grad(first_row, per_head, j):
        start = pl.multiple_of(j * width, width)
        values = v_ref[first_row : first_row + 4 * per_head, :]
        return dot(values, do_s[pl.ds(start, width), :], NT)

    def add(first_row, per_head, j, probs, grads_in):
        rows = pl.ds(first_row, 4 * per_head)
        start = pl.multiple_of(j * width, width)
        score_low = []
        for h in range(4):
            part = slice(h * per_head, (h + 1) * per_head)
            shifted_grad = grads_in[part] - delta_s[h : h + 1, pl.ds(start, width)]
            score_low.append((probs[part].astype(F32) * shifted_grad).astype(BF16))
        dv_ref[rows, :] += dot(probs, do_s[pl.ds(start, width), :], NN)
        queries = q_s[pl.ds(start, width), :]
        dk_ref[rows, :] += dot(jnp.concatenate(score_low, axis=0), queries, NN)

    low = jnp.minimum(own[0], own[1])
    last = total // tile_blocks - 1

    @pl.when(step == low // pair)
    def _():
        d_buf[0] = prob_grad(0, 2 * BLK, 2 * step)

    @pl.when(step >= low // pair)
    def _():
        d_buf[1] = prob_grad(0, 2 * BLK, 2 * step + 1)
        add(0, 2 * BLK, 2 * step, p_ref[0, :, :width], d_buf[0])
        d_buf[0] = prob_grad(0, 2 * BLK, jnp.minimum(2 * step + 2, last))
        add(0, 2 * BLK, 2 * step + 1, p_ref[0, :, width:], d_buf[1])

    def collect(ref, blk):
        tile_sum = None
        for h in range(4):
            m, g = h // 2, h % 2
            part = ref[place(blk, h) : place(blk, h) + BLK, m * LANES : (m + 1) * LANES]
            moved = to_half(part, g, m)
            tile_sum = moved if tile_sum is None else tile_sum + moved
        return tile_sum

    @pl.when(step == pl.num_programs(0) - 1)
    def _():
        for which in range(2):
            _, first, stop, base = cont_tiles(own, which, half, tile_blocks)

            def cont_tile(j, carry, which=which, base=base):
                first_row = (8 + 4 * which) * BLK
                grads_in = prob_grad(first_row, BLK, j)
                add(first_row, BLK, j, pc_ref[which, j - base], grads_in)
                return carry

            lax.fori_loop(first, stop, cont_tile, 0)
        for blk in range(4):
            rows = slice(blk * BLK, (blk + 1) * BLK)
            out_ref[rows, :LANES] = turn(collect(dk_ref, blk), cos_ref[rows, :], -sin_ref[rows, :])
            out_ref[rows, LANES:] = collect(dv_ref, blk)


def down_strips(w_ref, pair, width):
    strips = [w_ref[u, :, 2 * width : 3 * width] for u in (2 * pair, 2 * pair + 1)]
    return jnp.concatenate(strips, axis=1)


def expert_kernel(quarters, width, x_ref, w_ref, out_ref, gate_ref, up_ref):
    acts = []
    for u in range(quarters):
        cols = slice(u * width, (u + 1) * width)
        pre = dot(x_ref[...], w_ref[u, :, : 2 * width], NN)
        gate, up = pre[:, :width], pre[:, width:]
        gate_ref[:, cols] = gate
        up_ref[:, cols] = up
        acts.append((gate * jax.nn.sigmoid(gate) * up).astype(BF16))
    out = None
    for pair in range(quarters // 2):
        act = jnp.concatenate(acts[2 * pair : 2 * pair + 2], axis=1)
        part = dot(act, down_strips(w_ref, pair, width), NT)
        out = part if out is None else out + part
    out_ref[...] = out.astype(BF16)


def expert_grad_kernel(
    quarters, width, dy_ref, gate_ref, up_ref, w_ref, wt_ref, dx_ref, dgate_ref, dup_ref, act_ref
):
    total = None
    for pair in range(quarters // 2):
        both = dot(dy_ref[...], down_strips(w_ref, pair, width), NN)
        for side in range(2):
            u = 2 * pair + side
            cols = slice(u * width, (u + 1) * width)
            act_grad = both[:, side * width : (side + 1) * width]
            gate, up = gate_ref[:, cols], up_ref[:, cols]
            sig = jax.nn.sigmoid(gate)
            gate_act = gate * sig
            act_ref[:, cols] = (gate_act * up).astype(BF16)
            gate_grad = (act_grad * up * sig * (1.0 + gate * (1.0 - sig))).astype(BF16)
            up_grad = (act_grad * gate_act).astype(BF16)
            dgate_ref[:, cols] = gate_grad
            dup_ref[:, cols] = up_grad
            grads = jnp.concatenate([gate_grad, up_grad], axis=1)
            part = dot(grads, wt_ref[u], NN)
            total = part if total is None else total + part
    dx_ref[...] = total.astype(BF16)


def block_of_whole(shape):
    return pl.BlockSpec(shape, lambda i, *_: (0,) * len(shape))


def kernel_call(kernel, name, prefetch, ins, outs, scratch, flops):
    hbm = pl.BlockSpec(memory_space=pl.ANY)
    moved = sum(x.size * x.dtype.itemsize for x, _ in ins)
    return pl.pallas_call(
        kernel,
        out_shape=tuple(outs),
        grid_spec=pltpu.PrefetchScalarGridSpec(
            num_scalar_prefetch=len(prefetch),
            grid=(1,),
            in_specs=[hbm if far else block_of_whole(x.shape) for x, far in ins],
            out_specs=tuple(block_of_whole(out.shape) for out in outs),
            scratch_shapes=scratch,
        ),
        compiler_params=pltpu.CompilerParams(vmem_limit_bytes=48 << 20),
        cost_estimate=pl.CostEstimate(flops=flops, bytes_accessed=moved, transcendentals=0),
        name=name,
    )(*prefetch, *(x for x, _ in ins))


def by_rows(kernel, name, rows, ins, outs, flops):
    def spec(shape):
        if len(shape) == 3:
            return pl.BlockSpec(shape, lambda i: (0, 0, 0))
        return pl.BlockSpec((rows, shape[1]), lambda i: (i, 0))

    return pl.pallas_call(
        kernel,
        out_shape=tuple(pltpu.HBM(out.shape, out.dtype) for out in outs),
        grid=(outs[0].shape[0] // rows,),
        in_specs=[spec(x.shape) for x in ins],
        out_specs=tuple(spec(out.shape) for out in outs),
        compiler_params=pltpu.CompilerParams(vmem_limit_bytes=40 << 20),
        cost_estimate=pl.CostEstimate(flops=flops, bytes_accessed=10**7, transcendentals=0),
        name=name,
    )(*(pltpu.with_memory_space_constraint(x, pltpu.HBM) for x in ins))


def expert_forward(rows_in, weights):
    slots, model_width = rows_in.shape
    quarters, _, cols = weights.shape
    width = cols // 3
    hidden = jax.ShapeDtypeStruct((slots, quarters * width), F32)
    return by_rows(
        functools.partial(expert_kernel, quarters, width),
        "expert",
        slots // 5,
        [rows_in, weights],
        [jax.ShapeDtypeStruct((slots, model_width), BF16), hidden, hidden],
        6 * slots * model_width * quarters * width,
    )


def expert_backward(rows_grad, gate_pre, up_pre, weights, turned):
    slots, model_width = rows_grad.shape
    quarters, _, cols = weights.shape
    width = cols // 3
    hidden = jax.ShapeDtypeStruct((slots, quarters * width), BF16)
    return by_rows(
        functools.partial(expert_grad_kernel, quarters, width),
        "expert_grad",
        slots // 2,
        [rows_grad, gate_pre, up_pre, weights, turned],
        [jax.ShapeDtypeStruct((slots, model_width), BF16), hidden, hidden, hidden],
        6 * slots * model_width * quarters * width,
    )


def turn_heads(projected, scales, gain, cosine, sine):
    rows = projected.shape[0]
    out = jax.ShapeDtypeStruct((rows, 2 * LANES), BF16)
    ins = [(x, False) for x in (projected, scales, gain, cosine, sine)]
    return kernel_call(turn_kernel, "turn_heads", (), ins, [out, out], [], 10**6)


def attend(table, own, q, kv_all):
    total = table.shape[0]
    return kernel_call(
        functools.partial(attend_kernel, total, total // 2, 8),
        "attend",
        (table, own),
        [(q, False), (kv_all, True)],
        [
            jax.ShapeDtypeStruct((4 * BLK, 2 * LANES), F32),
            jax.ShapeDtypeStruct((2, 4, 2 * BLK), F32),
        ],
        [
            pltpu.VMEM((total * BLK, 3 * LANES), BF16),
            pltpu.VMEM((4 * BLK, LANES), BF16),
            pltpu.VMEM((4 * BLK, 2 * LANES), F32),
            pltpu.VMEM((4 * BLK, LANES), F32),
            pltpu.VMEM((2, 4 * BLK, 8 * BLK), F32),
            pltpu.SemaphoreType.DMA((1,)),
        ],
        20 * 10**9,
    )


def query_grad(table, own, q, out_grad, heads, lse, cosine, sine, kv_all):
    total = table.shape[0]
    ins = [(x, False) for x in (q, out_grad, heads, lse, cosine, sine)]
    return kernel_call(
        functools.partial(query_grad_kernel, total, total // 2, 4),
        "query_grad",
        (table, own),
        ins + [(kv_all, True)],
        [jax.ShapeDtypeStruct((4 * BLK, 2 * LANES), F32)],
        [
            pltpu.VMEM((total * BLK, 2 * LANES), BF16),
            pltpu.VMEM((4 * BLK, LANES), BF16),
            pltpu.VMEM((4 * BLK, LANES), BF16),
            pltpu.VMEM((4 * BLK, LANES), F32),
            pltpu.VMEM((4 * BLK, LANES), F32),
            pltpu.VMEM((4 * BLK, LANES), F32),
            pltpu.SemaphoreType.DMA((1,)),
        ],
        30 * 10**9,
    )[0]


def pair_call(kernel, name, table, own, ins, blocks, outs, out_blocks, scratch, flops):
    steps = table.shape[0] // 8

    def tile_place(step, table_ref, own_ref):
        return (jnp.maximum(step, jnp.minimum(own_ref[0], own_ref[1]) // 8), 0, 0)

    def spec(shape, block):
        if block is None:
            return pl.BlockSpec(memory_space=pl.ANY)
        if block == shape:
            return pl.BlockSpec(shape, lambda *_: (0,) * len(shape))
        return pl.BlockSpec(block, tile_place)

    return pl.pallas_call(
        kernel,
        out_shape=tuple(
            out if out.dtype == F32 else pltpu.HBM(out.shape, out.dtype) for out in outs
        ),
        grid_spec=pltpu.PrefetchScalarGridSpec(
            num_scalar_prefetch=2,
            grid=(steps,),
            in_specs=[spec(x.shape, block) for x, block in zip(ins, blocks)],
            out_specs=tuple(spec(x.shape, block) for x, block in zip(outs, out_blocks)),
            scratch_shapes=scratch,
        ),
        compiler_params=pltpu.CompilerParams(vmem_limit_bytes=48 << 20),
        cost_estimate=pl.CostEstimate(flops=flops, bytes_accessed=4 * 10**7, transcendentals=0),
        name=name,
    )(table, own, *ins)


PROB_BLOCK = (1, 8 * BLK, 8 * BLK)
CONT_SHAPE = (2, CONT_BLKS // 4, 4 * BLK, 4 * BLK)


def pair_probs(table, own, kv, q_all, q_rows, lse_all):
    total = table.shape[0]
    return pair_call(
        functools.partial(pair_probs_kernel, total, total // 2, 4, q_rows),
        "pair_probs",
        table,
        own,
        [kv, q_all, lse_all],
        [kv.shape, None, None],
        [
            jax.ShapeDtypeStruct((total // 8,) + PROB_BLOCK[1:], BF16),
            jax.ShapeDtypeStruct(CONT_SHAPE, BF16),
        ],
        [PROB_BLOCK, CONT_SHAPE],
        [
            pltpu.VMEM((total * BLK, 2 * LANES), BF16),
            pltpu.VMEM((8, total * BLK), F32),
            pltpu.VMEM((16 * BLK, 2 * LANES), BF16),
            pltpu.SemaphoreType.DMA((2,)),
        ],
        20 * 10**9,
    )


def pair_grad(table, own, kv, cosine, sine, q_all, q_rows, do_all, do_rows, delta_all, probs):
    total = table.shape[0]
    return pair_call(
        functools.partial(pair_grad_kernel, total, total // 2, 4, q_rows, do_rows),
        "pair_grad",
        table,
        own,
        [kv, cosine, sine, q_all, do_all, delta_all, *probs],
        [kv.shape, cosine.shape, sine.shape, None, None, None, PROB_BLOCK, CONT_SHAPE],
        [jax.ShapeDtypeStruct((4 * BLK, 2 * LANES), F32)],
        [(4 * BLK, 2 * LANES)],
        [
            pltpu.VMEM((total * BLK, 2 * LANES), BF16),
            pltpu.VMEM((total * BLK, 2 * LANES), BF16),
            pltpu.VMEM((8, total * BLK), F32),
            pltpu.VMEM((16 * BLK, 2 * LANES), BF16),
            pltpu.VMEM((16 * BLK, 2 * LANES), F32),
            pltpu.VMEM((16 * BLK, 2 * LANES), F32),
            pltpu.VMEM((2, 8 * BLK, 4 * BLK), F32),
            pltpu.SemaphoreType.DMA((3,)),
        ],
        30 * 10**9,
    )[0]


def turn_tables(position):
    half_dim = HD // 2
    frequency = ROPE_BASE ** (-(jnp.arange(half_dim, dtype=F32) * 2.0 / HD))
    angles = position[:, None] * frequency[None, :]
    cosine, sine = jnp.cos(angles), jnp.sin(angles)
    return jnp.concatenate([cosine] * 4, axis=1), jnp.concatenate([-sine, sine] * 2, axis=1)


def norm_back(grad_normed, hat_values, scale_values, gain_values):
    grad_hat = grad_normed * gain_values
    return scale_values * (
        grad_hat - hat_values * jnp.mean(grad_hat * hat_values, axis=-1, keepdims=True)
    )


def pieces(values, count):
    parts = []
    for _ in range(count):
        part = lax.reduce_precision(values, 8, 7)
        parts.append(part.astype(BF16))
        values = values - part
    return parts


def exchange(values, axis):
    return lax.all_to_all(values, axis, split_axis=0, concat_axis=0, tiled=True)


def spread(values, axis, count):
    return exchange(jnp.broadcast_to(values[None], (count,) + values.shape), axis)


def shifted(values, axis, count):
    parts = [values]
    for step in range(1, count):
        parts.append(lax.ppermute(values, axis, [(i, (i + step) % count) for i in range(count)]))
    return parts


def exchange_short(values, axis, index, count):
    rows = values.shape[0] // count
    come = []
    for step in range(count):
        to = (index + step) % count
        part = lax.dynamic_slice_in_dim(values, to * rows, rows, 0)
        if step > 0:
            part = lax.ppermute(part, axis, [(i, (i + step) % count) for i in range(count)])
        come.append(part)
    return jnp.concatenate(come, axis=1)


def in_order(parts, index, count):
    ordered = []
    for place in range(count):
        back = (index - place) % count
        part = parts[0]
        for step in range(1, count):
            part = jnp.where(back == step, parts[step], part)
        ordered.append(part)
    return jnp.stack(ordered, axis=0)


def with_stats(rows, stats):
    stats = jnp.pad(stats, ((0, 0), (0, 4), (0, 0)))
    parts = jnp.stack(pieces(stats, 3), axis=0).reshape(-1, rows.shape[1])
    return jnp.concatenate([rows, parts], axis=0)


def stats_in(gathered, first):
    parts = gathered[:, first:].reshape(-1, 3, 2, 8, gathered.shape[2])
    return jnp.sum(parts.astype(F32), axis=1)


def ride_along(values):
    parts = jnp.concatenate(pieces(values, 3), axis=-1)
    return jnp.pad(parts, ((0, 0), (0, 0), (0, LANES - parts.shape[-1])))


def parted(sums, count):
    return sum(sums[:, i * count : (i + 1) * count] for i in range(3))


def on_device(
    hidden_in,
    teacher,
    valid,
    block_of,
    routes,
    gates,
    w_query,
    w_key,
    w_value,
    w_out,
    gain_attn,
    gain_query,
    gain_key,
    gain_ffn,
    w_gate,
    w_up,
    w_down,
):
    ctx_count = lax.axis_size("ctx")
    exp_count = lax.axis_size("exp")
    ctx_index = lax.axis_index("ctx")
    exp_index = lax.axis_index("exp")
    ctx_rows, model_width = hidden_in.shape
    own_rows = ctx_rows // exp_count
    token_total = block_of.shape[0] * BLK
    head_cols = w_query.shape[1]
    kv_cols = w_key.shape[1]
    kv_total = kv_cols * exp_count
    qkv_cols = head_cols + 2 * kv_cols
    shard_rows = w_query.shape[0]

    own_weights = jnp.concatenate([w_query, w_key, w_value], axis=1)
    gain_row = jnp.concatenate([gain_attn, gain_query, gain_ffn, gain_key])
    gain_rows = jnp.pad(
        gain_row, (0, 8 * own_weights.shape[1] - gain_row.shape[0])
    ).reshape(8, -1)
    first_parts = spread(jnp.concatenate([own_weights, gain_rows], axis=0), "ctx", ctx_count)
    full_qkv = first_parts[:, :shard_rows].reshape(model_width, qkv_cols)
    gains = first_parts[:, shard_rows:].reshape(ctx_count, -1)[:, : gain_row.shape[0]].astype(F32)
    attn_gain = gains[:, :shard_rows].reshape(model_width)
    query_gain_all = gains[:, shard_rows : 2 * shard_rows].reshape(model_width)
    ffn_gain = gains[:, 2 * shard_rows : 3 * shard_rows].reshape(model_width)
    key_gain_all = gains[:, 3 * shard_rows :].reshape(kv_total)
    query_gain = lax.dynamic_slice_in_dim(query_gain_all, exp_index * head_cols, head_cols)
    key_gain = lax.dynamic_slice_in_dim(key_gain_all, exp_index * kv_cols, kv_cols)

    width = w_gate.shape[2]
    own_expert = jnp.concatenate([w_gate[0], w_up[0], w_down[0].T], axis=1)
    expert = lax.all_gather(own_expert, "exp", axis=0, tiled=False)

    hidden_f = hidden_in.astype(F32)
    attn_scale = lax.rsqrt(jnp.mean(hidden_f * hidden_f, axis=-1, keepdims=True) + NORM_EPSILON)
    attn_hat = hidden_f * attn_scale
    normed = (attn_hat * attn_gain).astype(BF16)
    projected = dot(normed, full_qkv, NN)
    query_pre = projected[:, :head_cols]
    key_pre = projected[:, head_cols : head_cols + kv_cols]
    query_square, key_square = lax.psum(
        jnp.stack([jnp.sum(query_pre * query_pre, axis=1), jnp.sum(key_pre * key_pre, axis=1)]),
        "exp",
    )
    query_scale = lax.rsqrt(query_square / model_width + NORM_EPSILON)[:, None]
    key_scale = lax.rsqrt(key_square / kv_total + NORM_EPSILON)[:, None]
    query_hat = query_pre * query_scale
    key_hat = key_pre * key_scale
    own_blocks = lax.dynamic_slice_in_dim(block_of, ctx_index * 4, 4)
    token_ids = (own_blocks[:, None] * BLK + jnp.arange(BLK, dtype=jnp.int32)[None]).reshape(-1)
    prompt_len = token_total // 2
    position = jnp.where(
        token_ids >= prompt_len, prompt_len + (token_ids - prompt_len) % CONT_LEN, token_ids
    ).astype(F32)
    cosine, sine = turn_tables(position)
    queries_rot, own_kv = turn_heads(
        projected,
        jnp.concatenate([query_scale, key_scale], axis=1),
        jnp.concatenate([query_gain, key_gain])[None],
        cosine,
        sine,
    )
    own_kv, expert = lax.optimization_barrier((own_kv, expert))
    kv_all = lax.all_gather(own_kv, "ctx", axis=0, tiled=True)
    own_out, _ = lax.optimization_barrier((w_out, own_kv))
    out_parts = shifted(
        spread(own_out, "ctx", ctx_count).reshape(model_width, head_cols), "exp", exp_count
    )
    wide_out = jnp.concatenate(out_parts, axis=1)
    full_out = in_order(out_parts, exp_index, exp_count)
    full_out, later_q = lax.optimization_barrier((full_out, queries_rot))
    q_all = lax.all_gather(later_q, "ctx", axis=0, tiled=True)
    expert_total = ctx_count
    capacity = max(2, own_rows * routes.shape[1] * 5 // (expert_total * 4))
    slots = expert_total * capacity
    names = routes[:, :, None] == jnp.arange(expert_total, dtype=jnp.int32)[None, None, :]
    named = jnp.any(names, axis=1)
    gate_of = jnp.sum(jnp.where(names, gates[:, :, None], 0.0), axis=1)
    before = jnp.tril(jnp.ones((own_rows, own_rows), BF16), -1)
    rank = dot(before, named.astype(BF16), NN).astype(jnp.int32)
    slot_rank = jnp.where(named, rank, -1).T[:, None, :]
    holds = slot_rank == jnp.arange(capacity, dtype=jnp.int32)[None, :, None]
    pick = holds.astype(BF16).reshape(slots, own_rows)
    weigh = jnp.where(holds, gate_of.T[:, None, :], 0.0).reshape(slots, own_rows)
    slot_gate = jnp.sum(weigh, axis=1, keepdims=True)

    kv_all, wide_out, full_out, pick, weigh, slot_gate = lax.optimization_barrier(
        (kv_all, wide_out, full_out, pick, weigh, slot_gate)
    )
    heads_f, lse = attend(block_of, own_blocks, queries_rot, kv_all)
    heads_low = heads_f.astype(BF16)

    own_heads = exchange_short(heads_low, "exp", exp_index, exp_count)
    stat_rows = jnp.pad(lse, ((0, 0), (0, 28), (0, 0)))
    lse_all = lax.all_gather(stat_rows, "ctx", axis=0, tiled=False)
    attn_rows = dot(own_heads, wide_out, NT)
    hidden_rows = lax.dynamic_slice_in_dim(hidden_in, exp_index * own_rows, own_rows, 0)
    hidden_rows = hidden_rows.astype(F32)
    resid = hidden_rows + attn_rows
    ffn_scale = lax.rsqrt(jnp.mean(resid * resid, axis=-1, keepdims=True) + NORM_EPSILON)
    ffn_hat = resid * ffn_scale
    normed_ffn = (ffn_hat * ffn_gain).astype(BF16)

    def send(rows):
        return exchange(rows.reshape(ctx_count, capacity, model_width), "ctx").reshape(
            slots, model_width
        )

    expert_in = send(dot(pick, normed_ffn, NN).astype(BF16))
    expert_in, q_all = lax.optimization_barrier((expert_in, q_all))
    expert_out, gate_pre, up_pre = expert_forward(expert_in, expert)
    returned = send(expert_out)
    turned = expert[:, :, : 2 * width].transpose(0, 2, 1)
    returned, q_all, lse_all, later_qkv, turned = lax.optimization_barrier(
        (returned, q_all, lse_all[:, :, :8], full_qkv, turned)
    )
    probs = pair_probs(
        block_of,
        own_blocks,
        own_kv,
        q_all,
        ctx_rows,
        lse_all,
    )
    wide_qkv = jnp.concatenate(shifted(later_qkv, "exp", exp_count), axis=1)
    moe_parts = dot(jnp.concatenate(pieces(weigh, 2), axis=1), returned, TN)
    moe_rows = moe_parts[:own_rows] + moe_parts[own_rows:]
    block_out = resid + moe_rows

    row_start = (ctx_index * exp_count + exp_index) * own_rows
    row_valid = lax.dynamic_slice_in_dim(valid, row_start, own_rows, 0).astype(F32)
    valid_count = jnp.sum(valid.astype(F32))
    misfit = block_out - teacher.astype(F32)
    local_loss = jnp.sum(row_valid[:, None] * misfit * misfit)
    out_grad_rows = misfit * row_valid[:, None] * (token_total / valid_count)
    copy_grad = dot(
        jnp.concatenate([pick, pick], axis=1),
        jnp.concatenate(pieces(out_grad_rows, 2), axis=0),
        NN,
    )
    grad_copies = send((slot_gate * copy_grad).astype(BF16))
    grad_copies, probs = lax.optimization_barrier((grad_copies, probs))
    input_grad, gate_grad, up_grad, hidden_act = expert_backward(
        grad_copies, gate_pre, up_pre, expert, turned
    )
    arrived_grad = send(input_grad)

    gate_part = dot(expert_in, gate_grad, TN)
    up_part = dot(expert_in, up_grad, TN)
    down_part = dot(hidden_act, grad_copies, TN)
    gate_part = gate_part.reshape(model_width, exp_count, width).transpose(1, 0, 2)
    up_part = up_part.reshape(model_width, exp_count, width).transpose(1, 0, 2)
    arrived_grad, wide_qkv, gate_part, up_part, down_part = lax.optimization_barrier(
        (arrived_grad, wide_qkv, gate_part, up_part, down_part)
    )
    ffn_normed_grad = dot(pick, arrived_grad, TN)

    ffn_gain_part = jnp.sum(ffn_normed_grad * ffn_hat, axis=0)
    resid_grad = out_grad_rows + norm_back(ffn_normed_grad, ffn_hat, ffn_scale, ffn_gain)
    branch_rows = resid_grad.astype(BF16)

    do_rows = jnp.einsum("ro,eok->erk", branch_rows, full_out, preferred_element_type=F32)
    out_grad = exchange(do_rows.astype(BF16), "exp").reshape(ctx_rows, head_cols)
    branch_parts = shifted(branch_rows, "exp", exp_count)
    head_of = jnp.arange(head_cols, dtype=jnp.int32)[None] // HD
    head_ones = (head_of == jnp.arange(4, dtype=jnp.int32)[:, None]).astype(F32)
    delta = lax.dot_general(
        head_ones,
        out_grad.astype(F32) * heads_f,
        NT,
        precision=lax.Precision.HIGHEST,
        preferred_element_type=F32,
    )
    delta = delta.reshape(4, 2, 2 * BLK).transpose(1, 0, 2)
    do_all = lax.all_gather(with_stats(out_grad, delta), "ctx", axis=0, tiled=False)
    query_n_grad = query_grad(
        block_of, own_blocks, queries_rot, out_grad, heads_f, lse, cosine, sine, kv_all
    )

    grad_out = None
    for step, part in enumerate(branch_parts):
        first = (exp_index - step) % exp_count * own_rows
        term = dot(part, lax.dynamic_slice_in_dim(heads_low, first, own_rows, 0), TN)
        grad_out = term if grad_out is None else grad_out + term

    do_all, query_n_grad, grad_out, gate_part, up_part, down_part = lax.optimization_barrier(
        (do_all, query_n_grad, grad_out, gate_part, up_part, down_part)
    )
    grad_w_gate = lax.psum_scatter(gate_part, "exp", scatter_dimension=0, tiled=True)
    grad_w_up = lax.psum_scatter(up_part, "exp", scatter_dimension=0, tiled=True)
    grad_w_down = lax.psum_scatter(down_part, "exp", scatter_dimension=0, tiled=True)[None]

    pair_grads = pair_grad(
        block_of,
        own_blocks,
        own_kv,
        cosine,
        sine,
        q_all,
        ctx_rows,
        do_all.reshape(-1, head_cols),
        do_all.shape[1],
        stats_in(do_all, ctx_rows),
        probs,
    )
    key_n_grad = pair_grads[:, :kv_cols]
    value_grad = pair_grads[:, kv_cols:].astype(BF16)
    query_gain_part = jnp.sum(query_n_grad * query_hat, axis=0)
    key_gain_part = jnp.sum(key_n_grad * key_hat, axis=0)
    query_hat_grad = query_n_grad * query_gain
    key_hat_grad = key_n_grad * key_gain
    stats = jnp.concatenate(
        [
            jnp.sum(query_hat_grad * query_hat, axis=1),
            jnp.sum(key_hat_grad * key_hat, axis=1),
            lax.dynamic_update_slice_in_dim(
                jnp.zeros((model_width,), F32), query_gain_part, exp_index * head_cols, 0
            ),
            ffn_gain_part,
            lax.dynamic_update_slice_in_dim(
                jnp.zeros((kv_total,), F32), key_gain_part, exp_index * kv_cols, 0
            ),
            jnp.full((kv_total,), local_loss),
        ]
    )
    stats = lax.psum(stats.reshape(-1, LANES), "exp").reshape(-1)
    query_stat = stats[:ctx_rows, None] / model_width
    key_stat = stats[ctx_rows : 2 * ctx_rows, None] / kv_total
    sums = stats[2 * ctx_rows :]
    query_low = (query_scale * (query_hat_grad - query_hat * query_stat)).astype(BF16)
    key_low = (key_scale * (key_hat_grad - key_hat * key_stat)).astype(BF16)
    grad_low = jnp.concatenate([query_low, key_low, value_grad], axis=1)

    wide_sums = jnp.stack(
        [
            sums[:model_width].reshape(ctx_count, shard_rows),
            sums[model_width : 2 * model_width].reshape(ctx_count, shard_rows),
            jnp.repeat(
                sums[2 * model_width : 2 * model_width + kv_total].reshape(ctx_count, -1), 2, axis=1
            ),
            jnp.broadcast_to(sums[-1], (ctx_count, shard_rows)),
        ],
        axis=-1,
    )
    grad_qkv = dot(normed, grad_low, TN)
    shards = exchange(
        jnp.concatenate(
            [
                grad_qkv.astype(BF16).reshape(ctx_count, shard_rows, qkv_cols),
                grad_out.astype(BF16).reshape(ctx_count, shard_rows, head_cols),
                ride_along(wide_sums),
            ],
            axis=2,
        ),
        "ctx",
    )
    back = exchange_short(grad_low, "exp", exp_index, exp_count)
    shards = jnp.sum(shards.astype(F32), axis=0)
    grad_w_query = shards[:, :head_cols]
    grad_w_key = shards[:, head_cols : head_cols + kv_cols]
    grad_w_value = shards[:, head_cols + kv_cols : qkv_cols]
    grad_w_out = shards[:, qkv_cols : qkv_cols + head_cols]
    tail = parted(shards[:, qkv_cols + head_cols :], 4)
    loss = tail[0, 3] / (valid_count * model_width)

    gain_part = jnp.sum(grad_w_query * w_query.astype(F32), axis=1)
    gain_part += jnp.sum(grad_w_key * w_key.astype(F32), axis=1)
    gain_part += jnp.sum(grad_w_value * w_value.astype(F32), axis=1)
    grad_gain_attn = lax.psum(gain_part, "exp") / gain_attn.astype(F32)
    normed_rows = dot(back, wide_qkv, NT)
    own_scale = lax.dynamic_slice_in_dim(attn_scale, exp_index * own_rows, own_rows, 0)
    own_hat = hidden_rows * own_scale
    grad_hidden = resid_grad + norm_back(normed_rows, own_hat, own_scale, attn_gain)
    return (
        block_out,
        loss,
        grad_hidden,
        grad_w_query,
        grad_w_key,
        grad_w_value,
        grad_w_out,
        grad_gain_attn,
        tail[:, 0],
        tail[::2, 2],
        tail[:, 1],
        grad_w_gate,
        grad_w_up,
        grad_w_down,
    )


def solution(mesh):
    return jax.shard_map(
        on_device,
        mesh=mesh,
        in_specs=(
            P("ctx", None),
            P(("ctx", "exp"), None),
            P(),
            P(),
            P(("ctx", "exp"), None),
            P(("ctx", "exp"), None),
            P("ctx", "exp"),
            P("ctx", "exp"),
            P("ctx", "exp"),
            P("ctx", "exp"),
            P("ctx"),
            P("ctx"),
            P("ctx"),
            P("ctx"),
            P("ctx", None, "exp"),
            P("ctx", None, "exp"),
            P("ctx", "exp", None),
        ),
        out_specs=(
            P(("ctx", "exp"), None),
            P(),
            P(("ctx", "exp"), None),
            P("ctx", "exp"),
            P("ctx", "exp"),
            P("ctx", "exp"),
            P("ctx", "exp"),
            P("ctx"),
            P("ctx"),
            P("ctx"),
            P("ctx"),
            P("ctx", None, "exp"),
            P("ctx", None, "exp"),
            P("ctx", "exp", None),
        ),
        check_vma=False,
    )
```

```python
import functools

import jax
import jax.numpy as jnp
from jax import lax
from jax.experimental import pallas as pl
from jax.experimental.pallas import tpu as pltpu
from jax.sharding import PartitionSpec as P

HD = 64
BLK = 128
CONT_LEN = 1024
CONT_BLKS = CONT_LEN // BLK
LANES = 128

NORM_EPSILON = 1e-05
ROPE_BASE = 10000.0
MASK_FLOOR = -1e30
F32 = jnp.float32
BF16 = jnp.bfloat16
NT = (((1,), (1,)), ((), ()))
NN = (((1,), (0,)), ((), ()))
TN = (((0,), (0,)), ((), ()))


def dot(left, right, dims):
    return lax.dot_general(left, right, dims, preferred_element_type=F32)


def key_ranges(block, half, tile_blocks):
    cont = block >= half
    inner = jnp.where(cont, (block - half) % CONT_BLKS, 0)
    n_a = jnp.where(cont, half // tile_blocks, block // tile_blocks)
    cont_base = half + (block - half) // CONT_BLKS * CONT_BLKS
    base = jnp.where(cont, cont_base, block // tile_blocks * tile_blocks) * BLK
    return n_a, base, inner // tile_blocks


def gather_blocks(table, total, moves):
    def start(i, carry):
        to = pl.multiple_of(table[i] * BLK, BLK)
        for source, target, sem in moves:
            pltpu.make_async_copy(source(i), target(to), sem).start()
        return carry

    lax.fori_loop(0, total, start, 0)


def wait_all(ref, sem):
    pltpu.make_async_copy(ref, ref, sem).wait()


def rows_of(ref, per_ctx):
    def place(i):
        first = i // 4 * per_ctx + i % 4 * BLK
        return ref.at[pl.ds(pl.multiple_of(first, 16), BLK)]

    return place


def stats_of(ref):
    return lambda i: ref.at[i // 4, i // 2 % 2, :, pl.ds(pl.multiple_of(i % 2 * BLK, BLK), BLK)]


def causal(shape, key_first, query_first, rows_are_queries):
    row = lax.broadcasted_iota(jnp.int32, shape, 0) % BLK
    col = lax.broadcasted_iota(jnp.int32, shape, 1)
    if rows_are_queries:
        return key_first + col <= query_first + row
    return key_first + row <= query_first + col


def to_half(tile, source, target):
    values = tile.astype(F32)
    if source != target:
        values = pltpu.roll(values, HD, 1)
    lane = lax.broadcasted_iota(jnp.int32, values.shape, 1)
    return jnp.where(lane // HD == target, values, 0.0)


def turn(tile, cosine, sine):
    lane = lax.broadcasted_iota(jnp.int32, tile.shape, 1)
    ahead = pltpu.roll(tile, LANES - HD // 2, 1)
    behind = pltpu.roll(tile, HD // 2, 1)
    return tile * cosine + jnp.where(lane % HD < HD // 2, ahead, behind) * sine


def rows_by_head(source_ref, block_rows, target_ref):
    for h in range(4):
        m, g = h // 2, h % 2
        tile = source_ref[block_rows, m * LANES : (m + 1) * LANES]
        target_ref[h * BLK : (h + 1) * BLK, :] = to_half(tile, g, m).astype(BF16)


def rows_by_token(values):
    tiles = []
    for m in range(2):
        first = values[2 * m * BLK : (2 * m + 1) * BLK]
        second = values[(2 * m + 1) * BLK : (2 * m + 2) * BLK]
        tiles.append(to_half(first, m, 0) + to_half(second, m, 1))
    return tiles


def turn_kernel(pre_ref, scale_ref, gain_ref, cos_ref, sin_ref, q_ref, kv_ref):
    for col in range(3):
        lanes = slice(col * LANES, (col + 1) * LANES)
        which = 0 if col < 2 else 1
        hat = pre_ref[:, lanes] * scale_ref[:, which : which + 1]
        turned = turn(hat * gain_ref[:, lanes], cos_ref[...], sin_ref[...]).astype(BF16)
        if which == 0:
            q_ref[:, lanes] = (turned.astype(F32) * HD**-0.5).astype(BF16)
        else:
            kv_ref[:, :LANES] = turned
    kv_ref[:, LANES:] = pre_ref[:, 3 * LANES :].astype(BF16)


def attend_kernel(
    total, half, tile_blocks, table, own, q_in, kv, o_ref, lse_ref, kv_s, q_ref, acc, peak, s_buf, sem
):
    gather_blocks(
        table,
        total,
        [
            (
                rows_of(kv, 4 * BLK),
                lambda to: kv_s.at[pl.ds(to, BLK)],
                sem.at[0],
            )
        ],
    )
    wait_all(kv_s, sem.at[0])
    width = tile_blocks * BLK
    ones = jnp.ones((width, LANES), BF16)

    def query_block(i, carry):
        block = own[i]
        n_a, base, n_b = key_ranges(block, half, tile_blocks)
        rows = pl.ds(pl.multiple_of(i * BLK, BLK), BLK)
        lanes = pl.ds(pl.multiple_of(i % 2 * BLK, BLK), BLK)
        rows_by_head(q_in, rows, q_ref)

        def first_key(j):
            return pl.multiple_of(jnp.where(j < n_a, j * width, base + (j - n_a) * width), BLK)

        def tile(start, masked):
            scores = dot(q_ref[...], kv_s[pl.ds(start, width), :LANES], NT)
            probs = jnp.exp(scores)
            if masked:
                probs = jnp.where(causal(probs.shape, start, block * BLK, True), probs, 0.0)
            acc[...] += dot(probs.astype(BF16), values_at(start), NN)

        def clear_tile(j, carry):
            tile(first_key(j), False)
            return carry

        def store(out, log_sum):
            first, second = rows_by_token(out)
            o_ref[rows, :LANES] = first
            o_ref[rows, LANES:] = second
            for h in range(4):
                lse_ref[i // 2, h : h + 1, lanes] = log_sum[h * BLK : (h + 1) * BLK].T[:1]

        def values_at(start):
            return jnp.concatenate([kv_s[pl.ds(start, width), LANES:], ones], axis=1)

        def score(j):
            return dot(q_ref[...], kv_s[pl.ds(first_key(j), width), :LANES], NT)

        def weigh(scores, j, masked):
            start = first_key(j)
            probs = jnp.exp(scores)
            if masked:
                probs = jnp.where(causal(probs.shape, start, block * BLK, True), probs, 0.0)
            acc[...] += dot(probs.astype(BF16), values_at(start), NN)

        acc[...] = jnp.zeros_like(acc)
        count = n_a + n_b
        s_buf[0] = score(0)

        def two_tiles(i2, carry):
            j = 2 * i2
            s_buf[1] = score(j + 1)
            weigh(s_buf[0], j, False)
            s_buf[0] = score(j + 2)
            weigh(s_buf[1], j + 1, False)
            return carry

        lax.fori_loop(0, count // 2, two_tiles, 0)

        @pl.when(count % 2 == 1)
        def _():
            s_buf[1] = score(count)
            weigh(s_buf[0], count - 1, False)
            weigh(s_buf[1], count, True)

        @pl.when(count % 2 == 0)
        def _():
            weigh(s_buf[0], count, True)

        sums = acc[:, LANES:]
        in_range = (jnp.max(sums) < 2.0**100) & (jnp.min(sums) > 2.0**-40)

        @pl.when(in_range)
        def _():
            store(acc[:, :LANES] / sums, jnp.log(sums))

        @pl.when(jnp.logical_not(in_range))
        def _():
            acc[...] = jnp.zeros_like(acc)
            peak[...] = jnp.full_like(peak, MASK_FLOOR)

            def safe_tile(j, carry):
                start = first_key(j)
                scores = dot(q_ref[...], kv_s[pl.ds(start, width), :LANES], NT)
                seen = causal(scores.shape, start, block * BLK, True)
                scores = jnp.where(seen, scores, MASK_FLOOR)
                old = peak[...]
                new = jnp.maximum(old, jnp.max(scores, axis=1, keepdims=True))
                probs = jnp.where(seen, jnp.exp(scores - new[:, :1]), 0.0)
                keep = jnp.exp(old - new)
                acc[...] = acc[...] * keep[:, :1] + dot(
                    probs.astype(BF16), values_at(start), NN
                )
                peak[...] = new
                return carry

            lax.fori_loop(0, n_a + n_b + 1, safe_tile, 0)
            safe_sums = acc[:, LANES:]
            store(acc[:, :LANES] / safe_sums, peak[...] + jnp.log(safe_sums))

        return carry

    lax.fori_loop(0, 4, query_block, 0)


def query_grad_kernel(
    total,
    half,
    tile_blocks,
    table,
    own,
    q_in,
    do_in,
    o_in,
    lse_in,
    cos_ref,
    sin_ref,
    kv,
    dq_ref,
    kv_s,
    q_ref,
    do_ref,
    lse_ref,
    delta_ref,
    acc,
    sem,
):
    gather_blocks(
        table, total, [(rows_of(kv, 4 * BLK), lambda to: kv_s.at[pl.ds(to, BLK)], sem.at[0])]
    )
    wait_all(kv_s, sem.at[0])
    width = tile_blocks * BLK

    def query_block(i, carry):
        block = own[i]
        n_a, base, n_b = key_ranges(block, half, tile_blocks)
        rows = pl.ds(pl.multiple_of(i * BLK, BLK), BLK)
        lanes = pl.ds(pl.multiple_of(i % 2 * BLK, BLK), BLK)
        rows_by_head(q_in, rows, q_ref)
        rows_by_head(do_in, rows, do_ref)
        for h in range(4):
            part = slice(h * BLK, (h + 1) * BLK)
            pair = slice(h // 2 * LANES, (h // 2 + 1) * LANES)
            product = do_in[rows, pair].astype(F32) * o_in[rows, pair]
            own_half = to_half(product, h % 2, h % 2)
            delta = jnp.sum(own_half, axis=1, keepdims=True)
            delta_ref[part, :] = jnp.broadcast_to(delta, (BLK, LANES))
            row = lse_in[i // 2, h : h + 1, lanes]
            lse_ref[part, :] = jnp.broadcast_to(row, (LANES, BLK)).T

        def first_key(j):
            return pl.multiple_of(jnp.where(j < n_a, j * width, base + (j - n_a) * width), BLK)

        def tile(start, masked):
            keys = kv_s[pl.ds(start, width), :LANES]
            scores = dot(q_ref[...], keys, NT)
            prob_grad = dot(do_ref[...], kv_s[pl.ds(start, width), LANES:], NT)
            probs = jnp.exp(scores - lse_ref[:, :1])
            score_grad = probs * (prob_grad - delta_ref[:, :1])
            if masked:
                seen = causal(probs.shape, start, block * BLK, True)
                score_grad = jnp.where(seen, score_grad, 0.0)
            acc[...] += dot(score_grad.astype(BF16), keys, NN)

        def clear_tile(j, carry):
            tile(first_key(j), False)
            return carry

        acc[...] = jnp.zeros_like(acc)
        lax.fori_loop(0, n_a + n_b, clear_tile, 0)
        tile(first_key(n_a + n_b), True)
        for m, gradient in enumerate(rows_by_token(acc[...])):
            back = turn(gradient * HD**-0.5, cos_ref[rows, :], -sin_ref[rows, :])
            dq_ref[rows, m * LANES : (m + 1) * LANES] = back
        return carry

    lax.fori_loop(0, 4, query_block, 0)


def place(blk, h):
    return (h * 2 + blk) * BLK if blk < 2 else ((blk * 4) + h) * BLK


def spread_heads(source_ref, lanes, target_ref):
    target_ref[...] = jnp.zeros_like(target_ref)
    for blk in range(4):
        for h in range(4):
            m, g = h // 2, h % 2
            rows = slice(place(blk, h), place(blk, h) + BLK)
            tile = source_ref[blk * BLK : (blk + 1) * BLK, lanes]
            target_ref[rows, m * LANES : (m + 1) * LANES] = to_half(tile, m, g).astype(BF16)


def cont_tiles(own, which, half, tile_blocks):
    block = own[2 + which]
    base = half + (block - half) // CONT_BLKS * CONT_BLKS
    return block, block // tile_blocks, (base + CONT_BLKS) // tile_blocks, base // tile_blocks


def pair_probs_kernel(
    total, half, tile_blocks, q_rows, table, own, kv_in, q_all, lse_all, p_ref, pc_ref, q_s, lse_s, k_ref, sem
):
    step = pl.program_id(0)
    width = tile_blocks * BLK
    pair = 2 * tile_blocks

    @pl.when(step == 0)
    def _():
        gather_blocks(
            table,
            total,
            [
                (rows_of(q_all, q_rows), lambda to: q_s.at[pl.ds(to, BLK)], sem.at[0]),
                (stats_of(lse_all), lambda to: lse_s.at[:, pl.ds(to, BLK)], sem.at[1]),
            ],
        )
        spread_heads(kv_in, slice(0, LANES), k_ref)
        wait_all(q_s, sem.at[0])
        wait_all(lse_s, sem.at[1])

    def probs_of(first_row, per_head, j, keys_first, store):
        start = pl.multiple_of(j * width, width)
        keys = k_ref[first_row : first_row + 4 * per_head, :]
        scores = dot(keys, q_s[pl.ds(start, width), :], NT)
        for h in range(4):
            part = slice(h * per_head, (h + 1) * per_head)
            probs = jnp.exp(scores[part] - lse_s[h : h + 1, pl.ds(start, width)])
            if keys_first is not None:
                seen = [causal((BLK, width), first, start, False) for first in keys_first]
                probs = jnp.where(jnp.concatenate(seen, axis=0), probs, 0.0)
            store(part, probs.astype(BF16))

    low = jnp.minimum(own[0], own[1])
    high = jnp.maximum(own[0], own[1])

    def prompt(keys_first):
        for side in range(2):

            def store(part, probs, side=side):
                p_ref[0, part, side * width : (side + 1) * width] = probs

            probs_of(0, 2 * BLK, 2 * step + side, keys_first, store)

    @pl.when((step >= low // pair) & (step <= high // pair))
    def _():
        prompt([own[0] * BLK, own[1] * BLK])

    @pl.when(step > high // pair)
    def _():
        prompt(None)

    @pl.when(step == pl.num_programs(0) - 1)
    def _():
        for which in range(2):
            block, first, stop, base = cont_tiles(own, which, half, tile_blocks)

            def cont_tile(j, carry, which=which, block=block, base=base):
                def store(part, probs):
                    pc_ref[which, j - base, part, :] = probs

                probs_of((8 + 4 * which) * BLK, BLK, j, [block * BLK], store)
                return carry

            lax.fori_loop(first, stop, cont_tile, 0)


def pair_grad_kernel(
    total,
    half,
    tile_blocks,
    q_rows,
    table,
    own,
    kv_in,
    cos_ref,
    sin_ref,
    q_all,
    do_all,
    p_ref,
    pc_ref,
    out_ref,
    q_s,
    do_s,
    parts_s,
    delta_s,
    v_ref,
    dk_ref,
    dv_ref,
    d_buf,
    sem,
):
    step = pl.program_id(0)
    width = tile_blocks * BLK
    pair = 2 * tile_blocks

    @pl.when(step == 0)
    def _():
        gather_blocks(
            table,
            total,
            [
                (rows_of(q_all, q_rows), lambda to: q_s.at[pl.ds(to, BLK)], sem.at[0]),
                (
                    lambda i: do_all.at[i // 4, pl.ds(pl.multiple_of(i % 4 * BLK, BLK), BLK)],
                    lambda to: do_s.at[pl.ds(to, BLK)],
                    sem.at[1],
                ),
            ],
        )
        stats = pltpu.make_async_copy(do_all.at[:, pl.ds(4 * BLK, 48)], parts_s, sem.at[2])
        stats.start()
        dk_ref[...] = jnp.zeros_like(dk_ref)
        dv_ref[...] = jnp.zeros_like(dv_ref)
        spread_heads(kv_in, slice(LANES, 2 * LANES), v_ref)
        wait_all(q_s, sem.at[0])
        wait_all(do_s, sem.at[1])
        stats.wait()

        def place_stats(c, carry):
            parts = parts_s[c].astype(F32)
            sums = parts[:16] + parts[16:32] + parts[32:]
            for blk in range(4):
                to = pl.multiple_of(table[4 * c + blk] * BLK, BLK)
                first, lane = blk // 2 * 8, blk % 2 * BLK
                delta_s[:, pl.ds(to, BLK)] = sums[first : first + 8, lane : lane + BLK]
            return carry

        lax.fori_loop(0, total // 4, place_stats, 0)

    def prob_grad(first_row, per_head, j):
        start = pl.multiple_of(j * width, width)
        values = v_ref[first_row : first_row + 4 * per_head, :]
        return dot(values, do_s[pl.ds(start, width), :], NT)

    def add(first_row, per_head, j, probs, grads_in):
        rows = pl.ds(first_row, 4 * per_head)
        start = pl.multiple_of(j * width, width)
        score_low = []
        for h in range(4):
            part = slice(h * per_head, (h + 1) * per_head)
            shifted_grad = grads_in[part] - delta_s[h : h + 1, pl.ds(start, width)]
            score_low.append((probs[part].astype(F32) * shifted_grad).astype(BF16))
        dv_ref[rows, :] += dot(probs, do_s[pl.ds(start, width), :], NN)
        queries = q_s[pl.ds(start, width), :]
        dk_ref[rows, :] += dot(jnp.concatenate(score_low, axis=0), queries, NN)

    low = jnp.minimum(own[0], own[1])
    last = total // tile_blocks - 1

    @pl.when(step == low // pair)
    def _():
        d_buf[0] = prob_grad(0, 2 * BLK, 2 * step)

    @pl.when(step >= low // pair)
    def _():
        d_buf[1] = prob_grad(0, 2 * BLK, 2 * step + 1)
        add(0, 2 * BLK, 2 * step, p_ref[0, :, :width], d_buf[0])
        d_buf[0] = prob_grad(0, 2 * BLK, jnp.minimum(2 * step + 2, last))
        add(0, 2 * BLK, 2 * step + 1, p_ref[0, :, width:], d_buf[1])

    def collect(ref, blk):
        tile_sum = None
        for h in range(4):
            m, g = h // 2, h % 2
            part = ref[place(blk, h) : place(blk, h) + BLK, m * LANES : (m + 1) * LANES]
            moved = to_half(part, g, m)
            tile_sum = moved if tile_sum is None else tile_sum + moved
        return tile_sum

    @pl.when(step == pl.num_programs(0) - 1)
    def _():
        for which in range(2):
            _, first, stop, base = cont_tiles(own, which, half, tile_blocks)

            def cont_tile(j, carry, which=which, base=base):
                first_row = (8 + 4 * which) * BLK
                grads_in = prob_grad(first_row, BLK, j)
                add(first_row, BLK, j, pc_ref[which, j - base], grads_in)
                return carry

            lax.fori_loop(first, stop, cont_tile, 0)
        for blk in range(4):
            rows = slice(blk * BLK, (blk + 1) * BLK)
            out_ref[rows, :LANES] = turn(collect(dk_ref, blk), cos_ref[rows, :], -sin_ref[rows, :])
            out_ref[rows, LANES:] = collect(dv_ref, blk)


def down_strips(w_ref, pair, width):
    strips = [w_ref[u, :, 2 * width : 3 * width] for u in (2 * pair, 2 * pair + 1)]
    return jnp.concatenate(strips, axis=1)


def expert_kernel(quarters, width, x_ref, w_ref, out_ref, gate_ref, up_ref):
    acts = []
    for u in range(quarters):
        cols = slice(u * width, (u + 1) * width)
        pre = dot(x_ref[...], w_ref[u, :, : 2 * width], NN)
        gate, up = pre[:, :width], pre[:, width:]
        gate_ref[:, cols] = gate
        up_ref[:, cols] = up
        acts.append((gate * jax.nn.sigmoid(gate) * up).astype(BF16))
    out = None
    for pair in range(quarters // 2):
        act = jnp.concatenate(acts[2 * pair : 2 * pair + 2], axis=1)
        part = dot(act, down_strips(w_ref, pair, width), NT)
        out = part if out is None else out + part
    out_ref[...] = out.astype(BF16)


def expert_grad_kernel(
    quarters, width, dy_ref, gate_ref, up_ref, w_ref, wt_ref, dx_ref, dgate_ref, dup_ref, act_ref
):
    total = None
    for pair in range(quarters // 2):
        both = dot(dy_ref[...], down_strips(w_ref, pair, width), NN)
        for side in range(2):
            u = 2 * pair + side
            cols = slice(u * width, (u + 1) * width)
            act_grad = both[:, side * width : (side + 1) * width]
            gate, up = gate_ref[:, cols], up_ref[:, cols]
            sig = jax.nn.sigmoid(gate)
            gate_act = gate * sig
            act_ref[:, cols] = (gate_act * up).astype(BF16)
            gate_grad = (act_grad * up * sig * (1.0 + gate * (1.0 - sig))).astype(BF16)
            up_grad = (act_grad * gate_act).astype(BF16)
            dgate_ref[:, cols] = gate_grad
            dup_ref[:, cols] = up_grad
            grads = jnp.concatenate([gate_grad, up_grad], axis=1)
            part = dot(grads, wt_ref[u], NN)
            total = part if total is None else total + part
    dx_ref[...] = total.astype(BF16)


def in_hbm(values):
    return pltpu.with_memory_space_constraint(values, pltpu.HBM)


def block_of_whole(shape):
    return pl.BlockSpec(shape, lambda i, *_: (0,) * len(shape))


def kernel_call(kernel, name, prefetch, ins, outs, scratch, flops):
    hbm = pl.BlockSpec(memory_space=pl.ANY)
    moved = sum(x.size * x.dtype.itemsize for x, _ in ins)
    return pl.pallas_call(
        kernel,
        out_shape=tuple(outs),
        grid_spec=pltpu.PrefetchScalarGridSpec(
            num_scalar_prefetch=len(prefetch),
            grid=(1,),
            in_specs=[hbm if far else block_of_whole(x.shape) for x, far in ins],
            out_specs=tuple(block_of_whole(out.shape) for out in outs),
            scratch_shapes=scratch,
        ),
        compiler_params=pltpu.CompilerParams(vmem_limit_bytes=48 << 20),
        cost_estimate=pl.CostEstimate(flops=flops, bytes_accessed=moved, transcendentals=0),
        name=name,
    )(*prefetch, *(x for x, _ in ins))


def by_rows(kernel, name, rows, ins, outs, flops):
    def spec(shape):
        if len(shape) == 3:
            return pl.BlockSpec(shape, lambda i: (0, 0, 0))
        return pl.BlockSpec((rows, shape[1]), lambda i: (i, 0))

    return pl.pallas_call(
        kernel,
        out_shape=tuple(pltpu.HBM(out.shape, out.dtype) for out in outs),
        grid=(outs[0].shape[0] // rows,),
        in_specs=[spec(x.shape) for x in ins],
        out_specs=tuple(spec(out.shape) for out in outs),
        compiler_params=pltpu.CompilerParams(vmem_limit_bytes=40 << 20),
        cost_estimate=pl.CostEstimate(flops=flops, bytes_accessed=10**7, transcendentals=0),
        name=name,
    )(*(in_hbm(x) for x in ins))


def expert_forward(rows_in, weights):
    slots, model_width = rows_in.shape
    quarters, _, cols = weights.shape
    width = cols // 3
    hidden = jax.ShapeDtypeStruct((slots, quarters * width), F32)
    return by_rows(
        functools.partial(expert_kernel, quarters, width),
        "expert",
        slots // 5,
        [rows_in, weights],
        [jax.ShapeDtypeStruct((slots, model_width), BF16), hidden, hidden],
        6 * slots * model_width * quarters * width,
    )


def expert_backward(rows_grad, gate_pre, up_pre, weights, turned):
    slots, model_width = rows_grad.shape
    quarters, _, cols = weights.shape
    width = cols // 3
    hidden = jax.ShapeDtypeStruct((slots, quarters * width), BF16)
    return by_rows(
        functools.partial(expert_grad_kernel, quarters, width),
        "expert_grad",
        slots // 2,
        [rows_grad, gate_pre, up_pre, weights, turned],
        [jax.ShapeDtypeStruct((slots, model_width), BF16), hidden, hidden, hidden],
        6 * slots * model_width * quarters * width,
    )


def turn_heads(projected, scales, gain, cosine, sine):
    rows = projected.shape[0]
    out = jax.ShapeDtypeStruct((rows, 2 * LANES), BF16)
    ins = [(x, False) for x in (projected, scales, gain, cosine, sine)]
    return kernel_call(turn_kernel, "turn_heads", (), ins, [out, out], [], 10**6)


def attend(table, own, q, kv_all):
    total = table.shape[0]
    return kernel_call(
        functools.partial(attend_kernel, total, total // 2, 8),
        "attend",
        (table, own),
        [(q, False), (kv_all, True)],
        [
            jax.ShapeDtypeStruct((4 * BLK, 2 * LANES), F32),
            jax.ShapeDtypeStruct((2, 4, 2 * BLK), F32),
        ],
        [
            pltpu.VMEM((total * BLK, 2 * LANES), BF16),
            pltpu.VMEM((4 * BLK, LANES), BF16),
            pltpu.VMEM((4 * BLK, 2 * LANES), F32),
            pltpu.VMEM((4 * BLK, LANES), F32),
            pltpu.VMEM((2, 4 * BLK, 8 * BLK), F32),
            pltpu.SemaphoreType.DMA((1,)),
        ],
        20 * 10**9,
    )


def query_grad(table, own, q, out_grad, heads, lse, cosine, sine, kv_all):
    total = table.shape[0]
    ins = [(x, False) for x in (q, out_grad, heads, lse, cosine, sine)]
    return kernel_call(
        functools.partial(query_grad_kernel, total, total // 2, 4),
        "query_grad",
        (table, own),
        ins + [(kv_all, True)],
        [jax.ShapeDtypeStruct((4 * BLK, 2 * LANES), F32)],
        [
            pltpu.VMEM((total * BLK, 2 * LANES), BF16),
            pltpu.VMEM((4 * BLK, LANES), BF16),
            pltpu.VMEM((4 * BLK, LANES), BF16),
            pltpu.VMEM((4 * BLK, LANES), F32),
            pltpu.VMEM((4 * BLK, LANES), F32),
            pltpu.VMEM((4 * BLK, LANES), F32),
            pltpu.SemaphoreType.DMA((1,)),
        ],
        30 * 10**9,
    )[0]


def pair_call(kernel, name, table, own, ins, blocks, outs, out_blocks, scratch, flops):
    steps = table.shape[0] // 8

    def tile_place(step, table_ref, own_ref):
        return (jnp.maximum(step, jnp.minimum(own_ref[0], own_ref[1]) // 8), 0, 0)

    def spec(shape, block):
        if block is None:
            return pl.BlockSpec(memory_space=pl.ANY)
        if block == shape:
            return pl.BlockSpec(shape, lambda *_: (0,) * len(shape))
        return pl.BlockSpec(block, tile_place)

    return pl.pallas_call(
        kernel,
        out_shape=tuple(
            out if out.dtype == F32 else pltpu.HBM(out.shape, out.dtype) for out in outs
        ),
        grid_spec=pltpu.PrefetchScalarGridSpec(
            num_scalar_prefetch=2,
            grid=(steps,),
            in_specs=[spec(x.shape, block) for x, block in zip(ins, blocks)],
            out_specs=tuple(spec(x.shape, block) for x, block in zip(outs, out_blocks)),
            scratch_shapes=scratch,
        ),
        compiler_params=pltpu.CompilerParams(vmem_limit_bytes=48 << 20),
        cost_estimate=pl.CostEstimate(flops=flops, bytes_accessed=4 * 10**7, transcendentals=0),
        name=name,
    )(table, own, *ins)


PROB_BLOCK = (1, 8 * BLK, 8 * BLK)
CONT_SHAPE = (2, CONT_BLKS // 4, 4 * BLK, 4 * BLK)


def pair_probs(table, own, kv, q_all, q_rows, lse_all):
    total = table.shape[0]
    return pair_call(
        functools.partial(pair_probs_kernel, total, total // 2, 4, q_rows),
        "pair_probs",
        table,
        own,
        [kv, q_all, lse_all],
        [kv.shape, None, None],
        [
            jax.ShapeDtypeStruct((total // 8,) + PROB_BLOCK[1:], BF16),
            jax.ShapeDtypeStruct(CONT_SHAPE, BF16),
        ],
        [PROB_BLOCK, CONT_SHAPE],
        [
            pltpu.VMEM((total * BLK, 2 * LANES), BF16),
            pltpu.VMEM((8, total * BLK), F32),
            pltpu.VMEM((16 * BLK, 2 * LANES), BF16),
            pltpu.SemaphoreType.DMA((2,)),
        ],
        20 * 10**9,
    )


def pair_grad(table, own, kv, cosine, sine, q_all, q_rows, do_all, probs):
    total = table.shape[0]
    return pair_call(
        functools.partial(pair_grad_kernel, total, total // 2, 4, q_rows),
        "pair_grad",
        table,
        own,
        [kv, cosine, sine, q_all, do_all, *(in_hbm(x) for x in probs)],
        [kv.shape, cosine.shape, sine.shape, None, None, PROB_BLOCK, CONT_SHAPE],
        [jax.ShapeDtypeStruct((4 * BLK, 2 * LANES), F32)],
        [(4 * BLK, 2 * LANES)],
        [
            pltpu.VMEM((total * BLK, 2 * LANES), BF16),
            pltpu.VMEM((total * BLK, 2 * LANES), BF16),
            pltpu.VMEM((total // 4, 48, 2 * LANES), BF16),
            pltpu.VMEM((8, total * BLK), F32),
            pltpu.VMEM((16 * BLK, 2 * LANES), BF16),
            pltpu.VMEM((16 * BLK, 2 * LANES), F32),
            pltpu.VMEM((16 * BLK, 2 * LANES), F32),
            pltpu.VMEM((2, 8 * BLK, 4 * BLK), F32),
            pltpu.SemaphoreType.DMA((3,)),
        ],
        30 * 10**9,
    )[0]


def turn_tables(position):
    half_dim = HD // 2
    frequency = ROPE_BASE ** (-(jnp.arange(half_dim, dtype=F32) * 2.0 / HD))
    angles = position[:, None] * frequency[None, :]
    cosine, sine = jnp.cos(angles), jnp.sin(angles)
    return jnp.concatenate([cosine] * 4, axis=1), jnp.concatenate([-sine, sine] * 2, axis=1)


def norm_back(grad_normed, hat_values, scale_values, gain_values):
    grad_hat = grad_normed * gain_values
    return scale_values * (
        grad_hat - hat_values * jnp.mean(grad_hat * hat_values, axis=-1, keepdims=True)
    )


def pieces(values, count):
    parts = []
    for _ in range(count):
        part = lax.reduce_precision(values, 8, 7)
        parts.append(part.astype(BF16))
        values = values - part
    return parts


def exchange(values, axis):
    return lax.all_to_all(values, axis, split_axis=0, concat_axis=0, tiled=True)


def spread(values, axis, count):
    return exchange(jnp.broadcast_to(values[None], (count,) + values.shape), axis)


def shifted(values, axis, count):
    parts = [values]
    for step in range(1, count):
        parts.append(lax.ppermute(values, axis, [(i, (i + step) % count) for i in range(count)]))
    return parts


def sum_short(values, axis, count):
    parts = shifted(values, axis, count)
    while len(parts) > 1:
        half = len(parts) // 2
        parts = [parts[i] + parts[i + half] for i in range(half)]
    return parts[0]


def exchange_short(values, axis, index, count):
    rows = values.shape[0] // count
    come = []
    for step in range(count):
        to = (index + step) % count
        part = lax.dynamic_slice_in_dim(values, to * rows, rows, 0)
        if step > 0:
            part = lax.ppermute(part, axis, [(i, (i + step) % count) for i in range(count)])
        come.append(part)
    return jnp.concatenate(come, axis=1)


def in_order(parts, index, count):
    ordered = []
    for place in range(count):
        back = (index - place) % count
        part = parts[0]
        for step in range(1, count):
            part = jnp.where(back == step, parts[step], part)
        ordered.append(part)
    return jnp.stack(ordered, axis=0)


def with_stats(rows, stats):
    stats = jnp.pad(stats, ((0, 0), (0, 4), (0, 0)))
    parts = jnp.stack(pieces(stats, 3), axis=0).reshape(-1, rows.shape[1])
    return jnp.concatenate([rows, parts], axis=0)


def ride_along(values):
    parts = jnp.concatenate(pieces(values, 3), axis=-1)
    return jnp.pad(parts, ((0, 0), (0, 0), (0, LANES - parts.shape[-1])))


def parted(sums, count):
    return sum(sums[:, i * count : (i + 1) * count] for i in range(3))


def on_device(
    hidden_in,
    teacher,
    valid,
    block_of,
    routes,
    gates,
    w_query,
    w_key,
    w_value,
    w_out,
    gain_attn,
    gain_query,
    gain_key,
    gain_ffn,
    w_gate,
    w_up,
    w_down,
):
    ctx_count = lax.axis_size("ctx")
    exp_count = lax.axis_size("exp")
    ctx_index = lax.axis_index("ctx")
    exp_index = lax.axis_index("exp")
    ctx_rows, model_width = hidden_in.shape
    own_rows = ctx_rows // exp_count
    token_total = block_of.shape[0] * BLK
    head_cols = w_query.shape[1]
    kv_cols = w_key.shape[1]
    kv_total = kv_cols * exp_count
    qkv_cols = head_cols + 2 * kv_cols
    shard_rows = w_query.shape[0]

    own_weights = jnp.concatenate([w_query, w_key, w_value], axis=1)
    gain_row = jnp.concatenate([gain_attn, gain_query, gain_ffn, gain_key])
    gain_rows = jnp.pad(
        gain_row, (0, 8 * own_weights.shape[1] - gain_row.shape[0])
    ).reshape(8, -1)
    first_parts = spread(jnp.concatenate([own_weights, gain_rows], axis=0), "ctx", ctx_count)
    full_qkv = first_parts[:, :shard_rows].reshape(model_width, qkv_cols)
    gains = first_parts[:, shard_rows:].reshape(ctx_count, -1)[:, : gain_row.shape[0]].astype(F32)
    attn_gain = gains[:, :shard_rows].reshape(model_width)
    query_gain_all = gains[:, shard_rows : 2 * shard_rows].reshape(model_width)
    ffn_gain = gains[:, 2 * shard_rows : 3 * shard_rows].reshape(model_width)
    key_gain_all = gains[:, 3 * shard_rows :].reshape(kv_total)
    query_gain = lax.dynamic_slice_in_dim(query_gain_all, exp_index * head_cols, head_cols)
    key_gain = lax.dynamic_slice_in_dim(key_gain_all, exp_index * kv_cols, kv_cols)

    width = w_gate.shape[2]
    own_expert = jnp.concatenate([w_gate[0], w_up[0], w_down[0].T], axis=1)
    expert = lax.all_gather(own_expert, "exp", axis=0, tiled=False)

    hidden_f = hidden_in.astype(F32)
    attn_scale = lax.rsqrt(jnp.mean(hidden_f * hidden_f, axis=-1, keepdims=True) + NORM_EPSILON)
    attn_hat = hidden_f * attn_scale
    normed = (attn_hat * attn_gain).astype(BF16)
    projected = dot(normed, full_qkv, NN)
    query_pre = projected[:, :head_cols]
    key_pre = projected[:, head_cols : head_cols + kv_cols]
    squares = jnp.stack(
        [jnp.sum(query_pre * query_pre, axis=1), jnp.sum(key_pre * key_pre, axis=1)]
    )
    query_square, key_square = sum_short(squares, "exp", exp_count)
    query_scale = lax.rsqrt(query_square / model_width + NORM_EPSILON)[:, None]
    key_scale = lax.rsqrt(key_square / kv_total + NORM_EPSILON)[:, None]
    query_hat = query_pre * query_scale
    key_hat = key_pre * key_scale
    own_blocks = lax.dynamic_slice_in_dim(block_of, ctx_index * 4, 4)
    token_ids = (own_blocks[:, None] * BLK + jnp.arange(BLK, dtype=jnp.int32)[None]).reshape(-1)
    prompt_len = token_total // 2
    position = jnp.where(
        token_ids >= prompt_len, prompt_len + (token_ids - prompt_len) % CONT_LEN, token_ids
    ).astype(F32)
    cosine, sine = turn_tables(position)
    queries_rot, own_kv = turn_heads(
        projected,
        jnp.concatenate([query_scale, key_scale], axis=1),
        jnp.concatenate([query_gain, key_gain])[None],
        cosine,
        sine,
    )
    own_kv, expert = lax.optimization_barrier((own_kv, expert))
    kv_all = lax.all_gather(own_kv, "ctx", axis=0, tiled=True)
    own_out, _ = lax.optimization_barrier((w_out, own_kv))
    out_parts = shifted(
        spread(own_out, "ctx", ctx_count).reshape(model_width, head_cols), "exp", exp_count
    )
    wide_out = jnp.concatenate(out_parts, axis=1)
    full_out = in_order(out_parts, exp_index, exp_count)
    full_out, later_q = lax.optimization_barrier((full_out, queries_rot))
    q_all = lax.all_gather(later_q, "ctx", axis=0, tiled=True)
    expert_total = ctx_count
    capacity = max(2, own_rows * routes.shape[1] * 5 // (expert_total * 4))
    slots = expert_total * capacity
    names = routes[:, :, None] == jnp.arange(expert_total, dtype=jnp.int32)[None, None, :]
    named = jnp.any(names, axis=1)
    gate_of = jnp.sum(jnp.where(names, gates[:, :, None], 0.0), axis=1)
    before = jnp.tril(jnp.ones((own_rows, own_rows), BF16), -1)
    rank = dot(before, named.astype(BF16), NN).astype(jnp.int32)
    slot_rank = jnp.where(named, rank, -1).T[:, None, :]
    holds = slot_rank == jnp.arange(capacity, dtype=jnp.int32)[None, :, None]
    pick = holds.astype(BF16).reshape(slots, own_rows)
    weigh = jnp.where(holds, gate_of.T[:, None, :], 0.0).reshape(slots, own_rows)
    slot_gate = jnp.sum(weigh, axis=1, keepdims=True)

    kv_all, wide_out, full_out, pick, weigh, slot_gate = lax.optimization_barrier(
        (kv_all, wide_out, full_out, pick, weigh, slot_gate)
    )
    heads_f, lse = attend(block_of, own_blocks, queries_rot, kv_all)
    heads_low = heads_f.astype(BF16)

    own_heads = exchange_short(heads_low, "exp", exp_index, exp_count)
    stat_rows = jnp.pad(lse, ((0, 0), (0, 28), (0, 0)))
    lse_all = lax.all_gather(stat_rows, "ctx", axis=0, tiled=False)
    attn_rows = dot(own_heads, wide_out, NT)
    hidden_rows = lax.dynamic_slice_in_dim(hidden_in, exp_index * own_rows, own_rows, 0)
    hidden_rows = hidden_rows.astype(F32)
    resid = hidden_rows + attn_rows
    ffn_scale = lax.rsqrt(jnp.mean(resid * resid, axis=-1, keepdims=True) + NORM_EPSILON)
    ffn_hat = resid * ffn_scale
    normed_ffn = (ffn_hat * ffn_gain).astype(BF16)

    def send(rows):
        return exchange(rows.reshape(ctx_count, capacity, model_width), "ctx").reshape(
            slots, model_width
        )

    expert_in = send(dot(pick, normed_ffn, NN).astype(BF16))
    expert_in, q_all = lax.optimization_barrier((expert_in, q_all))
    expert_out, gate_pre, up_pre = expert_forward(expert_in, expert)
    returned = send(expert_out)
    turned = expert[:, :, : 2 * width].transpose(0, 2, 1)
    returned, q_all, later_qkv, turned = lax.optimization_barrier(
        (returned, q_all, full_qkv, turned)
    )
    probs = pair_probs(
        block_of,
        own_blocks,
        own_kv,
        q_all,
        ctx_rows,
        lse_all[:, :, :8],
    )
    wide_qkv = jnp.concatenate(shifted(later_qkv, "exp", exp_count), axis=1)
    moe_parts = dot(jnp.concatenate(pieces(weigh, 2), axis=1), returned, TN)
    moe_rows = moe_parts[:own_rows] + moe_parts[own_rows:]
    block_out = resid + moe_rows

    row_start = (ctx_index * exp_count + exp_index) * own_rows
    row_valid = lax.dynamic_slice_in_dim(valid, row_start, own_rows, 0).astype(F32)
    valid_count = jnp.sum(valid.astype(F32))
    misfit = block_out - teacher.astype(F32)
    local_loss = jnp.sum(row_valid[:, None] * misfit * misfit)
    out_grad_rows = misfit * row_valid[:, None] * (token_total / valid_count)
    copy_grad = dot(
        jnp.concatenate([pick, pick], axis=1),
        jnp.concatenate(pieces(out_grad_rows, 2), axis=0),
        NN,
    )
    grad_copies = send((slot_gate * copy_grad).astype(BF16))
    grad_copies, probs = lax.optimization_barrier((grad_copies, probs))
    input_grad, gate_grad, up_grad, hidden_act = expert_backward(
        grad_copies, gate_pre, up_pre, expert, turned
    )
    arrived_grad = send(input_grad)

    gate_part = dot(expert_in, gate_grad, TN)
    up_part = dot(expert_in, up_grad, TN)
    down_part = dot(hidden_act, grad_copies, TN)
    gate_part = gate_part.reshape(model_width, exp_count, width).transpose(1, 0, 2)
    up_part = up_part.reshape(model_width, exp_count, width).transpose(1, 0, 2)
    arrived_grad, wide_qkv, gate_part, up_part, down_part = lax.optimization_barrier(
        (arrived_grad, wide_qkv, gate_part, up_part, down_part)
    )
    ffn_normed_grad = dot(pick, arrived_grad, TN)

    ffn_gain_part = jnp.sum(ffn_normed_grad * ffn_hat, axis=0)
    resid_grad = out_grad_rows + norm_back(ffn_normed_grad, ffn_hat, ffn_scale, ffn_gain)
    branch_rows = resid_grad.astype(BF16)

    do_rows = jnp.einsum("ro,eok->erk", branch_rows, full_out, preferred_element_type=F32)
    out_grad = exchange(do_rows.astype(BF16), "exp").reshape(ctx_rows, head_cols)
    branch_parts = shifted(branch_rows, "exp", exp_count)
    head_of = jnp.arange(head_cols, dtype=jnp.int32)[None] // HD
    head_ones = (head_of == jnp.arange(4, dtype=jnp.int32)[:, None]).astype(F32)
    delta = lax.dot_general(
        head_ones,
        out_grad.astype(F32) * heads_f,
        NT,
        precision=lax.Precision.HIGHEST,
        preferred_element_type=F32,
    )
    delta = delta.reshape(4, 2, 2 * BLK).transpose(1, 0, 2)
    do_all = lax.all_gather(with_stats(out_grad, delta), "ctx", axis=0, tiled=False)
    query_n_grad = query_grad(
        block_of, own_blocks, queries_rot, out_grad, heads_f, lse, cosine, sine, kv_all
    )

    grad_out = None
    for step, part in enumerate(branch_parts):
        first = (exp_index - step) % exp_count * own_rows
        term = dot(part, lax.dynamic_slice_in_dim(heads_low, first, own_rows, 0), TN)
        grad_out = term if grad_out is None else grad_out + term

    do_all, query_n_grad, grad_out, gate_part, up_part, down_part = lax.optimization_barrier(
        (do_all, query_n_grad, grad_out, gate_part, up_part, down_part)
    )
    grad_w_gate = lax.psum_scatter(gate_part, "exp", scatter_dimension=0, tiled=True)
    grad_w_up = lax.psum_scatter(up_part, "exp", scatter_dimension=0, tiled=True)
    grad_w_down = lax.psum_scatter(down_part, "exp", scatter_dimension=0, tiled=True)[None]

    pair_grads = pair_grad(
        block_of,
        own_blocks,
        own_kv,
        cosine,
        sine,
        q_all,
        ctx_rows,
        do_all,
        probs,
    )
    key_n_grad = pair_grads[:, :kv_cols]
    value_grad = pair_grads[:, kv_cols:].astype(BF16)
    query_gain_part = jnp.sum(query_n_grad * query_hat, axis=0)
    key_gain_part = jnp.sum(key_n_grad * key_hat, axis=0)
    query_hat_grad = query_n_grad * query_gain
    key_hat_grad = key_n_grad * key_gain
    stats = jnp.concatenate(
        [
            jnp.sum(query_hat_grad * query_hat, axis=1),
            jnp.sum(key_hat_grad * key_hat, axis=1),
            lax.dynamic_update_slice_in_dim(
                jnp.zeros((model_width,), F32), query_gain_part, exp_index * head_cols, 0
            ),
            ffn_gain_part,
            lax.dynamic_update_slice_in_dim(
                jnp.zeros((kv_total,), F32), key_gain_part, exp_index * kv_cols, 0
            ),
            jnp.full((kv_total,), local_loss),
        ]
    )
    stats = sum_short(stats.reshape(-1, LANES), "exp", exp_count).reshape(-1)
    query_stat = stats[:ctx_rows, None] / model_width
    key_stat = stats[ctx_rows : 2 * ctx_rows, None] / kv_total
    sums = stats[2 * ctx_rows :]
    query_low = (query_scale * (query_hat_grad - query_hat * query_stat)).astype(BF16)
    key_low = (key_scale * (key_hat_grad - key_hat * key_stat)).astype(BF16)
    grad_low = jnp.concatenate([query_low, key_low, value_grad], axis=1)

    wide_sums = jnp.stack(
        [
            sums[:model_width].reshape(ctx_count, shard_rows),
            sums[model_width : 2 * model_width].reshape(ctx_count, shard_rows),
            jnp.repeat(
                sums[2 * model_width : 2 * model_width + kv_total].reshape(ctx_count, -1), 2, axis=1
            ),
            jnp.broadcast_to(sums[-1], (ctx_count, shard_rows)),
        ],
        axis=-1,
    )
    grad_qkv = dot(normed, grad_low, TN)
    shards = exchange(
        jnp.concatenate(
            [
                grad_qkv.astype(BF16).reshape(ctx_count, shard_rows, qkv_cols),
                grad_out.astype(BF16).reshape(ctx_count, shard_rows, head_cols),
                ride_along(wide_sums),
            ],
            axis=2,
        ),
        "ctx",
    )
    back = exchange_short(grad_low, "exp", exp_index, exp_count)
    shards = jnp.sum(shards.astype(F32), axis=0)
    grad_w_query = shards[:, :head_cols]
    grad_w_key = shards[:, head_cols : head_cols + kv_cols]
    grad_w_value = shards[:, head_cols + kv_cols : qkv_cols]
    grad_w_out = shards[:, qkv_cols : qkv_cols + head_cols]
    tail = parted(shards[:, qkv_cols + head_cols :], 4)
    loss = tail[0, 3] / (valid_count * model_width)

    gain_part = jnp.sum(grad_w_query * w_query.astype(F32), axis=1)
    gain_part += jnp.sum(grad_w_key * w_key.astype(F32), axis=1)
    gain_part += jnp.sum(grad_w_value * w_value.astype(F32), axis=1)
    grad_gain_attn = sum_short(gain_part, "exp", exp_count) / gain_attn.astype(F32)
    normed_rows = dot(back, wide_qkv, NT)
    own_scale = lax.dynamic_slice_in_dim(attn_scale, exp_index * own_rows, own_rows, 0)
    own_hat = hidden_rows * own_scale
    grad_hidden = resid_grad + norm_back(normed_rows, own_hat, own_scale, attn_gain)
    return (
        block_out,
        loss,
        grad_hidden,
        grad_w_query,
        grad_w_key,
        grad_w_value,
        grad_w_out,
        grad_gain_attn,
        tail[:, 0],
        tail[::2, 2],
        tail[:, 1],
        grad_w_gate,
        grad_w_up,
        grad_w_down,
    )


def solution(mesh):
    return jax.shard_map(
        on_device,
        mesh=mesh,
        in_specs=(
            P("ctx", None),
            P(("ctx", "exp"), None),
            P(),
            P(),
            P(("ctx", "exp"), None),
            P(("ctx", "exp"), None),
            P("ctx", "exp"),
            P("ctx", "exp"),
            P("ctx", "exp"),
            P("ctx", "exp"),
            P("ctx"),
            P("ctx"),
            P("ctx"),
            P("ctx"),
            P("ctx", None, "exp"),
            P("ctx", None, "exp"),
            P("ctx", "exp", None),
        ),
        out_specs=(
            P(("ctx", "exp"), None),
            P(),
            P(("ctx", "exp"), None),
            P("ctx", "exp"),
            P("ctx", "exp"),
            P("ctx", "exp"),
            P("ctx", "exp"),
            P("ctx"),
            P("ctx"),
            P("ctx"),
            P("ctx"),
            P("ctx", None, "exp"),
            P("ctx", None, "exp"),
            P("ctx", "exp", None),
        ),
        check_vma=False,
    )
```

```python
import functools

import jax
import jax.numpy as jnp
from jax import lax
from jax.experimental import pallas as pl
from jax.experimental.pallas import tpu as pltpu
from jax.sharding import PartitionSpec as P

HD = 64
BLK = 128
CONT_LEN = 1024
CONT_BLKS = CONT_LEN // BLK
LANES = 128

NORM_EPSILON = 1e-05
ROPE_BASE = 10000.0
MASK_FLOOR = -1e30
F32 = jnp.float32
BF16 = jnp.bfloat16
NT = (((1,), (1,)), ((), ()))
NN = (((1,), (0,)), ((), ()))
TN = (((0,), (0,)), ((), ()))


def dot(left, right, dims):
    return lax.dot_general(left, right, dims, preferred_element_type=F32)


def key_ranges(block, half, tile_blocks):
    cont = block >= half
    inner = jnp.where(cont, (block - half) % CONT_BLKS, 0)
    n_a = jnp.where(cont, half // tile_blocks, block // tile_blocks)
    cont_base = half + (block - half) // CONT_BLKS * CONT_BLKS
    base = jnp.where(cont, cont_base, block // tile_blocks * tile_blocks) * BLK
    return n_a, base, inner // tile_blocks


def gather_blocks(table, total, moves):
    def start(i, carry):
        to = pl.multiple_of(table[i] * BLK, BLK)
        for source, target, sem in moves:
            pltpu.make_async_copy(source(i), target(to), sem).start()
        return carry

    lax.fori_loop(0, total, start, 0)


def wait_all(ref, sem):
    pltpu.make_async_copy(ref, ref, sem).wait()


def rows_of(ref, per_ctx):
    def place(i):
        first = i // 4 * per_ctx + i % 4 * BLK
        return ref.at[pl.ds(pl.multiple_of(first, 16), BLK)]

    return place


def stats_of(ref):
    return lambda i: ref.at[i // 4, i // 2 % 2, :, pl.ds(pl.multiple_of(i % 2 * BLK, BLK), BLK)]


def causal(shape, key_first, query_first, rows_are_queries):
    row = lax.broadcasted_iota(jnp.int32, shape, 0) % BLK
    col = lax.broadcasted_iota(jnp.int32, shape, 1)
    if rows_are_queries:
        return key_first + col <= query_first + row
    return key_first + row <= query_first + col


def to_half(tile, source, target):
    values = tile.astype(F32)
    if source != target:
        values = pltpu.roll(values, HD, 1)
    lane = lax.broadcasted_iota(jnp.int32, values.shape, 1)
    return jnp.where(lane // HD == target, values, 0.0)


def turn(tile, cosine, sine):
    lane = lax.broadcasted_iota(jnp.int32, tile.shape, 1)
    ahead = pltpu.roll(tile, LANES - HD // 2, 1)
    behind = pltpu.roll(tile, HD // 2, 1)
    return tile * cosine + jnp.where(lane % HD < HD // 2, ahead, behind) * sine


def rows_by_head(source_ref, block_rows, target_ref):
    for h in range(4):
        m, g = h // 2, h % 2
        tile = source_ref[block_rows, m * LANES : (m + 1) * LANES]
        target_ref[h * BLK : (h + 1) * BLK, :] = to_half(tile, g, m).astype(BF16)


def rows_by_token(values):
    tiles = []
    for m in range(2):
        first = values[2 * m * BLK : (2 * m + 1) * BLK]
        second = values[(2 * m + 1) * BLK : (2 * m + 2) * BLK]
        tiles.append(to_half(first, m, 0) + to_half(second, m, 1))
    return tiles


def turn_kernel(pre_ref, scale_ref, gain_ref, cos_ref, sin_ref, q_ref, kv_ref):
    for col in range(3):
        lanes = slice(col * LANES, (col + 1) * LANES)
        which = 0 if col < 2 else 1
        hat = pre_ref[:, lanes] * scale_ref[:, which : which + 1]
        turned = turn(hat * gain_ref[:, lanes], cos_ref[...], sin_ref[...]).astype(BF16)
        if which == 0:
            q_ref[:, lanes] = (turned.astype(F32) * HD**-0.5).astype(BF16)
        else:
            kv_ref[:, :LANES] = turned
    kv_ref[:, LANES:] = pre_ref[:, 3 * LANES :].astype(BF16)


def attend_kernel(
    total, half, tile_blocks, table, own, q_in, kv, o_ref, lse_ref, kv_s, q_ref, acc, peak, s_buf, sem
):
    gather_blocks(
        table,
        total,
        [
            (
                rows_of(kv, 4 * BLK),
                lambda to: kv_s.at[pl.ds(to, BLK)],
                sem.at[0],
            )
        ],
    )
    wait_all(kv_s, sem.at[0])
    width = tile_blocks * BLK
    ones = jnp.ones((width, LANES), BF16)

    def query_block(i, carry):
        block = own[i]
        n_a, base, n_b = key_ranges(block, half, tile_blocks)
        rows = pl.ds(pl.multiple_of(i * BLK, BLK), BLK)
        lanes = pl.ds(pl.multiple_of(i % 2 * BLK, BLK), BLK)
        rows_by_head(q_in, rows, q_ref)

        def first_key(j):
            return pl.multiple_of(jnp.where(j < n_a, j * width, base + (j - n_a) * width), BLK)

        def tile(start, masked):
            scores = dot(q_ref[...], kv_s[pl.ds(start, width), :LANES], NT)
            probs = jnp.exp(scores)
            if masked:
                probs = jnp.where(causal(probs.shape, start, block * BLK, True), probs, 0.0)
            acc[...] += dot(probs.astype(BF16), values_at(start), NN)

        def clear_tile(j, carry):
            tile(first_key(j), False)
            return carry

        def store(out, log_sum):
            first, second = rows_by_token(out)
            o_ref[rows, :LANES] = first
            o_ref[rows, LANES:] = second
            for h in range(4):
                lse_ref[i // 2, h : h + 1, lanes] = log_sum[h * BLK : (h + 1) * BLK].T[:1]

        def values_at(start):
            return jnp.concatenate([kv_s[pl.ds(start, width), LANES:], ones], axis=1)

        def score(j):
            return dot(q_ref[...], kv_s[pl.ds(first_key(j), width), :LANES], NT)

        def weigh(scores, j, masked):
            start = first_key(j)
            probs = jnp.exp(scores)
            if masked:
                probs = jnp.where(causal(probs.shape, start, block * BLK, True), probs, 0.0)
            acc[...] += dot(probs.astype(BF16), values_at(start), NN)

        acc[...] = jnp.zeros_like(acc)
        count = n_a + n_b
        s_buf[0] = score(0)

        def two_tiles(i2, carry):
            j = 2 * i2
            s_buf[1] = score(j + 1)
            weigh(s_buf[0], j, False)
            s_buf[0] = score(j + 2)
            weigh(s_buf[1], j + 1, False)
            return carry

        lax.fori_loop(0, count // 2, two_tiles, 0)

        @pl.when(count % 2 == 1)
        def _():
            s_buf[1] = score(count)
            weigh(s_buf[0], count - 1, False)
            weigh(s_buf[1], count, True)

        @pl.when(count % 2 == 0)
        def _():
            weigh(s_buf[0], count, True)

        sums = acc[:, LANES:]
        in_range = (jnp.max(sums) < 2.0**100) & (jnp.min(sums) > 2.0**-40)

        @pl.when(in_range)
        def _():
            store(acc[:, :LANES] / sums, jnp.log(sums))

        @pl.when(jnp.logical_not(in_range))
        def _():
            acc[...] = jnp.zeros_like(acc)
            peak[...] = jnp.full_like(peak, MASK_FLOOR)

            def safe_tile(j, carry):
                start = first_key(j)
                scores = dot(q_ref[...], kv_s[pl.ds(start, width), :LANES], NT)
                seen = causal(scores.shape, start, block * BLK, True)
                scores = jnp.where(seen, scores, MASK_FLOOR)
                old = peak[...]
                new = jnp.maximum(old, jnp.max(scores, axis=1, keepdims=True))
                probs = jnp.where(seen, jnp.exp(scores - new[:, :1]), 0.0)
                keep = jnp.exp(old - new)
                acc[...] = acc[...] * keep[:, :1] + dot(
                    probs.astype(BF16), values_at(start), NN
                )
                peak[...] = new
                return carry

            lax.fori_loop(0, n_a + n_b + 1, safe_tile, 0)
            safe_sums = acc[:, LANES:]
            store(acc[:, :LANES] / safe_sums, peak[...] + jnp.log(safe_sums))

        return carry

    lax.fori_loop(0, 4, query_block, 0)


def query_grad_kernel(
    total,
    half,
    tile_blocks,
    table,
    own,
    q_in,
    do_in,
    o_in,
    lse_in,
    cos_ref,
    sin_ref,
    kv,
    dq_ref,
    kv_s,
    q_ref,
    do_ref,
    lse_ref,
    delta_ref,
    acc,
    sem,
):
    gather_blocks(
        table, total, [(rows_of(kv, 4 * BLK), lambda to: kv_s.at[pl.ds(to, BLK)], sem.at[0])]
    )
    wait_all(kv_s, sem.at[0])
    width = tile_blocks * BLK

    def query_block(i, carry):
        block = own[i]
        n_a, base, n_b = key_ranges(block, half, tile_blocks)
        rows = pl.ds(pl.multiple_of(i * BLK, BLK), BLK)
        lanes = pl.ds(pl.multiple_of(i % 2 * BLK, BLK), BLK)
        rows_by_head(q_in, rows, q_ref)
        do_block = (i + 4 - own[4]) % 4
        do_rows = pl.ds(pl.multiple_of(do_block * BLK, BLK), BLK)
        rows_by_head(do_in, do_rows, do_ref)
        for h in range(4):
            part = slice(h * BLK, (h + 1) * BLK)
            pair = slice(h // 2 * LANES, (h // 2 + 1) * LANES)
            product = do_in[do_rows, pair].astype(F32) * o_in[rows, pair]
            own_half = to_half(product, h % 2, h % 2)
            delta = jnp.sum(own_half, axis=1, keepdims=True)
            delta_ref[part, :] = jnp.broadcast_to(delta, (BLK, LANES))
            row = lse_in[i // 2, h : h + 1, lanes]
            lse_ref[part, :] = jnp.broadcast_to(row, (LANES, BLK)).T

        def first_key(j):
            return pl.multiple_of(jnp.where(j < n_a, j * width, base + (j - n_a) * width), BLK)

        def tile(start, masked):
            keys = kv_s[pl.ds(start, width), :LANES]
            scores = dot(q_ref[...], keys, NT)
            prob_grad = dot(do_ref[...], kv_s[pl.ds(start, width), LANES:], NT)
            probs = jnp.exp(scores - lse_ref[:, :1])
            score_grad = probs * (prob_grad - delta_ref[:, :1])
            if masked:
                seen = causal(probs.shape, start, block * BLK, True)
                score_grad = jnp.where(seen, score_grad, 0.0)
            acc[...] += dot(score_grad.astype(BF16), keys, NN)

        def clear_tile(j, carry):
            tile(first_key(j), False)
            return carry

        acc[...] = jnp.zeros_like(acc)
        lax.fori_loop(0, n_a + n_b, clear_tile, 0)
        tile(first_key(n_a + n_b), True)
        for m, gradient in enumerate(rows_by_token(acc[...])):
            back = turn(gradient * HD**-0.5, cos_ref[rows, :], -sin_ref[rows, :])
            dq_ref[rows, m * LANES : (m + 1) * LANES] = back
        return carry

    lax.fori_loop(0, 4, query_block, 0)


def place(blk, h):
    return (h * 2 + blk) * BLK if blk < 2 else ((blk * 4) + h) * BLK


def spread_heads(source_ref, lanes, target_ref):
    target_ref[...] = jnp.zeros_like(target_ref)
    for blk in range(4):
        for h in range(4):
            m, g = h // 2, h % 2
            rows = slice(place(blk, h), place(blk, h) + BLK)
            tile = source_ref[blk * BLK : (blk + 1) * BLK, lanes]
            target_ref[rows, m * LANES : (m + 1) * LANES] = to_half(tile, m, g).astype(BF16)


def cont_tiles(own, which, half, tile_blocks):
    block = own[2 + which]
    base = half + (block - half) // CONT_BLKS * CONT_BLKS
    return block, block // tile_blocks, (base + CONT_BLKS) // tile_blocks, base // tile_blocks


def pair_probs_kernel(
    total, half, tile_blocks, q_rows, table, own, kv_in, q_all, lse_all, p_ref, pc_ref, q_s, lse_s, k_ref, sem
):
    step = pl.program_id(0)
    width = tile_blocks * BLK
    pair = 2 * tile_blocks

    @pl.when(step == 0)
    def _():
        gather_blocks(
            table,
            total,
            [
                (rows_of(q_all, q_rows), lambda to: q_s.at[pl.ds(to, BLK)], sem.at[0]),
                (stats_of(lse_all), lambda to: lse_s.at[:, pl.ds(to, BLK)], sem.at[1]),
            ],
        )
        spread_heads(kv_in, slice(0, LANES), k_ref)
        wait_all(q_s, sem.at[0])
        wait_all(lse_s, sem.at[1])

    def probs_of(first_row, per_head, j, keys_first, store):
        start = pl.multiple_of(j * width, width)
        keys = k_ref[first_row : first_row + 4 * per_head, :]
        scores = dot(keys, q_s[pl.ds(start, width), :], NT)
        for h in range(4):
            part = slice(h * per_head, (h + 1) * per_head)
            probs = jnp.exp(scores[part] - lse_s[h : h + 1, pl.ds(start, width)])
            if keys_first is not None:
                seen = [causal((BLK, width), first, start, False) for first in keys_first]
                probs = jnp.where(jnp.concatenate(seen, axis=0), probs, 0.0)
            store(part, probs.astype(BF16))

    low = jnp.minimum(own[0], own[1])
    high = jnp.maximum(own[0], own[1])

    def prompt(keys_first):
        for side in range(2):

            def store(part, probs, side=side):
                p_ref[0, part, side * width : (side + 1) * width] = probs

            probs_of(0, 2 * BLK, 2 * step + side, keys_first, store)

    @pl.when((step >= low // pair) & (step <= high // pair))
    def _():
        prompt([own[0] * BLK, own[1] * BLK])

    @pl.when(step > high // pair)
    def _():
        prompt(None)

    @pl.when(step == pl.num_programs(0) - 1)
    def _():
        for which in range(2):
            block, first, stop, base = cont_tiles(own, which, half, tile_blocks)

            def cont_tile(j, carry, which=which, block=block, base=base):
                def store(part, probs):
                    pc_ref[which, j - base, part, :] = probs

                probs_of((8 + 4 * which) * BLK, BLK, j, [block * BLK], store)
                return carry

            lax.fori_loop(first, stop, cont_tile, 0)


def pair_grad_kernel(
    total,
    half,
    tile_blocks,
    q_rows,
    table,
    own,
    kv_in,
    cos_ref,
    sin_ref,
    q_all,
    do_all,
    p_ref,
    pc_ref,
    out_ref,
    q_s,
    do_s,
    parts_s,
    delta_s,
    v_ref,
    dk_ref,
    dv_ref,
    d_buf,
    sem,
):
    step = pl.program_id(0)
    width = tile_blocks * BLK
    pair = 2 * tile_blocks

    @pl.when(step == 0)
    def _():
        gather_blocks(
            table,
            total,
            [
                (rows_of(q_all, q_rows), lambda to: q_s.at[pl.ds(to, BLK)], sem.at[0]),
                (
                    lambda i: do_all.at[
                        i // 4, pl.ds(pl.multiple_of((i + 4 - own[4]) % 4 * BLK, BLK), BLK)
                    ],
                    lambda to: do_s.at[pl.ds(to, BLK)],
                    sem.at[1],
                ),
            ],
        )
        stats = pltpu.make_async_copy(do_all.at[:, pl.ds(4 * BLK, 48)], parts_s, sem.at[2])
        stats.start()
        dk_ref[...] = jnp.zeros_like(dk_ref)
        dv_ref[...] = jnp.zeros_like(dv_ref)
        spread_heads(kv_in, slice(LANES, 2 * LANES), v_ref)
        wait_all(q_s, sem.at[0])
        wait_all(do_s, sem.at[1])
        stats.wait()

        def place_stats(c, carry):
            parts = parts_s[c].astype(F32)
            sums = parts[:16] + parts[16:32] + parts[32:]
            for blk in range(4):
                to = pl.multiple_of(table[4 * c + (blk + own[4]) % 4] * BLK, BLK)
                first, lane = blk // 2 * 8, blk % 2 * BLK
                delta_s[:, pl.ds(to, BLK)] = sums[first : first + 8, lane : lane + BLK]
            return carry

        lax.fori_loop(0, total // 4, place_stats, 0)

    def prob_grad(first_row, per_head, j):
        start = pl.multiple_of(j * width, width)
        values = v_ref[first_row : first_row + 4 * per_head, :]
        return dot(values, do_s[pl.ds(start, width), :], NT)

    def add(first_row, per_head, j, probs, grads_in):
        rows = pl.ds(first_row, 4 * per_head)
        start = pl.multiple_of(j * width, width)
        score_low = []
        for h in range(4):
            part = slice(h * per_head, (h + 1) * per_head)
            shifted_grad = grads_in[part] - delta_s[h : h + 1, pl.ds(start, width)]
            score_low.append((probs[part].astype(F32) * shifted_grad).astype(BF16))
        dv_ref[rows, :] += dot(probs, do_s[pl.ds(start, width), :], NN)
        queries = q_s[pl.ds(start, width), :]
        dk_ref[rows, :] += dot(jnp.concatenate(score_low, axis=0), queries, NN)

    low = jnp.minimum(own[0], own[1])
    last = total // tile_blocks - 1

    @pl.when(step == low // pair)
    def _():
        d_buf[0] = prob_grad(0, 2 * BLK, 2 * step)

    @pl.when(step >= low // pair)
    def _():
        d_buf[1] = prob_grad(0, 2 * BLK, 2 * step + 1)
        add(0, 2 * BLK, 2 * step, p_ref[0, :, :width], d_buf[0])
        d_buf[0] = prob_grad(0, 2 * BLK, jnp.minimum(2 * step + 2, last))
        add(0, 2 * BLK, 2 * step + 1, p_ref[0, :, width:], d_buf[1])

    def collect(ref, blk):
        tile_sum = None
        for h in range(4):
            m, g = h // 2, h % 2
            part = ref[place(blk, h) : place(blk, h) + BLK, m * LANES : (m + 1) * LANES]
            moved = to_half(part, g, m)
            tile_sum = moved if tile_sum is None else tile_sum + moved
        return tile_sum

    @pl.when(step == pl.num_programs(0) - 1)
    def _():
        for which in range(2):
            _, first, stop, base = cont_tiles(own, which, half, tile_blocks)

            def cont_tile(j, carry, which=which, base=base):
                first_row = (8 + 4 * which) * BLK
                grads_in = prob_grad(first_row, BLK, j)
                add(first_row, BLK, j, pc_ref[which, j - base], grads_in)
                return carry

            lax.fori_loop(first, stop, cont_tile, 0)
        for blk in range(4):
            rows = slice(blk * BLK, (blk + 1) * BLK)
            out_ref[rows, :LANES] = turn(collect(dk_ref, blk), cos_ref[rows, :], -sin_ref[rows, :])
            out_ref[rows, LANES:] = collect(dv_ref, blk)


def down_strips(w_ref, pair, width):
    strips = [w_ref[u, :, 2 * width : 3 * width] for u in (2 * pair, 2 * pair + 1)]
    return jnp.concatenate(strips, axis=1)


def expert_kernel(quarters, width, x_ref, w_ref, out_ref, gate_ref, up_ref):
    acts = []
    for u in range(quarters):
        cols = slice(u * width, (u + 1) * width)
        pre = dot(x_ref[...], w_ref[u, :, : 2 * width], NN)
        gate, up = pre[:, :width], pre[:, width:]
        gate_ref[:, cols] = gate
        up_ref[:, cols] = up
        acts.append((gate * jax.nn.sigmoid(gate) * up).astype(BF16))
    out = None
    for pair in range(quarters // 2):
        act = jnp.concatenate(acts[2 * pair : 2 * pair + 2], axis=1)
        part = dot(act, down_strips(w_ref, pair, width), NT)
        out = part if out is None else out + part
    out_ref[...] = out.astype(BF16)


def expert_grad_kernel(
    quarters, width, dy_ref, gate_ref, up_ref, w_ref, wt_ref, dx_ref, dgate_ref, dup_ref, act_ref
):
    total = None
    for pair in range(quarters // 2):
        both = dot(dy_ref[...], down_strips(w_ref, pair, width), NN)
        for side in range(2):
            u = 2 * pair + side
            cols = slice(u * width, (u + 1) * width)
            act_grad = both[:, side * width : (side + 1) * width]
            gate, up = gate_ref[:, cols], up_ref[:, cols]
            sig = jax.nn.sigmoid(gate)
            gate_act = gate * sig
            act_ref[:, cols] = (gate_act * up).astype(BF16)
            gate_grad = (act_grad * up * sig * (1.0 + gate * (1.0 - sig))).astype(BF16)
            up_grad = (act_grad * gate_act).astype(BF16)
            dgate_ref[:, cols] = gate_grad
            dup_ref[:, cols] = up_grad
            grads = jnp.concatenate([gate_grad, up_grad], axis=1)
            part = dot(grads, wt_ref[u], NN)
            total = part if total is None else total + part
    dx_ref[...] = total.astype(BF16)


def in_hbm(values):
    return pltpu.with_memory_space_constraint(values, pltpu.HBM)


def block_of_whole(shape):
    return pl.BlockSpec(shape, lambda i, *_: (0,) * len(shape))


def kernel_call(kernel, name, prefetch, ins, outs, scratch, flops):
    hbm = pl.BlockSpec(memory_space=pl.ANY)
    moved = sum(x.size * x.dtype.itemsize for x, _ in ins)
    return pl.pallas_call(
        kernel,
        out_shape=tuple(outs),
        grid_spec=pltpu.PrefetchScalarGridSpec(
            num_scalar_prefetch=len(prefetch),
            grid=(1,),
            in_specs=[hbm if far else block_of_whole(x.shape) for x, far in ins],
            out_specs=tuple(block_of_whole(out.shape) for out in outs),
            scratch_shapes=scratch,
        ),
        compiler_params=pltpu.CompilerParams(vmem_limit_bytes=48 << 20),
        cost_estimate=pl.CostEstimate(flops=flops, bytes_accessed=moved, transcendentals=0),
        name=name,
    )(*prefetch, *(x for x, _ in ins))


def by_rows(kernel, name, rows, ins, outs, flops):
    def spec(shape):
        if len(shape) == 3:
            return pl.BlockSpec(shape, lambda i: (0, 0, 0))
        return pl.BlockSpec((rows, shape[1]), lambda i: (i, 0))

    return pl.pallas_call(
        kernel,
        out_shape=tuple(pltpu.HBM(out.shape, out.dtype) for out in outs),
        grid=(outs[0].shape[0] // rows,),
        in_specs=[spec(x.shape) for x in ins],
        out_specs=tuple(spec(out.shape) for out in outs),
        compiler_params=pltpu.CompilerParams(vmem_limit_bytes=40 << 20),
        cost_estimate=pl.CostEstimate(flops=flops, bytes_accessed=10**7, transcendentals=0),
        name=name,
    )(*(in_hbm(x) for x in ins))


def expert_forward(rows_in, weights):
    slots, model_width = rows_in.shape
    quarters, _, cols = weights.shape
    width = cols // 3
    hidden = jax.ShapeDtypeStruct((slots, quarters * width), F32)
    return by_rows(
        functools.partial(expert_kernel, quarters, width),
        "expert",
        slots // 5,
        [rows_in, weights],
        [jax.ShapeDtypeStruct((slots, model_width), BF16), hidden, hidden],
        6 * slots * model_width * quarters * width,
    )


def expert_backward(rows_grad, gate_pre, up_pre, weights, turned):
    slots, model_width = rows_grad.shape
    quarters, _, cols = weights.shape
    width = cols // 3
    hidden = jax.ShapeDtypeStruct((slots, quarters * width), BF16)
    return by_rows(
        functools.partial(expert_grad_kernel, quarters, width),
        "expert_grad",
        slots // 2,
        [rows_grad, gate_pre, up_pre, weights, turned],
        [jax.ShapeDtypeStruct((slots, model_width), BF16), hidden, hidden, hidden],
        6 * slots * model_width * quarters * width,
    )


def turn_heads(projected, scales, gain, cosine, sine):
    rows = projected.shape[0]
    out = jax.ShapeDtypeStruct((rows, 2 * LANES), BF16)
    ins = [(x, False) for x in (projected, scales, gain, cosine, sine)]
    return kernel_call(turn_kernel, "turn_heads", (), ins, [out, out], [], 10**6)


def attend(table, own, q, kv_all):
    total = table.shape[0]
    return kernel_call(
        functools.partial(attend_kernel, total, total // 2, 8),
        "attend",
        (table, own),
        [(q, False), (kv_all, True)],
        [
            jax.ShapeDtypeStruct((4 * BLK, 2 * LANES), F32),
            jax.ShapeDtypeStruct((2, 4, 2 * BLK), F32),
        ],
        [
            pltpu.VMEM((total * BLK, 2 * LANES), BF16),
            pltpu.VMEM((4 * BLK, LANES), BF16),
            pltpu.VMEM((4 * BLK, 2 * LANES), F32),
            pltpu.VMEM((4 * BLK, LANES), F32),
            pltpu.VMEM((2, 4 * BLK, 8 * BLK), F32),
            pltpu.SemaphoreType.DMA((1,)),
        ],
        20 * 10**9,
    )


def query_grad(table, own, q, out_grad, heads, lse, cosine, sine, kv_all):
    total = table.shape[0]
    ins = [(x, False) for x in (q, out_grad, heads, lse, cosine, sine)]
    return kernel_call(
        functools.partial(query_grad_kernel, total, total // 2, 4),
        "query_grad",
        (table, own),
        ins + [(kv_all, True)],
        [jax.ShapeDtypeStruct((4 * BLK, 2 * LANES), F32)],
        [
            pltpu.VMEM((total * BLK, 2 * LANES), BF16),
            pltpu.VMEM((4 * BLK, LANES), BF16),
            pltpu.VMEM((4 * BLK, LANES), BF16),
            pltpu.VMEM((4 * BLK, LANES), F32),
            pltpu.VMEM((4 * BLK, LANES), F32),
            pltpu.VMEM((4 * BLK, LANES), F32),
            pltpu.SemaphoreType.DMA((1,)),
        ],
        30 * 10**9,
    )[0]


def pair_call(kernel, name, table, own, ins, blocks, outs, out_blocks, scratch, flops):
    steps = table.shape[0] // 8

    def tile_place(step, table_ref, own_ref):
        return (jnp.maximum(step, jnp.minimum(own_ref[0], own_ref[1]) // 8), 0, 0)

    def spec(shape, block):
        if block is None:
            return pl.BlockSpec(memory_space=pl.ANY)
        if block == shape:
            return pl.BlockSpec(shape, lambda *_: (0,) * len(shape))
        return pl.BlockSpec(block, tile_place)

    return pl.pallas_call(
        kernel,
        out_shape=tuple(
            out if out.dtype == F32 else pltpu.HBM(out.shape, out.dtype) for out in outs
        ),
        grid_spec=pltpu.PrefetchScalarGridSpec(
            num_scalar_prefetch=2,
            grid=(steps,),
            in_specs=[spec(x.shape, block) for x, block in zip(ins, blocks)],
            out_specs=tuple(spec(x.shape, block) for x, block in zip(outs, out_blocks)),
            scratch_shapes=scratch,
        ),
        compiler_params=pltpu.CompilerParams(vmem_limit_bytes=48 << 20),
        cost_estimate=pl.CostEstimate(flops=flops, bytes_accessed=4 * 10**7, transcendentals=0),
        name=name,
    )(table, own, *ins)


PROB_BLOCK = (1, 8 * BLK, 8 * BLK)
CONT_SHAPE = (2, CONT_BLKS // 4, 4 * BLK, 4 * BLK)


def pair_probs(table, own, kv, q_all, q_rows, lse_all):
    total = table.shape[0]
    return pair_call(
        functools.partial(pair_probs_kernel, total, total // 2, 4, q_rows),
        "pair_probs",
        table,
        own,
        [kv, q_all, lse_all],
        [kv.shape, None, None],
        [
            jax.ShapeDtypeStruct((total // 8,) + PROB_BLOCK[1:], BF16),
            jax.ShapeDtypeStruct(CONT_SHAPE, BF16),
        ],
        [PROB_BLOCK, CONT_SHAPE],
        [
            pltpu.VMEM((total * BLK, 2 * LANES), BF16),
            pltpu.VMEM((8, total * BLK), F32),
            pltpu.VMEM((16 * BLK, 2 * LANES), BF16),
            pltpu.SemaphoreType.DMA((2,)),
        ],
        20 * 10**9,
    )


def pair_grad(table, own, kv, cosine, sine, q_all, q_rows, do_all, probs):
    total = table.shape[0]
    return pair_call(
        functools.partial(pair_grad_kernel, total, total // 2, 4, q_rows),
        "pair_grad",
        table,
        own,
        [kv, cosine, sine, q_all, do_all, *(in_hbm(x) for x in probs)],
        [kv.shape, cosine.shape, sine.shape, None, None, PROB_BLOCK, CONT_SHAPE],
        [jax.ShapeDtypeStruct((4 * BLK, 2 * LANES), F32)],
        [(4 * BLK, 2 * LANES)],
        [
            pltpu.VMEM((total * BLK, 2 * LANES), BF16),
            pltpu.VMEM((total * BLK, 2 * LANES), BF16),
            pltpu.VMEM((total // 4, 48, 2 * LANES), BF16),
            pltpu.VMEM((8, total * BLK), F32),
            pltpu.VMEM((16 * BLK, 2 * LANES), BF16),
            pltpu.VMEM((16 * BLK, 2 * LANES), F32),
            pltpu.VMEM((16 * BLK, 2 * LANES), F32),
            pltpu.VMEM((2, 8 * BLK, 4 * BLK), F32),
            pltpu.SemaphoreType.DMA((3,)),
        ],
        30 * 10**9,
    )[0]


def turn_tables(position):
    half_dim = HD // 2
    frequency = ROPE_BASE ** (-(jnp.arange(half_dim, dtype=F32) * 2.0 / HD))
    angles = position[:, None] * frequency[None, :]
    cosine, sine = jnp.cos(angles), jnp.sin(angles)
    return jnp.concatenate([cosine] * 4, axis=1), jnp.concatenate([-sine, sine] * 2, axis=1)


def norm_back(grad_normed, hat_values, scale_values, gain_values):
    grad_hat = grad_normed * gain_values
    return scale_values * (
        grad_hat - hat_values * jnp.mean(grad_hat * hat_values, axis=-1, keepdims=True)
    )


def pieces(values, count):
    parts = []
    for _ in range(count):
        part = lax.reduce_precision(values, 8, 7)
        parts.append(part.astype(BF16))
        values = values - part
    return parts


def exchange(values, axis):
    return lax.all_to_all(values, axis, split_axis=0, concat_axis=0, tiled=True)


def spread(values, axis, count):
    return exchange(jnp.broadcast_to(values[None], (count,) + values.shape), axis)


def shifted(values, axis, count):
    parts = [values]
    for step in range(1, count):
        parts.append(lax.ppermute(values, axis, [(i, (i + step) % count) for i in range(count)]))
    return parts


def sum_short(values, axis, count):
    parts = shifted(values, axis, count)
    while len(parts) > 1:
        half = len(parts) // 2
        parts = [parts[i] + parts[i + half] for i in range(half)]
    return parts[0]


def exchange_short(values, axis, index, count):
    rows = values.shape[0] // count
    come = []
    for step in range(count):
        to = (index + step) % count
        part = lax.dynamic_slice_in_dim(values, to * rows, rows, 0)
        if step > 0:
            part = lax.ppermute(part, axis, [(i, (i + step) % count) for i in range(count)])
        come.append(part)
    return jnp.concatenate(come, axis=1)


def with_stats(rows, stats):
    stats = jnp.pad(stats, ((0, 0), (0, 4), (0, 0)))
    parts = jnp.stack(pieces(stats, 3), axis=0).reshape(-1, rows.shape[1])
    return jnp.concatenate([rows, parts], axis=0)


def ride_along(values):
    parts = jnp.concatenate(pieces(values, 3), axis=-1)
    return jnp.pad(parts, ((0, 0), (0, 0), (0, LANES - parts.shape[-1])))


def parted(sums, count):
    return sum(sums[:, i * count : (i + 1) * count] for i in range(3))


def on_device(
    hidden_in,
    teacher,
    valid,
    block_of,
    routes,
    gates,
    w_query,
    w_key,
    w_value,
    w_out,
    gain_attn,
    gain_query,
    gain_key,
    gain_ffn,
    w_gate,
    w_up,
    w_down,
):
    ctx_count = lax.axis_size("ctx")
    exp_count = lax.axis_size("exp")
    ctx_index = lax.axis_index("ctx")
    exp_index = lax.axis_index("exp")
    ctx_rows, model_width = hidden_in.shape
    own_rows = ctx_rows // exp_count
    token_total = block_of.shape[0] * BLK
    head_cols = w_query.shape[1]
    kv_cols = w_key.shape[1]
    kv_total = kv_cols * exp_count
    qkv_cols = head_cols + 2 * kv_cols
    shard_rows = w_query.shape[0]

    own_weights = jnp.concatenate([w_query, w_key, w_value], axis=1)
    gain_row = jnp.concatenate([gain_attn, gain_query, gain_ffn, gain_key])
    gain_rows = jnp.pad(
        gain_row, (0, 8 * own_weights.shape[1] - gain_row.shape[0])
    ).reshape(8, -1)
    first_parts = spread(jnp.concatenate([own_weights, gain_rows], axis=0), "ctx", ctx_count)
    full_qkv = first_parts[:, :shard_rows].reshape(model_width, qkv_cols)
    gains = first_parts[:, shard_rows:].reshape(ctx_count, -1)[:, : gain_row.shape[0]].astype(F32)
    attn_gain = gains[:, :shard_rows].reshape(model_width)
    query_gain_all = gains[:, shard_rows : 2 * shard_rows].reshape(model_width)
    ffn_gain = gains[:, 2 * shard_rows : 3 * shard_rows].reshape(model_width)
    key_gain_all = gains[:, 3 * shard_rows :].reshape(kv_total)
    query_gain = lax.dynamic_slice_in_dim(query_gain_all, exp_index * head_cols, head_cols)
    key_gain = lax.dynamic_slice_in_dim(key_gain_all, exp_index * kv_cols, kv_cols)

    width = w_gate.shape[2]
    own_expert = jnp.concatenate([w_gate[0], w_up[0], w_down[0].T], axis=1)
    expert = lax.all_gather(own_expert, "exp", axis=0, tiled=False)

    hidden_f = hidden_in.astype(F32)
    attn_scale = lax.rsqrt(jnp.mean(hidden_f * hidden_f, axis=-1, keepdims=True) + NORM_EPSILON)
    attn_hat = hidden_f * attn_scale
    normed = (attn_hat * attn_gain).astype(BF16)
    projected = dot(normed, full_qkv, NN)
    query_pre = projected[:, :head_cols]
    key_pre = projected[:, head_cols : head_cols + kv_cols]
    squares = jnp.stack(
        [jnp.sum(query_pre * query_pre, axis=1), jnp.sum(key_pre * key_pre, axis=1)]
    )
    query_square, key_square = sum_short(squares, "exp", exp_count)
    query_scale = lax.rsqrt(query_square / model_width + NORM_EPSILON)[:, None]
    key_scale = lax.rsqrt(key_square / kv_total + NORM_EPSILON)[:, None]
    query_hat = query_pre * query_scale
    key_hat = key_pre * key_scale
    own_blocks = lax.dynamic_slice_in_dim(block_of, ctx_index * 4, 4)
    own = jnp.concatenate([own_blocks, jnp.full((1,), exp_index, jnp.int32)])
    token_ids = (own_blocks[:, None] * BLK + jnp.arange(BLK, dtype=jnp.int32)[None]).reshape(-1)
    prompt_len = token_total // 2
    position = jnp.where(
        token_ids >= prompt_len, prompt_len + (token_ids - prompt_len) % CONT_LEN, token_ids
    ).astype(F32)
    cosine, sine = turn_tables(position)
    queries_rot, own_kv = turn_heads(
        projected,
        jnp.concatenate([query_scale, key_scale], axis=1),
        jnp.concatenate([query_gain, key_gain])[None],
        cosine,
        sine,
    )
    own_kv, expert = lax.optimization_barrier((own_kv, expert))
    kv_all = lax.all_gather(own_kv, "ctx", axis=0, tiled=True)
    own_out, _ = lax.optimization_barrier((w_out, own_kv))
    out_parts = shifted(
        spread(own_out, "ctx", ctx_count).reshape(model_width, head_cols), "exp", exp_count
    )
    wide_out = jnp.concatenate(out_parts, axis=1)
    wide_out, later_q = lax.optimization_barrier((wide_out, queries_rot))
    q_all = lax.all_gather(later_q, "ctx", axis=0, tiled=True)
    expert_total = ctx_count
    capacity = max(2, own_rows * routes.shape[1] * 5 // (expert_total * 4))
    slots = expert_total * capacity
    names = routes[:, :, None] == jnp.arange(expert_total, dtype=jnp.int32)[None, None, :]
    named = jnp.any(names, axis=1)
    gate_of = jnp.sum(jnp.where(names, gates[:, :, None], 0.0), axis=1)
    before = jnp.tril(jnp.ones((own_rows, own_rows), BF16), -1)
    rank = dot(before, named.astype(BF16), NN).astype(jnp.int32)
    slot_rank = jnp.where(named, rank, -1).T[:, None, :]
    holds = slot_rank == jnp.arange(capacity, dtype=jnp.int32)[None, :, None]
    pick = holds.astype(BF16).reshape(slots, own_rows)
    weigh = jnp.where(holds, gate_of.T[:, None, :], 0.0).reshape(slots, own_rows)
    slot_gate = jnp.sum(weigh, axis=1, keepdims=True)

    kv_all, wide_out, pick, weigh, slot_gate = lax.optimization_barrier(
        (kv_all, wide_out, pick, weigh, slot_gate)
    )
    heads_f, lse = attend(block_of, own, queries_rot, kv_all)
    heads_low = heads_f.astype(BF16)

    own_heads = exchange_short(heads_low, "exp", exp_index, exp_count)
    stat_rows = jnp.pad(lse, ((0, 0), (0, 28), (0, 0)))
    lse_all = lax.all_gather(stat_rows, "ctx", axis=0, tiled=False)
    attn_rows = dot(own_heads, wide_out, NT)
    hidden_rows = lax.dynamic_slice_in_dim(hidden_in, exp_index * own_rows, own_rows, 0)
    hidden_rows = hidden_rows.astype(F32)
    resid = hidden_rows + attn_rows
    ffn_scale = lax.rsqrt(jnp.mean(resid * resid, axis=-1, keepdims=True) + NORM_EPSILON)
    ffn_hat = resid * ffn_scale
    normed_ffn = (ffn_hat * ffn_gain).astype(BF16)

    def send(rows):
        return exchange(rows.reshape(ctx_count, capacity, model_width), "ctx").reshape(
            slots, model_width
        )

    expert_in = send(dot(pick, normed_ffn, NN).astype(BF16))
    expert_in, q_all = lax.optimization_barrier((expert_in, q_all))
    expert_out, gate_pre, up_pre = expert_forward(expert_in, expert)
    returned = send(expert_out)
    turned = expert[:, :, : 2 * width].transpose(0, 2, 1)
    returned, q_all, later_qkv, turned = lax.optimization_barrier(
        (returned, q_all, full_qkv, turned)
    )
    moe_parts = dot(jnp.concatenate(pieces(weigh, 2), axis=1), returned, TN)
    moe_rows = moe_parts[:own_rows] + moe_parts[own_rows:]
    block_out = resid + moe_rows

    row_start = (ctx_index * exp_count + exp_index) * own_rows
    row_valid = lax.dynamic_slice_in_dim(valid, row_start, own_rows, 0).astype(F32)
    valid_count = jnp.sum(valid.astype(F32))
    misfit = block_out - teacher.astype(F32)
    local_loss = jnp.sum(row_valid[:, None] * misfit * misfit)
    out_grad_rows = misfit * row_valid[:, None] * (token_total / valid_count)
    copy_grad = dot(
        jnp.concatenate([pick, pick], axis=1),
        jnp.concatenate(pieces(out_grad_rows, 2), axis=0),
        NN,
    )
    copy_grad = (slot_gate * copy_grad).astype(BF16)
    copy_grad, lse_all = lax.optimization_barrier((copy_grad, lse_all))
    grad_copies = send(copy_grad)
    probs = pair_probs(
        block_of,
        own,
        own_kv,
        q_all,
        ctx_rows,
        lse_all[:, :, :8],
    )
    wide_qkv = jnp.concatenate(shifted(later_qkv, "exp", exp_count), axis=1)
    grad_copies, probs = lax.optimization_barrier((grad_copies, probs))
    input_grad, gate_grad, up_grad, hidden_act = expert_backward(
        grad_copies, gate_pre, up_pre, expert, turned
    )
    arrived_grad = send(input_grad)

    gate_part = dot(expert_in, gate_grad, TN)
    up_part = dot(expert_in, up_grad, TN)
    down_part = dot(hidden_act, grad_copies, TN)
    gate_part = gate_part.reshape(model_width, exp_count, width).transpose(1, 0, 2)
    up_part = up_part.reshape(model_width, exp_count, width).transpose(1, 0, 2)
    arrived_grad, wide_qkv, gate_part, up_part, down_part = lax.optimization_barrier(
        (arrived_grad, wide_qkv, gate_part, up_part, down_part)
    )
    ffn_normed_grad = dot(pick, arrived_grad, TN)

    ffn_gain_part = jnp.sum(ffn_normed_grad * ffn_hat, axis=0)
    resid_grad = out_grad_rows + norm_back(ffn_normed_grad, ffn_hat, ffn_scale, ffn_gain)
    branch_rows = resid_grad.astype(BF16)

    do_parts = dot(branch_rows, wide_out, NN).astype(BF16)
    come = [do_parts[:, :head_cols]]
    for step in range(1, exp_count):
        part = do_parts[:, step * head_cols : (step + 1) * head_cols]
        turns = [(i, (i - step) % exp_count) for i in range(exp_count)]
        come.append(lax.ppermute(part, "exp", turns))
    out_grad = jnp.concatenate(come, axis=0)
    heads_turned = lax.dynamic_slice_in_dim(
        jnp.concatenate([heads_f, heads_f], axis=0), exp_index * own_rows, ctx_rows, 0
    )
    branch_parts = shifted(branch_rows, "exp", exp_count)
    head_of = jnp.arange(head_cols, dtype=jnp.int32)[None] // HD
    head_ones = (head_of == jnp.arange(4, dtype=jnp.int32)[:, None]).astype(F32)
    delta = lax.dot_general(
        head_ones,
        out_grad.astype(F32) * heads_turned,
        NT,
        precision=lax.Precision.HIGHEST,
        preferred_element_type=F32,
    )
    delta = delta.reshape(4, 2, 2 * BLK).transpose(1, 0, 2)
    do_all = lax.all_gather(with_stats(out_grad, delta), "ctx", axis=0, tiled=False)
    query_n_grad = query_grad(
        block_of, own, queries_rot, out_grad, heads_f, lse, cosine, sine, kv_all
    )

    grad_out = None
    for step, part in enumerate(branch_parts):
        first = (exp_index - step) % exp_count * own_rows
        term = dot(part, lax.dynamic_slice_in_dim(heads_low, first, own_rows, 0), TN)
        grad_out = term if grad_out is None else grad_out + term

    do_all, query_n_grad, grad_out, gate_part, up_part, down_part = lax.optimization_barrier(
        (do_all, query_n_grad, grad_out, gate_part, up_part, down_part)
    )
    grad_w_gate = lax.psum_scatter(gate_part, "exp", scatter_dimension=0, tiled=True)
    grad_w_up = lax.psum_scatter(up_part, "exp", scatter_dimension=0, tiled=True)
    grad_w_down = lax.psum_scatter(down_part, "exp", scatter_dimension=0, tiled=True)[None]

    pair_grads = pair_grad(
        block_of,
        own,
        own_kv,
        cosine,
        sine,
        q_all,
        ctx_rows,
        do_all,
        probs,
    )
    key_n_grad = pair_grads[:, :kv_cols]
    value_grad = pair_grads[:, kv_cols:].astype(BF16)
    query_gain_part = jnp.sum(query_n_grad * query_hat, axis=0)
    key_gain_part = jnp.sum(key_n_grad * key_hat, axis=0)
    query_hat_grad = query_n_grad * query_gain
    key_hat_grad = key_n_grad * key_gain
    stats = jnp.concatenate(
        [
            jnp.sum(query_hat_grad * query_hat, axis=1),
            jnp.sum(key_hat_grad * key_hat, axis=1),
            lax.dynamic_update_slice_in_dim(
                jnp.zeros((model_width,), F32), query_gain_part, exp_index * head_cols, 0
            ),
            ffn_gain_part,
            lax.dynamic_update_slice_in_dim(
                jnp.zeros((kv_total,), F32), key_gain_part, exp_index * kv_cols, 0
            ),
            jnp.full((kv_total,), local_loss),
        ]
    )
    stats = sum_short(stats.reshape(-1, LANES), "exp", exp_count).reshape(-1)
    query_stat = stats[:ctx_rows, None] / model_width
    key_stat = stats[ctx_rows : 2 * ctx_rows, None] / kv_total
    sums = stats[2 * ctx_rows :]
    query_low = (query_scale * (query_hat_grad - query_hat * query_stat)).astype(BF16)
    key_low = (key_scale * (key_hat_grad - key_hat * key_stat)).astype(BF16)
    grad_low = jnp.concatenate([query_low, key_low, value_grad], axis=1)

    wide_sums = jnp.stack(
        [
            sums[:model_width].reshape(ctx_count, shard_rows),
            sums[model_width : 2 * model_width].reshape(ctx_count, shard_rows),
            jnp.repeat(
                sums[2 * model_width : 2 * model_width + kv_total].reshape(ctx_count, -1), 2, axis=1
            ),
            jnp.broadcast_to(sums[-1], (ctx_count, shard_rows)),
        ],
        axis=-1,
    )
    grad_qkv = dot(normed, grad_low, TN)
    shards = exchange(
        jnp.concatenate(
            [
                grad_qkv.astype(BF16).reshape(ctx_count, shard_rows, qkv_cols),
                grad_out.astype(BF16).reshape(ctx_count, shard_rows, head_cols),
                ride_along(wide_sums),
            ],
            axis=2,
        ),
        "ctx",
    )
    back = exchange_short(grad_low, "exp", exp_index, exp_count)
    shards = jnp.sum(shards.astype(F32), axis=0)
    grad_w_query = shards[:, :head_cols]
    grad_w_key = shards[:, head_cols : head_cols + kv_cols]
    grad_w_value = shards[:, head_cols + kv_cols : qkv_cols]
    grad_w_out = shards[:, qkv_cols : qkv_cols + head_cols]
    tail = parted(shards[:, qkv_cols + head_cols :], 4)
    loss = tail[0, 3] / (valid_count * model_width)

    gain_part = jnp.sum(grad_w_query * w_query.astype(F32), axis=1)
    gain_part += jnp.sum(grad_w_key * w_key.astype(F32), axis=1)
    gain_part += jnp.sum(grad_w_value * w_value.astype(F32), axis=1)
    grad_gain_attn = sum_short(gain_part, "exp", exp_count) / gain_attn.astype(F32)
    normed_rows = dot(back, wide_qkv, NT)
    own_scale = lax.dynamic_slice_in_dim(attn_scale, exp_index * own_rows, own_rows, 0)
    own_hat = hidden_rows * own_scale
    grad_hidden = resid_grad + norm_back(normed_rows, own_hat, own_scale, attn_gain)
    return (
        block_out,
        loss,
        grad_hidden,
        grad_w_query,
        grad_w_key,
        grad_w_value,
        grad_w_out,
        grad_gain_attn,
        tail[:, 0],
        tail[::2, 2],
        tail[:, 1],
        grad_w_gate,
        grad_w_up,
        grad_w_down,
    )


def solution(mesh):
    return jax.shard_map(
        on_device,
        mesh=mesh,
        in_specs=(
            P("ctx", None),
            P(("ctx", "exp"), None),
            P(),
            P(),
            P(("ctx", "exp"), None),
            P(("ctx", "exp"), None),
            P("ctx", "exp"),
            P("ctx", "exp"),
            P("ctx", "exp"),
            P("ctx", "exp"),
            P("ctx"),
            P("ctx"),
            P("ctx"),
            P("ctx"),
            P("ctx", None, "exp"),
            P("ctx", None, "exp"),
            P("ctx", "exp", None),
        ),
        out_specs=(
            P(("ctx", "exp"), None),
            P(),
            P(("ctx", "exp"), None),
            P("ctx", "exp"),
            P("ctx", "exp"),
            P("ctx", "exp"),
            P("ctx", "exp"),
            P("ctx"),
            P("ctx"),
            P("ctx"),
            P("ctx"),
            P("ctx", None, "exp"),
            P("ctx", None, "exp"),
            P("ctx", "exp", None),
        ),
        check_vma=False,
    )
```

```python
import functools

import jax
import jax.numpy as jnp
from jax import lax
from jax.experimental import pallas as pl
from jax.experimental.pallas import tpu as pltpu
from jax.sharding import PartitionSpec as P

HD = 64
BLK = 128
CONT_LEN = 1024
CONT_BLKS = CONT_LEN // BLK
LANES = 128

NORM_EPSILON = 1e-05
ROPE_BASE = 10000.0
MASK_FLOOR = -1e30
F32 = jnp.float32
BF16 = jnp.bfloat16
NT = (((1,), (1,)), ((), ()))
NN = (((1,), (0,)), ((), ()))
TN = (((0,), (0,)), ((), ()))


def dot(left, right, dims):
    return lax.dot_general(left, right, dims, preferred_element_type=F32)


def key_ranges(block, half, tile_blocks):
    cont = block >= half
    inner = jnp.where(cont, (block - half) % CONT_BLKS, 0)
    n_a = jnp.where(cont, half // tile_blocks, block // tile_blocks)
    cont_base = half + (block - half) // CONT_BLKS * CONT_BLKS
    base = jnp.where(cont, cont_base, block // tile_blocks * tile_blocks) * BLK
    return n_a, base, inner // tile_blocks


def gather_blocks(table, total, moves):
    def start(i, carry):
        to = pl.multiple_of(table[i] * BLK, BLK)
        for source, target, sem in moves:
            pltpu.make_async_copy(source(i), target(to), sem).start()
        return carry

    lax.fori_loop(0, total, start, 0)


def wait_all(ref, sem):
    pltpu.make_async_copy(ref, ref, sem).wait()


def rows_of(ref, per_ctx):
    def place(i):
        first = i // 4 * per_ctx + i % 4 * BLK
        return ref.at[pl.ds(pl.multiple_of(first, 16), BLK)]

    return place


def stats_of(ref):
    return lambda i: ref.at[i // 4, i // 2 % 2, :, pl.ds(pl.multiple_of(i % 2 * BLK, BLK), BLK)]


def causal(shape, key_first, query_first, rows_are_queries):
    row = lax.broadcasted_iota(jnp.int32, shape, 0) % BLK
    col = lax.broadcasted_iota(jnp.int32, shape, 1)
    if rows_are_queries:
        return key_first + col <= query_first + row
    return key_first + row <= query_first + col


def to_half(tile, source, target):
    values = tile.astype(F32)
    if source != target:
        values = pltpu.roll(values, HD, 1)
    lane = lax.broadcasted_iota(jnp.int32, values.shape, 1)
    return jnp.where(lane // HD == target, values, 0.0)


def turn(tile, cosine, sine):
    lane = lax.broadcasted_iota(jnp.int32, tile.shape, 1)
    ahead = pltpu.roll(tile, LANES - HD // 2, 1)
    behind = pltpu.roll(tile, HD // 2, 1)
    return tile * cosine + jnp.where(lane % HD < HD // 2, ahead, behind) * sine


def rows_by_head(source_ref, block_rows, target_ref):
    for h in range(4):
        m, g = h // 2, h % 2
        tile = source_ref[block_rows, m * LANES : (m + 1) * LANES]
        target_ref[h * BLK : (h + 1) * BLK, :] = to_half(tile, g, m).astype(BF16)


def rows_by_token(values):
    tiles = []
    for m in range(2):
        first = values[2 * m * BLK : (2 * m + 1) * BLK]
        second = values[(2 * m + 1) * BLK : (2 * m + 2) * BLK]
        tiles.append(to_half(first, m, 0) + to_half(second, m, 1))
    return tiles


def turn_kernel(pre_ref, scale_ref, gain_ref, cos_ref, sin_ref, q_ref, kv_ref):
    for col in range(3):
        lanes = slice(col * LANES, (col + 1) * LANES)
        which = 0 if col < 2 else 1
        hat = pre_ref[:, lanes] * scale_ref[:, which : which + 1]
        turned = turn(hat * gain_ref[:, lanes], cos_ref[...], sin_ref[...]).astype(BF16)
        if which == 0:
            q_ref[:, lanes] = (turned.astype(F32) * HD**-0.5).astype(BF16)
        else:
            kv_ref[:, :LANES] = turned
    kv_ref[:, LANES:] = pre_ref[:, 3 * LANES :].astype(BF16)


def attend_kernel(
    total, half, tile_blocks, table, own, q_in, kv, o_ref, lse_ref, kv_s, q_ref, acc, peak, s_buf, sem
):
    gather_blocks(
        table,
        total,
        [
            (
                rows_of(kv, 4 * BLK),
                lambda to: kv_s.at[pl.ds(to, BLK)],
                sem.at[0],
            )
        ],
    )
    wait_all(kv_s, sem.at[0])
    width = tile_blocks * BLK
    ones = jnp.ones((width, LANES), BF16)

    def query_block(i, carry):
        block = own[i]
        n_a, base, n_b = key_ranges(block, half, tile_blocks)
        rows = pl.ds(pl.multiple_of(i * BLK, BLK), BLK)
        lanes = pl.ds(pl.multiple_of(i % 2 * BLK, BLK), BLK)
        rows_by_head(q_in, rows, q_ref)

        def first_key(j):
            return pl.multiple_of(jnp.where(j < n_a, j * width, base + (j - n_a) * width), BLK)

        def tile(start, masked):
            scores = dot(q_ref[...], kv_s[pl.ds(start, width), :LANES], NT)
            probs = jnp.exp(scores)
            if masked:
                probs = jnp.where(causal(probs.shape, start, block * BLK, True), probs, 0.0)
            acc[...] += dot(probs.astype(BF16), values_at(start), NN)

        def clear_tile(j, carry):
            tile(first_key(j), False)
            return carry

        def store(out, log_sum):
            first, second = rows_by_token(out)
            o_ref[rows, :LANES] = first
            o_ref[rows, LANES:] = second
            for h in range(4):
                lse_ref[i // 2, h : h + 1, lanes] = log_sum[h * BLK : (h + 1) * BLK].T[:1]

        def values_at(start):
            return jnp.concatenate([kv_s[pl.ds(start, width), LANES:], ones], axis=1)

        def score(j):
            return dot(q_ref[...], kv_s[pl.ds(first_key(j), width), :LANES], NT)

        def weigh(scores, j, masked):
            start = first_key(j)
            probs = jnp.exp(scores)
            if masked:
                probs = jnp.where(causal(probs.shape, start, block * BLK, True), probs, 0.0)
            acc[...] += dot(probs.astype(BF16), values_at(start), NN)

        acc[...] = jnp.zeros_like(acc)
        count = n_a + n_b
        s_buf[0] = score(0)

        def two_tiles(i2, carry):
            j = 2 * i2
            s_buf[1] = score(j + 1)
            weigh(s_buf[0], j, False)
            s_buf[0] = score(j + 2)
            weigh(s_buf[1], j + 1, False)
            return carry

        lax.fori_loop(0, count // 2, two_tiles, 0)

        @pl.when(count % 2 == 1)
        def _():
            s_buf[1] = score(count)
            weigh(s_buf[0], count - 1, False)
            weigh(s_buf[1], count, True)

        @pl.when(count % 2 == 0)
        def _():
            weigh(s_buf[0], count, True)

        sums = acc[:, LANES:]
        in_range = (jnp.max(sums) < 2.0**100) & (jnp.min(sums) > 2.0**-40)

        @pl.when(in_range)
        def _():
            store(acc[:, :LANES] / sums, jnp.log(sums))

        @pl.when(jnp.logical_not(in_range))
        def _():
            acc[...] = jnp.zeros_like(acc)
            peak[...] = jnp.full_like(peak, MASK_FLOOR)

            def safe_tile(j, carry):
                start = first_key(j)
                scores = dot(q_ref[...], kv_s[pl.ds(start, width), :LANES], NT)
                seen = causal(scores.shape, start, block * BLK, True)
                scores = jnp.where(seen, scores, MASK_FLOOR)
                old = peak[...]
                new = jnp.maximum(old, jnp.max(scores, axis=1, keepdims=True))
                probs = jnp.where(seen, jnp.exp(scores - new[:, :1]), 0.0)
                keep = jnp.exp(old - new)
                acc[...] = acc[...] * keep[:, :1] + dot(
                    probs.astype(BF16), values_at(start), NN
                )
                peak[...] = new
                return carry

            lax.fori_loop(0, n_a + n_b + 1, safe_tile, 0)
            safe_sums = acc[:, LANES:]
            store(acc[:, :LANES] / safe_sums, peak[...] + jnp.log(safe_sums))

        return carry

    lax.fori_loop(0, 4, query_block, 0)


def query_grad_kernel(
    total,
    half,
    tile_blocks,
    table,
    own,
    q_in,
    do_in,
    o_in,
    lse_in,
    cos_ref,
    sin_ref,
    kv,
    dq_ref,
    kv_s,
    q_ref,
    do_ref,
    lse_ref,
    delta_ref,
    acc,
    sem,
):
    gather_blocks(
        table, total, [(rows_of(kv, 4 * BLK), lambda to: kv_s.at[pl.ds(to, BLK)], sem.at[0])]
    )
    wait_all(kv_s, sem.at[0])
    width = tile_blocks * BLK

    def query_block(i, carry):
        block = own[i]
        n_a, base, n_b = key_ranges(block, half, tile_blocks)
        rows = pl.ds(pl.multiple_of(i * BLK, BLK), BLK)
        lanes = pl.ds(pl.multiple_of(i % 2 * BLK, BLK), BLK)
        rows_by_head(q_in, rows, q_ref)
        do_block = (i + 4 - own[4]) % 4
        do_rows = pl.ds(pl.multiple_of(do_block * BLK, BLK), BLK)
        rows_by_head(do_in, do_rows, do_ref)
        for h in range(4):
            part = slice(h * BLK, (h + 1) * BLK)
            pair = slice(h // 2 * LANES, (h // 2 + 1) * LANES)
            product = do_in[do_rows, pair].astype(F32) * o_in[rows, pair]
            own_half = to_half(product, h % 2, h % 2)
            delta = jnp.sum(own_half, axis=1, keepdims=True)
            delta_ref[part, :] = jnp.broadcast_to(delta, (BLK, LANES))
            row = lse_in[i // 2, h : h + 1, lanes]
            lse_ref[part, :] = jnp.broadcast_to(row, (LANES, BLK)).T

        def first_key(j):
            return pl.multiple_of(jnp.where(j < n_a, j * width, base + (j - n_a) * width), BLK)

        def tile(start, masked):
            keys = kv_s[pl.ds(start, width), :LANES]
            scores = dot(q_ref[...], keys, NT)
            prob_grad = dot(do_ref[...], kv_s[pl.ds(start, width), LANES:], NT)
            probs = jnp.exp(scores - lse_ref[:, :1])
            score_grad = probs * (prob_grad - delta_ref[:, :1])
            if masked:
                seen = causal(probs.shape, start, block * BLK, True)
                score_grad = jnp.where(seen, score_grad, 0.0)
            acc[...] += dot(score_grad.astype(BF16), keys, NN)

        def clear_tile(j, carry):
            tile(first_key(j), False)
            return carry

        acc[...] = jnp.zeros_like(acc)
        lax.fori_loop(0, n_a + n_b, clear_tile, 0)
        tile(first_key(n_a + n_b), True)
        for m, gradient in enumerate(rows_by_token(acc[...])):
            back = turn(gradient * HD**-0.5, cos_ref[rows, :], -sin_ref[rows, :])
            dq_ref[rows, m * LANES : (m + 1) * LANES] = back
        return carry

    lax.fori_loop(0, 4, query_block, 0)


def place(blk, h):
    return (h * 2 + blk) * BLK if blk < 2 else ((blk * 4) + h) * BLK


def spread_heads(source_ref, lanes, target_ref):
    target_ref[...] = jnp.zeros_like(target_ref)
    for blk in range(4):
        for h in range(4):
            m, g = h // 2, h % 2
            rows = slice(place(blk, h), place(blk, h) + BLK)
            tile = source_ref[blk * BLK : (blk + 1) * BLK, lanes]
            target_ref[rows, m * LANES : (m + 1) * LANES] = to_half(tile, m, g).astype(BF16)


def cont_tiles(own, which, half, tile_blocks):
    block = own[2 + which]
    base = half + (block - half) // CONT_BLKS * CONT_BLKS
    return block, block // tile_blocks, (base + CONT_BLKS) // tile_blocks, base // tile_blocks


def pair_probs_kernel(
    total, half, tile_blocks, q_rows, table, own, kv_in, q_all, lse_all, p_ref, pc_ref, q_s, lse_s, k_ref, sem
):
    step = pl.program_id(0)
    width = tile_blocks * BLK
    pair = 2 * tile_blocks

    @pl.when(step == 0)
    def _():
        gather_blocks(
            table,
            total,
            [
                (rows_of(q_all, q_rows), lambda to: q_s.at[pl.ds(to, BLK)], sem.at[0]),
                (stats_of(lse_all), lambda to: lse_s.at[:, pl.ds(to, BLK)], sem.at[1]),
            ],
        )
        spread_heads(kv_in, slice(0, LANES), k_ref)
        wait_all(q_s, sem.at[0])
        wait_all(lse_s, sem.at[1])

    def probs_of(first_row, per_head, j, keys_first, store):
        start = pl.multiple_of(j * width, width)
        keys = k_ref[first_row : first_row + 4 * per_head, :]
        scores = dot(keys, q_s[pl.ds(start, width), :], NT)
        for h in range(4):
            part = slice(h * per_head, (h + 1) * per_head)
            probs = jnp.exp(scores[part] - lse_s[h : h + 1, pl.ds(start, width)])
            if keys_first is not None:
                seen = [causal((BLK, width), first, start, False) for first in keys_first]
                probs = jnp.where(jnp.concatenate(seen, axis=0), probs, 0.0)
            store(part, probs.astype(BF16))

    low = jnp.minimum(own[0], own[1])
    high = jnp.maximum(own[0], own[1])

    def prompt(keys_first):
        for side in range(2):

            def store(part, probs, side=side):
                p_ref[0, part, side * width : (side + 1) * width] = probs

            probs_of(0, 2 * BLK, 2 * step + side, keys_first, store)

    @pl.when((step >= low // pair) & (step <= high // pair))
    def _():
        prompt([own[0] * BLK, own[1] * BLK])

    @pl.when(step > high // pair)
    def _():
        prompt(None)

    @pl.when(step == pl.num_programs(0) - 1)
    def _():
        for which in range(2):
            block, first, stop, base = cont_tiles(own, which, half, tile_blocks)

            def cont_tile(j, carry, which=which, block=block, base=base):
                def store(part, probs):
                    pc_ref[which, j - base, part, :] = probs

                probs_of((8 + 4 * which) * BLK, BLK, j, [block * BLK], store)
                return carry

            lax.fori_loop(first, stop, cont_tile, 0)


def pair_grad_kernel(
    total,
    half,
    tile_blocks,
    q_rows,
    table,
    own,
    kv_in,
    cos_ref,
    sin_ref,
    q_all,
    do_all,
    p_ref,
    pc_ref,
    out_ref,
    q_s,
    do_s,
    parts_s,
    delta_s,
    v_ref,
    dk_ref,
    dv_ref,
    d_buf,
    sem,
):
    step = pl.program_id(0)
    width = tile_blocks * BLK
    pair = 2 * tile_blocks

    @pl.when(step == 0)
    def _():
        gather_blocks(
            table,
            total,
            [
                (rows_of(q_all, q_rows), lambda to: q_s.at[pl.ds(to, BLK)], sem.at[0]),
                (
                    lambda i: do_all.at[
                        i // 4, pl.ds(pl.multiple_of((i + 4 - own[4]) % 4 * BLK, BLK), BLK)
                    ],
                    lambda to: do_s.at[pl.ds(to, BLK)],
                    sem.at[1],
                ),
            ],
        )
        stats = pltpu.make_async_copy(do_all.at[:, pl.ds(4 * BLK, 48)], parts_s, sem.at[2])
        stats.start()
        dk_ref[...] = jnp.zeros_like(dk_ref)
        dv_ref[...] = jnp.zeros_like(dv_ref)
        spread_heads(kv_in, slice(LANES, 2 * LANES), v_ref)
        wait_all(q_s, sem.at[0])
        wait_all(do_s, sem.at[1])
        stats.wait()

        def place_stats(c, carry):
            parts = parts_s[c].astype(F32)
            sums = parts[:16] + parts[16:32] + parts[32:]
            for blk in range(4):
                to = pl.multiple_of(table[4 * c + (blk + own[4]) % 4] * BLK, BLK)
                first, lane = blk // 2 * 8, blk % 2 * BLK
                delta_s[:, pl.ds(to, BLK)] = sums[first : first + 8, lane : lane + BLK]
            return carry

        lax.fori_loop(0, total // 4, place_stats, 0)

    def prob_grad(first_row, per_head, j):
        start = pl.multiple_of(j * width, width)
        values = v_ref[first_row : first_row + 4 * per_head, :]
        return dot(values, do_s[pl.ds(start, width), :], NT)

    def add(first_row, per_head, j, probs, grads_in):
        rows = pl.ds(first_row, 4 * per_head)
        start = pl.multiple_of(j * width, width)
        score_low = []
        for h in range(4):
            part = slice(h * per_head, (h + 1) * per_head)
            shifted_grad = grads_in[part] - delta_s[h : h + 1, pl.ds(start, width)]
            score_low.append((probs[part].astype(F32) * shifted_grad).astype(BF16))
        dv_ref[rows, :] += dot(probs, do_s[pl.ds(start, width), :], NN)
        queries = q_s[pl.ds(start, width), :]
        dk_ref[rows, :] += dot(jnp.concatenate(score_low, axis=0), queries, NN)

    low = jnp.minimum(own[0], own[1])
    last = total // tile_blocks - 1

    @pl.when(step == low // pair)
    def _():
        d_buf[0] = prob_grad(0, 2 * BLK, 2 * step)

    @pl.when(step >= low // pair)
    def _():
        d_buf[1] = prob_grad(0, 2 * BLK, 2 * step + 1)
        add(0, 2 * BLK, 2 * step, p_ref[0, :, :width], d_buf[0])
        d_buf[0] = prob_grad(0, 2 * BLK, jnp.minimum(2 * step + 2, last))
        add(0, 2 * BLK, 2 * step + 1, p_ref[0, :, width:], d_buf[1])

    def collect(ref, blk):
        tile_sum = None
        for h in range(4):
            m, g = h // 2, h % 2
            part = ref[place(blk, h) : place(blk, h) + BLK, m * LANES : (m + 1) * LANES]
            moved = to_half(part, g, m)
            tile_sum = moved if tile_sum is None else tile_sum + moved
        return tile_sum

    @pl.when(step == pl.num_programs(0) - 1)
    def _():
        for which in range(2):
            _, first, stop, base = cont_tiles(own, which, half, tile_blocks)

            def cont_tile(j, carry, which=which, base=base):
                first_row = (8 + 4 * which) * BLK
                grads_in = prob_grad(first_row, BLK, j)
                add(first_row, BLK, j, pc_ref[which, j - base], grads_in)
                return carry

            lax.fori_loop(first, stop, cont_tile, 0)
        for blk in range(4):
            rows = slice(blk * BLK, (blk + 1) * BLK)
            out_ref[rows, :LANES] = turn(collect(dk_ref, blk), cos_ref[rows, :], -sin_ref[rows, :])
            out_ref[rows, LANES:] = collect(dv_ref, blk)


def down_strips(w_ref, pair, width):
    strips = [w_ref[u, :, 2 * width : 3 * width] for u in (2 * pair, 2 * pair + 1)]
    return jnp.concatenate(strips, axis=1)


def expert_kernel(quarters, width, x_ref, w_ref, out_ref, gate_ref, up_ref):
    acts = []
    for u in range(quarters):
        cols = slice(u * width, (u + 1) * width)
        pre = dot(x_ref[...], w_ref[u, :, : 2 * width], NN)
        gate, up = pre[:, :width], pre[:, width:]
        gate_ref[:, cols] = gate
        up_ref[:, cols] = up
        acts.append((gate * jax.nn.sigmoid(gate) * up).astype(BF16))
    out = None
    for pair in range(quarters // 2):
        act = jnp.concatenate(acts[2 * pair : 2 * pair + 2], axis=1)
        part = dot(act, down_strips(w_ref, pair, width), NT)
        out = part if out is None else out + part
    out_ref[...] = out.astype(BF16)


def expert_grad_kernel(
    quarters, width, dy_ref, gate_ref, up_ref, w_ref, wt_ref, dx_ref, dgate_ref, dup_ref, act_ref
):
    total = None
    for pair in range(quarters // 2):
        both = dot(dy_ref[...], down_strips(w_ref, pair, width), NN)
        for side in range(2):
            u = 2 * pair + side
            cols = slice(u * width, (u + 1) * width)
            act_grad = both[:, side * width : (side + 1) * width]
            gate, up = gate_ref[:, cols], up_ref[:, cols]
            sig = jax.nn.sigmoid(gate)
            gate_act = gate * sig
            act_ref[:, cols] = (gate_act * up).astype(BF16)
            gate_grad = (act_grad * up * sig * (1.0 + gate * (1.0 - sig))).astype(BF16)
            up_grad = (act_grad * gate_act).astype(BF16)
            dgate_ref[:, cols] = gate_grad
            dup_ref[:, cols] = up_grad
            grads = jnp.concatenate([gate_grad, up_grad], axis=1)
            part = dot(grads, wt_ref[u], NN)
            total = part if total is None else total + part
    dx_ref[...] = total.astype(BF16)


def in_hbm(values):
    return pltpu.with_memory_space_constraint(values, pltpu.HBM)


def block_of_whole(shape):
    return pl.BlockSpec(shape, lambda i, *_: (0,) * len(shape))


def kernel_call(kernel, name, prefetch, ins, outs, scratch, flops):
    hbm = pl.BlockSpec(memory_space=pl.ANY)
    moved = sum(x.size * x.dtype.itemsize for x, _ in ins)
    return pl.pallas_call(
        kernel,
        out_shape=tuple(outs),
        grid_spec=pltpu.PrefetchScalarGridSpec(
            num_scalar_prefetch=len(prefetch),
            grid=(1,),
            in_specs=[hbm if far else block_of_whole(x.shape) for x, far in ins],
            out_specs=tuple(block_of_whole(out.shape) for out in outs),
            scratch_shapes=scratch,
        ),
        compiler_params=pltpu.CompilerParams(vmem_limit_bytes=48 << 20),
        cost_estimate=pl.CostEstimate(flops=flops, bytes_accessed=moved, transcendentals=0),
        name=name,
    )(*prefetch, *(x for x, _ in ins))


def by_rows(kernel, name, rows, ins, outs, flops):
    def spec(shape):
        if len(shape) == 3:
            return pl.BlockSpec(shape, lambda i: (0, 0, 0))
        return pl.BlockSpec((rows, shape[1]), lambda i: (i, 0))

    return pl.pallas_call(
        kernel,
        out_shape=tuple(pltpu.HBM(out.shape, out.dtype) for out in outs),
        grid=(outs[0].shape[0] // rows,),
        in_specs=[spec(x.shape) for x in ins],
        out_specs=tuple(spec(out.shape) for out in outs),
        compiler_params=pltpu.CompilerParams(vmem_limit_bytes=40 << 20),
        cost_estimate=pl.CostEstimate(flops=flops, bytes_accessed=10**7, transcendentals=0),
        name=name,
    )(*(in_hbm(x) for x in ins))


def expert_forward(rows_in, weights):
    slots, model_width = rows_in.shape
    quarters, _, cols = weights.shape
    width = cols // 3
    hidden = jax.ShapeDtypeStruct((slots, quarters * width), F32)
    return by_rows(
        functools.partial(expert_kernel, quarters, width),
        "expert",
        slots // 5,
        [rows_in, weights],
        [jax.ShapeDtypeStruct((slots, model_width), BF16), hidden, hidden],
        6 * slots * model_width * quarters * width,
    )


def expert_backward(rows_grad, gate_pre, up_pre, weights, turned):
    slots, model_width = rows_grad.shape
    quarters, _, cols = weights.shape
    width = cols // 3
    hidden = jax.ShapeDtypeStruct((slots, quarters * width), BF16)
    return by_rows(
        functools.partial(expert_grad_kernel, quarters, width),
        "expert_grad",
        slots // 2,
        [rows_grad, gate_pre, up_pre, weights, turned],
        [jax.ShapeDtypeStruct((slots, model_width), BF16), hidden, hidden, hidden],
        6 * slots * model_width * quarters * width,
    )


def turn_heads(projected, scales, gain, cosine, sine):
    rows = projected.shape[0]
    out = jax.ShapeDtypeStruct((rows, 2 * LANES), BF16)
    ins = [(x, False) for x in (projected, scales, gain, cosine, sine)]
    return kernel_call(turn_kernel, "turn_heads", (), ins, [out, out], [], 10**6)


def attend(table, own, q, kv_all):
    total = table.shape[0]
    return kernel_call(
        functools.partial(attend_kernel, total, total // 2, 8),
        "attend",
        (table, own),
        [(q, False), (kv_all, True)],
        [
            jax.ShapeDtypeStruct((4 * BLK, 2 * LANES), F32),
            jax.ShapeDtypeStruct((2, 4, 2 * BLK), F32),
        ],
        [
            pltpu.VMEM((total * BLK, 2 * LANES), BF16),
            pltpu.VMEM((4 * BLK, LANES), BF16),
            pltpu.VMEM((4 * BLK, 2 * LANES), F32),
            pltpu.VMEM((4 * BLK, LANES), F32),
            pltpu.VMEM((2, 4 * BLK, 8 * BLK), F32),
            pltpu.SemaphoreType.DMA((1,)),
        ],
        20 * 10**9,
    )


def query_grad(table, own, q, out_grad, heads, lse, cosine, sine, kv_all):
    total = table.shape[0]
    ins = [(x, False) for x in (q, out_grad, heads, lse, cosine, sine)]
    return kernel_call(
        functools.partial(query_grad_kernel, total, total // 2, 4),
        "query_grad",
        (table, own),
        ins + [(kv_all, True)],
        [jax.ShapeDtypeStruct((4 * BLK, 2 * LANES), F32)],
        [
            pltpu.VMEM((total * BLK, 2 * LANES), BF16),
            pltpu.VMEM((4 * BLK, LANES), BF16),
            pltpu.VMEM((4 * BLK, LANES), BF16),
            pltpu.VMEM((4 * BLK, LANES), F32),
            pltpu.VMEM((4 * BLK, LANES), F32),
            pltpu.VMEM((4 * BLK, LANES), F32),
            pltpu.SemaphoreType.DMA((1,)),
        ],
        30 * 10**9,
    )[0]


def pair_call(kernel, name, table, own, ins, blocks, outs, out_blocks, scratch, flops):
    steps = table.shape[0] // 8

    def tile_place(step, table_ref, own_ref):
        return (jnp.maximum(step, jnp.minimum(own_ref[0], own_ref[1]) // 8), 0, 0)

    def spec(shape, block):
        if block is None:
            return pl.BlockSpec(memory_space=pl.ANY)
        if block == shape:
            return pl.BlockSpec(shape, lambda *_: (0,) * len(shape))
        return pl.BlockSpec(block, tile_place)

    return pl.pallas_call(
        kernel,
        out_shape=tuple(
            out if out.dtype == F32 else pltpu.HBM(out.shape, out.dtype) for out in outs
        ),
        grid_spec=pltpu.PrefetchScalarGridSpec(
            num_scalar_prefetch=2,
            grid=(steps,),
            in_specs=[spec(x.shape, block) for x, block in zip(ins, blocks)],
            out_specs=tuple(spec(x.shape, block) for x, block in zip(outs, out_blocks)),
            scratch_shapes=scratch,
        ),
        compiler_params=pltpu.CompilerParams(vmem_limit_bytes=48 << 20),
        cost_estimate=pl.CostEstimate(flops=flops, bytes_accessed=4 * 10**7, transcendentals=0),
        name=name,
    )(table, own, *ins)


PROB_BLOCK = (1, 8 * BLK, 8 * BLK)
CONT_SHAPE = (2, CONT_BLKS // 4, 4 * BLK, 4 * BLK)


def pair_probs(table, own, kv, q_all, q_rows, lse_all):
    total = table.shape[0]
    return pair_call(
        functools.partial(pair_probs_kernel, total, total // 2, 4, q_rows),
        "pair_probs",
        table,
        own,
        [kv, q_all, lse_all],
        [kv.shape, None, None],
        [
            jax.ShapeDtypeStruct((total // 8,) + PROB_BLOCK[1:], BF16),
            jax.ShapeDtypeStruct(CONT_SHAPE, BF16),
        ],
        [PROB_BLOCK, CONT_SHAPE],
        [
            pltpu.VMEM((total * BLK, 2 * LANES), BF16),
            pltpu.VMEM((8, total * BLK), F32),
            pltpu.VMEM((16 * BLK, 2 * LANES), BF16),
            pltpu.SemaphoreType.DMA((2,)),
        ],
        20 * 10**9,
    )


def pair_grad(table, own, kv, cosine, sine, q_all, q_rows, do_all, probs):
    total = table.shape[0]
    return pair_call(
        functools.partial(pair_grad_kernel, total, total // 2, 4, q_rows),
        "pair_grad",
        table,
        own,
        [kv, cosine, sine, q_all, do_all, *(in_hbm(x) for x in probs)],
        [kv.shape, cosine.shape, sine.shape, None, None, PROB_BLOCK, CONT_SHAPE],
        [jax.ShapeDtypeStruct((4 * BLK, 2 * LANES), F32)],
        [(4 * BLK, 2 * LANES)],
        [
            pltpu.VMEM((total * BLK, 2 * LANES), BF16),
            pltpu.VMEM((total * BLK, 2 * LANES), BF16),
            pltpu.VMEM((total // 4, 48, 2 * LANES), BF16),
            pltpu.VMEM((8, total * BLK), F32),
            pltpu.VMEM((16 * BLK, 2 * LANES), BF16),
            pltpu.VMEM((16 * BLK, 2 * LANES), F32),
            pltpu.VMEM((16 * BLK, 2 * LANES), F32),
            pltpu.VMEM((2, 8 * BLK, 4 * BLK), F32),
            pltpu.SemaphoreType.DMA((3,)),
        ],
        30 * 10**9,
    )[0]


def turn_tables(position):
    half_dim = HD // 2
    frequency = ROPE_BASE ** (-(jnp.arange(half_dim, dtype=F32) * 2.0 / HD))
    angles = position[:, None] * frequency[None, :]
    cosine, sine = jnp.cos(angles), jnp.sin(angles)
    return jnp.concatenate([cosine] * 4, axis=1), jnp.concatenate([-sine, sine] * 2, axis=1)


def norm_back(grad_normed, hat_values, scale_values, gain_values):
    grad_hat = grad_normed * gain_values
    return scale_values * (
        grad_hat - hat_values * jnp.mean(grad_hat * hat_values, axis=-1, keepdims=True)
    )


def pieces(values, count):
    parts = []
    for _ in range(count):
        part = lax.reduce_precision(values, 8, 7)
        parts.append(part.astype(BF16))
        values = values - part
    return parts


def exchange(values, axis):
    return lax.all_to_all(values, axis, split_axis=0, concat_axis=0, tiled=True)


def spread(values, axis, count):
    return exchange(jnp.broadcast_to(values[None], (count,) + values.shape), axis)


def shifted(values, axis, count):
    parts = [values]
    for step in range(1, count):
        parts.append(lax.ppermute(values, axis, [(i, (i + step) % count) for i in range(count)]))
    return parts


def sum_short(values, axis, count):
    parts = shifted(values, axis, count)
    while len(parts) > 1:
        half = len(parts) // 2
        parts = [parts[i] + parts[i + half] for i in range(half)]
    return parts[0]


def exchange_short(values, axis, index, count):
    rows = values.shape[0] // count
    come = []
    for step in range(count):
        to = (index + step) % count
        part = lax.dynamic_slice_in_dim(values, to * rows, rows, 0)
        if step > 0:
            part = lax.ppermute(part, axis, [(i, (i + step) % count) for i in range(count)])
        come.append(part)
    return jnp.concatenate(come, axis=1)


def with_stats(rows, stats):
    stats = jnp.pad(stats, ((0, 0), (0, 4), (0, 0)))
    parts = jnp.stack(pieces(stats, 3), axis=0).reshape(-1, rows.shape[1])
    return jnp.concatenate([rows, parts], axis=0)


def ride_along(values):
    parts = jnp.concatenate(pieces(values, 3), axis=-1)
    return jnp.pad(parts, ((0, 0), (0, 0), (0, LANES - parts.shape[-1])))


def parted(sums, count):
    return sum(sums[:, i * count : (i + 1) * count] for i in range(3))


def on_device(
    hidden_in,
    teacher,
    valid,
    block_of,
    routes,
    gates,
    w_query,
    w_key,
    w_value,
    w_out,
    gain_attn,
    gain_query,
    gain_key,
    gain_ffn,
    w_gate,
    w_up,
    w_down,
):
    ctx_count = lax.axis_size("ctx")
    exp_count = lax.axis_size("exp")
    ctx_index = lax.axis_index("ctx")
    exp_index = lax.axis_index("exp")
    ctx_rows, model_width = hidden_in.shape
    own_rows = ctx_rows // exp_count
    token_total = block_of.shape[0] * BLK
    head_cols = w_query.shape[1]
    kv_cols = w_key.shape[1]
    kv_total = kv_cols * exp_count
    qkv_cols = head_cols + 2 * kv_cols
    shard_rows = w_query.shape[0]

    own_weights = jnp.concatenate([w_query, w_key, w_value], axis=1)
    gain_row = jnp.concatenate([gain_attn, gain_query, gain_ffn, gain_key])
    gain_rows = jnp.pad(
        gain_row, (0, 8 * own_weights.shape[1] - gain_row.shape[0])
    ).reshape(8, -1)
    first_parts = spread(jnp.concatenate([own_weights, gain_rows], axis=0), "ctx", ctx_count)
    full_qkv = first_parts[:, :shard_rows].reshape(model_width, qkv_cols)
    gains = first_parts[:, shard_rows:].reshape(ctx_count, -1)[:, : gain_row.shape[0]].astype(F32)
    attn_gain = gains[:, :shard_rows].reshape(model_width)
    query_gain_all = gains[:, shard_rows : 2 * shard_rows].reshape(model_width)
    ffn_gain = gains[:, 2 * shard_rows : 3 * shard_rows].reshape(model_width)
    key_gain_all = gains[:, 3 * shard_rows :].reshape(kv_total)
    query_gain = lax.dynamic_slice_in_dim(query_gain_all, exp_index * head_cols, head_cols)
    key_gain = lax.dynamic_slice_in_dim(key_gain_all, exp_index * kv_cols, kv_cols)

    width = w_gate.shape[2]
    own_expert = jnp.concatenate([w_gate[0], w_up[0], w_down[0].T], axis=1)
    expert = lax.all_gather(own_expert, "exp", axis=0, tiled=False)

    hidden_f = hidden_in.astype(F32)
    attn_scale = lax.rsqrt(jnp.mean(hidden_f * hidden_f, axis=-1, keepdims=True) + NORM_EPSILON)
    attn_hat = hidden_f * attn_scale
    normed = (attn_hat * attn_gain).astype(BF16)
    projected = dot(normed, full_qkv, NN)
    query_pre = projected[:, :head_cols]
    key_pre = projected[:, head_cols : head_cols + kv_cols]
    squares = jnp.stack(
        [jnp.sum(query_pre * query_pre, axis=1), jnp.sum(key_pre * key_pre, axis=1)]
    )
    query_square, key_square = sum_short(squares, "exp", exp_count)
    query_scale = lax.rsqrt(query_square / model_width + NORM_EPSILON)[:, None]
    key_scale = lax.rsqrt(key_square / kv_total + NORM_EPSILON)[:, None]
    query_hat = query_pre * query_scale
    key_hat = key_pre * key_scale
    own_blocks = lax.dynamic_slice_in_dim(block_of, ctx_index * 4, 4)
    own = jnp.concatenate([own_blocks, jnp.full((1,), exp_index, jnp.int32)])
    token_ids = (own_blocks[:, None] * BLK + jnp.arange(BLK, dtype=jnp.int32)[None]).reshape(-1)
    prompt_len = token_total // 2
    position = jnp.where(
        token_ids >= prompt_len, prompt_len + (token_ids - prompt_len) % CONT_LEN, token_ids
    ).astype(F32)
    cosine, sine = turn_tables(position)
    queries_rot, own_kv = turn_heads(
        projected,
        jnp.concatenate([query_scale, key_scale], axis=1),
        jnp.concatenate([query_gain, key_gain])[None],
        cosine,
        sine,
    )
    kv_all = lax.all_gather(own_kv, "ctx", axis=0, tiled=True)
    own_out, _, expert = lax.optimization_barrier((w_out, own_kv, expert))
    out_parts = shifted(
        spread(own_out, "ctx", ctx_count).reshape(model_width, head_cols), "exp", exp_count
    )
    wide_out = jnp.concatenate(out_parts, axis=1)
    wide_out, later_q = lax.optimization_barrier((wide_out, queries_rot))
    q_all = lax.all_gather(later_q, "ctx", axis=0, tiled=True)
    expert_total = ctx_count
    capacity = max(2, own_rows * routes.shape[1] * 5 // (expert_total * 4))
    slots = expert_total * capacity
    names = routes[:, :, None] == jnp.arange(expert_total, dtype=jnp.int32)[None, None, :]
    named = jnp.any(names, axis=1)
    gate_of = jnp.sum(jnp.where(names, gates[:, :, None], 0.0), axis=1)
    before = jnp.tril(jnp.ones((own_rows, own_rows), BF16), -1)
    rank = dot(before, named.astype(BF16), NN).astype(jnp.int32)
    slot_rank = jnp.where(named, rank, -1).T[:, None, :]
    holds = slot_rank == jnp.arange(capacity, dtype=jnp.int32)[None, :, None]
    pick = holds.astype(BF16).reshape(slots, own_rows)
    weigh = jnp.where(holds, gate_of.T[:, None, :], 0.0).reshape(slots, own_rows)
    slot_gate = jnp.sum(weigh, axis=1, keepdims=True)

    kv_all, wide_out, pick, weigh, slot_gate = lax.optimization_barrier(
        (kv_all, wide_out, pick, weigh, slot_gate)
    )
    heads_f, lse = attend(block_of, own, queries_rot, kv_all)
    heads_low = heads_f.astype(BF16)

    own_heads = exchange_short(heads_low, "exp", exp_index, exp_count)
    stat_rows = jnp.pad(lse, ((0, 0), (0, 28), (0, 0)))
    lse_all = lax.all_gather(stat_rows, "ctx", axis=0, tiled=False)
    attn_rows = dot(own_heads, wide_out, NT)
    hidden_rows = lax.dynamic_slice_in_dim(hidden_in, exp_index * own_rows, own_rows, 0)
    hidden_rows = hidden_rows.astype(F32)
    resid = hidden_rows + attn_rows
    ffn_scale = lax.rsqrt(jnp.mean(resid * resid, axis=-1, keepdims=True) + NORM_EPSILON)
    ffn_hat = resid * ffn_scale
    normed_ffn = (ffn_hat * ffn_gain).astype(BF16)

    def send(rows):
        return exchange(rows.reshape(ctx_count, capacity, model_width), "ctx").reshape(
            slots, model_width
        )

    expert_in = send(dot(pick, normed_ffn, NN).astype(BF16))
    expert_in, q_all = lax.optimization_barrier((expert_in, q_all))
    expert_out, gate_pre, up_pre = expert_forward(expert_in, expert)
    returned = send(expert_out)
    turned = expert[:, :, : 2 * width].transpose(0, 2, 1)
    returned, q_all, later_qkv, turned = lax.optimization_barrier(
        (returned, q_all, full_qkv, turned)
    )
    moe_parts = dot(jnp.concatenate(pieces(weigh, 2), axis=1), returned, TN)
    moe_rows = moe_parts[:own_rows] + moe_parts[own_rows:]
    block_out = resid + moe_rows

    row_start = (ctx_index * exp_count + exp_index) * own_rows
    row_valid = lax.dynamic_slice_in_dim(valid, row_start, own_rows, 0).astype(F32)
    valid_count = jnp.sum(valid.astype(F32))
    misfit = block_out - teacher.astype(F32)
    local_loss = jnp.sum(row_valid[:, None] * misfit * misfit)
    out_grad_rows = misfit * row_valid[:, None] * (token_total / valid_count)
    copy_grad = dot(
        jnp.concatenate([pick, pick], axis=1),
        jnp.concatenate(pieces(out_grad_rows, 2), axis=0),
        NN,
    )
    copy_grad = (slot_gate * copy_grad).astype(BF16)
    copy_grad, lse_all = lax.optimization_barrier((copy_grad, lse_all))
    grad_copies = send(copy_grad)
    probs = pair_probs(
        block_of,
        own,
        own_kv,
        q_all,
        ctx_rows,
        lse_all[:, :, :8],
    )
    wide_qkv = jnp.concatenate(shifted(later_qkv, "exp", exp_count), axis=1)
    grad_copies, probs = lax.optimization_barrier((grad_copies, probs))
    input_grad, gate_grad, up_grad, hidden_act = expert_backward(
        grad_copies, gate_pre, up_pre, expert, turned
    )
    arrived_grad = send(input_grad)

    gate_part = dot(expert_in, gate_grad, TN)
    up_part = dot(expert_in, up_grad, TN)
    down_part = dot(hidden_act, grad_copies, TN)
    gate_part = gate_part.reshape(model_width, exp_count, width).transpose(1, 0, 2)
    up_part = up_part.reshape(model_width, exp_count, width).transpose(1, 0, 2)
    arrived_grad, wide_qkv, gate_part, up_part, down_part = lax.optimization_barrier(
        (arrived_grad, wide_qkv, gate_part, up_part, down_part)
    )
    ffn_normed_grad = dot(pick, arrived_grad, TN)

    ffn_gain_part = jnp.sum(ffn_normed_grad * ffn_hat, axis=0)
    resid_grad = out_grad_rows + norm_back(ffn_normed_grad, ffn_hat, ffn_scale, ffn_gain)
    branch_rows = resid_grad.astype(BF16)

    do_parts = dot(branch_rows, wide_out, NN).astype(BF16)
    come = [do_parts[:, :head_cols]]
    for step in range(1, exp_count):
        part = do_parts[:, step * head_cols : (step + 1) * head_cols]
        turns = [(i, (i - step) % exp_count) for i in range(exp_count)]
        come.append(lax.ppermute(part, "exp", turns))
    out_grad = jnp.concatenate(come, axis=0)
    heads_turned = lax.dynamic_slice_in_dim(
        jnp.concatenate([heads_f, heads_f], axis=0), exp_index * own_rows, ctx_rows, 0
    )
    branch_parts = shifted(branch_rows, "exp", exp_count)
    head_of = jnp.arange(head_cols, dtype=jnp.int32)[None] // HD
    head_ones = (head_of == jnp.arange(4, dtype=jnp.int32)[:, None]).astype(F32)
    delta = lax.dot_general(
        head_ones,
        out_grad.astype(F32) * heads_turned,
        NT,
        precision=lax.Precision.HIGHEST,
        preferred_element_type=F32,
    )
    delta = delta.reshape(4, 2, 2 * BLK).transpose(1, 0, 2)
    do_all = lax.all_gather(with_stats(out_grad, delta), "ctx", axis=0, tiled=False)
    query_n_grad = query_grad(
        block_of, own, queries_rot, out_grad, heads_f, lse, cosine, sine, kv_all
    )

    grad_out = None
    for step, part in enumerate(branch_parts):
        first = (exp_index - step) % exp_count * own_rows
        term = dot(part, lax.dynamic_slice_in_dim(heads_low, first, own_rows, 0), TN)
        grad_out = term if grad_out is None else grad_out + term

    do_all, query_n_grad, grad_out, gate_part, up_part, down_part = lax.optimization_barrier(
        (do_all, query_n_grad, grad_out, gate_part, up_part, down_part)
    )
    grad_w_gate = lax.psum_scatter(gate_part, "exp", scatter_dimension=0, tiled=True)
    grad_w_up = lax.psum_scatter(up_part, "exp", scatter_dimension=0, tiled=True)
    grad_w_down = lax.psum_scatter(down_part, "exp", scatter_dimension=0, tiled=True)[None]

    pair_grads = pair_grad(
        block_of,
        own,
        own_kv,
        cosine,
        sine,
        q_all,
        ctx_rows,
        do_all,
        probs,
    )
    key_n_grad = pair_grads[:, :kv_cols]
    value_grad = pair_grads[:, kv_cols:].astype(BF16)
    query_gain_part = jnp.sum(query_n_grad * query_hat, axis=0)
    key_gain_part = jnp.sum(key_n_grad * key_hat, axis=0)
    query_hat_grad = query_n_grad * query_gain
    key_hat_grad = key_n_grad * key_gain
    stats = jnp.concatenate(
        [
            jnp.sum(query_hat_grad * query_hat, axis=1),
            jnp.sum(key_hat_grad * key_hat, axis=1),
            lax.dynamic_update_slice_in_dim(
                jnp.zeros((model_width,), F32), query_gain_part, exp_index * head_cols, 0
            ),
            ffn_gain_part,
            lax.dynamic_update_slice_in_dim(
                jnp.zeros((kv_total,), F32), key_gain_part, exp_index * kv_cols, 0
            ),
            jnp.full((kv_total,), local_loss),
        ]
    )
    stats = sum_short(stats.reshape(-1, LANES), "exp", exp_count).reshape(-1)
    query_stat = stats[:ctx_rows, None] / model_width
    key_stat = stats[ctx_rows : 2 * ctx_rows, None] / kv_total
    sums = stats[2 * ctx_rows :]
    query_low = (query_scale * (query_hat_grad - query_hat * query_stat)).astype(BF16)
    key_low = (key_scale * (key_hat_grad - key_hat * key_stat)).astype(BF16)
    grad_low = jnp.concatenate([query_low, key_low, value_grad], axis=1)

    wide_sums = jnp.stack(
        [
            sums[:model_width].reshape(ctx_count, shard_rows),
            sums[model_width : 2 * model_width].reshape(ctx_count, shard_rows),
            jnp.repeat(
                sums[2 * model_width : 2 * model_width + kv_total].reshape(ctx_count, -1), 2, axis=1
            ),
            jnp.broadcast_to(sums[-1], (ctx_count, shard_rows)),
        ],
        axis=-1,
    )
    grad_qkv = dot(normed, grad_low, TN)
    shards = exchange(
        jnp.concatenate(
            [
                grad_qkv.astype(BF16).reshape(ctx_count, shard_rows, qkv_cols),
                grad_out.astype(BF16).reshape(ctx_count, shard_rows, head_cols),
                ride_along(wide_sums),
            ],
            axis=2,
        ),
        "ctx",
    )
    back = exchange_short(grad_low, "exp", exp_index, exp_count)
    shards = jnp.sum(shards.astype(F32), axis=0)
    grad_w_query = shards[:, :head_cols]
    grad_w_key = shards[:, head_cols : head_cols + kv_cols]
    grad_w_value = shards[:, head_cols + kv_cols : qkv_cols]
    grad_w_out = shards[:, qkv_cols : qkv_cols + head_cols]
    tail = parted(shards[:, qkv_cols + head_cols :], 4)
    loss = tail[0, 3] / (valid_count * model_width)

    gain_part = jnp.sum(grad_w_query * w_query.astype(F32), axis=1)
    gain_part += jnp.sum(grad_w_key * w_key.astype(F32), axis=1)
    gain_part += jnp.sum(grad_w_value * w_value.astype(F32), axis=1)
    grad_gain_attn = sum_short(gain_part, "exp", exp_count) / gain_attn.astype(F32)
    normed_rows = dot(back, wide_qkv, NT)
    own_scale = lax.dynamic_slice_in_dim(attn_scale, exp_index * own_rows, own_rows, 0)
    own_hat = hidden_rows * own_scale
    grad_hidden = resid_grad + norm_back(normed_rows, own_hat, own_scale, attn_gain)
    return (
        block_out,
        loss,
        grad_hidden,
        grad_w_query,
        grad_w_key,
        grad_w_value,
        grad_w_out,
        grad_gain_attn,
        tail[:, 0],
        tail[::2, 2],
        tail[:, 1],
        grad_w_gate,
        grad_w_up,
        grad_w_down,
    )


def solution(mesh):
    return jax.shard_map(
        on_device,
        mesh=mesh,
        in_specs=(
            P("ctx", None),
            P(("ctx", "exp"), None),
            P(),
            P(),
            P(("ctx", "exp"), None),
            P(("ctx", "exp"), None),
            P("ctx", "exp"),
            P("ctx", "exp"),
            P("ctx", "exp"),
            P("ctx", "exp"),
            P("ctx"),
            P("ctx"),
            P("ctx"),
            P("ctx"),
            P("ctx", None, "exp"),
            P("ctx", None, "exp"),
            P("ctx", "exp", None),
        ),
        out_specs=(
            P(("ctx", "exp"), None),
            P(),
            P(("ctx", "exp"), None),
            P("ctx", "exp"),
            P("ctx", "exp"),
            P("ctx", "exp"),
            P("ctx", "exp"),
            P("ctx"),
            P("ctx"),
            P("ctx"),
            P("ctx"),
            P("ctx", None, "exp"),
            P("ctx", None, "exp"),
            P("ctx", "exp", None),
        ),
        check_vma=False,
    )
```
